32 devices in a mesh: section: 2 (over core), dp: 8 (over z, y), tensor: 2 (over x).
Axes of the slice: x: 2, y: 2, z: 4, core: 2. Of those that a mesh axis runs over, the one named last changes fastest.
Arguments:
- inputs: bfloat16 [2, 4096, 767], P(None, ('dp', 'tensor')), may hold values from -6 to 6
- doc_lengths: int32 [2, 8, 4], P(None, 'dp'), may hold values from 1 to 256, 512 in all within a row
- attn_gain: float32 [2, 768], P('section'), may hold values from 0.5 to 1.5
- qkv_weight: bfloat16 [2, 768, 3, 768], P('section', None, None, 'tensor'), may hold values from -0.21875 to 0.21875
- qv_bias: float32 [2, 2, 768], P('section', None, 'tensor'), may hold values from -3 to 3
- out_weight: bfloat16 [2, 768, 768], P('section', 'tensor'), may hold values from -1.25 to 1.25
- out_bias: float32 [2, 768], P('section'), may hold values from -3 to 3
- mlp_gain: float32 [2, 768], P('section'), may hold values from 0.5 to 1.5
- up_weight: bfloat16 [2, 768, 3072], P('section', None, 'tensor'), may hold values from -0.21875 to 0.21875
- up_bias: float32 [2, 3072], P('section', 'tensor'), may hold values from -3 to 3
- down_weight: bfloat16 [2, 3072, 768], P('section', 'tensor'), may hold values from -0.21875 to 0.21875
- down_bias: float32 [2, 768], P('section'), may hold values from -3 to 3
- cotangent: bfloat16 [2, 4096, 767], P(None, ('dp', 'tensor')), may hold values from -6 to 6
Outputs:
- out: bfloat16 [2, 4096, 767], P('section', ('dp', 'tensor'))
- grad_in: bfloat16 [2, 4096, 767], P('section', ('dp', 'tensor'))
- grad_attn_gain: float32 [2, 768], P('section')
- grad_qkv_weight: float32 [2, 768, 3, 768], P('section', None, None, 'tensor')
- grad_qv_bias: float32 [2, 2, 768], P('section', None, 'tensor')
- grad_out_weight: float32 [2, 768, 768], P('section', 'tensor')
- grad_out_bias: float32 [2, 768], P('section')
- grad_mlp_gain: float32 [2, 768], P('section')
- grad_up_weight: float32 [2, 768, 3072], P('section', None, 'tensor')
- grad_up_bias: float32 [2, 3072], P('section', 'tensor')
- grad_down_weight: float32 [2, 3072, 768], P('section', 'tensor')
- grad_down_bias: float32 [2, 768], P('section')
The draws below stay inside these ranges and needn't reach their ends.
Inputs may be any that keep to these rules, and one draw needn't show every extreme that they name: `doc_lengths`: each micro-batch of a data group holds 4 documents whose lengths sum to 512; the longest is 256.
All inputs are finite; a program needn't handle non-finite values.
Results may differ from the reference program's by a relative error of at most 0.02.
Values may be sent and summed in bfloat16 or wider, within the bound.
No kernel may reach another device: no remote copies, remote signals or barrier semaphores. Data moves between devices by JAX's collectives and lax.ppermute only.
A program may use at most 192 MiB of HBM per device.

```python
import math
import jax
import jax.numpy as jnp
import numpy as np
from jax import lax

D = 768
HEADS = 12
HEAD_DIM = 64
FF = 3072
MB = 512
MICRO = 2
DOCS = 4
CW = 767
LAYERS = 2
GROUPS = 8
ROWS = 4096
N_DP = 8


def block_levels(own_key, dims, pieces, least, largest):
    gain = 1.0
    for position, parts in pieces:
        draws = jax.random.uniform(jax.random.fold_in(jax.random.fold_in(own_key, 6), position), (parts,), jnp.float32, least / len(pieces), largest / len(pieces))
        gain = gain * jnp.repeat(jnp.exp(draws), dims[position] // parts).reshape((-1,) + (1,) * (len(dims) - 1 - position))
    return gain


def length_profile(count, total, reach, lean):
    loads = [(1 << 20) // math.isqrt(grade ** lean) + 1 for grade in range(2, count + 1)]
    rest, given = total - reach - (count - 1), [1] * (count - 1)
    while rest > 0:
        candidates = [i for i in range(count - 1) if given[i] < reach]
        pool, budget = sum([loads[i] for i in candidates]), rest
        for i in candidates:
            more = min(reach - given[i], max(1, budget * loads[i] // pool), rest)
            given[i] = given[i] + more
            rest = rest - more
    return np.array([reach] + given)


def ragged(key, amount, total, limit, lean):
    if amount == 2:
        one = jax.random.randint(key, (), max(1, total - limit), min(limit, total - 1) + 1)
        return jnp.stack([one, total - one])
    sizes = jnp.asarray(length_profile(amount, total, limit, lean), jnp.int32)
    couples = (amount - 1) // 2
    giver, sink = sizes[1:1 + 2 * couples:2], sizes[2:2 + 2 * couples:2]
    room = jnp.minimum(giver - 1, limit - sink)
    shifted = jax.random.randint(jax.random.fold_in(key, 1), (couples,), 0, 1 << 20) % (room + 1)
    sizes = sizes.at[1:1 + 2 * couples:2].set(giver - shifted).at[2:2 + 2 * couples:2].set(sink + shifted)
    return sizes[jax.random.permutation(jax.random.fold_in(key, 2), amount)]


def bell_draw(rng, shape, scale, bound, cuts=(), held_as=jnp.bfloat16):
    values = jax.random.normal(rng, shape, jnp.float32) * scale
    if len(cuts) > 0:
        values = block_levels(rng, shape, cuts, -0.22, 0.18) * values
    return jnp.clip(values, min=-bound, max=bound).astype(held_as)


def setup_inputs(seed: int = 0) -> dict:
    key_of = jax.random.split(jax.random.key(seed), 14)
    return {
        "inputs": bell_draw(key_of[0], (MICRO, ROWS, CW), 1.0, 6.0, ((1, 16),)),
        "doc_lengths": jax.vmap(lambda own: ragged(own, DOCS, MB, MB // 2, 2))(jax.random.split(key_of[1], MICRO * GROUPS)).reshape((MICRO, GROUPS, DOCS)).astype(jnp.int32),
        "attn_gain": jnp.clip(1.0 + 0.1 * jax.random.normal(key_of[2], (LAYERS, D), jnp.float32), 0.5, 1.5),
        "qkv_weight": bell_draw(key_of[3], (LAYERS, D, 3, D), D ** -0.5, 0.21875, ((0, 2), (3, 2))),
        "qv_bias": bell_draw(key_of[4], (LAYERS, 2, D), 0.5, 3.0, ((0, 2), (2, 2)), jnp.float32),
        "out_weight": bell_draw(key_of[5], (LAYERS, D, D), (D // 32) ** -0.5, 1.25, ((0, 2), (1, 2))),
        "out_bias": bell_draw(key_of[6], (LAYERS, D), 0.5, 3.0, ((0, 2),), jnp.float32),
        "mlp_gain": jnp.clip(1.0 + 0.1 * jax.random.normal(key_of[7], (LAYERS, D), jnp.float32), 0.5, 1.5),
        "up_weight": bell_draw(key_of[8], (LAYERS, D, FF), D ** -0.5, 0.21875, ((0, 2), (2, 2))),
        "up_bias": bell_draw(key_of[9], (LAYERS, FF), 0.5, 3.0, ((0, 2), (1, 2)), jnp.float32),
        "down_weight": bell_draw(key_of[10], (LAYERS, FF, D), (FF // 4) ** -0.5, 0.21875, ((0, 2), (1, 2))),
        "down_bias": bell_draw(key_of[11], (LAYERS, D), 0.5, 3.0, ((0, 2),), jnp.float32),
        "cotangent": bell_draw(key_of[12], (MICRO, ROWS, CW), 1.0, 6.0, ((1, 16),)),
    }


@jax.custom_vjp
def low(v):
    return lax.optimization_barrier(v.astype(jnp.bfloat16)).astype(jnp.float32)

@jax.custom_vjp
def low_back(v):
    return v

def low_keep(v):
    return (low(v), None)

def low_pass(kept, grad):
    return (grad,)

def back_keep(v):
    return (v, None)

def back_low(kept, grad):
    return (low(grad),)
low.defvjp(low_keep, low_pass)
low_back.defvjp(back_keep, back_low)
EPS = 1e-05
NEG = -1e+30
HIGH = lax.Precision.HIGHEST

def compress_rows(branch):
    return (branch - lax.optimization_barrier(jnp.mean(branch, axis=-1, keepdims=True)))[:, :-1]

def crms_norm(rows_in, gain_vec):
    expanded = jnp.concatenate([rows_in, -lax.optimization_barrier(jnp.sum(rows_in, axis=-1, keepdims=True))], axis=-1)
    scaling = lax.rsqrt(lax.optimization_barrier(jnp.mean(expanded * expanded, axis=-1, keepdims=True)) + EPS)
    return expanded * scaling * gain_vec

def doc_mask(lengths, row_count):
    bounds = jnp.cumsum(lengths)
    places = jnp.arange(row_count, dtype=jnp.int32)
    owners = lax.optimization_barrier(jnp.sum((places[:, None] >= bounds[None, :-1]).astype(jnp.int32), axis=1))
    return (owners[:, None] == owners[None, :]) & (places[None, :] <= places[:, None])

def attend(queries, key_rows, value_rows, allowed):
    row_count = queries.shape[0]
    block_rows = min(512, row_count)
    scaling = HEAD_DIM ** (-0.5)

    def one_block(block_index):
        first_row = (block_index * block_rows).astype(jnp.int32)
        query_block = lax.dynamic_slice_in_dim(queries, first_row, block_rows, 0)
        mask_block = lax.dynamic_slice_in_dim(allowed, first_row, block_rows, 0)
        scores = low_back(jnp.einsum('qhd,khd->hqk', query_block, key_rows, precision=HIGH) * scaling)
        scores = jnp.where(mask_block[None], scores, NEG)
        row_peak = lax.optimization_barrier(jnp.max(scores, axis=-1, keepdims=True))
        exponents = jnp.exp(scores - row_peak)
        probs_low = low(exponents / lax.optimization_barrier(jnp.sum(exponents, axis=-1, keepdims=True)))
        return jnp.einsum('hqk,khd->qhd', probs_low, value_rows, precision=HIGH)
    blocks = lax.map(jax.checkpoint(one_block), jnp.arange(row_count // block_rows, dtype=jnp.int32))
    return blocks.reshape(row_count, queries.shape[1], queries.shape[2])

def layer(rows_in, allowed, attn_gain, qkv_weight, qv_bias, out_weight, out_bias, mlp_gain, up_weight, up_bias, down_weight, down_bias):
    row_count = rows_in.shape[0]
    normed = low(crms_norm(rows_in, attn_gain))
    projected = jnp.dot(normed, qkv_weight.reshape(D, 3 * D), precision=HIGH).reshape(row_count, 3, D)
    queries = low_back(low(projected[:, 0] + qv_bias[0])).reshape(row_count, HEADS, HEAD_DIM)
    key_rows = low_back(low(projected[:, 1])).reshape(row_count, HEADS, HEAD_DIM)
    value_rows = low_back(low(projected[:, 2] + qv_bias[1])).reshape(row_count, HEADS, HEAD_DIM)
    attended = low_back(low(attend(queries, key_rows, value_rows, allowed).reshape(row_count, D)))
    branch = low_back(jnp.dot(attended, out_weight, precision=HIGH) + out_bias)
    middle = rows_in + compress_rows(branch)
    normed2 = low(crms_norm(middle, mlp_gain))
    hidden = low_back(jnp.dot(normed2, up_weight, precision=HIGH) + up_bias)
    active = low(jax.nn.gelu(hidden, approximate=True))
    branch2 = low_back(jnp.dot(active, down_weight, precision=HIGH) + down_bias)
    return middle + compress_rows(branch2)

def forward(rows_in, allowed, *weights):
    current = low_back(rows_in)
    for layer_index in range(LAYERS):
        current = layer(current, allowed, *(w[layer_index] for w in weights))
        if layer_index + 1 < LAYERS:
            current = low_back(low(current))
    return current

def reference(inputs, doc_lengths, attn_gain, qkv_weight, qv_bias, out_weight, out_bias, mlp_gain, up_weight, up_bias, down_weight, down_bias, cotangent):
    params = tuple((w.astype(jnp.float32) for w in (attn_gain, qkv_weight, qv_bias, out_weight, out_bias, mlp_gain, up_weight, up_bias, down_weight, down_bias)))
    units = inputs.reshape(MICRO * N_DP, MB, CW)
    unit_lengths = doc_lengths.reshape(MICRO * N_DP, DOCS)
    unit_cot = cotangent.reshape(MICRO * N_DP, MB, CW)

    def step(totals, item):
        rows_in, lengths, cot_rows = item
        allowed = doc_mask(lengths, MB)
        result, pull = jax.vjp(lambda xin, *ws: forward(xin, allowed, *ws), rows_in.astype(jnp.float32), *params)
        grads = pull(cot_rows.astype(jnp.float32))
        fresh = tuple((t + g for t, g in zip(totals, grads[1:])))
        return (fresh, (result.astype(jnp.bfloat16), grads[0].astype(jnp.bfloat16)))
    zeros = tuple((jnp.zeros_like(w) for w in params))
    totals, (outs, grads_in) = lax.scan(step, zeros, (units, unit_lengths, unit_cot))
    shape = (MICRO, N_DP * MB, CW)
    return (outs.reshape(shape), grads_in.reshape(shape), totals[0], totals[1], totals[2], totals[3], totals[4], totals[5], totals[6], totals[7], totals[8], totals[9])
```

```python
import functools

import jax
import jax.numpy as jnp
from jax import lax
from jax.experimental import pallas as pl
from jax.experimental.pallas import tpu as pltpu
from jax.sharding import PartitionSpec as P

HEAD_DIM = 64
LANES = 128
EPS = 1e-05
NEG = -1e30
VMEM_BYTES = 56 * 1024 * 1024

F32 = jnp.float32
BF16 = jnp.bfloat16

VMEM = pl.BlockSpec(memory_space=pltpu.VMEM)
SMEM = pl.BlockSpec(memory_space=pltpu.SMEM)
ANY = pl.BlockSpec(memory_space=pl.ANY)


def mm(left, right):
    return jnp.dot(left, right, preferred_element_type=F32)


def mm_t(left, right):
    return lax.dot_general(left, right, (((1,), (1,)), ((), ())), preferred_element_type=F32)


def t_mm(left, right):
    return lax.dot_general(left, right, (((0,), (0,)), ((), ())), preferred_element_type=F32)


def row_mean(array):
    return jnp.mean(array, axis=-1, keepdims=True)


def center(array):
    return array - row_mean(array)


def last_lane(shape):
    return lax.broadcasted_iota(jnp.int32, shape, 1) == shape[1] - 1


def expand(rows):
    return jnp.where(last_lane(rows.shape), -jnp.sum(rows, axis=-1, keepdims=True), rows)


def inv_rms(rows):
    return lax.rsqrt(row_mean(rows * rows) + EPS)


def norm_pull(rows, scaling, gain, grad):
    gained = gain * grad
    inner = row_mean(gained * rows)
    grad_rows = scaling * gained - rows * (scaling * scaling * scaling * inner)
    return center(grad_rows), grad * rows * scaling


def col_sum(array):
    return jnp.sum(array.astype(F32), axis=0, keepdims=True)


def pick(meta, layer, own, other, dst, sem):
    @pl.when(meta[0] == layer)
    def _():
        pltpu.make_async_copy(own, dst, sem).start()

    @pl.when(meta[0] != layer)
    def _():
        pltpu.make_async_copy(other, dst, sem).start()


def done(src, dst, sem):
    pltpu.make_async_copy(src, dst, sem).wait()


def halves(pair):
    first = lax.broadcasted_iota(jnp.int32, pair.shape, 1) < HEAD_DIM
    zero = jnp.zeros_like(pair)
    return jnp.concatenate([jnp.where(first, pair, zero), jnp.where(first, zero, pair)], axis=0)


def merge(stacked):
    rows = stacked.shape[0] // 2
    first = lax.broadcasted_iota(jnp.int32, (rows, stacked.shape[1]), 1) < HEAD_DIM
    return jnp.where(first, stacked[:rows], stacked[rows:])


def owner(meta, places):
    total = jnp.zeros(places.shape, jnp.int32)
    bound = 0
    for doc in range(3):
        bound = bound + meta[2 + doc]
        total = total + (places >= bound).astype(jnp.int32)
    return total


def mask_bias(meta, half, rows, keys):
    row_at = lax.broadcasted_iota(jnp.int32, (rows, 1), 0) + half * rows
    key_at = lax.broadcasted_iota(jnp.int32, (1, keys), 1)
    allowed = (owner(meta, row_at) == owner(meta, key_at)) & (key_at <= row_at)
    return jnp.where(allowed, 0.0, NEG).astype(F32)


class Vec:
    def __init__(self, width, heads_width, hidden):
        self.cuts = {}
        at = 0
        for name, size in (
            ("attn_gain", width),
            ("q_bias", heads_width),
            ("v_bias", heads_width),
            ("out_bias", width),
            ("mlp_gain", width),
            ("up_bias", hidden),
            ("down_bias", width),
        ):
            self.cuts[name] = (at, at + size)
            at += size
        self.size = at

    def get(self, ref, name):
        first, last = self.cuts[name]
        return ref[:, first:last]


def attn_forward_kernel(layer, half, vec, *refs):
    refs = list(refs)
    meta = refs.pop(0)
    vec_ref = refs.pop(0)
    if layer == 0:
        rows_ref = refs.pop(0)
    else:
        prev_vec, middle_ref, own_ref, other_ref = refs.pop(0), refs.pop(0), refs.pop(0), refs.pop(0)
    kv_ref = refs.pop(0) if half else None
    qkv_own, qkv_other, out_own, out_other = refs[:4]
    rows_out, normed_out, qkv_out, att_out, probs_out, part_out = refs[4:10]
    wqkv, wout, keys_all, sems = refs[10:]
    width = wqkv.shape[1]
    local = wqkv.shape[2]
    pick(meta, layer, qkv_own, qkv_other, wqkv, sems.at[0])
    pick(meta, layer, out_own, out_other, wout, sems.at[1])
    if layer == 0:
        rows = rows_ref[...].astype(F32)
    else:
        branch = own_ref[...].astype(F32) + other_ref[...].astype(F32) + vec.get(prev_vec, "down_bias")
        rows = (middle_ref[...] + center(branch)).astype(BF16).astype(F32)
        rows = jnp.where(last_lane(rows.shape), 0.0, rows)
    rows = expand(rows)
    rows_out[...] = rows
    normed = (rows * inv_rms(rows) * vec.get(vec_ref, "attn_gain")).astype(BF16)
    normed_out[...] = normed
    count = rows.shape[0]
    done(qkv_own, wqkv, sems.at[0])
    query = ((mm(normed, wqkv[0]) + vec.get(vec_ref, "q_bias")) * HEAD_DIM**-0.5).astype(BF16)
    key = mm(normed, wqkv[1]).astype(BF16)
    value = (mm(normed, wqkv[2]) + vec.get(vec_ref, "v_bias")).astype(BF16)
    qkv_out[:, :local] = query
    qkv_out[:, local : 2 * local] = key
    qkv_out[:, 2 * local :] = value
    if half:
        keys_all[:count] = kv_ref[...]
    keys_all[half * count : (half + 1) * count, :local] = key
    keys_all[half * count : (half + 1) * count, local:] = value
    keys = (half + 1) * count
    bias = mask_bias(meta, half, count, keys)
    for pair in range(local // LANES):
        cols = slice(pair * LANES, (pair + 1) * LANES)
        vcols = slice(local + pair * LANES, local + (pair + 1) * LANES)
        scores = mm_t(halves(query[:, cols]), keys_all[:keys, cols])
        scores = (scores.reshape(2, count, keys) + bias[None]).reshape(2 * count, keys)
        expo = jnp.exp(scores - jnp.max(scores, axis=-1, keepdims=True))
        probs = (expo * (1.0 / jnp.sum(expo, axis=-1, keepdims=True))).astype(BF16)
        probs_out[pair] = probs
        att_out[:, cols] = merge(mm(probs, keys_all[:keys, vcols])).astype(BF16)
    done(out_own, wout, sems.at[1])
    part_out[...] = mm(att_out[...], wout[...]).astype(BF16)


def mlp_forward_kernel(layer, last, vec, chunk, *refs):
    refs = list(refs)
    meta, vec_ref, rows_ref, own_ref, other_ref = (refs.pop(0) for _ in range(5))
    if last:
        cot_ref = refs.pop(0)
        sums_ref = refs.pop(0)
    up_own, up_other, down_own, down_other = (refs.pop(0) for _ in range(4))
    if last:
        middle_out, normed_out, active_out, part_out, low_out, hid_out, gpart_out, sums_out = refs[:8]
        wup, wdown, sems = refs[8:]
    else:
        middle_out, normed_out, active_out, part_out, slope_out = refs[:5]
        wup, wdown, sems = refs[5:]
    hidden_width = wup.shape[1]
    pieces = hidden_width // chunk
    for at in range(pieces):
        cols = pl.ds(at * chunk, chunk)
        pick(meta, layer, up_own.at[:, cols], up_other.at[:, cols], wup.at[:, cols], sems.at[0, at])
        pick(meta, layer, down_own.at[cols], down_other.at[cols], wdown.at[cols], sems.at[1, at])
    branch = own_ref[...].astype(F32) + other_ref[...].astype(F32) + vec.get(vec_ref, "out_bias")
    middle = rows_ref[...] + center(branch)
    middle_out[...] = middle
    normed = (middle * inv_rms(middle) * vec.get(vec_ref, "mlp_gain")).astype(BF16)
    normed_out[...] = normed
    if last:
        low = center(cot_ref[...].astype(F32)).astype(BF16)
        low_out[...] = low
        width = low.shape[1]
        sums_out[:, :width] = col_sum(low) + sums_ref[:, :width]
    first_bias = vec.cuts["up_bias"][0]
    part = None
    gpart = None
    for at in range(pieces):
        cols = pl.ds(at * chunk, chunk)
        here = slice(at * chunk, (at + 1) * chunk)
        done(up_own.at[:, cols], wup.at[:, cols], sems.at[0, at])
        hidden = mm(normed, wup[:, here])
        hidden = hidden + vec_ref[:, first_bias + at * chunk : first_bias + (at + 1) * chunk]
        square = hidden * hidden
        root = (2.0 / jnp.pi) ** 0.5
        bent = jnp.tanh(hidden * (root + (root * 0.044715) * square))
        half_up = 0.5 + 0.5 * bent
        active = (hidden * half_up).astype(BF16)
        slope = half_up + hidden * (0.5 - 0.5 * bent * bent) * (root + (3 * root * 0.044715) * square)
        active_out[:, here] = active
        done(down_own.at[cols], wdown.at[cols], sems.at[1, at])
        term = mm(active, wdown[here, :])
        part = term if part is None else part + term
        if last:
            hid = (mm_t(low, wdown[here, :]) * slope).astype(BF16)
            hid_out[:, here] = hid
            places = slice(width + at * chunk, width + (at + 1) * chunk)
            sums_out[:, places] = col_sum(hid) + sums_ref[:, places]
            term = mm_t(hid, wup[:, here])
            gpart = term if gpart is None else gpart + term
        else:
            slope_out[:, here] = slope.astype(BF16)
    part_out[...] = part.astype(BF16)
    if last:
        gpart_out[...] = gpart.astype(BF16)


def mlp_backward_kernel(vec, chunk, *refs):
    refs = list(refs)
    meta, vec_ref, grad_ref, own_ref, other_ref, rows_ref, slope_ref, sums_ref = (refs.pop(0) for _ in range(8))
    up_own, up_other, down_own, down_other = (refs.pop(0) for _ in range(4))
    grad_out, low_out, hid_out, gpart_out, sums_out = refs[:5]
    wup, wdown, sems = refs[5:]
    pieces = wup.shape[1] // chunk
    for at in range(pieces):
        cols = pl.ds(at * chunk, chunk)
        pick(meta, 0, down_own.at[cols], down_other.at[cols], wdown.at[cols], sems.at[1, at])
        pick(meta, 0, up_own.at[:, cols], up_other.at[:, cols], wup.at[:, cols], sems.at[0, at])
    rows = rows_ref[...]
    grad = own_ref[...].astype(F32) + other_ref[...].astype(F32)
    pulled, gain_terms = norm_pull(rows, inv_rms(rows), vec.get(vec_ref, "attn_gain"), grad)
    grad_in = grad_ref[...] + pulled
    width = rows.shape[1]
    grad_in = (grad_in - grad_in[:, width - 1 :]).astype(BF16).astype(F32)
    grad_in = center(grad_in)
    grad_out[...] = grad_in
    low = grad_in.astype(BF16)
    low_out[...] = low
    sums_out[:, :width] = col_sum(low) + sums_ref[:, :width]
    sums_out[:, width + wup.shape[1] :] = col_sum(gain_terms) + sums_ref[:, width + wup.shape[1] :]
    gpart = None
    for at in range(pieces):
        cols = pl.ds(at * chunk, chunk)
        here = slice(at * chunk, (at + 1) * chunk)
        done(down_own.at[cols], wdown.at[cols], sems.at[1, at])
        hid = (mm_t(low, wdown[here, :]) * slope_ref[:, here].astype(F32)).astype(BF16)
        hid_out[:, here] = hid
        places = slice(width + at * chunk, width + (at + 1) * chunk)
        sums_out[:, places] = col_sum(hid) + sums_ref[:, places]
        done(up_own.at[:, cols], wup.at[:, cols], sems.at[0, at])
        term = mm_t(hid, wup[:, here])
        gpart = term if gpart is None else gpart + term
    gpart_out[...] = gpart.astype(BF16)


def attn_backward_kernel(layer, half, vec, *refs):
    refs = list(refs)
    meta, vec_ref, grad_ref, own_ref, other_ref, middle_ref, qkv_ref = (refs.pop(0) for _ in range(7))
    probs_ref, sums_ref = refs.pop(0), refs.pop(0)
    rows_ref = refs.pop(0) if layer == 0 else None
    tail_ref = refs.pop(0) if half else None
    later_ref = None if half else refs.pop(0)
    qkv_own, qkv_other, out_own, out_other = (refs.pop(0) for _ in range(4))
    grad_out, low_out, dqkv_out, gpart_out, sums_out = refs[:5]
    refs = refs[5:]
    early_out = refs.pop(0) if half else None
    wqkv, wout, keys_all, sems = refs
    width = wqkv.shape[1]
    local = wqkv.shape[2]
    pick(meta, layer, out_own, out_other, wout, sems.at[1])
    pick(meta, layer, qkv_own, qkv_other, wqkv, sems.at[0])
    middle = middle_ref[...]
    grad = own_ref[...].astype(F32) + other_ref[...].astype(F32)
    pulled, gain_terms = norm_pull(middle, inv_rms(middle), vec.get(vec_ref, "mlp_gain"), grad)
    upstream = grad_ref[...].astype(F32)
    if layer == 1:
        upstream = center(upstream)
    grad_mid = upstream + pulled
    grad_out[...] = grad_mid
    low = grad_mid.astype(BF16)
    low_out[...] = low
    sums_out[:, :width] = col_sum(gain_terms) + sums_ref[:, :width]
    sums_out[:, width : 2 * width] = col_sum(low) + sums_ref[:, width : 2 * width]
    count = middle.shape[0]
    keys = (half + 1) * count
    if half:
        keys_all[:count] = tail_ref[...]
    keys_all[half * count : (half + 1) * count] = qkv_ref[:, local:]
    done(out_own, wout, sems.at[1])
    grad_att = mm_t(low, wout[...]).astype(BF16)
    at = 2 * width
    for pair in range(local // LANES):
        cols = slice(pair * LANES, (pair + 1) * LANES)
        vcols = slice(local + pair * LANES, local + (pair + 1) * LANES)
        v2cols = slice(2 * local + pair * LANES, 2 * local + (pair + 1) * LANES)
        grads = halves(grad_att[:, cols])
        queries = halves(qkv_ref[:, cols])
        low_probs = probs_ref[pair]
        probs = low_probs.astype(F32)
        grad_probs = mm_t(grads, keys_all[:keys, vcols])
        inner = jnp.sum(grad_probs * probs, axis=-1, keepdims=True)
        grad_scores = (probs * (grad_probs - inner)).astype(BF16)
        grad_query = merge(mm(grad_scores, keys_all[:keys, cols])) * HEAD_DIM**-0.5
        grad_key = t_mm(grad_scores, queries)
        grad_value = t_mm(low_probs, grads)
        if half:
            early_out[:, cols] = grad_key[:count]
            early_out[:, vcols] = grad_value[:count]
            grad_key = grad_key[count:]
            grad_value = grad_value[count:]
        else:
            grad_key = grad_key + later_ref[:, cols]
            grad_value = grad_value + later_ref[:, vcols]
        grad_query = grad_query.astype(BF16)
        grad_value = grad_value.astype(BF16)
        dqkv_out[:, cols] = grad_query
        dqkv_out[:, vcols] = grad_key.astype(BF16)
        dqkv_out[:, v2cols] = grad_value
        places = slice(at + pair * LANES, at + (pair + 1) * LANES)
        sums_out[:, places] = col_sum(grad_query) + sums_ref[:, places]
        places = slice(at + local + pair * LANES, at + local + (pair + 1) * LANES)
        sums_out[:, places] = col_sum(grad_value) + sums_ref[:, places]
    done(qkv_own, wqkv, sems.at[0])
    gpart = mm_t(dqkv_out[:, :local], wqkv[0])
    gpart = gpart + mm_t(dqkv_out[:, local : 2 * local], wqkv[1])
    gpart = gpart + mm_t(dqkv_out[:, 2 * local :], wqkv[2])
    gpart_out[...] = gpart.astype(BF16)
    if layer == 0:
        rows = rows_ref[...]
        at = 2 * width + 2 * local
        terms = gpart * rows * inv_rms(rows)
        sums_out[:, at:] = col_sum(terms) + sums_ref[:, at:]


def mlp_weights_kernel(meta, act0, act1, low0, low1, norm0, norm1, hid0, hid1, mine_out, theirs_out):
    width = low0.shape[1]
    hidden = act0.shape[1]
    block = mine_out.shape[1]
    for out, part in ((mine_out, meta[0]), (theirs_out, 1 - meta[0])):
        rows = width // 2
        cols = pl.ds(pl.multiple_of(part * rows, LANES), rows)
        left0, left1 = norm0[:, cols], norm1[:, cols]
        for at in range(hidden // block):
            here = slice(at * block, (at + 1) * block)
            total = t_mm(left0, hid0[:, here]) + t_mm(left1, hid1[:, here])
            out[at * rows : (at + 1) * rows] = total.astype(BF16)
        base = hidden // block * rows
        rows = hidden // 2
        cols = pl.ds(pl.multiple_of(part * rows, LANES), rows)
        left0, left1 = act0[:, cols], act1[:, cols]
        for at in range(width // block):
            here = slice(at * block, (at + 1) * block)
            total = t_mm(left0, low0[:, here]) + t_mm(left1, low1[:, here])
            out[base + at * rows : base + (at + 1) * rows] = total.astype(BF16)


def attn_weights_kernel(extra, *refs):
    meta, norm0, norm1, dqkv0, dqkv1, att0, att1, low0, low1 = refs[:9]
    refs = refs[9:]
    if extra:
        small = refs[0]
        refs = refs[1:]
    mine_out, theirs_out = refs
    width = low0.shape[1]
    local = att0.shape[1]
    piece = mine_out.shape[0] // 8 - extra

    def put(out, first, total):
        for at in range(0, total.shape[0], piece):
            where = (first + at) // piece * (piece + extra)
            out[where : where + piece] = total[at : at + piece].astype(BF16)

    for out, part in ((mine_out, meta[0]), (theirs_out, 1 - meta[0])):
        rows = width // 2
        cols = pl.ds(pl.multiple_of(part * rows, LANES), rows)
        left0, left1 = norm0[:, cols], norm1[:, cols]
        for at in range(3):
            here = slice(at * local, (at + 1) * local)
            put(out, at * rows, t_mm(left0, dqkv0[:, here]) + t_mm(left1, dqkv1[:, here]))
        put(out, 3 * rows, t_mm(att0[...], low0[:, cols]) + t_mm(att1[...], low1[:, cols]))
        if extra:
            out[piece : piece + extra] = small[part]
            for at in range(1, 8):
                where = at * (piece + extra) + piece
                out[where : where + extra] = jnp.zeros((extra, out.shape[1]), BF16)


def place_kernel(kinds, extra, *refs):
    meta, first_own, second_own, first_other, second_other = refs[:5]
    outs = refs[5:-4]
    low, wide, in_sems, out_sems = refs[-4:]
    piece = low.shape[1]
    step = piece + extra

    def source(ref, block):
        return ref.at[pl.ds(pl.multiple_of((block ^ meta[6]) * step, 16), piece)]

    for side, (first, second) in enumerate(((first_own, second_own), (first_other, second_other))):
        for block in range(8):
            at = side * 8 + block
            pick(meta, 0, source(first, block), source(second, block), low.at[at], in_sems.at[at])
    copies = []
    for side in range(2):
        part = meta[0] if side == 0 else 1 - meta[0]
        for block in range(8):
            at = side * 8 + block
            done(source(first_own, block), low.at[at], in_sems.at[at])
            wide[at] = low[at].astype(F32)
            which, where = kinds[block]
            copies.append(pltpu.make_async_copy(wide.at[at], outs[which].at[where(part)], out_sems.at[at]))
            copies[-1].start()
    for copy in copies:
        copy.wait()


def shape(dims, dtype=BF16):
    return jax.ShapeDtypeStruct(dims, dtype)


def call(kernel, in_specs, outs, scratch, args, flops=0, out_specs=None):
    moved = sum(a.size * a.dtype.itemsize for a in args) + sum(o.size * o.dtype.itemsize for o in outs)
    return pl.pallas_call(
        kernel,
        out_shape=tuple(outs),
        in_specs=in_specs,
        out_specs=tuple(out_specs if out_specs else [VMEM] * len(outs)),
        scratch_shapes=scratch,
        compiler_params=pltpu.CompilerParams(vmem_limit_bytes=VMEM_BYTES),
        cost_estimate=pl.CostEstimate(flops=flops, bytes_accessed=moved, transcendentals=0),
    )(*args)


def swap(array, axis):
    return lax.ppermute(array, axis, [(0, 1), (1, 0)])


def sum_over_groups(mine, theirs, order):
    count = lax.axis_size("dp")
    index = lax.axis_index("dp")
    received = swap(theirs, "section")

    def total(left, right):
        return (left.astype(F32) + right.astype(F32)).astype(BF16)

    held = mine
    for bit in order:
        side = (index >> bit) & 1
        rows = held.shape[0] // 2
        both = total(held, received)
        held = lax.dynamic_slice_in_dim(both, side * rows, rows, 0)
        send = lax.dynamic_slice_in_dim(both, (1 - side) * rows, rows, 0)
        received = lax.ppermute(send, "dp", [(i, i ^ (1 << bit)) for i in range(count)])
    held = total(held, received)
    for bit in reversed(order):
        received = lax.ppermute(held, "dp", [(i, i ^ (1 << bit)) for i in range(count)])
        held = jnp.concatenate([held, received], axis=0)
    return held


def place_of(index, order):
    place = jnp.int32(0)
    for bit in order:
        place = place * 2 + ((index >> bit) & 1)
    return place


def in_order(array, place, count):
    blocks = array.reshape((count, array.shape[0] // count) + array.shape[1:])
    return jnp.take(blocks, jnp.arange(count, dtype=jnp.int32) ^ place, axis=0).reshape(array.shape)


def local(
    inputs,
    doc_lengths,
    attn_gain,
    qkv_weight,
    qv_bias,
    out_weight,
    out_bias,
    mlp_gain,
    up_weight,
    up_bias,
    down_weight,
    down_bias,
    cotangent,
):
    core = lax.axis_index("section")
    side = lax.axis_index("tensor")
    group = lax.axis_index("dp")
    groups = lax.axis_size("dp")
    bits = groups.bit_length() - 1
    order = list(range(bits))
    place = place_of(group, order)
    rows = inputs.shape[1]
    width = attn_gain.shape[1]
    heads = qkv_weight.shape[3]
    hidden = up_weight.shape[2]
    pairs = heads // LANES
    vec = Vec(width, heads, hidden)
    chunk = 384

    def own_rows(array):
        mine = lax.dynamic_index_in_dim(array, core, 0, keepdims=False)
        return jnp.pad(mine, ((0, 0), (0, width - mine.shape[1])))

    def both_halves(mine, other):
        return jnp.where(side == 0, mine, other), jnp.where(side == 0, other, mine)

    lengths = lax.dynamic_index_in_dim(doc_lengths[:, 0, :], core, 0, keepdims=False)
    known = place if groups == 8 else jnp.int32(0)
    meta = jnp.concatenate([jnp.stack([core, side]).astype(jnp.int32), lengths, jnp.stack([known, known])])

    mine = own_rows(inputs)
    other = swap(mine, "tensor")
    entry = both_halves(mine, other)

    qkv = jnp.transpose(qkv_weight[0], (1, 0, 2))
    out, up, down = out_weight[0], up_weight[0], down_weight[0]
    vector = jnp.concatenate(
        [attn_gain, qv_bias[0].reshape(1, 2 * heads), out_bias, mlp_gain, up_bias, down_bias], axis=1
    )
    qkv_pair = (qkv, swap(qkv, "section"))
    vector_other = swap(vector, "section")
    out_pair = (out, swap(out, "section"))
    up_pair = (up, swap(up, "section"))
    down_pair = (down, swap(down, "section"))
    vectors = (jnp.where(core == 0, vector, vector_other), jnp.where(core == 0, vector_other, vector))

    cot_mine = own_rows(cotangent)
    cot_mine, _ = lax.optimization_barrier((cot_mine, other))
    cots = both_halves(cot_mine, swap(cot_mine, "tensor"))

    attn_scratch = [
        pltpu.VMEM(qkv.shape, BF16),
        pltpu.VMEM(out.shape, BF16),
        pltpu.VMEM((2 * rows, 2 * heads), BF16),
        pltpu.SemaphoreType.DMA((2,)),
    ]
    mlp_scratch = [
        pltpu.VMEM(up.shape, BF16),
        pltpu.VMEM(down.shape, BF16),
        pltpu.SemaphoreType.DMA((2, hidden // chunk)),
    ]
    attn_flops = 2 * rows * width * heads * 4
    mlp_flops = 4 * rows * width * hidden

    def attn_forward(layer, half, rows_in, kv):
        args = [meta, vectors[layer], *rows_in]
        specs = [SMEM] + [VMEM] * (len(args) - 1)
        if half:
            args.append(kv)
            specs.append(VMEM)
        args += [*qkv_pair, *out_pair]
        specs += [ANY] * 4
        outs = [
            shape((rows, width), F32),
            shape((rows, width)),
            shape((rows, 3 * heads)),
            shape((rows, heads)),
            shape((pairs, 2 * rows, (half + 1) * rows)),
            shape((rows, width)),
        ]
        kernel = functools.partial(attn_forward_kernel, layer, half, vec)
        return call(kernel, specs, outs, attn_scratch, args, attn_flops)

    def mlp_forward(layer, rows_in, own, given, cot=None, sums=None):
        last = cot is not None
        args = [meta, vectors[layer], rows_in, own, given] + ([cot, sums] if last else [])
        specs = [SMEM] + [VMEM] * (len(args) - 1) + [ANY] * 4
        args += [*up_pair, *down_pair]
        outs = [shape((rows, width), F32), shape((rows, width)), shape((rows, hidden)), shape((rows, width))]
        if last:
            outs += [shape((rows, width)), shape((rows, hidden)), shape((rows, width)), shape(sums.shape, F32)]
        else:
            outs += [shape((rows, hidden))]
        kernel = functools.partial(mlp_forward_kernel, layer, last, vec, chunk)
        return call(kernel, specs, outs, mlp_scratch, args, mlp_flops * (2 if last else 1))

    def mlp_backward(grad, own, given, rows_in, slope, sums):
        args = [meta, vectors[1], grad, own, given, rows_in, slope, sums]
        specs = [SMEM] + [VMEM] * (len(args) - 1) + [ANY] * 4
        args += [*up_pair, *down_pair]
        outs = [
            shape((rows, width), F32),
            shape((rows, width)),
            shape((rows, hidden)),
            shape((rows, width)),
            shape(sums.shape, F32),
        ]
        kernel = functools.partial(mlp_backward_kernel, vec, chunk)
        return call(kernel, specs, outs, mlp_scratch, args, mlp_flops)

    def attn_backward(layer, half, grad, own, given, middle, saved, probs, sums, rows_in, link):
        args = [meta, vectors[layer], grad, own, given, middle, saved, probs, sums]
        if layer == 0:
            args.append(rows_in)
        args.append(link)
        specs = [SMEM] + [VMEM] * (len(args) - 1) + [ANY] * 4
        args += [*qkv_pair, *out_pair]
        outs = [
            shape((rows, width), F32),
            shape((rows, width)),
            shape((rows, 3 * heads)),
            shape((rows, width)),
            shape(sums.shape, F32),
        ]
        if half:
            outs.append(shape((rows, 2 * heads), F32))
        kernel = functools.partial(attn_backward_kernel, layer, half, vec)
        return call(kernel, specs, outs, attn_scratch, args, 2 * attn_flops)

    def mlp_weights(*args):
        outs = [shape((hidden * width * 2 // 2 // 384, 384))] * 2
        return call(mlp_weights_kernel, [SMEM] + [VMEM] * 8, outs, [], [meta, *args], 2 * mlp_flops)

    def attn_weights(extra, *args):
        outs = [shape((4 * width * heads // 2 // 384 + 8 * extra, 384))] * 2
        kernel = functools.partial(attn_weights_kernel, extra)
        return call(kernel, [SMEM] + [VMEM] * (len(args)), outs, [], [meta, *args], 2 * attn_flops)

    rows0, normed0, qkv0, att0, probs0, part0 = [[None, None] for _ in range(6)]
    given0 = [None, None]
    for half in range(2):
        kv = qkv0[0][:, heads:] if half else None
        rows0[half], normed0[half], qkv0[half], att0[half], probs0[half], part0[half] = attn_forward(
            0, half, [entry[half]], kv
        )
        given0[half] = swap(part0[half], "tensor")
    mid0, low_n0, act0, mpart0, slope0 = [[None, None] for _ in range(5)]
    mgiven0 = [None, None]
    for half in range(2):
        mid0[half], low_n0[half], act0[half], mpart0[half], slope0[half] = mlp_forward(
            0, rows0[half], part0[half], given0[half]
        )
        mgiven0[half] = swap(mpart0[half], "tensor")
    rows1, normed1, qkv1, att1, probs1, part1 = [[None, None] for _ in range(6)]
    given1 = [None, None]
    for half in range(2):
        kv = qkv1[0][:, heads:] if half else None
        rows1[half], normed1[half], qkv1[half], att1[half], probs1[half], part1[half] = attn_forward(
            1, half, [vectors[0], mid0[half], mpart0[half], mgiven0[half]], kv
        )
        given1[half] = swap(part1[half], "tensor")
    mid1, low_n1, act1, mpart1, low1, hid1, gpart1, ggiven1 = [[None, None] for _ in range(8)]
    sums_m1 = jnp.zeros((1, width + hidden), F32)
    for half in range(2):
        (
            mid1[half],
            low_n1[half],
            act1[half],
            mpart1[half],
            low1[half],
            hid1[half],
            gpart1[half],
            sums_m1,
        ) = mlp_forward(1, rows1[half], part1[half], given1[half], cots[half], sums_m1)
        ggiven1[half] = swap(gpart1[half], "tensor")
    mlp1 = mlp_weights(act1[0], act1[1], low1[0], low1[1], low_n1[0], low_n1[1], hid1[0], hid1[1])
    mlp1 = sum_over_groups(*mlp1, order)
    grad1, glow1, dqkv1, apart1, agiven1 = [[None, None] for _ in range(5)]
    sums_a1 = jnp.zeros((1, 2 * width + 2 * heads), F32)
    link = qkv1[0][:, heads:]
    for half in (1, 0):
        grad1[half], glow1[half], dqkv1[half], apart1[half], sums_a1, *rest = attn_backward(
            1,
            half,
            cots[half],
            gpart1[half],
            ggiven1[half],
            mid1[half],
            qkv1[half],
            probs1[half],
            sums_a1,
            None,
            link,
        )
        link = rest[0] if half else None
        agiven1[half] = swap(apart1[half], "tensor")
    attn1 = attn_weights(0, normed1[0], normed1[1], dqkv1[0], dqkv1[1], att1[0], att1[1], glow1[0], glow1[1])
    attn1 = sum_over_groups(*attn1, order)
    grad0, low0, hid0, gpart0, ggiven0 = [[None, None] for _ in range(5)]
    sums_m0 = jnp.zeros((1, 2 * width + hidden), F32)
    for half in (1, 0):
        grad0[half], low0[half], hid0[half], gpart0[half], sums_m0 = mlp_backward(
            grad1[half], apart1[half], agiven1[half], rows1[half], slope0[half], sums_m0
        )
        ggiven0[half] = swap(gpart0[half], "tensor")
    mlp0 = mlp_weights(act0[0], act0[1], low0[0], low0[1], low_n0[0], low_n0[1], hid0[0], hid0[1])
    mlp0 = sum_over_groups(*mlp0, order)
    gmid0, glow0, dqkv0, apart0 = [[None, None] for _ in range(4)]
    sums_a0 = jnp.zeros((1, 3 * width + 2 * heads), F32)
    link = qkv0[0][:, heads:]
    for half in (1, 0):
        gmid0[half], glow0[half], dqkv0[half], apart0[half], sums_a0, *rest = attn_backward(
            0,
            half,
            grad0[half],
            gpart0[half],
            ggiven0[half],
            mid0[half],
            qkv0[half],
            probs0[half],
            sums_a0,
            rows0[half],
            link,
        )
        link = rest[0] if half else None
    gain0 = sums_a0[:, 2 * width + 2 * heads :]
    gain0 = gain0 + swap(gain0, "tensor")

    def small_rows(gain, attn_sums, mlp_sums):
        row = jnp.concatenate(
            [
                gain,
                attn_sums[:, 2 * width : 2 * width + 2 * heads],
                attn_sums[:, width : 2 * width],
                attn_sums[:, :width],
                mlp_sums[:, width : width + hidden],
                mlp_sums[:, :width],
            ],
            axis=1,
        )
        row = jnp.pad(row, ((0, 0), (0, extra * 384 - vec.size)))
        return row.reshape(extra, 384)

    extra = 16
    small = jnp.stack(
        [small_rows(gain0, sums_a0, sums_m0), small_rows(sums_m0[:, width + hidden :], sums_a1, sums_m1)]
    ).astype(BF16)
    attn0 = attn_weights(extra, normed0[0], normed0[1], dqkv0[0], dqkv0[1], att0[0], att0[1], glow0[0], glow0[1], small)
    attn0 = sum_over_groups(*attn0, order)

    def own_half(parts):
        first = lax.ppermute(parts[0], "tensor", [(1, 0)])
        second = lax.ppermute(parts[1], "tensor", [(0, 1)])
        mine = jnp.where(side == 0, parts[0], parts[1])
        return mine.astype(F32) + (first + second).astype(F32)

    def chosen(pair):
        return jnp.where(side == 0, pair[0], pair[1])

    branch = own_half(mpart1) + vectors[1][:, vec.cuts["down_bias"][0] : vec.cuts["down_bias"][1]]
    result = (chosen(mid1) + center(branch))[:, : width - 1].astype(BF16)
    entry_rows = chosen(rows0)
    pulled, _ = norm_pull(
        entry_rows, inv_rms(entry_rows), vectors[0][:, : vec.cuts["attn_gain"][1]], own_half(apart0)
    )
    grad_in = chosen(gmid0) + pulled
    grad_in = (grad_in[:, : width - 1] - grad_in[:, width - 1 :]).astype(BF16)

    if groups != 8:
        mlp0, mlp1, attn0, attn1 = (in_order(a, place, groups) for a in (mlp0, mlp1, attn0, attn1))

    def over(array, layer):
        return lax.ppermute(array, "section", [(1 - layer, layer)])

    up_rows, down_rows = width // 2, hidden // 2

    def mlp_kind(block):
        if block < 4:
            return 0, lambda part: (pl.ds(pl.multiple_of(part * up_rows, 8), up_rows), pl.ds(block * 384, 384))
        col, row = (block - 4) // 2, (block - 4) % 2
        return 1, lambda part: (
            pl.ds(pl.multiple_of(part * down_rows + row * 384, 8), 384),
            pl.ds(col * 384, 384),
        )

    def attn_kind(block):
        which, row = block // 2, block % 2
        if which < 3:
            return 0, lambda part: (which, pl.ds(pl.multiple_of(part * up_rows + row * 192, 8), 192), slice(None))
        return 1, lambda part: (pl.ds(row * 192, 192), pl.ds(pl.multiple_of(part * 384, 128), 384))

    def placed(kinds, extra_rows, first, second, outs):
        piece = first.shape[0] // 8 - extra_rows
        args = [meta, first, second, over(first, 0), over(second, 1)]
        scratch = [
            pltpu.VMEM((16, piece, 384), BF16),
            pltpu.VMEM((16, piece, 384), F32),
            pltpu.SemaphoreType.DMA((16,)),
            pltpu.SemaphoreType.DMA((16,)),
        ]
        kernel = functools.partial(place_kernel, kinds, extra_rows)
        return call(kernel, [SMEM] + [ANY] * 4, outs, scratch, args, 0, [ANY] * len(outs))

    grad_up, grad_down = placed(
        [mlp_kind(b) for b in range(8)], 0, mlp0, mlp1, [shape((width, hidden), F32), shape((hidden, width), F32)]
    )
    step = attn0.shape[0] // 8
    attn1 = jnp.pad(attn1.reshape(8, step - extra, 384), ((0, 0), (0, extra), (0, 0))).reshape(attn0.shape)
    grad_qkv, grad_out = placed(
        [attn_kind(b) for b in range(8)], extra, attn0, attn1, [shape((3, width, heads), F32), shape((heads, width), F32)]
    )
    small = lax.dynamic_slice_in_dim(attn0, known * step + step - extra, extra, 0).astype(F32)
    small = small.reshape(1, extra * 384)

    def piece_of(first, last):
        return small[:, vec.cuts[first][0] : vec.cuts[last][1]]

    return (
        result[None],
        grad_in[None],
        piece_of("attn_gain", "attn_gain"),
        jnp.transpose(grad_qkv, (1, 0, 2))[None],
        piece_of("q_bias", "v_bias").reshape(1, 2, heads),
        grad_out[None],
        piece_of("out_bias", "out_bias"),
        piece_of("mlp_gain", "mlp_gain"),
        grad_up[None],
        piece_of("up_bias", "up_bias"),
        grad_down[None],
        piece_of("down_bias", "down_bias"),
    )


def solution(mesh):
    in_specs = (
        P(None, ("dp", "tensor"), None),
        P(None, "dp", None),
        P("section", None),
        P("section", None, None, "tensor"),
        P("section", None, "tensor"),
        P("section", "tensor", None),
        P("section", None),
        P("section", None),
        P("section", None, "tensor"),
        P("section", "tensor"),
        P("section", "tensor", None),
        P("section", None),
        P(None, ("dp", "tensor"), None),
    )
    out_specs = (
        P("section", ("dp", "tensor"), None),
        P("section", ("dp", "tensor"), None),
        P("section", None),
        P("section", None, None, "tensor"),
        P("section", None, "tensor"),
        P("section", "tensor", None),
        P("section", None),
        P("section", None),
        P("section", None, "tensor"),
        P("section", "tensor"),
        P("section", "tensor", None),
        P("section", None),
    )
    return jax.shard_map(local, mesh=mesh, in_specs=in_specs, out_specs=out_specs, check_vma=False)
```

```python
import functools
import math

import jax
import jax.numpy as jnp
from jax import lax
from jax.experimental import pallas as pl
from jax.experimental.pallas import tpu as pltpu
from jax.sharding import PartitionSpec as P

HEAD_DIM = 64
LANES = 128
EPS = 1e-05
NEG = -1e30
VMEM_BYTES = 24 * 1024 * 1024

F32 = jnp.float32
BF16 = jnp.bfloat16

SMEM = pl.BlockSpec(memory_space=pltpu.SMEM)
VMEM = pl.BlockSpec(memory_space=pltpu.VMEM)
HBM = pl.BlockSpec(memory_space=pltpu.HBM)


def mm(left, right):
    return jnp.dot(left, right, preferred_element_type=F32)


def mm_t(left, right):
    return lax.dot_general(left, right, (((1,), (1,)), ((), ())), preferred_element_type=F32)


def t_mm(left, right):
    return lax.dot_general(left, right, (((0,), (0,)), ((), ())), preferred_element_type=F32)


def row_mean(array):
    return jnp.mean(array, axis=-1, keepdims=True)


def center(array):
    return array - row_mean(array)


def last_lane(shape):
    return lax.broadcasted_iota(jnp.int32, shape, 1) == shape[1] - 1


def expand(rows):
    return jnp.where(last_lane(rows.shape), -jnp.sum(rows, axis=-1, keepdims=True), rows)


def inv_rms(rows):
    return lax.rsqrt(row_mean(rows * rows) + EPS)


def norm_pull(rows, scaling, gain, grad):
    gained = gain * grad
    inner = row_mean(gained * rows)
    grad_rows = scaling * gained - rows * (scaling * scaling * scaling * inner)
    return center(grad_rows), grad * rows * scaling


def col_sum(array):
    return jnp.sum(array.astype(F32), axis=0, keepdims=True)


def pick(meta, layer, own, other, dst, sem):
    @pl.when(meta[0] == layer)
    def _():
        pltpu.make_async_copy(own, dst, sem).start()

    @pl.when(meta[0] != layer)
    def _():
        pltpu.make_async_copy(other, dst, sem).start()


def done(src, dst, sem):
    pltpu.make_async_copy(src, dst, sem).wait()


def halves(pair):
    first = lax.broadcasted_iota(jnp.int32, pair.shape, 1) < HEAD_DIM
    zero = jnp.zeros_like(pair)
    return jnp.concatenate([jnp.where(first, pair, zero), jnp.where(first, zero, pair)], axis=0)


def merge(stacked):
    rows = stacked.shape[0] // 2
    first = lax.broadcasted_iota(jnp.int32, (rows, stacked.shape[1]), 1) < HEAD_DIM
    return jnp.where(first, stacked[:rows], stacked[rows:])


def owner(meta, places):
    total = jnp.zeros(places.shape, jnp.int32)
    bound = 0
    for doc in range(3):
        bound = bound + meta[2 + doc]
        total = total + (places >= bound).astype(jnp.int32)
    return total


def mask_bias(meta, half, rows, keys):
    row_at = lax.broadcasted_iota(jnp.int32, (rows, 1), 0) + half * rows
    key_at = lax.broadcasted_iota(jnp.int32, (1, keys), 1)
    allowed = (owner(meta, row_at) == owner(meta, key_at)) & (key_at <= row_at)
    return jnp.where(allowed, 0.0, NEG).astype(F32)


class Load:
    def __init__(self, src, dst, sem):
        self.copy = pltpu.make_async_copy(src, dst, sem)
        self.copy.start()
        self.ref = dst
        self.waited = False

    def __call__(self):
        if not self.waited:
            self.copy.wait()
            self.waited = True
        return self.ref

    def get(self):
        return self()[...]


class Held:
    def __init__(self, ref):
        self.ref = ref

    def __call__(self):
        return self.ref

    def get(self):
        return self.ref[...]


class Store:
    def __init__(self, ref):
        self.ref = ref
        self.copies = []
        self.sent = False

    def put(self, value):
        self.ref[...] = value
        self.send()

    def send(self):
        self.sent = True
        for copy in self.copies:
            copy.start()


def take(refs, count):
    out = refs[:count]
    del refs[:count]
    return out


def framed(body, held, n_weights, places, *refs):
    refs = list(refs)
    (meta,) = take(refs, 1)
    sources, weights = take(refs, len(held)), take(refs, n_weights)
    targets = [take(refs, 2 if place == "both" else 1) for place in places]
    buffers = take(refs, held.count(False))
    made = take(refs, places.count("hbm"))
    in_sems, out_sems = take(refs, 2)
    loads = []
    moved = 0
    for source, here in zip(sources, held):
        if here:
            loads.append(Held(source))
        else:
            loads.append(Load(source, buffers[moved], in_sems.at[moved]))
            moved += 1
    stores = []
    for at, (place, target) in enumerate(zip(places, targets)):
        store = Store(made.pop(0) if place == "hbm" else target[0])
        if place != "vmem":
            store.copies.append(pltpu.make_async_copy(store.ref, target[-1], out_sems.at[at]))
        stores.append(store)
    body(meta, list(loads), weights, stores, *refs)
    for load in loads:
        load()
    for store in stores:
        if not store.sent:
            store.send()
    for store in stores:
        for copy in store.copies:
            copy.wait()


ATTN_GAIN, QV_BIAS, OUT_BIAS, MLP_GAIN, UP_BIAS, DOWN_BIAS = range(6)


def pack_kernel(*refs):
    out = refs[-1]
    out[...] = jnp.zeros(out.shape, F32)
    for row, ref in enumerate(refs[:-1]):
        if ref.shape[0] == 2:
            half = ref.shape[1]
            out[row : row + 1, :half] = ref[0:1]
            out[row : row + 1, half : 2 * half] = ref[1:2]
        else:
            out[row : row + 1, : ref.shape[1]] = ref[...]


def attn_forward_kernel(layer, half, meta, loads, weights, outs, wqkv, wout, keys_all, vec, sems, vec_sems):
    if layer == 0:
        mine, far = take(loads, 2)
    else:
        middle_in, own, other = take(loads, 3)
    early_kv = take(loads, 1)[0] if half else None
    vec_own, vec_other, qkv_own, qkv_other, out_own, out_other = weights
    rows_out, normed_out, query_out, kv_out, att_out, probs_out, part_out = outs
    width = wqkv.shape[1]
    local = wqkv.shape[2]
    pick(meta, 0, vec_own, vec_other, vec.at[0], vec_sems.at[0])
    if layer:
        pick(meta, layer, vec_own, vec_other, vec.at[layer], vec_sems.at[layer])
    pick(meta, layer, qkv_own, qkv_other, wqkv, sems.at[0])
    pick(meta, layer, out_own, out_other, wout, sems.at[1])
    done(vec_own, vec.at[0], vec_sems.at[0])
    if layer:
        done(vec_own, vec.at[layer], vec_sems.at[layer])
    if layer == 0:
        rows = jnp.where(meta[1] == half, mine.get(), far.get()).astype(F32).T
    else:
        branch = own.get().astype(F32) + other.get().astype(F32) + vec[0, DOWN_BIAS : DOWN_BIAS + 1, :width]
        rows = (middle_in.get() + center(branch)).astype(BF16).astype(F32)
        rows = jnp.where(last_lane(rows.shape), 0.0, rows)
    rows_out.put(rows.astype(BF16))
    rows = expand(rows)
    normed = (rows * inv_rms(rows) * vec[layer, ATTN_GAIN : ATTN_GAIN + 1, :width]).astype(BF16)
    normed_out.put(normed)
    count = rows.shape[0]
    done(qkv_own, wqkv, sems.at[0])
    query_bias = vec[layer, QV_BIAS : QV_BIAS + 1, :local]
    value_bias = vec[layer, QV_BIAS : QV_BIAS + 1, local : 2 * local]
    query = ((mm(normed, wqkv[0]) + query_bias) * HEAD_DIM**-0.5).astype(BF16)
    key = mm(normed, wqkv[1]).astype(BF16)
    value = (mm(normed, wqkv[2]) + value_bias).astype(BF16)
    query_out.put(query)
    kv_out.ref[:, :local] = key
    kv_out.ref[:, local:] = value
    kv_out.send()
    if half:
        keys_all[:count] = early_kv.get()
    keys_all[half * count : (half + 1) * count, :local] = key
    keys_all[half * count : (half + 1) * count, local:] = value
    keys = (half + 1) * count
    masked = mask_bias(meta, half, count, keys)
    for pair in range(local // LANES):
        cols = slice(pair * LANES, (pair + 1) * LANES)
        vcols = slice(local + pair * LANES, local + (pair + 1) * LANES)
        scores = mm_t(halves(query[:, cols]), keys_all[:keys, cols])
        scores = (scores.reshape(2, count, keys) + masked[None]).reshape(2 * count, keys)
        expo = jnp.exp(scores - jnp.max(scores, axis=-1, keepdims=True))
        probs = (expo * (1.0 / jnp.sum(expo, axis=-1, keepdims=True))).astype(BF16)
        probs_out.ref[pair] = probs
        att_out.ref[:, cols] = merge(mm(probs, keys_all[:keys, vcols])).astype(BF16)
    probs_out.send()
    att_out.send()
    done(out_own, wout, sems.at[1])
    part_out.put(mm(att_out.ref[...], wout[...]).astype(BF16))


def load_mlp(meta, layer, weights, wup, wdown, vec, sems, vec_sem, chunk):
    vec_own, vec_other, up_own, up_other, down_own, down_other = weights
    pick(meta, layer, vec_own, vec_other, vec.at[0], vec_sem)
    for at in range(wup.shape[1] // chunk):
        cols = pl.ds(at * chunk, chunk)
        pick(meta, layer, up_own.at[:, cols], up_other.at[:, cols], wup.at[:, cols], sems.at[0, at])
        pick(meta, layer, down_own.at[cols], down_other.at[cols], wdown.at[cols], sems.at[1, at])


def await_mlp(at, weights, wup, wdown, sems, chunk):
    cols = pl.ds(at * chunk, chunk)
    done(weights[2].at[:, cols], wup.at[:, cols], sems.at[0, at])
    done(weights[4].at[cols], wdown.at[cols], sems.at[1, at])


def mlp_forward_kernel(layer, half, last, chunk, meta, loads, weights, outs, wup, wdown, vec, sems, vec_sem):
    rows_in, own, other = take(loads, 3)
    if last:
        cot_mine, cot_far = take(loads, 2)
        sums_in = loads[0] if loads else None
        middle_out, normed_out, active_out, part_out, cot_out, low_out, hid_out, gpart_out, sums_out = outs
    else:
        middle_out, normed_out, active_out, part_out, slope_out = outs
    width = wup.shape[0]
    load_mlp(meta, layer, weights, wup, wdown, vec, sems, vec_sem, chunk)
    done(weights[0], vec.at[0], vec_sem)
    branch = own.get().astype(F32) + other.get().astype(F32) + vec[0, OUT_BIAS : OUT_BIAS + 1, :width]
    middle = expand(rows_in.get().astype(F32)) + center(branch)
    middle_out.put(middle)
    normed = (middle * inv_rms(middle) * vec[0, MLP_GAIN : MLP_GAIN + 1, :width]).astype(BF16)
    normed_out.put(normed)

    def add_sums(places, terms):
        terms = col_sum(terms)
        sums_out.ref[:, places] = terms if sums_in is None else terms + sums_in()[:, places]

    if last:
        cot = jnp.where(meta[1] == half, cot_mine.get(), cot_far.get()).astype(F32).T
        cot_out.put(cot.astype(BF16))
        low = center(cot).astype(BF16)
        low_out.put(low)
        add_sums(slice(0, width), low)
    part = None
    gpart = None
    for at in range(wup.shape[1] // chunk):
        here = slice(at * chunk, (at + 1) * chunk)
        await_mlp(at, weights, wup, wdown, sems, chunk)
        hidden = mm(normed, wup[:, here]) + vec[0, UP_BIAS : UP_BIAS + 1, here]
        square = hidden * hidden
        root = (2.0 / jnp.pi) ** 0.5
        bent = jnp.tanh(hidden * (root + (root * 0.044715) * square))
        half_up = 0.5 + 0.5 * bent
        active = (hidden * half_up).astype(BF16)
        slope = half_up + hidden * (0.5 - 0.5 * bent * bent) * (root + (3 * root * 0.044715) * square)
        active_out.ref[:, here] = active
        term = mm(active, wdown[here, :])
        part = term if part is None else part + term
        if last:
            hid = (mm_t(low, wdown[here, :]) * slope).astype(BF16)
            hid_out.ref[:, here] = hid
            add_sums(slice(width + at * chunk, width + (at + 1) * chunk), hid)
            term = mm_t(hid, wup[:, here])
            gpart = term if gpart is None else gpart + term
        else:
            slope_out.ref[:, here] = slope.astype(BF16)
    if last:
        gpart_out.put(gpart.astype(BF16))
    part_out.put(part.astype(BF16))


def mlp_backward_kernel(chunk, meta, loads, weights, outs, wup, wdown, vec, sems, vec_sem, later_vec, later_sem):
    grad_later, own, other, rows_in, slope_in = take(loads, 5)
    sums_in = loads[0] if loads else None
    grad_out, low_out, hid_out, gpart_out, sums_out = outs
    width = wup.shape[0]
    hidden = wup.shape[1]
    pick(meta, 1, weights[0], weights[1], later_vec, later_sem)
    load_mlp(meta, 0, weights, wup, wdown, vec, sems, vec_sem, chunk)
    done(weights[0], later_vec, later_sem)
    rows = expand(rows_in.get().astype(F32))
    grad = own.get().astype(F32) + other.get().astype(F32)
    pulled, gain_terms = norm_pull(rows, inv_rms(rows), later_vec[ATTN_GAIN : ATTN_GAIN + 1, :width], grad)
    grad_in = grad_later.get() + pulled
    grad_in = (grad_in - grad_in[:, width - 1 :]).astype(BF16).astype(F32)
    grad_in = center(grad_in)
    grad_out.put(grad_in)
    low = grad_in.astype(BF16)
    low_out.put(low)

    def add_sums(places, terms):
        terms = col_sum(terms)
        sums_out.ref[:, places] = terms if sums_in is None else terms + sums_in()[:, places]

    add_sums(slice(0, width), low)
    add_sums(slice(width + hidden, 2 * width + hidden), gain_terms)
    gpart = None
    slope = slope_in()
    done(weights[0], vec.at[0], vec_sem)
    for at in range(hidden // chunk):
        here = slice(at * chunk, (at + 1) * chunk)
        await_mlp(at, weights, wup, wdown, sems, chunk)
        hid = (mm_t(low, wdown[here, :]) * slope[:, here].astype(F32)).astype(BF16)
        hid_out.ref[:, here] = hid
        add_sums(slice(width + at * chunk, width + (at + 1) * chunk), hid)
        term = mm_t(hid, wup[:, here])
        gpart = term if gpart is None else gpart + term
    gpart_out.put(gpart.astype(BF16))


def attn_backward_kernel(layer, half, meta, loads, weights, outs, wqkv, wout, keys_all, vec, sems, vec_sems):
    upstream_in, own, other, middle_in, query_in, kv_in, probs_in = take(loads, 7)
    rows_in = take(loads, 1)[0] if layer == 0 else None
    (link,) = take(loads, 1)
    sums_in = loads[0] if loads else None
    vec_own, vec_other, qkv_own, qkv_other, out_own, out_other = weights
    grad_out, low_out, dqkv_out, gpart_out, sums_out = outs[:5]
    width = wqkv.shape[1]
    local = wqkv.shape[2]
    pick(meta, layer, vec_own, vec_other, vec.at[0], vec_sems.at[0])
    pick(meta, layer, out_own, out_other, wout, sems.at[1])
    pick(meta, layer, qkv_own, qkv_other, wqkv, sems.at[0])
    done(vec_own, vec.at[0], vec_sems.at[0])
    middle = middle_in.get()
    grad = own.get().astype(F32) + other.get().astype(F32)
    pulled, gain_terms = norm_pull(middle, inv_rms(middle), vec[0, MLP_GAIN : MLP_GAIN + 1, :width], grad)
    upstream = upstream_in.get()
    if layer == 1:
        upstream = center(upstream.astype(F32))
    grad_mid = upstream + pulled
    grad_out.put(grad_mid)
    low = grad_mid.astype(BF16)
    low_out.put(low)

    def add_sums(places, terms):
        terms = col_sum(terms)
        sums_out.ref[:, places] = terms if sums_in is None else terms + sums_in()[:, places]

    add_sums(slice(0, width), gain_terms)
    add_sums(slice(width, 2 * width), low)
    count = middle.shape[0]
    keys = (half + 1) * count
    if half:
        keys_all[:count] = link.get()
    keys_all[half * count : (half + 1) * count] = kv_in.get()
    done(out_own, wout, sems.at[1])
    grad_att = mm_t(low, wout[...]).astype(BF16)
    at = 2 * width
    query = query_in()
    all_probs = probs_in()
    later = link()
    dqkv = dqkv_out.ref
    for pair in range(local // LANES):
        cols = slice(pair * LANES, (pair + 1) * LANES)
        vcols = slice(local + pair * LANES, local + (pair + 1) * LANES)
        v2cols = slice(2 * local + pair * LANES, 2 * local + (pair + 1) * LANES)
        grads = halves(grad_att[:, cols])
        queries = halves(query[:, cols])
        low_probs = all_probs[pair]
        probs = low_probs.astype(F32)
        grad_probs = mm_t(grads, keys_all[:keys, vcols])
        inner = jnp.sum(grad_probs * probs, axis=-1, keepdims=True)
        grad_scores = (probs * (grad_probs - inner)).astype(BF16)
        grad_query = merge(mm(grad_scores, keys_all[:keys, cols])) * HEAD_DIM**-0.5
        grad_key = t_mm(grad_scores, queries)
        grad_value = t_mm(low_probs, grads)
        if half:
            outs[5].ref[:, cols] = grad_key[:count]
            outs[5].ref[:, vcols] = grad_value[:count]
            grad_key = grad_key[count:]
            grad_value = grad_value[count:]
        else:
            grad_key = grad_key + later[:, cols]
            grad_value = grad_value + later[:, vcols]
        grad_query = grad_query.astype(BF16)
        grad_value = grad_value.astype(BF16)
        dqkv[:, cols] = grad_query
        dqkv[:, vcols] = grad_key.astype(BF16)
        dqkv[:, v2cols] = grad_value
        add_sums(slice(at + pair * LANES, at + (pair + 1) * LANES), grad_query)
        add_sums(slice(at + local + pair * LANES, at + local + (pair + 1) * LANES), grad_value)
    done(qkv_own, wqkv, sems.at[0])
    gpart = mm_t(dqkv[:, :local], wqkv[0])
    gpart = gpart + mm_t(dqkv[:, local : 2 * local], wqkv[1])
    gpart = gpart + mm_t(dqkv[:, 2 * local :], wqkv[2])
    gpart_out.put(gpart.astype(BF16))
    if layer == 0:
        rows = expand(rows_in.get().astype(F32))
        at = 2 * width + 2 * local
        add_sums(slice(at, at + width), gpart * rows * inv_rms(rows))


def mlp_weights_kernel(meta, loads, weights, outs):
    norm0, hid0, norm1, hid1, act0, low0, act1, low1 = [load() for load in loads]
    width = low0.shape[1]
    hidden = act0.shape[1]
    block = outs[0].ref.shape[1]
    for out, part in ((outs[1], 1 - meta[0]), (outs[0], meta[0])):
        rows = width // 2
        cols = pl.ds(pl.multiple_of(part * rows, LANES), rows)
        left0, left1 = norm0[:, cols], norm1[:, cols]
        for at in range(hidden // block):
            here = slice(at * block, (at + 1) * block)
            total = t_mm(left0, hid0[:, here]) + t_mm(left1, hid1[:, here])
            out.ref[at * rows : (at + 1) * rows] = total.astype(BF16)
        base = hidden // block * rows
        rows = hidden // 2
        cols = pl.ds(pl.multiple_of(part * rows, LANES), rows)
        left0, left1 = act0[:, cols], act1[:, cols]
        for at in range(width // block):
            here = slice(at * block, (at + 1) * block)
            total = t_mm(left0, low0[:, here]) + t_mm(left1, low1[:, here])
            out.ref[base + at * rows : base + (at + 1) * rows] = total.astype(BF16)
        out.send()


def attn_weights_kernel(extra, meta, loads, weights, outs):
    norm0, dqkv0, norm1, dqkv1, att0, low0, att1, low1 = [load() for load in take(loads, 8)]
    width = low0.shape[1]
    local = att0.shape[1]
    piece = outs[0].ref.shape[0] // 8 - extra

    def put(out, first, total):
        for at in range(0, total.shape[0], piece):
            where = (first + at) // piece * (piece + extra)
            out[where : where + piece] = total[at : at + piece].astype(BF16)

    if extra:
        attn0, mlp0, attn1, mlp1, gain_own, gain_other = [load() for load in loads]
        hidden = mlp1.shape[1] - width
        smalls = []
        for gain, attn, mlp in (
            (gain_own[...] + gain_other[...], attn0, mlp0),
            (mlp0[:, width + hidden :], attn1, mlp1),
        ):
            row = [gain, attn[:, 2 * width : 2 * width + 2 * local], attn[:, width : 2 * width], attn[:, :width]]
            row += [mlp[:, width : width + hidden], mlp[:, :width]]
            lines = [part[:, at : at + local] for part in row for at in range(0, part.shape[1], local)]
            lines += [jnp.zeros((1, local), F32)] * (extra - len(lines))
            smalls.append(jnp.concatenate(lines, axis=0))

    for out, part in ((outs[1], 1 - meta[0]), (outs[0], meta[0])):
        rows = width // 2
        cols = pl.ds(pl.multiple_of(part * rows, LANES), rows)
        left0, left1 = norm0[:, cols], norm1[:, cols]
        for at in range(3):
            here = slice(at * local, (at + 1) * local)
            put(out.ref, at * rows, t_mm(left0, dqkv0[:, here]) + t_mm(left1, dqkv1[:, here]))
        put(out.ref, 3 * rows, t_mm(att0[...], low0[:, cols]) + t_mm(att1[...], low1[:, cols]))
        if extra:
            out.ref[piece : piece + extra] = jnp.where(part == 0, smalls[0], smalls[1]).astype(BF16)
            for at in range(1, 8):
                where = at * (piece + extra) + piece
                out.ref[where : where + extra] = jnp.zeros((extra, local), BF16)
        out.send()


def place_kernel(kinds, extra, *refs):
    refs = list(refs)
    (meta,) = take(refs, 1)
    sources = take(refs, 8)
    if extra:
        lines, line_sem = refs[-2:]
        del refs[-2:]
    outs = refs[:-4]
    low, wide, in_sems, out_sems = refs[-4:]
    piece = low.shape[1]
    step = piece + extra
    if extra:
        at = pl.multiple_of((meta[6] & 3) * step + piece, 16)
        for high in range(2):

            @pl.when((meta[6] >> 2) == high)
            def _():
                pltpu.make_async_copy(sources[high].at[pl.ds(at, extra)], lines, line_sem).start()

    def source(ref, block, place, layer):
        every = piece if layer else step
        return ref.at[pl.ds(pl.multiple_of(((block ^ place) & 3) * every, 16), piece)]

    for side in range(2):
        first_low, first_high, second_low, second_high = sources[4 * side : 4 * side + 4]
        place = meta[6 + side]
        for block in range(8):
            at = side * 8 + block
            for high, first, second in ((0, first_low, second_low), (1, first_high, second_high)):

                @pl.when(((block ^ place) >> 2) == high)
                def _():
                    parts = source(first, block, place, 0), source(second, block, place, 1)
                    pick(meta, 0, *parts, low.at[at], in_sems.at[at])

    if extra:
        done(sources[0].at[pl.ds(0, extra)], lines, line_sem)
        small = lines[...].astype(F32)
        at = 0
        for out in outs[2:]:
            for row in range(out.shape[0]):
                for col in range(0, out.shape[1], small.shape[1]):
                    out[row : row + 1, col : col + small.shape[1]] = small[at : at + 1]
                    at += 1

    copies = []
    for side in range(2):
        part = meta[0] if side == 0 else 1 - meta[0]
        for block in range(8):
            at = side * 8 + block
            done(source(sources[0], block, 0, 0), low.at[at], in_sems.at[at])
            wide[at] = low[at].astype(F32)
            which, where = kinds[block]
            copies.append(pltpu.make_async_copy(wide.at[at], outs[which].at[where(part)], out_sems.at[at]))
            copies[-1].start()
    for copy in copies:
        copy.wait()


def shape(dims, dtype=BF16):
    return jax.ShapeDtypeStruct(dims, dtype)


def call(kernel, in_specs, outs, scratch, args, flops, out_specs):
    return pl.pallas_call(
        kernel,
        out_shape=tuple(outs),
        in_specs=in_specs,
        out_specs=tuple(out_specs),
        scratch_shapes=scratch,
        compiler_params=pltpu.CompilerParams(vmem_limit_bytes=VMEM_BYTES),
        cost_estimate=pl.CostEstimate(flops=1, bytes_accessed=1, transcendentals=0),
    )(*args)


def in_vmem(array):
    return jax.typeof(array).memory_space == pltpu.VMEM


def framed_call(body, meta, loads, weights, outs, scratch, flops):
    held = [in_vmem(a) for a in loads]
    places = [out[0] for out in outs]
    kernel = functools.partial(framed, body, held, len(weights), places)
    moving = [a for a, here in zip(loads, held) if not here]
    scratch = [
        *[pltpu.VMEM(a.shape, a.dtype) for a in moving],
        *[pltpu.VMEM(dims, dtype) for place, dims, dtype in outs if place == "hbm"],
        pltpu.SemaphoreType.DMA((len(moving) + 1,)),
        pltpu.SemaphoreType.DMA((len(outs),)),
        *scratch,
    ]
    specs = [SMEM] + [VMEM if here else HBM for here in held] + [HBM] * len(weights)
    shapes, out_specs = [], []
    for place, dims, dtype in outs:
        for space in ("vmem", "hbm"):
            if place in (space, "both"):
                shapes.append((pltpu.VMEM if space == "vmem" else pltpu.HBM)(dims, dtype))
                out_specs.append(VMEM if space == "vmem" else HBM)
    flat = list(call(kernel, specs, shapes, scratch, [meta, *loads, *weights], flops, out_specs))
    return [tuple(take(flat, 2)) if place == "both" else take(flat, 1)[0] for place in places]


def swap(array, axis):
    return lax.ppermute(array, axis, [(0, 1), (1, 0)])


def total(left, right):
    return (left.astype(F32) + right.astype(F32)).astype(BF16)


class GroupSum:
    def __init__(self, mine, theirs):
        self.flow = self.run(mine, theirs)
        self.pending = next(self.flow)
        self.result = None

    def tie(self, value):
        if self.result is not None:
            return value
        value, *arrays = lax.optimization_barrier((value, *self.pending))
        self.advance(arrays)
        return value

    def advance(self, arrays):
        try:
            self.pending = self.flow.send(arrays)
        except StopIteration as stop:
            self.result = stop.value

    def finish(self):
        while self.result is None:
            self.advance(self.pending)
        return self.result

    @staticmethod
    def orders(bits):
        first = list(range(bits))
        second = [1, 0] + first[2:] if bits > 1 else first
        return first, second

    @staticmethod
    def exchange(array, bits):
        count = lax.axis_size("dp")
        pairs = [(core * count + i, core * count + (i ^ (1 << bit))) for core, bit in enumerate(bits) for i in range(count)]
        return lax.ppermute(array, ("section", "dp"), pairs)

    @staticmethod
    def place(bits, core):
        index = lax.axis_index("dp")
        out = jnp.int32(0)
        for first, second in zip(*GroupSum.orders(bits)):
            out = out * 2 + ((index >> jnp.where(core == 0, first, second)) & 1)
        return out

    def run(self, mine, theirs):
        core = lax.axis_index("section")
        index = lax.axis_index("dp")
        steps = list(zip(*self.orders(lax.axis_size("dp").bit_length() - 1)))
        mine, theirs = yield mine, theirs
        held, received = mine, swap(theirs, "section")
        for bits in steps:
            side = (index >> jnp.where(core == 0, bits[0], bits[1])) & 1
            rows = held.shape[0] // 2
            both = total(held, received)
            held = lax.dynamic_slice_in_dim(both, side * rows, rows, 0)
            send = lax.dynamic_slice_in_dim(both, (1 - side) * rows, rows, 0)
            held, send = yield held, send
            received = self.exchange(send, bits)
        (held,) = yield (total(held, received),)
        for bits in steps[:0:-1]:
            received = self.exchange(held, bits)
            (held,) = yield (jnp.concatenate([held, received], axis=0),)
        received = self.exchange(held, steps[0])
        return held, received


def in_order(pieces, place, count):
    array = jnp.concatenate(pieces, axis=0)
    blocks = array.reshape((count, array.shape[0] // count) + array.shape[1:])
    array = jnp.take(blocks, jnp.arange(count, dtype=jnp.int32) ^ place, axis=0).reshape(array.shape)
    rows = array.shape[0] // 2
    return array[:rows], array[rows:]


def local(
    inputs,
    doc_lengths,
    attn_gain,
    qkv_weight,
    qv_bias,
    out_weight,
    out_bias,
    mlp_gain,
    up_weight,
    up_bias,
    down_weight,
    down_bias,
    cotangent,
):
    core = lax.axis_index("section")
    side = lax.axis_index("tensor")
    groups = lax.axis_size("dp")
    bits = groups.bit_length() - 1
    place = GroupSum.place(bits, core)
    rows = inputs.shape[1]
    width = attn_gain.shape[1]
    heads = qkv_weight.shape[3]
    hidden = up_weight.shape[2]
    pairs = heads // LANES
    chunk = 768

    def own_rows(array):
        mine = lax.dynamic_index_in_dim(jnp.transpose(array, (2, 0, 1)), core, 1, keepdims=False)
        return jnp.pad(mine, ((0, width - mine.shape[0]), (0, 0)))

    lengths = lax.dynamic_index_in_dim(doc_lengths[:, 0, :], core, 0, keepdims=False)
    if groups == 8:
        places = [place, GroupSum.place(bits, 1 - core)]
    else:
        places = [jnp.int32(0)] * 2
    meta = jnp.concatenate([jnp.stack([core, side]).astype(jnp.int32), lengths, jnp.stack(places)])

    entry = own_rows(inputs)
    small_in = (attn_gain, qv_bias[0], out_bias, mlp_gain, up_bias, down_bias)
    qkv, out = jnp.transpose(qkv_weight[0], (1, 0, 2)), out_weight[0]
    entry, qkv, out, *small_in = lax.optimization_barrier((entry, qkv, out, *small_in))
    entry = (entry, swap(entry, "tensor"))
    qkv_pair = (qkv, swap(qkv, "section"))
    out_pair = (out, swap(out, "section"))
    (vector,) = call(
        pack_kernel, [VMEM] * len(small_in), [shape((8, hidden), F32)], [], small_in, 0, [VMEM]
    )
    vec_pair = (vector, swap(vector, "section"))
    up, down, _ = lax.optimization_barrier((up_weight[0], down_weight[0], vector))
    up_pair = (up, swap(up, "section"))
    down_pair = (down, swap(down, "section"))
    cotangent, _ = lax.optimization_barrier((cotangent, entry[1]))
    cots = own_rows(cotangent)
    cots = (cots, swap(cots, "tensor"))

    attn_scratch = [
        pltpu.VMEM(qkv.shape, BF16),
        pltpu.VMEM(out.shape, BF16),
        pltpu.VMEM((2 * rows, 2 * heads), BF16),
        pltpu.VMEM((2,) + vector.shape, F32),
        pltpu.SemaphoreType.DMA((2,)),
        pltpu.SemaphoreType.DMA((2,)),
    ]
    mlp_scratch = [
        pltpu.VMEM(up.shape, BF16),
        pltpu.VMEM(down.shape, BF16),
        pltpu.VMEM((1,) + vector.shape, F32),
        pltpu.SemaphoreType.DMA((2, hidden // chunk)),
        pltpu.SemaphoreType.DMA,
    ]
    attn_flops = 2 * rows * width * heads * 4
    mlp_flops = 4 * rows * width * hidden
    attn_all = [*vec_pair, *qkv_pair, *out_pair]
    mlp_all = [*vec_pair, *up_pair, *down_pair]

    def attn_forward(layer, half, rows_in, kv):
        args = [*rows_in] + ([kv] if half else [])
        outs = [
            ("both", (rows, width), BF16),
            ("hbm", (rows, width), BF16),
            ("hbm", (rows, heads), BF16),
            ("hbm" if half else "both", (rows, 2 * heads), BF16),
            ("hbm", (rows, heads), BF16),
            ("hbm", (pairs, 2 * rows, (half + 1) * rows), BF16),
            ("vmem", (rows, width), BF16),
        ]
        kernel = functools.partial(attn_forward_kernel, layer, half)
        return framed_call(kernel, meta, args, attn_all, outs, attn_scratch, attn_flops)

    def mlp_forward(half, rows_in, own, given):
        outs = [
            ("both", (rows, width), F32),
            ("hbm", (rows, width), BF16),
            ("hbm", (rows, hidden), BF16),
            ("vmem", (rows, width), BF16),
            ("hbm", (rows, hidden), BF16),
        ]
        kernel = functools.partial(mlp_forward_kernel, 0, half, False, chunk)
        return framed_call(kernel, meta, [rows_in, own, given], mlp_all, outs, mlp_scratch, mlp_flops)

    def mlp_both(half, rows_in, own, given, sums):
        outs = [
            ("both", (rows, width), F32),
            ("vmem", (rows, width), BF16),
            ("vmem", (rows, hidden), BF16),
            ("hbm", (rows, width), BF16),
            ("vmem", (rows, width), BF16),
            ("vmem", (rows, width), BF16),
            ("vmem", (rows, hidden), BF16),
            ("vmem", (rows, width), BF16),
            ("hbm" if half else "vmem", (1, width + hidden), F32),
        ]
        kernel = functools.partial(mlp_forward_kernel, 1, half, True, chunk)
        args = [rows_in, own, given, *cots, *sums]
        return framed_call(kernel, meta, args, mlp_all, outs, mlp_scratch, 2 * mlp_flops)

    def mlp_backward(meta, half, grad, own, given, rows_in, slope, sums):
        outs = [
            ("vmem", (rows, width), F32),
            ("vmem", (rows, width), BF16),
            ("vmem", (rows, hidden), BF16),
            ("vmem", (rows, width), BF16),
            ("vmem" if half else "hbm", (1, 2 * width + hidden), F32),
        ]
        kernel = functools.partial(mlp_backward_kernel, chunk)
        scratch = [*mlp_scratch, pltpu.VMEM(vector.shape, F32), pltpu.SemaphoreType.DMA]
        args = [grad, own, given, rows_in, slope, *sums]
        return framed_call(kernel, meta, args, mlp_all, outs, scratch, mlp_flops)

    def attn_backward(meta, layer, half, grad, own, given, middle, query, kv, probs, rows_in, link, sums):
        args = [grad, own, given, middle, query, kv, probs]
        if layer == 0:
            args.append(rows_in)
        args += [link, *sums]
        outs = [
            ("vmem" if layer else "hbm", (rows, width), F32),
            ("vmem", (rows, width), BF16),
            ("vmem", (rows, 3 * heads), BF16),
            ("vmem", (rows, width), BF16),
            ("vmem" if half else "hbm", (1, (2 if layer else 3) * width + 2 * heads), F32),
        ]
        if half:
            outs.append(("vmem", (rows, 2 * heads), F32))
        kernel = functools.partial(attn_backward_kernel, layer, half)
        return framed_call(kernel, meta, args, attn_all, outs, attn_scratch, 2 * attn_flops)

    def mlp_weights(*args):
        outs = [("hbm", (hidden * width // 384, 384), BF16)] * 2
        return GroupSum(*framed_call(mlp_weights_kernel, meta, args, [], outs, [], 2 * mlp_flops))

    def attn_weights(meta, extra, *args):
        outs = [("hbm", (2 * width * heads // 384 + 8 * extra, 384), BF16)] * 2
        kernel = functools.partial(attn_weights_kernel, extra)
        return GroupSum(*framed_call(kernel, meta, args, [], outs, [], 2 * attn_flops))

    rows0, normed0, query0, kv0, att0, probs0, part0, given0 = [[None, None] for _ in range(8)]
    for half in range(2):
        rows0[half], normed0[half], query0[half], kv0[half], att0[half], probs0[half], part0[half] = attn_forward(
            0, half, entry, kv0[0][0] if half else None
        )
        given0[half] = swap(part0[half], "tensor")
    mid0, low_n0, act0, mpart0, slope0, mgiven0 = [[None, None] for _ in range(6)]
    for half in range(2):
        mid0[half], low_n0[half], act0[half], mpart0[half], slope0[half] = mlp_forward(
            half, rows0[half][0], part0[half], given0[half]
        )
        mgiven0[half] = swap(mpart0[half], "tensor")
    rows1, normed1, query1, kv1, att1, probs1, part1, given1 = [[None, None] for _ in range(8)]
    for half in range(2):
        rows1[half], normed1[half], query1[half], kv1[half], att1[half], probs1[half], part1[half] = attn_forward(
            1, half, [mid0[half][0], mpart0[half], mgiven0[half]], kv1[0][0] if half else None
        )
        given1[half] = swap(part1[half], "tensor")
    mid1, low_n1, act1, mpart1, cot, low1, hid1, gpart1, ggiven1 = [[None, None] for _ in range(9)]
    sums_m1 = []
    for half in range(2):
        (
            mid1[half],
            low_n1[half],
            act1[half],
            mpart1[half],
            cot[half],
            low1[half],
            hid1[half],
            gpart1[half],
            sums,
        ) = mlp_both(half, rows1[half][0], part1[half], given1[half], sums_m1)
        sums_m1 = [sums]
        ggiven1[half] = swap(gpart1[half], "tensor")
    mlp1 = mlp_weights(low_n1[0], hid1[0], low_n1[1], hid1[1], act1[0], low1[0], act1[1], low1[1])
    grad1, glow1, dqkv1, apart1, agiven1 = [[None, None] for _ in range(5)]
    sums_a1 = []
    link = kv1[0][1]
    for half in (1, 0):
        tied = mlp1.tie(meta)
        grad1[half], glow1[half], dqkv1[half], apart1[half], sums, *rest = attn_backward(
            tied,
            1,
            half,
            cot[half],
            gpart1[half],
            ggiven1[half],
            mid1[half][0],
            query1[half],
            kv1[half] if half else kv1[half][1],
            probs1[half],
            None,
            link,
            sums_a1,
        )
        sums_a1 = [sums]
        link = rest[0] if half else None
        agiven1[half] = swap(apart1[half], "tensor")
    attn1 = attn_weights(meta, 0, normed1[0], dqkv1[0], normed1[1], dqkv1[1], att1[0], glow1[0], att1[1], glow1[1])
    grad0, low0, hid0, gpart0, ggiven0 = [[None, None] for _ in range(5)]
    sums_m0 = []
    for half in (1, 0):
        tied = mlp1.tie(attn1.tie(meta))
        grad0[half], low0[half], hid0[half], gpart0[half], sums = mlp_backward(
            tied, half, grad1[half], apart1[half], agiven1[half], rows1[half][1], slope0[half], sums_m0
        )
        sums_m0 = [sums]
        ggiven0[half] = swap(gpart0[half], "tensor")
    mlp0 = mlp_weights(low_n0[0], hid0[0], low_n0[1], hid0[1], act0[0], low0[0], act0[1], low0[1])
    gmid0, glow0, dqkv0, apart0 = [[None, None] for _ in range(4)]
    sums_a0 = []
    link = kv0[0][1]
    for half in (1, 0):
        tied = mlp1.tie(attn1.tie(mlp0.tie(meta)))
        gmid0[half], glow0[half], dqkv0[half], apart0[half], sums, *rest = attn_backward(
            tied,
            0,
            half,
            grad0[half],
            gpart0[half],
            ggiven0[half],
            mid0[half][1],
            query0[half],
            kv0[half] if half else kv0[half][1],
            probs0[half],
            rows0[half][1],
            link,
            sums_a0,
        )
        sums_a0 = [sums]
        link = rest[0] if half else None
    gain0 = sums_a0[0][:, 2 * width + 2 * heads :]
    gain0 = (gain0, swap(gain0, "tensor"))
    extra = 16
    tied = mlp1.tie(attn1.tie(mlp0.tie(meta)))
    attn0 = attn_weights(
        tied,
        extra,
        *[normed0[0], dqkv0[0], normed0[1], dqkv0[1], att0[0], glow0[0], att0[1], glow0[1]],
        *[*sums_a0, *sums_m0, *sums_a1, *sums_m1, *gain0],
    )

    def chosen(pair):
        return jnp.where(side == 0, pair[0], pair[1])

    def own_half(parts):
        return chosen(parts).astype(F32) + swap(chosen(parts[::-1]), "tensor").astype(F32)

    def vector_of(layer, row):
        mine, other = (v[row : row + 1, :width] for v in vec_pair)
        return jnp.where(core == layer, mine, other)

    mpart1[0], mpart1[1], _ = lax.optimization_barrier((mpart1[0], mpart1[1], apart0[1]))
    branch = own_half(mpart1) + vector_of(1, DOWN_BIAS)
    result = (chosen([m[1] for m in mid1]) + center(branch))[:, : width - 1].astype(BF16)
    entry_rows = expand(chosen([r[1] for r in rows0]).astype(F32))
    pulled, _ = norm_pull(entry_rows, inv_rms(entry_rows), vector_of(0, ATTN_GAIN), own_half(apart0))
    grad_in = chosen(gmid0) + pulled
    grad_in = (grad_in[:, : width - 1] - grad_in[:, width - 1 :]).astype(BF16)

    mlp1, attn1, mlp0, attn0 = (flow.finish() for flow in (mlp1, attn1, mlp0, attn0))
    if groups != 8:
        mlp0, mlp1, attn0, attn1 = (in_order(a, place, groups) for a in (mlp0, mlp1, attn0, attn1))

    def over(pieces, layer):
        return [lax.ppermute(a, "section", [(1 - layer, layer)]) for a in pieces]

    up_rows, down_rows = width // 2, hidden // 2

    def mlp_kind(block):
        if block < 4:
            return 0, lambda part: (pl.ds(pl.multiple_of(part * up_rows, 8), up_rows), pl.ds(block * 384, 384))
        col, row = (block - 4) // 2, (block - 4) % 2
        return 1, lambda part: (
            pl.ds(pl.multiple_of(part * down_rows + row * 384, 8), 384),
            pl.ds(col * 384, 384),
        )

    def attn_kind(block):
        which, row = block // 2, block % 2
        if which < 3:
            return 0, lambda part: (which, pl.ds(pl.multiple_of(part * up_rows + row * 192, 8), 192), slice(None))
        return 1, lambda part: (pl.ds(row * 192, 192), pl.ds(pl.multiple_of(part * 384, 128), 384))

    def placed(kinds, extra_rows, first, second, outs):
        piece = first[0].shape[0] // 4 - extra_rows
        args = [meta, *first, *second, *over(first, 0), *over(second, 1)]
        scratch = [
            pltpu.VMEM((16, piece, 384), BF16),
            pltpu.VMEM((16, piece, 384), F32),
            pltpu.SemaphoreType.DMA((16,)),
            pltpu.SemaphoreType.DMA((16,)),
        ]
        out_specs = [HBM, HBM] + [VMEM] * (len(outs) - 2)
        if extra_rows:
            scratch += [pltpu.VMEM((extra_rows, 384), BF16), pltpu.SemaphoreType.DMA]
        kernel = functools.partial(place_kernel, kinds, extra_rows)
        return call(kernel, [SMEM] + [HBM] * 8, outs, scratch, args, 0, out_specs)

    grad_up, grad_down = placed(
        [mlp_kind(b) for b in range(8)], 0, mlp0, mlp1, [shape((width, hidden), F32), shape((hidden, width), F32)]
    )
    grad_qkv, grad_out, *small = placed(
        [attn_kind(b) for b in range(8)],
        extra,
        attn0,
        attn1,
        [shape((3, width, heads), F32), shape((heads, width), F32)]
        + [shape(dims, F32) for dims in ((1, width), (2, heads), (1, width), (1, width), (1, hidden), (1, width))],
    )

    return (
        result[None],
        grad_in[None],
        small[0],
        jnp.transpose(grad_qkv, (1, 0, 2))[None],
        small[1][None],
        grad_out[None],
        small[2],
        small[3],
        grad_up[None],
        small[4],
        grad_down[None],
        small[5],
    )


def solution(mesh):
    in_specs = (
        P(None, ("dp", "tensor"), None),
        P(None, "dp", None),
        P("section", None),
        P("section", None, None, "tensor"),
        P("section", None, "tensor"),
        P("section", "tensor", None),
        P("section", None),
        P("section", None),
        P("section", None, "tensor"),
        P("section", "tensor"),
        P("section", "tensor", None),
        P("section", None),
        P(None, ("dp", "tensor"), None),
    )
    out_specs = (
        P("section", ("dp", "tensor"), None),
        P("section", ("dp", "tensor"), None),
        P("section", None),
        P("section", None, None, "tensor"),
        P("section", None, "tensor"),
        P("section", "tensor", None),
        P("section", None),
        P("section", None),
        P("section", None, "tensor"),
        P("section", "tensor"),
        P("section", "tensor", None),
        P("section", None),
    )
    return jax.shard_map(local, mesh=mesh, in_specs=in_specs, out_specs=out_specs, check_vma=False)
```

```python
import functools
import math

import jax
import jax.numpy as jnp
from jax import lax
from jax.experimental import pallas as pl
from jax.experimental.pallas import tpu as pltpu
from jax.sharding import PartitionSpec as P

HEAD_DIM = 64
LANES = 128
EPS = 1e-05
NEG = -1e30
VMEM_BYTES = 24 * 1024 * 1024

F32 = jnp.float32
BF16 = jnp.bfloat16

SMEM = pl.BlockSpec(memory_space=pltpu.SMEM)
VMEM = pl.BlockSpec(memory_space=pltpu.VMEM)
HBM = pl.BlockSpec(memory_space=pltpu.HBM)


def mm(left, right):
    return jnp.dot(left, right, preferred_element_type=F32)


def mm_t(left, right):
    return lax.dot_general(left, right, (((1,), (1,)), ((), ())), preferred_element_type=F32)


def t_mm(left, right):
    return lax.dot_general(left, right, (((0,), (0,)), ((), ())), preferred_element_type=F32)


def row_mean(array):
    return jnp.mean(array, axis=-1, keepdims=True)


def center(array):
    return array - row_mean(array)


def last_lane(shape):
    return lax.broadcasted_iota(jnp.int32, shape, 1) == shape[1] - 1


def expand(rows):
    return jnp.where(last_lane(rows.shape), -jnp.sum(rows, axis=-1, keepdims=True), rows)


def inv_rms(rows):
    return lax.rsqrt(row_mean(rows * rows) + EPS)


def norm_pull(rows, scaling, gain, grad):
    gained = gain * grad
    inner = row_mean(gained * rows)
    grad_rows = scaling * gained - rows * (scaling * scaling * scaling * inner)
    return center(grad_rows), grad * rows * scaling


def col_sum(array):
    return jnp.sum(array.astype(F32), axis=0, keepdims=True)


def pick(meta, layer, own, other, dst, sem):
    @pl.when(meta[0] == layer)
    def _():
        pltpu.make_async_copy(own, dst, sem).start()

    @pl.when(meta[0] != layer)
    def _():
        pltpu.make_async_copy(other, dst, sem).start()


def done(src, dst, sem):
    pltpu.make_async_copy(src, dst, sem).wait()


def halves(pair):
    first = lax.broadcasted_iota(jnp.int32, pair.shape, 1) < HEAD_DIM
    zero = jnp.zeros_like(pair)
    return jnp.concatenate([jnp.where(first, pair, zero), jnp.where(first, zero, pair)], axis=0)


def merge(stacked):
    rows = stacked.shape[0] // 2
    first = lax.broadcasted_iota(jnp.int32, (rows, stacked.shape[1]), 1) < HEAD_DIM
    return jnp.where(first, stacked[:rows], stacked[rows:])


def owner(meta, places):
    total = jnp.zeros(places.shape, jnp.int32)
    bound = 0
    for doc in range(3):
        bound = bound + meta[2 + doc]
        total = total + (places >= bound).astype(jnp.int32)
    return total


def mask_bias(meta, half, rows, keys):
    row_at = lax.broadcasted_iota(jnp.int32, (rows, 1), 0) + half * rows
    key_at = lax.broadcasted_iota(jnp.int32, (1, keys), 1)
    allowed = (owner(meta, row_at) == owner(meta, key_at)) & (key_at <= row_at)
    return jnp.where(allowed, 0.0, NEG).astype(F32)


class Load:
    def __init__(self, src, dst, sem):
        self.copy = pltpu.make_async_copy(src, dst, sem)
        self.copy.start()
        self.ref = dst
        self.waited = False

    def __call__(self):
        if not self.waited:
            self.copy.wait()
            self.waited = True
        return self.ref

    def get(self):
        return self()[...]


class Held:
    def __init__(self, ref):
        self.ref = ref

    def __call__(self):
        return self.ref

    def get(self):
        return self.ref[...]


class Store:
    def __init__(self, ref):
        self.ref = ref
        self.copies = []
        self.sent = False

    def put(self, value):
        self.ref[...] = value
        self.send()

    def send(self):
        self.sent = True
        for copy in self.copies:
            copy.start()


def take(refs, count):
    out = refs[:count]
    del refs[:count]
    return out


def framed(body, held, n_weights, places, *refs):
    refs = list(refs)
    (meta,) = take(refs, 1)
    sources, weights = take(refs, len(held)), take(refs, n_weights)
    targets = [take(refs, 2 if place == "both" else 1) for place in places]
    buffers = take(refs, held.count(False))
    made = take(refs, places.count("hbm"))
    in_sems, out_sems = take(refs, 2)
    loads = []
    moved = 0
    for source, here in zip(sources, held):
        if here:
            loads.append(Held(source))
        else:
            loads.append(Load(source, buffers[moved], in_sems.at[moved]))
            moved += 1
    stores = []
    for at, (place, target) in enumerate(zip(places, targets)):
        store = Store(made.pop(0) if place == "hbm" else target[0])
        if place != "vmem":
            store.copies.append(pltpu.make_async_copy(store.ref, target[-1], out_sems.at[at]))
        stores.append(store)
    body(meta, list(loads), weights, stores, *refs)
    for load in loads:
        load()
    for store in stores:
        if not store.sent:
            store.send()
    for store in stores:
        for copy in store.copies:
            copy.wait()


ATTN_GAIN, QV_BIAS, OUT_BIAS, MLP_GAIN, UP_BIAS, DOWN_BIAS = range(6)


def pack_kernel(*refs):
    *refs, target, out = refs
    out[...] = jnp.zeros(out.shape, F32)
    for row, ref in enumerate(refs):
        if ref.shape[0] == 2:
            half = ref.shape[1]
            out[row : row + 1, :half] = ref[0:1]
            out[row : row + 1, half : 2 * half] = ref[1:2]
        else:
            out[row : row + 1, : ref.shape[1]] = ref[...]
    pltpu.sync_copy(out, target.at[pl.ds(0, out.shape[0])])


def attn_forward_kernel(layer, half, meta, loads, weights, outs, wall, keys_all, vec, sems, vec_sems):
    if layer == 0:
        mine, far = take(loads, 2)
    else:
        middle_in, own, other = take(loads, 3)
    early_kv = take(loads, 1)[0] if half else None
    vec_own, vec_other, all_own, all_other = weights
    rows_out, normed_out, query_out, kv_out, att_out, probs_out, part_out = outs
    width = wall.shape[1]
    local = wall.shape[2]
    pick(meta, 0, vec_own.at[pl.ds(0, 8)], vec_other.at[pl.ds(0, 8)], vec.at[0], vec_sems.at[0])
    if layer:
        pick(meta, layer, vec_own.at[pl.ds(0, 8)], vec_other.at[pl.ds(0, 8)], vec.at[layer], vec_sems.at[layer])
    pick(meta, layer, all_own.at[pl.ds(0, 3)], all_other.at[pl.ds(0, 3)], wall.at[pl.ds(0, 3)], sems.at[0])
    pick(meta, layer, all_own.at[3], all_other.at[3], wall.at[3], sems.at[1])
    done(vec_own.at[pl.ds(0, 8)], vec.at[0], vec_sems.at[0])
    if layer:
        done(vec_own.at[pl.ds(0, 8)], vec.at[layer], vec_sems.at[layer])
    if layer == 0:
        rows = jnp.where(meta[1] == half, mine.get(), far.get()).astype(F32).T
    else:
        branch = own.get().astype(F32) + other.get().astype(F32) + vec[0, DOWN_BIAS : DOWN_BIAS + 1, :width]
        rows = (middle_in.get() + center(branch)).astype(BF16).astype(F32)
        rows = jnp.where(last_lane(rows.shape), 0.0, rows)
    rows_out.put(rows.astype(BF16))
    rows = expand(rows)
    normed = (rows * inv_rms(rows) * vec[layer, ATTN_GAIN : ATTN_GAIN + 1, :width]).astype(BF16)
    normed_out.put(normed)
    count = rows.shape[0]
    done(all_own.at[pl.ds(0, 3)], wall.at[pl.ds(0, 3)], sems.at[0])
    query_bias = vec[layer, QV_BIAS : QV_BIAS + 1, :local]
    value_bias = vec[layer, QV_BIAS : QV_BIAS + 1, local : 2 * local]
    query = ((mm(normed, wall[0]) + query_bias) * HEAD_DIM**-0.5).astype(BF16)
    key = mm(normed, wall[1]).astype(BF16)
    value = (mm(normed, wall[2]) + value_bias).astype(BF16)
    query_out.put(query)
    kv_out.ref[:, :local] = key
    kv_out.ref[:, local:] = value
    kv_out.send()
    if half:
        keys_all[:count] = early_kv.get()
    keys_all[half * count : (half + 1) * count, :local] = key
    keys_all[half * count : (half + 1) * count, local:] = value
    keys = (half + 1) * count
    masked = mask_bias(meta, half, count, keys)
    for pair in range(local // LANES):
        cols = slice(pair * LANES, (pair + 1) * LANES)
        vcols = slice(local + pair * LANES, local + (pair + 1) * LANES)
        scores = mm_t(halves(query[:, cols]), keys_all[:keys, cols])
        scores = (scores.reshape(2, count, keys) + masked[None]).reshape(2 * count, keys)
        expo = jnp.exp(scores - jnp.max(scores, axis=-1, keepdims=True))
        probs = (expo * (1.0 / jnp.sum(expo, axis=-1, keepdims=True))).astype(BF16)
        probs_out.ref[pair] = probs
        att_out.ref[:, cols] = merge(mm(probs, keys_all[:keys, vcols])).astype(BF16)
    probs_out.send()
    att_out.send()
    done(all_own.at[3], wall.at[3], sems.at[1])
    attended = att_out.ref[...]
    for at in range(2):
        cols = slice(at * local, (at + 1) * local)
        part_out.ref[:, cols] = mm(attended, wall[3, cols]).astype(BF16)
    part_out.send()


def load_mlp(meta, layer, weights, wup, wdown, vec, sems, vec_sem, chunk):
    vec_own, vec_other, up_own, up_other, down_own, down_other = weights
    pick(meta, layer, vec_own.at[pl.ds(0, 8)], vec_other.at[pl.ds(0, 8)], vec.at[0], vec_sem)
    for at in range(wup.shape[1] // chunk):
        cols = pl.ds(at * chunk, chunk)
        pick(meta, layer, up_own.at[:, cols], up_other.at[:, cols], wup.at[:, cols], sems.at[0, at])
        pick(meta, layer, down_own.at[cols], down_other.at[cols], wdown.at[cols], sems.at[1, at])


def await_mlp(at, weights, wup, wdown, sems, chunk):
    cols = pl.ds(at * chunk, chunk)
    done(weights[2].at[:, cols], wup.at[:, cols], sems.at[0, at])
    done(weights[4].at[cols], wdown.at[cols], sems.at[1, at])


def mlp_forward_kernel(layer, half, last, chunk, meta, loads, weights, outs, wup, wdown, vec, sems, vec_sem):
    rows_in, own, other = take(loads, 3)
    if last:
        cot_mine, cot_far = take(loads, 2)
        sums_in = loads[0] if loads else None
        middle_out, normed_out, active_out, part_out, cot_out, low_out, hid_out, gpart_out, sums_out = outs
    else:
        middle_out, normed_out, active_out, part_out, slope_out = outs
    width = wup.shape[0]
    load_mlp(meta, layer, weights, wup, wdown, vec, sems, vec_sem, chunk)
    done(weights[0].at[pl.ds(0, 8)], vec.at[0], vec_sem)
    branch = own.get().astype(F32) + other.get().astype(F32) + vec[0, OUT_BIAS : OUT_BIAS + 1, :width]
    middle = expand(rows_in.get().astype(F32)) + center(branch)
    middle_out.put(middle)
    normed = (middle * inv_rms(middle) * vec[0, MLP_GAIN : MLP_GAIN + 1, :width]).astype(BF16)
    normed_out.put(normed)

    def add_sums(places, terms):
        terms = col_sum(terms)
        sums_out.ref[:, places] = terms if sums_in is None else terms + sums_in()[:, places]

    if last:
        cot = jnp.where(meta[1] == half, cot_mine.get(), cot_far.get()).astype(F32).T
        cot_out.put(cot.astype(BF16))
        low = center(cot).astype(BF16)
        low_out.put(low)
        add_sums(slice(0, width), low)
    part = None
    gpart = None
    for at in range(wup.shape[1] // chunk):
        here = slice(at * chunk, (at + 1) * chunk)
        await_mlp(at, weights, wup, wdown, sems, chunk)
        hidden = mm(normed, wup[:, here]) + vec[0, UP_BIAS : UP_BIAS + 1, here]
        square = hidden * hidden
        root = (2.0 / jnp.pi) ** 0.5
        bent = jnp.tanh(hidden * (root + (root * 0.044715) * square))
        half_up = 0.5 + 0.5 * bent
        product = hidden * half_up
        active = product.astype(BF16)
        slope = half_up + product * (1.0 - half_up) * (2 * root + (6 * root * 0.044715) * square)
        active_out.ref[:, here] = active
        term = mm(active, wdown[here, :])
        part = term if part is None else part + term
        if last:
            hid = (mm_t(low, wdown[here, :]) * slope).astype(BF16)
            hid_out.ref[:, here] = hid
            add_sums(slice(width + at * chunk, width + (at + 1) * chunk), hid)
            term = mm_t(hid, wup[:, here])
            gpart = term if gpart is None else gpart + term
        else:
            slope_out.ref[:, here] = slope.astype(BF16)
    if last:
        gpart_out.put(gpart.astype(BF16))
    part_out.put(part.astype(BF16))


def mlp_backward_kernel(chunk, meta, loads, weights, outs, wup, wdown, vec, sems, vec_sem, later_vec, later_sem):
    grad_later, own, other, rows_in, slope_in = take(loads, 5)
    sums_in = loads[0] if loads else None
    grad_out, low_out, hid_out, gpart_out, sums_out = outs
    width = wup.shape[0]
    hidden = wup.shape[1]
    pick(meta, 1, weights[0].at[pl.ds(0, 8)], weights[1].at[pl.ds(0, 8)], later_vec, later_sem)
    load_mlp(meta, 0, weights, wup, wdown, vec, sems, vec_sem, chunk)
    done(weights[0].at[pl.ds(0, 8)], later_vec, later_sem)
    rows = expand(rows_in.get().astype(F32))
    grad = own.get().astype(F32) + other.get().astype(F32)
    pulled, gain_terms = norm_pull(rows, inv_rms(rows), later_vec[ATTN_GAIN : ATTN_GAIN + 1, :width], grad)
    grad_in = grad_later.get() + pulled
    grad_in = (grad_in - grad_in[:, width - 1 :]).astype(BF16).astype(F32)
    grad_in = center(grad_in)
    grad_out.put(grad_in)
    low = grad_in.astype(BF16)
    low_out.put(low)

    def add_sums(places, terms):
        terms = col_sum(terms)
        sums_out.ref[:, places] = terms if sums_in is None else terms + sums_in()[:, places]

    add_sums(slice(0, width), low)
    add_sums(slice(width + hidden, 2 * width + hidden), gain_terms)
    gpart = None
    slope = slope_in()
    done(weights[0].at[pl.ds(0, 8)], vec.at[0], vec_sem)
    for at in range(hidden // chunk):
        here = slice(at * chunk, (at + 1) * chunk)
        await_mlp(at, weights, wup, wdown, sems, chunk)
        hid = (mm_t(low, wdown[here, :]) * slope[:, here].astype(F32)).astype(BF16)
        hid_out.ref[:, here] = hid
        add_sums(slice(width + at * chunk, width + (at + 1) * chunk), hid)
        term = mm_t(hid, wup[:, here])
        gpart = term if gpart is None else gpart + term
    gpart_out.put(gpart.astype(BF16))


def attn_backward_kernel(layer, half, meta, loads, weights, outs, wall, keys_all, vec, sems, vec_sems):
    upstream_in, own, other, middle_in, query_in, kv_in, probs_in = take(loads, 7)
    rows_in = take(loads, 1)[0] if layer == 0 else None
    (link,) = take(loads, 1)
    sums_in = loads[0] if loads else None
    vec_own, vec_other, all_own, all_other = weights
    grad_out, low_out, dqkv_out, gpart_out, sums_out = outs[:5]
    width = wall.shape[1]
    local = wall.shape[2]
    pick(meta, layer, vec_own.at[pl.ds(0, 8)], vec_other.at[pl.ds(0, 8)], vec.at[0], vec_sems.at[0])
    pick(meta, layer, all_own.at[3], all_other.at[3], wall.at[3], sems.at[1])
    pick(meta, layer, all_own.at[pl.ds(0, 3)], all_other.at[pl.ds(0, 3)], wall.at[pl.ds(0, 3)], sems.at[0])
    done(vec_own.at[pl.ds(0, 8)], vec.at[0], vec_sems.at[0])
    middle = middle_in.get()
    grad = own.get().astype(F32) + other.get().astype(F32)
    pulled, gain_terms = norm_pull(middle, inv_rms(middle), vec[0, MLP_GAIN : MLP_GAIN + 1, :width], grad)
    upstream = upstream_in.get()
    if layer == 1:
        upstream = center(upstream.astype(F32))
    grad_mid = upstream + pulled
    grad_out.put(grad_mid)
    low = grad_mid.astype(BF16)
    low_out.put(low)

    def add_sums(places, terms):
        terms = col_sum(terms)
        sums_out.ref[:, places] = terms if sums_in is None else terms + sums_in()[:, places]

    add_sums(slice(0, width), gain_terms)
    add_sums(slice(width, 2 * width), low)
    count = middle.shape[0]
    keys = (half + 1) * count
    if half:
        keys_all[:count] = link.get()
    keys_all[half * count : (half + 1) * count] = kv_in.get()
    done(all_own.at[3], wall.at[3], sems.at[1])
    grad_att = (mm_t(low[:, :local], wall[3, :local]) + mm_t(low[:, local:], wall[3, local:])).astype(BF16)
    at = 2 * width
    query = query_in()
    all_probs = probs_in()
    later = link()
    dqkv = dqkv_out.ref
    for pair in range(local // LANES):
        cols = slice(pair * LANES, (pair + 1) * LANES)
        vcols = slice(local + pair * LANES, local + (pair + 1) * LANES)
        v2cols = slice(2 * local + pair * LANES, 2 * local + (pair + 1) * LANES)
        grads = halves(grad_att[:, cols])
        queries = halves(query[:, cols])
        low_probs = all_probs[pair]
        probs = low_probs.astype(F32)
        grad_probs = mm_t(grads, keys_all[:keys, vcols])
        inner = jnp.sum(grad_probs * probs, axis=-1, keepdims=True)
        grad_scores = (probs * (grad_probs - inner)).astype(BF16)
        grad_query = merge(mm(grad_scores, keys_all[:keys, cols])) * HEAD_DIM**-0.5
        grad_key = t_mm(grad_scores, queries)
        grad_value = t_mm(low_probs, grads)
        if half:
            outs[5].ref[:, cols] = grad_key[:count]
            outs[5].ref[:, vcols] = grad_value[:count]
            grad_key = grad_key[count:]
            grad_value = grad_value[count:]
        else:
            grad_key = grad_key + later[:, cols]
            grad_value = grad_value + later[:, vcols]
        grad_query = grad_query.astype(BF16)
        grad_value = grad_value.astype(BF16)
        dqkv[:, cols] = grad_query
        dqkv[:, vcols] = grad_key.astype(BF16)
        dqkv[:, v2cols] = grad_value
        add_sums(slice(at + pair * LANES, at + (pair + 1) * LANES), grad_query)
        add_sums(slice(at + local + pair * LANES, at + local + (pair + 1) * LANES), grad_value)
    done(all_own.at[pl.ds(0, 3)], wall.at[pl.ds(0, 3)], sems.at[0])
    gpart = mm_t(dqkv[:, :local], wall[0])
    gpart = gpart + mm_t(dqkv[:, local : 2 * local], wall[1])
    gpart = gpart + mm_t(dqkv[:, 2 * local :], wall[2])
    gpart_out.put(gpart.astype(BF16))
    if layer == 0:
        rows = expand(rows_in.get().astype(F32))
        at = 2 * width + 2 * local
        add_sums(slice(at, at + width), gpart * rows * inv_rms(rows))


def mlp_weights_kernel(meta, loads, weights, outs):
    norm0, hid0, norm1, hid1, act0, low0, act1, low1 = [load() for load in loads]
    width = low0.shape[1]
    hidden = act0.shape[1]
    block = outs[0].ref.shape[1]
    for out, part in ((outs[1], 1 - meta[0]), (outs[0], meta[0])):
        rows = width // 2
        cols = pl.ds(pl.multiple_of(part * rows, LANES), rows)
        left0, left1 = norm0[:, cols], norm1[:, cols]
        for at in range(hidden // block):
            here = slice(at * block, (at + 1) * block)
            total = t_mm(left0, hid0[:, here]) + t_mm(left1, hid1[:, here])
            out.ref[at * rows : (at + 1) * rows] = total.astype(BF16)
        base = hidden // block * rows
        rows = hidden // 2
        cols = pl.ds(pl.multiple_of(part * rows, LANES), rows)
        left0, left1 = act0[:, cols], act1[:, cols]
        for at in range(width // block):
            here = slice(at * block, (at + 1) * block)
            total = t_mm(left0, low0[:, here]) + t_mm(left1, low1[:, here])
            out.ref[base + at * rows : base + (at + 1) * rows] = total.astype(BF16)
        out.send()


def attn_weights_kernel(extra, meta, loads, weights, outs):
    norm0, dqkv0, norm1, dqkv1, att0, low0, att1, low1 = [load() for load in take(loads, 8)]
    width = low0.shape[1]
    local = att0.shape[1]
    piece = outs[0].ref.shape[0] // 8 - extra

    def put(out, first, total):
        for at in range(0, total.shape[0], piece):
            where = (first + at) // piece * (piece + extra)
            out[where : where + piece] = total[at : at + piece].astype(BF16)

    if extra:
        attn0, mlp0, attn1, mlp1, gain_own, gain_other = [load() for load in loads]
        hidden = mlp1.shape[1] - width
        smalls = []
        for gain, attn, mlp in (
            (gain_own[...] + gain_other[...], attn0, mlp0),
            (mlp0[:, width + hidden :], attn1, mlp1),
        ):
            row = [gain, attn[:, 2 * width : 2 * width + 2 * local], attn[:, width : 2 * width], attn[:, :width]]
            row += [mlp[:, width : width + hidden], mlp[:, :width]]
            lines = [part[:, at : at + local] for part in row for at in range(0, part.shape[1], local)]
            lines += [jnp.zeros((1, local), F32)] * (extra - len(lines))
            smalls.append(jnp.concatenate(lines, axis=0))

    for out, part in ((outs[1], 1 - meta[0]), (outs[0], meta[0])):
        rows = width // 2
        cols = pl.ds(pl.multiple_of(part * rows, LANES), rows)
        left0, left1 = norm0[:, cols], norm1[:, cols]
        for at in range(3):
            here = slice(at * local, (at + 1) * local)
            put(out.ref, at * rows, t_mm(left0, dqkv0[:, here]) + t_mm(left1, dqkv1[:, here]))
        put(out.ref, 3 * rows, t_mm(att0[...], low0[:, cols]) + t_mm(att1[...], low1[:, cols]))
        if extra:
            out.ref[piece : piece + extra] = jnp.where(part == 0, smalls[0], smalls[1]).astype(BF16)
            for at in range(1, 8):
                where = at * (piece + extra) + piece
                out.ref[where : where + extra] = jnp.zeros((extra, local), BF16)
        out.send()


def place_kernel(kinds, extra, *refs):
    refs = list(refs)
    (meta,) = take(refs, 1)
    sources = take(refs, 8)
    if extra:
        lines, line_sem = refs[-2:]
        del refs[-2:]
    outs = refs[:-4]
    low, wide, in_sems, out_sems = refs[-4:]
    piece = low.shape[1]
    step = piece + extra
    if extra:
        at = pl.multiple_of((meta[6] & 3) * step + piece, 16)
        for high in range(2):

            @pl.when((meta[6] >> 2) == high)
            def _():
                pltpu.make_async_copy(sources[high].at[pl.ds(at, extra)], lines, line_sem).start()

    def source(ref, block, place, layer):
        every = piece if layer else step
        return ref.at[pl.ds(pl.multiple_of(((block ^ place) & 3) * every, 16), piece)]

    for side in range(2):
        first_low, first_high, second_low, second_high = sources[4 * side : 4 * side + 4]
        place = meta[6 + side]
        for block in range(8):
            at = side * 8 + block
            for high, first, second in ((0, first_low, second_low), (1, first_high, second_high)):

                @pl.when(((block ^ place) >> 2) == high)
                def _():
                    parts = source(first, block, place, 0), source(second, block, place, 1)
                    pick(meta, 0, *parts, low.at[at], in_sems.at[at])

    if extra:
        done(sources[0].at[pl.ds(0, extra)], lines, line_sem)
        small = lines[...].astype(F32)
        at = 0
        for out in outs[2:]:
            for row in range(out.shape[0]):
                for col in range(0, out.shape[1], small.shape[1]):
                    out[row : row + 1, col : col + small.shape[1]] = small[at : at + 1]
                    at += 1

    copies = []
    for side in range(2):
        part = meta[0] if side == 0 else 1 - meta[0]
        for block in range(8):
            at = side * 8 + block
            done(source(sources[0], block, 0, 0), low.at[at], in_sems.at[at])
            wide[at] = low[at].astype(F32)
            which, where = kinds[block]
            copies.append(pltpu.make_async_copy(wide.at[at], outs[which].at[where(part)], out_sems.at[at]))
            copies[-1].start()
    for copy in copies:
        copy.wait()


def shape(dims, dtype=BF16):
    return jax.ShapeDtypeStruct(dims, dtype)


def call(kernel, in_specs, outs, scratch, args, out_specs):
    return pl.pallas_call(
        kernel,
        out_shape=tuple(outs),
        in_specs=in_specs,
        out_specs=tuple(out_specs),
        scratch_shapes=scratch,
        compiler_params=pltpu.CompilerParams(vmem_limit_bytes=VMEM_BYTES),
        cost_estimate=pl.CostEstimate(flops=1, bytes_accessed=1, transcendentals=0),
    )(*args)


class Near:
    def __init__(self, array):
        self.array = array


def framed_call(body, meta, loads, weights, outs, scratch):
    held = [isinstance(a, Near) for a in loads]
    places = [out[0] for out in outs]
    loads = [
        pltpu.with_memory_space_constraint(*((a.array, pltpu.VMEM) if here else (a, pltpu.HBM)))
        for a, here in zip(loads, held)
    ]
    weights = [pltpu.with_memory_space_constraint(a, pltpu.HBM) for a in weights]
    kernel = functools.partial(framed, body, held, len(weights), places)
    moving = [a for a, here in zip(loads, held) if not here]
    scratch = [
        *[pltpu.VMEM(a.shape, a.dtype) for a in moving],
        *[pltpu.VMEM(dims, dtype) for place, dims, dtype in outs if place == "hbm"],
        pltpu.SemaphoreType.DMA((len(moving) + 1,)),
        pltpu.SemaphoreType.DMA((len(outs),)),
        *scratch,
    ]
    specs = [SMEM] + [VMEM if here else HBM for here in held] + [HBM] * len(weights)
    shapes, out_specs = [], []
    for place, dims, dtype in outs:
        for space in ("vmem", "hbm"):
            if place in (space, "both"):
                shapes.append((pltpu.VMEM if space == "vmem" else pltpu.HBM)(dims, dtype))
                out_specs.append(VMEM if space == "vmem" else HBM)
    flat = list(call(kernel, specs, shapes, scratch, [meta, *loads, *weights], out_specs))
    return [tuple(take(flat, 2)) if place == "both" else take(flat, 1)[0] for place in places]


def swap(array, axis):
    return lax.ppermute(array, axis, [(0, 1), (1, 0)])


def total(left, right):
    return (left.astype(F32) + right.astype(F32)).astype(BF16)


class GroupSum:
    def __init__(self, mine, theirs):
        self.held, self.received = mine, theirs
        self.steps = list(zip(*self.orders(lax.axis_size("dp").bit_length() - 1)))
        self.todo = [("swap", None)] + [("halve", bits) for bits in self.steps] + [("add", self.steps[-1])]
        self.todo += [("join", bits) for bits in self.steps[-2::-1]]

    def make(self):
        kind, bits = self.todo[0]
        if kind == "swap":
            return [self.held, self.received]
        if kind == "halve":
            core = lax.axis_index("section")
            index = lax.axis_index("dp")
            side = (index >> jnp.where(core == 0, bits[0], bits[1])) & 1
            rows = self.held.shape[0] // 2
            both = total(self.held, self.received)
            return [lax.dynamic_slice_in_dim(both, at * rows, rows, 0) for at in (side, 1 - side)]
        if kind == "add":
            return [total(self.held, self.received)]
        return [jnp.concatenate([self.held, self.received], axis=0)]

    def send(self, arrays):
        kind, bits = self.todo.pop(0)
        self.held = arrays[0]
        self.received = swap(arrays[-1], "section") if kind == "swap" else self.exchange(arrays[-1], bits)

    def advance(self, value, after=None):
        if not self.todo:
            return value
        kind, bits = self.todo.pop(0)
        if after is not None and kind != "swap":
            self.received, _ = lax.optimization_barrier((self.received, after))
        if kind == "swap":
            value, self.held, send = lax.optimization_barrier((value, self.held, self.received))
            self.received = swap(send, "section")
            return value
        if kind == "halve":
            core = lax.axis_index("section")
            index = lax.axis_index("dp")
            side = (index >> jnp.where(core == 0, bits[0], bits[1])) & 1
            rows = self.held.shape[0] // 2
            both = total(self.held, self.received)
            held = lax.dynamic_slice_in_dim(both, side * rows, rows, 0)
            send = lax.dynamic_slice_in_dim(both, (1 - side) * rows, rows, 0)
            value, self.held, send = lax.optimization_barrier((value, held, send))
            self.received = self.exchange(send, bits)
            return value
        if kind == "add":
            held = total(self.held, self.received)
        else:
            held = jnp.concatenate([self.held, self.received], axis=0)
        value, self.held = lax.optimization_barrier((value, held))
        self.received = self.exchange(self.held, bits)
        return value

    @staticmethod
    def orders(bits):
        first = list(range(bits))
        second = [1, 0] + first[2:] if bits > 1 else first
        return first, second

    @staticmethod
    def exchange(array, bits):
        count = lax.axis_size("dp")
        pairs = [(core * count + i, core * count + (i ^ (1 << bit))) for core, bit in enumerate(bits) for i in range(count)]
        return lax.ppermute(array, ("section", "dp"), pairs)

    @staticmethod
    def place(bits, core):
        index = lax.axis_index("dp")
        out = jnp.int32(0)
        for first, second in zip(*GroupSum.orders(bits)):
            out = out * 2 + ((index >> jnp.where(core == 0, first, second)) & 1)
        return out


def boundary(values, flows, after=()):
    arrived = [flow for flow in flows if flow.todo[0][0] != "swap"]
    values = list(values)
    got = lax.optimization_barrier((*values, *[flow.received for flow in arrived], *after))
    values = list(got[: len(values)])
    for flow, received in zip(arrived, got[len(values) :]):
        flow.received = received
    arrays = [flow.make() for flow in flows]
    got = list(lax.optimization_barrier((*values, *[a for group in arrays for a in group])))
    values = take(got, len(values))
    for flow, group in zip(flows, arrays):
        flow.send(take(got, len(group)))
    return values


def in_order(pieces, place, count):
    array = jnp.concatenate(pieces, axis=0)
    blocks = array.reshape((count, array.shape[0] // count) + array.shape[1:])
    array = jnp.take(blocks, jnp.arange(count, dtype=jnp.int32) ^ place, axis=0).reshape(array.shape)
    rows = array.shape[0] // 2
    return array[:rows], array[rows:]


def local(
    inputs,
    doc_lengths,
    attn_gain,
    qkv_weight,
    qv_bias,
    out_weight,
    out_bias,
    mlp_gain,
    up_weight,
    up_bias,
    down_weight,
    down_bias,
    cotangent,
):
    core = lax.axis_index("section")
    side = lax.axis_index("tensor")
    groups = lax.axis_size("dp")
    bits = groups.bit_length() - 1
    place = GroupSum.place(bits, core)
    rows = inputs.shape[1]
    width = attn_gain.shape[1]
    heads = qkv_weight.shape[3]
    hidden = up_weight.shape[2]
    pairs = heads // LANES
    chunk = 768

    def own_rows(array):
        mine = lax.dynamic_index_in_dim(jnp.transpose(array, (2, 0, 1)), core, 1, keepdims=False)
        return jnp.pad(mine, ((0, width - mine.shape[0]), (0, 0)))

    lengths = lax.dynamic_index_in_dim(doc_lengths[:, 0, :], core, 0, keepdims=False)
    if groups == 8:
        places = [place, GroupSum.place(bits, 1 - core)]
    else:
        places = [jnp.int32(0)] * 2
    meta = jnp.concatenate([jnp.stack([core, side]).astype(jnp.int32), lengths, jnp.stack(places)])

    entry = own_rows(inputs)
    small_in = (attn_gain, qv_bias[0], out_bias, mlp_gain, up_bias, down_bias)
    out = out_weight[0]
    out = jnp.concatenate([out[:, :heads], out[:, heads:]], axis=0)
    attn_weight = jnp.concatenate([jnp.transpose(qkv_weight[0], (1, 0, 2)), out[None]], axis=0)
    (vector,) = call(
        pack_kernel,
        [VMEM] * len(small_in),
        [pltpu.HBM((512, hidden), F32)],
        [pltpu.VMEM((8, hidden), F32)],
        small_in,
        [HBM],
    )
    entry, vector, attn_weight = lax.optimization_barrier((entry, vector, attn_weight))
    far = swap(entry, "tensor")
    vec_pair = (vector, swap(vector, "section"))
    attn_pair = (attn_weight, swap(attn_weight, "section"))
    far, cots, up = lax.optimization_barrier((far, cotangent, up_weight[0]))
    entry = (entry, far)
    up_pair = (up, swap(up, "section"))
    cots = own_rows(cots)
    cots = (cots, swap(cots, "tensor"))
    down = down_weight[0]

    attn_scratch = [
        pltpu.VMEM(attn_weight.shape, BF16),
        pltpu.VMEM((2 * rows, 2 * heads), BF16),
        pltpu.VMEM((2, 8, hidden), F32),
        pltpu.SemaphoreType.DMA((2,)),
        pltpu.SemaphoreType.DMA((2,)),
    ]
    mlp_scratch = [
        pltpu.VMEM(up.shape, BF16),
        pltpu.VMEM(down.shape, BF16),
        pltpu.VMEM((1, 8, hidden), F32),
        pltpu.SemaphoreType.DMA((2, hidden // chunk)),
        pltpu.SemaphoreType.DMA,
    ]
    attn_all = [*vec_pair, *attn_pair]

    def attn_forward(layer, half, rows_in, kv):
        args = [Near(a) for a in (*rows_in, *([kv] if half else []))]
        outs = [
            ("both", (rows, width), BF16),
            ("hbm", (rows, width), BF16),
            ("hbm", (rows, heads), BF16),
            ("hbm" if half else "both", (rows, 2 * heads), BF16),
            ("hbm", (rows, heads), BF16),
            ("hbm", (pairs, 2 * rows, (half + 1) * rows), BF16),
            ("vmem", (rows, width), BF16),
        ]
        kernel = functools.partial(attn_forward_kernel, layer, half)
        return framed_call(kernel, meta, args, attn_all, outs, attn_scratch)

    def mlp_forward(half, rows_in, own, given):
        outs = [
            ("both", (rows, width), F32),
            ("hbm", (rows, width), BF16),
            ("hbm", (rows, hidden), BF16),
            ("vmem", (rows, width), BF16),
            ("hbm", (rows, hidden), BF16),
        ]
        kernel = functools.partial(mlp_forward_kernel, 0, half, False, chunk)
        return framed_call(kernel, meta, [Near(a) for a in (rows_in, own, given)], mlp_all, outs, mlp_scratch)

    def mlp_both(half, rows_in, own, given, sums):
        outs = [
            ("hbm", (rows, width), F32),
            ("vmem", (rows, width), BF16),
            ("vmem", (rows, hidden), BF16),
            ("hbm", (rows, width), BF16),
            ("hbm", (rows, width), BF16),
            ("vmem", (rows, width), BF16),
            ("vmem", (rows, hidden), BF16),
            ("hbm", (rows, width), BF16),
            ("hbm" if half else "vmem", (1, width + hidden), F32),
        ]
        kernel = functools.partial(mlp_forward_kernel, 1, half, True, chunk)
        args = [*(Near(a) for a in (rows_in, own, given)), *cots, *(Near(a) for a in sums)]
        return framed_call(kernel, meta, args, mlp_all, outs, mlp_scratch)

    def mlp_backward(half, grad, own, given, rows_in, slope, sums):
        outs = [
            ("hbm", (rows, width), F32),
            ("vmem", (rows, width), BF16),
            ("vmem", (rows, hidden), BF16),
            ("hbm", (rows, width), BF16),
            ("vmem" if half else "hbm", (1, 2 * width + hidden), F32),
        ]
        kernel = functools.partial(mlp_backward_kernel, chunk)
        scratch = [*mlp_scratch, pltpu.VMEM((8, hidden), F32), pltpu.SemaphoreType.DMA]
        args = [grad, own, Near(given), rows_in, slope, *(Near(a) for a in sums)]
        return framed_call(kernel, meta, args, mlp_all, outs, scratch)

    def attn_backward(layer, half, grad, own, given, middle, query, kv, probs, rows_in, link, sums):
        args = [grad, own, Near(given), middle, query, kv, probs]
        if layer == 0:
            args.append(rows_in)
        args += [link if half else Near(link), *(Near(a) for a in sums)]
        outs = [
            ("hbm", (rows, width), F32),
            ("vmem", (rows, width), BF16),
            ("vmem", (rows, 3 * heads), BF16),
            ("hbm", (rows, width), BF16),
            ("vmem" if half else "hbm", (1, (2 if layer else 3) * width + 2 * heads), F32),
        ]
        if half:
            outs.append(("vmem", (rows, 2 * heads), F32))
        kernel = functools.partial(attn_backward_kernel, layer, half)
        return framed_call(kernel, meta, args, attn_all, outs, attn_scratch)

    def mlp_weights(*args):
        outs = [("hbm", (hidden * width // 384, 384), BF16)] * 2
        return GroupSum(*framed_call(mlp_weights_kernel, meta, args, [], outs, []))

    def attn_weights(extra, *args):
        outs = [("hbm", (2 * width * heads // 384 + 8 * extra, 384), BF16)] * 2
        kernel = functools.partial(attn_weights_kernel, extra)
        return GroupSum(*framed_call(kernel, meta, args, [], outs, []))

    rows0, normed0, query0, kv0, att0, probs0, part0, given0 = [[None, None] for _ in range(8)]
    for half in range(2):
        rows0[half], normed0[half], query0[half], kv0[half], att0[half], probs0[half], part0[half] = attn_forward(
            0, half, entry, kv0[0][0] if half else None
        )
        given0[half] = swap(part0[half], "tensor")
        if half == 0:
            down, _ = lax.optimization_barrier((down, part0[0]))
            down_pair = (down, swap(down, "section"))
    given0[0], *cots = lax.optimization_barrier((given0[0], *cots))
    mlp_all = [*vec_pair, *up_pair, *down_pair]
    mid0, low_n0, act0, mpart0, slope0, mgiven0 = [[None, None] for _ in range(6)]
    for half in range(2):
        mid0[half], low_n0[half], act0[half], mpart0[half], slope0[half] = mlp_forward(
            half, rows0[half][0], part0[half], given0[half]
        )
        mgiven0[half] = swap(mpart0[half], "tensor")
    rows1, normed1, query1, kv1, att1, probs1, part1, given1 = [[None, None] for _ in range(8)]
    for half in range(2):
        rows1[half], normed1[half], query1[half], kv1[half], att1[half], probs1[half], part1[half] = attn_forward(
            1, half, [mid0[half][0], mpart0[half], mgiven0[half]], kv1[0][0] if half else None
        )
        given1[half] = swap(part1[half], "tensor")
    mid1, low_n1, act1, mpart1, cot, low1, hid1, gpart1, ggiven1 = [[None, None] for _ in range(9)]
    sums_m1 = []
    for half in range(2):
        (
            mid1[half],
            low_n1[half],
            act1[half],
            mpart1[half],
            cot[half],
            low1[half],
            hid1[half],
            gpart1[half],
            sums,
        ) = mlp_both(half, rows1[half][0], part1[half], given1[half], sums_m1)
        sums_m1 = [sums]
        ggiven1[half] = swap(gpart1[half], "tensor")
    mlp1 = [low_n1[0], hid1[0], low_n1[1], hid1[1], act1[0], low1[0], act1[1], low1[1]]
    mlp1 = mlp_weights(*(Near(a) for a in mlp1))
    grad1, glow1, dqkv1, apart1, agiven1 = [[None, None] for _ in range(5)]
    sums_a1 = []
    link = kv1[0][1]
    for half in (1, 0):
        ggiven1[half] = mlp1.advance(ggiven1[half], None if half else dqkv1[1])
        grad1[half], glow1[half], dqkv1[half], apart1[half], sums, *rest = attn_backward(
            1,
            half,
            cot[half],
            gpart1[half],
            ggiven1[half],
            mid1[half],
            query1[half],
            kv1[half] if half else kv1[half][1],
            probs1[half],
            None,
            link,
            sums_a1,
        )
        sums_a1 = [sums]
        link = rest[0] if half else None
        agiven1[half] = swap(apart1[half], "tensor")
    grads = [Near(a) for a in (*dqkv1, *glow1)]
    attn1 = attn_weights(0, normed1[0], grads[0], normed1[1], grads[1], att1[0], grads[2], att1[1], grads[3])
    grad0, low0, hid0, gpart0, ggiven0 = [[None, None] for _ in range(5)]
    sums_m0 = []
    for half in (1, 0):
        (agiven1[half],) = boundary([agiven1[half]], [mlp1, attn1], () if half else [hid0[1]])
        grad0[half], low0[half], hid0[half], gpart0[half], sums = mlp_backward(
            half, grad1[half], apart1[half], agiven1[half], rows1[half][1], slope0[half], sums_m0
        )
        sums_m0 = [sums]
        ggiven0[half] = swap(gpart0[half], "tensor")
    hid_near, low_near = [Near(a) for a in hid0], [Near(a) for a in low0]
    mlp0 = [low_n0[0], hid_near[0], low_n0[1], hid_near[1], act0[0], low_near[0], act0[1], low_near[1]]
    mlp0 = mlp_weights(*mlp0)
    gmid0, glow0, dqkv0, apart0 = [[None, None] for _ in range(4)]
    sums_a0 = []
    link = kv0[0][1]
    for half in (1, 0):
        if half:
            (ggiven0[1],) = boundary([ggiven0[1]], [mlp1, attn1, mlp0], [hid0[0]])
        else:
            (ggiven0[0],) = boundary([ggiven0[0]], [mlp1, attn1, mlp0], [dqkv0[1]])
        gmid0[half], glow0[half], dqkv0[half], apart0[half], sums, *rest = attn_backward(
            0,
            half,
            grad0[half],
            gpart0[half],
            ggiven0[half],
            mid0[half][1],
            query0[half],
            kv0[half] if half else kv0[half][1],
            probs0[half],
            rows0[half][1],
            link,
            sums_a0,
        )
        sums_a0 = [sums]
        link = rest[0] if half else None
    gain0 = sums_a0[0][:, 2 * width + 2 * heads :]
    gain0 = (gain0, swap(gain0, "tensor"))
    extra = 16
    grads = [Near(a) for a in (*dqkv0, *glow0)]
    (gain_far,) = boundary([gain0[1]], [mlp1, attn1], [dqkv0[0]])
    gain0 = (gain0[0], gain_far)
    attn0 = attn_weights(
        extra,
        *[normed0[0], grads[0], normed0[1], grads[1], att0[0], grads[2], att0[1], grads[3]],
        *[*sums_a0, *sums_m0, *sums_a1, *sums_m1, *(Near(a) for a in gain0)],
    )

    def chosen(pair):
        return jnp.where(side == 0, pair[0], pair[1])

    def own_half(parts):
        return chosen(parts).astype(F32) + swap(chosen(parts[::-1]), "tensor").astype(F32)

    def vector_of(layer, row):
        mine, other = (v[row : row + 1, :width] for v in vec_pair)
        return jnp.where(core == layer, mine, other)

    mpart1[0], mpart1[1], _ = lax.optimization_barrier((mpart1[0], mpart1[1], apart0[1]))
    branch = own_half(mpart1) + vector_of(1, DOWN_BIAS)
    result = (chosen(mid1) + center(branch))[:, : width - 1].astype(BF16)
    entry_rows = expand(chosen([r[1] for r in rows0]).astype(F32))
    pulled, _ = norm_pull(entry_rows, inv_rms(entry_rows), vector_of(0, ATTN_GAIN), own_half(apart0))
    grad_in = chosen(gmid0) + pulled
    grad_in = (grad_in[:, : width - 1] - grad_in[:, width - 1 :]).astype(BF16)

    token = [meta]
    sums = {}

    def end(name, flow):
        while flow.todo:
            token[:] = boundary(token, [flow])
        token[0], *pieces = lax.optimization_barrier((token[0], flow.held, flow.received))
        if groups != 8:
            pieces = in_order(pieces, place, groups)
        sums[name] = (*pieces, *[swap(piece, "section") for piece in pieces])

    for flows in ([mlp0, attn1, attn0], [attn0, mlp0, attn1]):
        token[:] = boundary(token, flows)
    end("mlp1", mlp1)
    token[:] = boundary(token, [attn0, mlp0])
    end("attn1", attn1)
    for _ in range(2):
        token[:] = boundary(token, [attn0, mlp0])
    token[:] = boundary(token, [attn0])
    end("mlp0", mlp0)
    while attn0.todo:
        token[:] = boundary(token, [attn0])

    up_rows, down_rows = width // 2, hidden // 2

    def mlp_kind(block):
        if block < 4:
            return 0, lambda part: (pl.ds(pl.multiple_of(part * up_rows, 8), up_rows), pl.ds(block * 384, 384))
        col, row = (block - 4) // 2, (block - 4) % 2
        return 1, lambda part: (
            pl.ds(pl.multiple_of(part * down_rows + row * 384, 8), 384),
            pl.ds(col * 384, 384),
        )

    def attn_kind(block):
        which, row = block // 2, block % 2
        if which < 3:
            return 0, lambda part: (which, pl.ds(pl.multiple_of(part * up_rows + row * 192, 8), 192), slice(None))
        return 1, lambda part: (pl.ds(row * 192, 192), pl.ds(pl.multiple_of(part * 384, 128), 384))

    def placed(kinds, extra_rows, first, second, outs):
        piece = first[0].shape[0] // 4 - extra_rows
        args = [token[0], *first[:2], *second[:2], *first[2:], *second[2:]]
        scratch = [
            pltpu.VMEM((16, piece, 384), BF16),
            pltpu.VMEM((16, piece, 384), F32),
            pltpu.SemaphoreType.DMA((16,)),
            pltpu.SemaphoreType.DMA((16,)),
        ]
        out_specs = [HBM, HBM] + [VMEM] * (len(outs) - 2)
        if extra_rows:
            scratch += [pltpu.VMEM((extra_rows, 384), BF16), pltpu.SemaphoreType.DMA]
        kernel = functools.partial(place_kernel, kinds, extra_rows)
        return call(kernel, [SMEM] + [HBM] * 8, outs, scratch, args, out_specs)

    grad_up, grad_down = placed(
        [mlp_kind(b) for b in range(8)],
        0,
        sums["mlp0"],
        sums["mlp1"],
        [shape((width, hidden), F32), shape((hidden, width), F32)],
    )
    token[0], grad_up, grad_down = lax.optimization_barrier((token[0], grad_up, grad_down))
    end("attn0", attn0)
    grad_qkv, grad_out, *small = placed(
        [attn_kind(b) for b in range(8)],
        extra,
        sums["attn0"],
        sums["attn1"],
        [shape((3, width, heads), F32), shape((heads, width), F32)]
        + [shape(dims, F32) for dims in ((1, width), (2, heads), (1, width), (1, width), (1, hidden), (1, width))],
    )

    return (
        result[None],
        grad_in[None],
        small[0],
        jnp.transpose(grad_qkv, (1, 0, 2))[None],
        small[1][None],
        grad_out[None],
        small[2],
        small[3],
        grad_up[None],
        small[4],
        grad_down[None],
        small[5],
    )


def solution(mesh):
    in_specs = (
        P(None, ("dp", "tensor"), None),
        P(None, "dp", None),
        P("section", None),
        P("section", None, None, "tensor"),
        P("section", None, "tensor"),
        P("section", "tensor", None),
        P("section", None),
        P("section", None),
        P("section", None, "tensor"),
        P("section", "tensor"),
        P("section", "tensor", None),
        P("section", None),
        P(None, ("dp", "tensor"), None),
    )
    out_specs = (
        P("section", ("dp", "tensor"), None),
        P("section", ("dp", "tensor"), None),
        P("section", None),
        P("section", None, None, "tensor"),
        P("section", None, "tensor"),
        P("section", "tensor", None),
        P("section", None),
        P("section", None),
        P("section", None, "tensor"),
        P("section", "tensor"),
        P("section", "tensor", None),
        P("section", None),
    )
    return jax.shard_map(local, mesh=mesh, in_specs=in_specs, out_specs=out_specs, check_vma=False)
```

```python
import functools
from typing import Any, NamedTuple

import jax
import jax.numpy as jnp
from jax import lax
from jax.experimental import pallas as pl
from jax.experimental.pallas import tpu as pltpu
from jax.sharding import PartitionSpec as P

HEAD_DIM = 64
LANES = 128
EPS = 1e-05
NEG = -1e30
VMEM_BYTES = 12 * 1024 * 1024

SECTION, GROUPS, TENSOR = "section", "dp", "tensor"

F32 = jnp.float32
BF16 = jnp.bfloat16

VMEM = pl.BlockSpec(memory_space=pltpu.VMEM)
SMEM = pl.BlockSpec(memory_space=pltpu.SMEM)
HBM = pl.BlockSpec(memory_space=pltpu.HBM)


def mm(left, right):
    return jnp.dot(left, right, preferred_element_type=F32)


def mm_t(left, right):
    return lax.dot_general(left, right, (((1,), (1,)), ((), ())), preferred_element_type=F32)


def t_mm(left, right):
    return lax.dot_general(left, right, (((0,), (0,)), ((), ())), preferred_element_type=F32)


def row_mean(array):
    return jnp.mean(array, axis=-1, keepdims=True)


def center(array):
    return array - row_mean(array)


def last_lane(shape):
    return lax.broadcasted_iota(jnp.int32, shape, 1) == shape[1] - 1


def expand(rows):
    return jnp.where(last_lane(rows.shape), -jnp.sum(rows, axis=-1, keepdims=True), rows)


def inv_rms(rows):
    return lax.rsqrt(row_mean(rows * rows) + EPS)


def norm_pull(rows, scaling, gain, grad):
    gained = gain * grad
    inner = row_mean(gained * rows)
    grad_rows = scaling * gained - rows * (scaling * scaling * scaling * inner)
    return center(grad_rows), grad * rows * scaling


def col_sum(array):
    return jnp.sum(array.astype(F32), axis=0, keepdims=True)


def pick(meta, layer, own, other, dst, sem):
    @pl.when(meta[0] == layer)
    def _():
        pltpu.make_async_copy(own, dst, sem).start()

    @pl.when(meta[0] != layer)
    def _():
        pltpu.make_async_copy(other, dst, sem).start()


def done(src, dst, sem):
    pltpu.make_async_copy(src, dst, sem).wait()


def halves(pair):
    first = lax.broadcasted_iota(jnp.int32, pair.shape, 1) < HEAD_DIM
    zero = jnp.zeros_like(pair)
    return jnp.concatenate([jnp.where(first, pair, zero), jnp.where(first, zero, pair)], axis=0)


def merge(stacked):
    rows = stacked.shape[0] // 2
    first = lax.broadcasted_iota(jnp.int32, (rows, stacked.shape[1]), 1) < HEAD_DIM
    return jnp.where(first, stacked[:rows], stacked[rows:])


def owner(meta, places):
    total = jnp.zeros(places.shape, jnp.int32)
    bound = 0
    for doc in range(3):
        bound = bound + meta[2 + doc]
        total = total + (places >= bound).astype(jnp.int32)
    return total


def mask_bias(meta, half, rows, keys):
    row_at = lax.broadcasted_iota(jnp.int32, (rows, 1), 0) + half * rows
    key_at = lax.broadcasted_iota(jnp.int32, (1, keys), 1)
    allowed = (owner(meta, row_at) == owner(meta, key_at)) & (key_at <= row_at)
    return jnp.where(allowed, 0.0, NEG).astype(F32)


def take(refs, count):
    out = refs[:count]
    del refs[:count]
    return out


class State(NamedTuple):
    vec: Any
    attn: Any
    up: Any
    down: Any
    rows: Any
    normed: Any
    low_normed: Any
    query: Any
    kv: Any
    att: Any
    probs: Any
    mid: Any
    act: Any
    hid: Any
    part: Any
    cot: Any
    low: Any
    grad: Any
    sums: Any


class Bench:
    def __init__(self, meta, shapes):
        self.meta = meta
        shapes, self.tree = jax.tree.flatten(shapes)
        self.arrays = shapes
        self.shapes = [pltpu.VMEM(a.shape, a.dtype) for a in shapes]

    def follow(self, arrays):
        self.meta, arrays[0] = lax.optimization_barrier((self.meta, arrays[0]))

    def run(self, body, ins=(), outs=(), hbm_ins=(), scratch=(), first=False):
        ins = [pltpu.with_memory_space_constraint(a, pltpu.VMEM) for a in ins]
        hbm_ins = [pltpu.with_memory_space_constraint(a, pltpu.HBM) for a in hbm_ins]
        held = [] if first else [pltpu.with_memory_space_constraint(a, pltpu.VMEM) for a in self.arrays]
        shapes = [(pltpu.VMEM if near else pltpu.HBM)(dims, dtype) for near, dims, dtype in outs]
        n_ins, n_hbm, n_outs, n_held = len(ins), len(hbm_ins), len(outs), len(self.shapes)

        def kernel(meta, *refs):
            refs = list(refs)
            near, far, _, made = take(refs, n_ins), take(refs, n_hbm), take(refs, len(held)), take(refs, n_outs)
            state = jax.tree.unflatten(self.tree, take(refs, n_held))
            body(meta, near, far, made, state, *refs)

        before = 1 + n_ins + n_hbm
        got = pl.pallas_call(
            kernel,
            out_shape=tuple(shapes + self.shapes),
            in_specs=[SMEM] + [VMEM] * n_ins + [HBM] * n_hbm + [VMEM] * len(held),
            out_specs=tuple([VMEM if near else HBM for near, _, _ in outs] + [VMEM] * n_held),
            input_output_aliases={before + i: n_outs + i for i in range(len(held))},
            scratch_shapes=list(scratch),
            compiler_params=pltpu.CompilerParams(vmem_limit_bytes=VMEM_BYTES),
            cost_estimate=pl.CostEstimate(flops=1, bytes_accessed=1, transcendentals=0),
        )(self.meta, *ins, *hbm_ins, *held)
        self.arrays = list(got[n_outs:])
        return list(got[:n_outs])


ATTN_GAIN, QV_BIAS, OUT_BIAS, MLP_GAIN, UP_BIAS, DOWN_BIAS = range(6)
MLP1, ATTN1, MLP0, ATTN0 = range(4)


def pack_kernel(*refs):
    *refs, target, out = refs
    out[...] = jnp.zeros(out.shape, F32)
    for row, ref in enumerate(refs):
        if ref.shape[0] == 2:
            half = ref.shape[1]
            out[row : row + 1, :half] = ref[0:1]
            out[row : row + 1, half : 2 * half] = ref[1:2]
        else:
            out[row : row + 1, : ref.shape[1]] = ref[...]
    pltpu.sync_copy(out, target.at[pl.ds(0, out.shape[0])])


def open_kernel(meta, near, far, made, st, sems):
    vec_own, vec_other, all_own, all_other = far
    for layer in range(2):
        rows = pl.ds(0, 8)
        pick(meta, layer, vec_own.at[rows], vec_other.at[rows], st.vec[layer], sems.at[layer])
    pick(meta, 0, all_own, all_other, st.attn[0], sems.at[2])
    for layer in range(2):
        done(vec_own.at[pl.ds(0, 8)], st.vec[layer], sems.at[layer])
    done(all_own, st.attn[0], sems.at[2])


def load_kernel(meta, near, far, made, st, sems):
    all_own, all_other, up_own, up_other, down_own, down_other = far
    work = []
    for layer in range(2):
        work.append((layer, up_own, up_other, st.up[layer]))
        work.append((layer, down_own, down_other, st.down[layer]))
    work.append((1, all_own, all_other, st.attn[1]))
    for at, (layer, own, other, dst) in enumerate(work):
        pick(meta, layer, own, other, dst, sems.at[at])
    for at, (layer, own, other, dst) in enumerate(work):
        done(own, dst, sems.at[at])


def vector(st, layer, row, first, last):
    return st.vec[layer][row : row + 1, first:last]


def attn_forward_kernel(layer, half, meta, near, far, made, st):
    weights = st.attn[layer]
    width, local = weights.shape[1:]
    count = st.part.shape[0] // 2
    here = slice(half * count, (half + 1) * count)
    if layer == 0:
        mine, other = near
        rows = jnp.where(meta[1] == half, mine[...], other[...]).astype(F32).T
    else:
        branch = st.part[here].astype(F32) + near[0][...].astype(F32) + vector(st, 0, DOWN_BIAS, 0, width)
        rows = (st.mid[0][here] + center(branch)).astype(BF16).astype(F32)
        rows = jnp.where(last_lane(rows.shape), 0.0, rows)
    st.rows[layer][here] = rows.astype(BF16)
    rows = expand(rows)
    normed = (rows * inv_rms(rows) * vector(st, layer, ATTN_GAIN, 0, width)).astype(BF16)
    st.normed[layer][here] = normed
    query = ((mm(normed, weights[0]) + vector(st, layer, QV_BIAS, 0, local)) * HEAD_DIM**-0.5).astype(BF16)
    st.query[layer][here] = query
    kv = st.kv[layer]
    kv[here, :local] = mm(normed, weights[1]).astype(BF16)
    kv[here, local:] = (mm(normed, weights[2]) + vector(st, layer, QV_BIAS, local, 2 * local)).astype(BF16)
    keys = (half + 1) * count
    masked = mask_bias(meta, half, count, keys)
    for pair in range(local // LANES):
        cols = slice(pair * LANES, (pair + 1) * LANES)
        vcols = slice(local + pair * LANES, local + (pair + 1) * LANES)
        scores = mm_t(halves(query[:, cols]), kv[:keys, cols])
        scores = (scores.reshape(2, count, keys) + masked[None]).reshape(2 * count, keys)
        expo = jnp.exp(scores - jnp.max(scores, axis=-1, keepdims=True))
        probs = (expo * (1.0 / jnp.sum(expo, axis=-1, keepdims=True))).astype(BF16)
        st.probs[layer][half][pair] = probs
        st.att[layer][here, cols] = merge(mm(probs, kv[:keys, vcols])).astype(BF16)
    attended = st.att[layer][here]
    for at in range(2):
        cols = slice(at * local, (at + 1) * local)
        part = mm(attended, weights[3, cols]).astype(BF16)
        st.part[here, cols] = part
        made[0][:, cols] = part


def mlp_middle(layer, here, received, st):
    width = st.part.shape[1]
    branch = st.part[here].astype(F32) + received[...].astype(F32) + vector(st, layer, OUT_BIAS, 0, width)
    middle = expand(st.rows[layer][here].astype(F32)) + center(branch)
    st.mid[layer][here] = middle
    normed = (middle * inv_rms(middle) * vector(st, layer, MLP_GAIN, 0, width)).astype(BF16)
    st.low_normed[layer][here] = normed
    return normed


def gelu_slope(hidden):
    root = (2.0 / jnp.pi) ** 0.5
    square = hidden * hidden
    half_up = 0.5 + 0.5 * jnp.tanh(hidden * (root + (root * 0.044715) * square))
    product = hidden * half_up
    return product, half_up + product * (1.0 - half_up) * (2 * root + (6 * root * 0.044715) * square)


def mlp_forward_kernel(chunk, half, meta, near, far, made, st, kept, sems):
    count = st.part.shape[0] // 2
    here = slice(half * count, (half + 1) * count)
    normed = mlp_middle(0, here, near[0], st)
    part = None
    for at in range(0, st.up[0].shape[1], chunk):
        cols = slice(at, at + chunk)
        hidden = mm(normed, st.up[0][:, cols]) + vector(st, 0, UP_BIAS, at, at + chunk)
        active, slope = gelu_slope(hidden)
        active = active.astype(BF16)
        kept[0, :, cols] = active
        kept[1, :, cols] = slope.astype(BF16)
        term = mm(active, st.down[0][cols, :])
        part = term if part is None else part + term
    copies = [pltpu.make_async_copy(kept.at[at], made[1 + at], sems.at[at]) for at in range(2)]
    for copy in copies:
        copy.start()
    part = part.astype(BF16)
    st.part[here] = part
    made[0][...] = part
    for copy in copies:
        copy.wait()


def add_sums(st, row, first, terms, fresh):
    places = slice(first, first + terms.shape[1])
    total = col_sum(terms)
    st.sums[row : row + 1, places] = total if fresh else total + st.sums[row : row + 1, places]


def mlp_both_kernel(chunk, half, meta, near, far, made, st, kept, sem):
    count, width = st.part.shape[0] // 2, st.part.shape[1]
    here = slice(half * count, (half + 1) * count)
    fresh = half == 0
    normed = mlp_middle(1, here, near[0], st)
    cot = jnp.where(meta[1] == half, near[1][...], near[2][...]).astype(F32).T
    st.cot[here] = cot.astype(BF16)
    low = center(cot).astype(BF16)
    st.low[here] = low
    add_sums(st, MLP1, 0, low, fresh)
    part, grad = None, None
    for at in range(0, st.up[1].shape[1], chunk):
        cols = slice(at, at + chunk)
        up, down = st.up[1][:, cols], st.down[1][cols, :]
        active, slope = gelu_slope(mm(normed, up) + vector(st, 1, UP_BIAS, at, at + chunk))
        active = active.astype(BF16)
        st.act[here, cols] = active
        hid = (mm_t(low, down) * slope).astype(BF16)
        st.hid[here, cols] = hid
        add_sums(st, MLP1, width + at, hid, fresh)
        terms = mm(active, down), mm_t(hid, up)
        part, grad = terms if part is None else (part + terms[0], grad + terms[1])
    grad = grad.astype(BF16)
    st.part[here] = grad
    made[0][...] = grad
    kept[...] = part.astype(BF16)
    pltpu.sync_copy(kept, made[1])


def mlp_backward_kernel(chunk, half, meta, near, far, made, st, slope, sem):
    load = pltpu.make_async_copy(far[0], slope, sem)
    load.start()
    count, width = st.part.shape[0] // 2, st.part.shape[1]
    here = slice(half * count, (half + 1) * count)
    fresh = half == 1
    hidden = st.up[0].shape[1]
    rows = expand(st.rows[1][here].astype(F32))
    grad = st.part[here].astype(F32) + near[0][...].astype(F32)
    pulled, gain_terms = norm_pull(rows, inv_rms(rows), vector(st, 1, ATTN_GAIN, 0, width), grad)
    grad_in = st.grad[here] + pulled
    grad_in = center((grad_in - grad_in[:, width - 1 :]).astype(BF16).astype(F32))
    st.grad[here] = grad_in
    low = grad_in.astype(BF16)
    st.low[here] = low
    add_sums(st, MLP0, 0, low, fresh)
    add_sums(st, MLP0, width + hidden, gain_terms, fresh)
    grad = None
    load.wait()
    for at in range(0, hidden, chunk):
        cols = slice(at, at + chunk)
        hid = (mm_t(low, st.down[0][cols, :]) * slope[:, cols].astype(F32)).astype(BF16)
        st.hid[here, cols] = hid
        add_sums(st, MLP0, width + at, hid, fresh)
        term = mm_t(hid, st.up[0][:, cols])
        grad = term if grad is None else grad + term
    grad = grad.astype(BF16)
    st.part[here] = grad
    made[0][...] = grad


def attn_backward_kernel(layer, half, meta, near, far, made, st, *refs):
    weights = st.attn[layer]
    width, local = weights.shape[1:]
    count = st.part.shape[0] // 2
    here = slice(half * count, (half + 1) * count)
    fresh = half == 1
    name = ATTN1 if layer else ATTN0
    middle = st.mid[layer][here]
    grad = st.part[here].astype(F32) + near[0][...].astype(F32)
    pulled, gain_terms = norm_pull(middle, inv_rms(middle), vector(st, layer, MLP_GAIN, 0, width), grad)
    upstream = center(st.cot[here].astype(F32)) if layer else st.grad[here]
    grad_mid = upstream + pulled
    st.grad[here] = grad_mid
    low = grad_mid.astype(BF16)
    st.low[here] = low
    add_sums(st, name, 0, gain_terms, fresh)
    add_sums(st, name, width, low, fresh)
    grad_att = (mm_t(low[:, :local], weights[3, :local]) + mm_t(low[:, local:], weights[3, local:])).astype(BF16)
    at = 2 * width
    query, kv, dqkv = st.query[layer], st.kv[layer], st.hid
    early = made[-1] if half else near[1]
    keys = (half + 1) * count
    for pair in range(local // LANES):
        cols = slice(pair * LANES, (pair + 1) * LANES)
        vcols = slice(local + pair * LANES, local + (pair + 1) * LANES)
        v2cols = slice(2 * local + pair * LANES, 2 * local + (pair + 1) * LANES)
        grads = halves(grad_att[:, cols])
        queries = halves(query[here, cols])
        low_probs = st.probs[layer][half][pair]
        probs = low_probs.astype(F32)
        grad_probs = mm_t(grads, kv[:keys, vcols])
        inner = jnp.sum(grad_probs * probs, axis=-1, keepdims=True)
        grad_scores = (probs * (grad_probs - inner)).astype(BF16)
        grad_query = (merge(mm(grad_scores, kv[:keys, cols])) * HEAD_DIM**-0.5).astype(BF16)
        grad_key = t_mm(grad_scores, queries)
        grad_value = t_mm(low_probs, grads)
        if half:
            early[:, cols] = grad_key[:count]
            early[:, vcols] = grad_value[:count]
            grad_key, grad_value = grad_key[count:], grad_value[count:]
        else:
            grad_key, grad_value = grad_key + early[:, cols], grad_value + early[:, vcols]
        grad_value = grad_value.astype(BF16)
        dqkv[here, cols] = grad_query
        dqkv[here, vcols] = grad_key.astype(BF16)
        dqkv[here, v2cols] = grad_value
        add_sums(st, name, at + pair * LANES, grad_query, fresh)
        add_sums(st, name, at + local + pair * LANES, grad_value, fresh)
    gpart = mm_t(dqkv[here, :local], weights[0])
    gpart = gpart + mm_t(dqkv[here, local : 2 * local], weights[1])
    gpart = gpart + mm_t(dqkv[here, 2 * local : 3 * local], weights[2])
    if layer == 0:
        rows = expand(st.rows[0][here].astype(F32))
        add_sums(st, name, at + 2 * local, gpart * rows * inv_rms(rows), fresh)
    st.part[here] = gpart.astype(BF16)
    if layer:
        made[0][...] = gpart.astype(BF16)
    elif half == 0:
        away = pl.ds(pl.multiple_of((1 - meta[1]) * count, 16), count)
        made[0][...] = st.part[away]
        row = name
        made[1][...] = st.sums[row : row + 1, at + 2 * local : at + 2 * local + width]
        own = pl.ds(pl.multiple_of(meta[1] * count, 16), count)
        sems = refs[0]
        copies = []
        for n, ref in enumerate((st.part, st.rows[0], st.grad, st.mid[1])):
            copies.append(pltpu.make_async_copy(ref.at[own], made[3 + n], sems.at[n]))
            copies[-1].start()
        for side in range(2):

            @pl.when(meta[1] == side)
            def _():
                pltpu.make_async_copy(far[1 - side], made[2], sems.at[4]).start()
                pltpu.make_async_copy(far[side], made[7], sems.at[5]).start()

        copies.append(pltpu.make_async_copy(far[0], made[2], sems.at[4]))
        copies.append(pltpu.make_async_copy(far[0], made[7], sems.at[5]))
        for copy in copies:
            copy.wait()


def mlp_weights_kernel(layer, meta, near, far, made, st, *refs):
    width, hidden = st.up[0].shape
    if far:
        active, load_sems = refs
        count = far[0].shape[0]
        loads = [
            pltpu.make_async_copy(ref, active.at[pl.ds(at * count, count)], load_sems.at[at]) for at, ref in enumerate(far)
        ]
        for load in loads:
            load.start()
    else:
        active, loads = st.act, []
    block = made[0].shape[1]
    for out, part in ((made[1], 1 - meta[0]), (made[0], meta[0])):
        rows = width // 2
        left = st.low_normed[layer][:, pl.ds(pl.multiple_of(part * rows, LANES), rows)]
        for n in range(hidden // block):
            out[n * rows : (n + 1) * rows] = t_mm(left, st.hid[:, n * block : (n + 1) * block]).astype(BF16)
        base = hidden // block * rows
        rows = hidden // 2
        while loads:
            loads.pop().wait()
        left = active[:, pl.ds(pl.multiple_of(part * rows, LANES), rows)]
        for n in range(width // block):
            total = t_mm(left, st.low[:, n * block : (n + 1) * block])
            out[base + n * rows : base + (n + 1) * rows] = total.astype(BF16)


def attn_weights_kernel(layer, extra, meta, near, far, made, st):
    width, local = st.attn[0].shape[1:]
    hidden = st.up[0].shape[1]
    piece = made[0].shape[0] // 8 - extra

    def put(out, first, total):
        for at in range(0, total.shape[0], piece):
            where = (first + at) // piece * (piece + extra)
            out[where : where + piece] = total[at : at + piece].astype(BF16)

    if extra:
        sums = st.sums
        rows = [sums[row : row + 1] for row in range(4)]
        smalls = []
        tail = 2 * width + 2 * local
        for gain, attn, mlp in (
            (rows[ATTN0][:, tail : tail + width] + near[0][...], rows[ATTN0], rows[MLP0]),
            (rows[MLP0][:, width + hidden : 2 * width + hidden], rows[ATTN1], rows[MLP1]),
        ):
            row = [gain, attn[:, 2 * width : tail], attn[:, width : 2 * width], attn[:, :width]]
            row += [mlp[:, width : width + hidden], mlp[:, :width]]
            lines = [part[:, at : at + local] for part in row for at in range(0, part.shape[1], local)]
            lines += [jnp.zeros((1, local), F32)] * (extra - len(lines))
            smalls.append(jnp.concatenate(lines, axis=0))

    for out, part in ((made[1], 1 - meta[0]), (made[0], meta[0])):
        rows = width // 2
        cols = pl.ds(pl.multiple_of(part * rows, LANES), rows)
        left = st.normed[layer][:, cols]
        for at in range(3):
            put(out, at * rows, t_mm(left, st.hid[:, at * local : (at + 1) * local]))
        put(out, 3 * rows, t_mm(st.att[layer][...], st.low[:, cols]))
        if extra:
            out[piece : piece + extra] = jnp.where(part == 0, smalls[0], smalls[1]).astype(BF16)
            for at in range(1, 8):
                where = at * (piece + extra) + piece
                out[where : where + extra] = jnp.zeros((extra, local), BF16)


def close_kernel(meta, vec_own, vec_other, grad_far, out_far, out_own, part, rows, grad, middle, result, grad_in, *refs):
    width = part.shape[1]

    *vecs, sems = refs
    for layer in range(2):
        pick(meta, layer, vec_own.at[pl.ds(0, 8)], vec_other.at[pl.ds(0, 8)], vecs[layer], sems.at[layer])
    for layer in range(2):
        done(vec_own.at[pl.ds(0, 8)], vecs[layer], sems.at[layer])

    def vec(layer, row):
        return vecs[layer][row : row + 1, :width]

    branch = out_own[...].astype(F32) + out_far[...].astype(F32) + vec(1, DOWN_BIAS)
    result[...] = (middle[...] + center(branch)).astype(BF16)
    rows = expand(rows[...].astype(F32))
    given = part[...].astype(F32) + grad_far[...].astype(F32)
    pulled, _ = norm_pull(rows, inv_rms(rows), vec(0, ATTN_GAIN), given)
    total = grad[...] + pulled
    grad_in[...] = (total - total[:, width - 1 :]).astype(BF16)


def place_kernel(kinds, extra, meta, *refs):
    refs = list(refs)
    sources = take(refs, 4)
    if extra:
        lines, line_sem = refs[-2:]
        del refs[-2:]
    outs = refs[:-4]
    low, wide, in_sems, out_sems = refs[-4:]
    piece = low.shape[1]
    step = piece + extra
    if extra:
        at = pl.multiple_of(meta[6] * step + piece, 16)
        small_load = pltpu.make_async_copy(sources[0].at[pl.ds(at, extra)], lines, line_sem)
        small_load.start()

    def load(layer, side, block):
        every = piece if layer else step
        at = pl.multiple_of((block ^ meta[6 + side]) * every, 16)
        n = side * 8 + block
        return pltpu.make_async_copy(sources[2 * side + layer].at[pl.ds(at, piece)], low.at[n], in_sems.at[n])

    for layer in range(2):

        @pl.when(meta[0] == layer)
        def _():
            for n in range(16):
                load(layer, n // 8, n % 8).start()

    copies = []
    for n in range(16):
        part = meta[0] if n < 8 else 1 - meta[0]
        load(0, n // 8, n % 8).wait()
        wide[n] = low[n].astype(F32)
        which, where = kinds[n % 8]
        copies.append(pltpu.make_async_copy(wide.at[n], outs[which].at[where(part)], out_sems.at[n]))
        copies[-1].start()
    if extra:
        small_load.wait()
        small = lines[...].astype(F32)
        at = 0
        for out in outs[2:]:
            for row in range(out.shape[0]):
                for col in range(0, out.shape[1], small.shape[1]):
                    out[row : row + 1, col : col + small.shape[1]] = small[at : at + 1]
                    at += 1
    for copy in copies:
        copy.wait()


def shape(dims, dtype=BF16):
    return jax.ShapeDtypeStruct(dims, dtype)


def call(kernel, in_specs, outs, scratch, args, out_specs, limit=VMEM_BYTES):
    return pl.pallas_call(
        kernel,
        out_shape=tuple(outs),
        in_specs=in_specs,
        out_specs=tuple(out_specs),
        scratch_shapes=scratch,
        compiler_params=pltpu.CompilerParams(vmem_limit_bytes=limit),
        cost_estimate=pl.CostEstimate(flops=1, bytes_accessed=1, transcendentals=0),
    )(*args)


def swap(array, axis):
    return lax.ppermute(array, axis, [(0, 1), (1, 0)])


def halve_kernel(step, sides, mine, other, *outs):
    rows = mine.shape[0] // len(outs)
    for at, out in enumerate(outs):
        here = slice(None)
        if len(outs) == 2:
            side = sides[step] if at == 0 else 1 - sides[step]
            here = pl.ds(pl.multiple_of(side * rows, 16), rows)
        out[...] = (mine[here].astype(F32) + other[here].astype(F32)).astype(BF16)


def join_kernel(first, second, out):
    rows = first.shape[0]
    out[:rows] = first[...]
    out[rows:] = second[...]


def in_vmem(*arrays):
    return [pltpu.with_memory_space_constraint(a, pltpu.VMEM) for a in arrays]


def add_halves(step, sides, mine, other):
    rows, width = mine.shape
    halves = 1 if step is None else 2
    outs = [pltpu.VMEM((rows // halves, width), BF16)] * halves
    kernel = functools.partial(halve_kernel, step)
    return call(kernel, [SMEM, VMEM, VMEM], outs, [], [sides, *in_vmem(mine, other)], [VMEM] * halves)


def join(first, second):
    rows, width = first.shape
    outs = [pltpu.VMEM((2 * rows, width), BF16)]
    return call(join_kernel, [VMEM, VMEM], outs, [], in_vmem(first, second), [VMEM])[0]


SWAP, HALVE, ADD, JOIN = range(4)


class GroupSum:
    def __init__(self, sides, mine, theirs):
        self.sides = sides
        self.held, self.received = mine, theirs
        self.steps = list(zip(*self.orders(lax.axis_size(GROUPS).bit_length() - 1)))
        self.todo = [(SWAP, None)] + [(HALVE, k) for k in range(len(self.steps))]
        self.todo += [(ADD, len(self.steps) - 1)] + [(JOIN, k) for k in range(len(self.steps) - 2, -1, -1)]

    def make(self):
        kind, at = self.todo[0]
        if kind == SWAP:
            return [self.held, self.received]
        if kind == JOIN:
            return [join(self.held, self.received)]
        return list(add_halves(at if kind == HALVE else None, self.sides, self.held, self.received))

    def send(self, arrays):
        kind, at = self.todo.pop(0)
        self.held = arrays[0]
        self.received = swap(arrays[-1], SECTION) if kind == SWAP else self.exchange(arrays[-1], self.steps[at])

    @staticmethod
    def orders(bits):
        first = list(range(bits))
        second = [1, 0] + first[2:] if bits > 1 else first
        return first, second

    @staticmethod
    def exchange(array, bits):
        count = lax.axis_size(GROUPS)
        pairs = [(core * count + i, core * count + (i ^ (1 << bit))) for core, bit in enumerate(bits) for i in range(count)]
        return lax.ppermute(array, (SECTION, GROUPS), pairs)

    @staticmethod
    def which_side(bits):
        core, index = lax.axis_index(SECTION), lax.axis_index(GROUPS)
        return jnp.stack([(index >> jnp.where(core == 0, *pair)) & 1 for pair in zip(*GroupSum.orders(bits))])

    @staticmethod
    def place(bits, core):
        index = lax.axis_index(GROUPS)
        out = jnp.int32(0)
        for first, second in zip(*GroupSum.orders(bits)):
            out = out * 2 + ((index >> jnp.where(core == 0, first, second)) & 1)
        return out


def boundary(values, flows, after=()):
    flows = [flow for flow in flows if flow.todo]
    arrived = [flow for flow in flows if flow.todo[0][0] != SWAP]
    values = list(values)
    got = lax.optimization_barrier((*values, *[flow.received for flow in arrived], *after))
    values = list(got[: len(values)])
    for flow, received in zip(arrived, got[len(values) :]):
        flow.received = received
    arrays = [flow.make() for flow in flows]
    got = list(lax.optimization_barrier((*values, *[a for group in arrays for a in group])))
    values = take(got, len(values))
    for flow, group in zip(flows, arrays):
        flow.send(take(got, len(group)))
    return values


def in_order(array, place, count):
    blocks = array.reshape((count, array.shape[0] // count) + array.shape[1:])
    return jnp.take(blocks, jnp.arange(count, dtype=jnp.int32) ^ place, axis=0).reshape(array.shape)


def local(
    inputs,
    doc_lengths,
    attn_gain,
    qkv_weight,
    qv_bias,
    out_weight,
    out_bias,
    mlp_gain,
    up_weight,
    up_bias,
    down_weight,
    down_bias,
    cotangent,
):
    core = lax.axis_index(SECTION)
    side = lax.axis_index(TENSOR)
    groups = lax.axis_size(GROUPS)
    bits = groups.bit_length() - 1
    place = GroupSum.place(bits, core)
    rows = inputs.shape[1]
    width = attn_gain.shape[1]
    heads = qkv_weight.shape[3]
    hidden = up_weight.shape[2]
    pairs = heads // LANES
    chunk = hidden // 2
    extra = 16

    def own_rows(array):
        mine = lax.dynamic_index_in_dim(jnp.transpose(array, (2, 0, 1)), core, 1, keepdims=False)
        return jnp.pad(mine, ((0, width - mine.shape[0]), (0, 0)))

    lengths = lax.dynamic_index_in_dim(doc_lengths[:, 0, :], core, 0, keepdims=False)
    if groups == 8:
        places = [place, GroupSum.place(bits, 1 - core)]
    else:
        places = [jnp.int32(0)] * 2
    meta = jnp.concatenate([jnp.stack([core, side]).astype(jnp.int32), lengths, jnp.stack(places)])
    def each(*dims, dtype=BF16):
        return (shape(dims, dtype),) * 2

    unit = 2 * rows
    layer_probs = (shape((pairs, unit, rows)), shape((pairs, unit, unit)))
    bench = Bench(
        meta,
        State(
            vec=each(8, hidden, dtype=F32),
            attn=each(4, width, heads),
            up=each(width, hidden),
            down=each(hidden, width),
            rows=each(unit, width),
            normed=each(unit, width),
            low_normed=each(unit, width),
            query=each(unit, heads),
            kv=each(unit, 2 * heads),
            att=each(unit, heads),
            probs=(layer_probs, layer_probs),
            mid=each(unit, width, dtype=F32),
            act=shape((unit, hidden)),
            hid=shape((unit, hidden)),
            part=shape((unit, width)),
            cot=shape((unit, width)),
            low=shape((unit, width)),
            grad=shape((unit, width), F32),
            sums=shape((8, 3 * width + 2 * heads), F32),
        ),
    )
    sides = GroupSum.which_side(bits)

    entry = own_rows(inputs)
    small_in = (attn_gain, qv_bias[0], out_bias, mlp_gain, up_bias, down_bias)
    out = out_weight[0]
    out = jnp.concatenate([out[:, :heads], out[:, heads:]], axis=0)
    attn_weight = jnp.concatenate([jnp.transpose(qkv_weight[0], (1, 0, 2)), out[None]], axis=0)
    (vectors,) = call(
        pack_kernel,
        [VMEM] * len(small_in),
        [pltpu.HBM((512, hidden), F32)],
        [pltpu.VMEM((8, hidden), F32)],
        small_in,
        [HBM],
    )
    entry, vectors, attn_weight = lax.optimization_barrier((entry, vectors, attn_weight))
    far = swap(entry, TENSOR)
    vec_pair = (vectors, swap(vectors, SECTION))
    attn_pair = (attn_weight, swap(attn_weight, SECTION))
    cots, _ = lax.optimization_barrier((cotangent, attn_weight))
    cots = own_rows(cots)
    *attn_pair, cots = lax.optimization_barrier((*attn_pair, cots))
    far, cots = lax.optimization_barrier((far, cots))
    entry = (entry, far)
    up, down = up_weight[0], down_weight[0]
    up_pair = (up, swap(up, SECTION))
    down_pair = (down, swap(down, SECTION))
    cots = (cots, swap(cots, TENSOR))

    sent = (True, (rows, width), BF16)
    partial = functools.partial
    bench.run(open_kernel, hbm_ins=[*vec_pair, *attn_pair], scratch=[pltpu.SemaphoreType.DMA((3,))], first=True)

    given = [None, None]
    for half in range(2):
        (part,) = bench.run(partial(attn_forward_kernel, 0, half), entry, [sent])
        given[half] = swap(part, TENSOR)
    *down_pair, cot_far = lax.optimization_barrier((*down_pair, cots[1]))
    cots = (cots[0], cot_far)
    bench.run(load_kernel, hbm_ins=[*attn_pair, *up_pair, *down_pair], scratch=[pltpu.SemaphoreType.DMA((5,))])
    acts, slopes = [], []
    for half in range(2):
        outs = [sent] + [(False, (rows, hidden), BF16)] * 2
        scratch = [pltpu.VMEM((2, rows, hidden), BF16), pltpu.SemaphoreType.DMA((2,))]
        part, *kept = bench.run(partial(mlp_forward_kernel, chunk, half), [given[half]], outs, scratch=scratch)
        given[half] = swap(part, TENSOR)
        acts.append(kept[0])
        slopes.append(kept[1])
    for half in range(2):
        (part,) = bench.run(partial(attn_forward_kernel, 1, half), [given[half]], [sent])
        given[half] = swap(part, TENSOR)
    mlp_parts = []
    kept = (False, (rows, width), BF16)
    for half in range(2):
        scratch = [pltpu.VMEM((rows, width), BF16), pltpu.SemaphoreType.DMA]
        body = partial(mlp_both_kernel, chunk, half)
        part, mlp_part = bench.run(body, [given[half], *cots], [sent, kept], scratch=scratch)
        given[half] = swap(part, TENSOR)
        mlp_parts.append(mlp_part)

    def weights(kernel, dims):
        ins = [gain_far] if kernel is attn_weights_kernel and dims[0] % (8 * 192) else []
        layer = 0 if ins or kernel is mlp_weights_kernel and mlp1 is not None else 1
        body = partial(kernel, layer) if kernel is mlp_weights_kernel else partial(kernel, layer, extra if ins else 0)
        far = acts if kernel is mlp_weights_kernel and layer == 0 else []
        scratch = [pltpu.VMEM((2 * rows, hidden), BF16), pltpu.SemaphoreType.DMA((2,))] if far else []
        return GroupSum(sides, *bench.run(body, ins, [(True, dims, BF16)] * 2, far, scratch))

    mlp_dims = (hidden * width // 384, 384)
    attn_dims = (2 * width * heads // 384, 384)
    mlp1 = None
    bench.follow(given)
    mlp1 = weights(mlp_weights_kernel, mlp_dims)
    early = (True, (rows, 2 * heads), F32)
    for half in (1, 0):
        (given[half],) = boundary([given[half]], [mlp1], () if half else [part])
        ins, outs = ([given[1]], [sent, early]) if half else ([given[0], link], [sent])
        part, *rest = bench.run(partial(attn_backward_kernel, 1, half), ins, outs)
        link = rest[0] if half else None
        given[half] = swap(part, TENSOR)
    attn1 = weights(attn_weights_kernel, attn_dims)
    for half in (1, 0):
        if half:
            given[1], attn1.held, attn1.received = lax.optimization_barrier((given[1], attn1.held, attn1.received))
        else:
            (given[0],) = boundary([given[0]], [mlp1, attn1], [part])
        scratch = [pltpu.VMEM((rows, hidden), BF16), pltpu.SemaphoreType.DMA]
        body = partial(mlp_backward_kernel, chunk, half)
        (part,) = bench.run(body, [given[half]], [sent], [slopes[half]], scratch)
        given[half] = swap(part, TENSOR)
    mlp0 = weights(mlp_weights_kernel, mlp_dims)
    (given[1],) = boundary([given[1]], [mlp1, attn1, mlp0], [part])
    (link,) = bench.run(partial(attn_backward_kernel, 0, 1), [given[1]], [early])
    given[0], link = boundary([given[0], link], [mlp1, attn1, mlp0])
    own = [(False, (rows, width), dtype) for dtype in (BF16, BF16, F32, F32)]
    outs = [sent, (True, (1, width), F32), sent, *own, sent]
    body = partial(attn_backward_kernel, 0, 0)
    scratch = [pltpu.SemaphoreType.DMA((6,))]
    away_grad, gain, away_out, *own = bench.run(body, [given[0], link], outs, mlp_parts, scratch)
    (gain_far,) = boundary([swap(gain, TENSOR)], [attn1], [gain])
    gain_far, away_grad, away_out = lax.optimization_barrier((gain_far, away_grad, away_out))
    backs = [swap(away_grad, TENSOR), swap(away_out, TENSOR)]
    attn0 = weights(attn_weights_kernel, (attn_dims[0] + 8 * extra, 384))

    token = [meta]

    def end(flow):
        while flow.todo:
            token[:] = boundary(token, [flow])
        token[0], *pieces = lax.optimization_barrier((token[0], flow.held, flow.received))
        whole = join(*pieces)
        if groups != 8:
            whole = in_order(whole, place, groups)
        token[0], whole = lax.optimization_barrier((token[0], whole))
        return whole, swap(whole, SECTION)

    def close(back_grad, back_out):
        args = [*in_vmem(back_grad, back_out, own[-1]), *own[:-1]]
        specs = [SMEM, HBM, HBM] + [VMEM] * len(args)
        scratch = [pltpu.VMEM((8, hidden), F32)] * 2 + [pltpu.SemaphoreType.DMA((2,))]
        outs = [shape((rows, width))] * 2
        return call(close_kernel, specs, outs, scratch, [token[0], *vec_pair, *args], [VMEM] * 2, 2 * VMEM_BYTES)

    token[:] = boundary(token, [mlp0, mlp1, attn1, attn0])
    token[:] = boundary(token, [attn0, mlp0, attn1], [mlp1.received])
    token[0], *backs = lax.optimization_barrier((token[0], *backs))
    token[:] = boundary(token, [attn0, mlp0, mlp1])
    result, grad_in = close(*backs)
    token[0], result, grad_in = lax.optimization_barrier((token[0], result, grad_in))
    token[:] = boundary(token, [attn0, mlp0, attn1])
    mlp1 = end(mlp1)
    token[:] = boundary(token, [attn0, mlp0])
    attn1 = end(attn1)
    token[:] = boundary(token, [attn0])
    mlp0 = end(mlp0)
    while attn0.todo:
        token[:] = boundary(token, [attn0])

    up_rows, down_rows = width // 2, hidden // 2

    def mlp_kind(block):
        if block < 4:
            return 0, lambda part: (pl.ds(pl.multiple_of(part * up_rows, 8), up_rows), pl.ds(block * 384, 384))
        col, row = (block - 4) // 2, (block - 4) % 2
        return 1, lambda part: (
            pl.ds(pl.multiple_of(part * down_rows + row * 384, 8), 384),
            pl.ds(col * 384, 384),
        )

    def attn_kind(block):
        which, row = block // 2, block % 2
        if which < 3:
            return 0, lambda part: (which, pl.ds(pl.multiple_of(part * up_rows + row * 192, 8), 192), slice(None))
        return 1, lambda part: (pl.ds(row * 192, 192), pl.ds(pl.multiple_of(part * 384, 128), 384))

    def placed(kinds, extra_rows, first, second, outs):
        piece = first[0].shape[0] // 8 - extra_rows
        args = [token[0], first[0], second[0], first[1], second[1]]
        scratch = [
            pltpu.VMEM((16, piece, 384), BF16),
            pltpu.VMEM((16, piece, 384), F32),
            pltpu.SemaphoreType.DMA((16,)),
            pltpu.SemaphoreType.DMA((16,)),
        ]
        out_specs = [HBM, HBM] + [VMEM] * (len(outs) - 2)
        if extra_rows:
            scratch += [pltpu.VMEM((extra_rows, 384), BF16), pltpu.SemaphoreType.DMA]
        kernel = functools.partial(place_kernel, kinds, extra_rows)
        return call(kernel, [SMEM] + [HBM] * 4, outs, scratch, args, out_specs, 2 * VMEM_BYTES)

    grad_up, grad_down = placed(
        [mlp_kind(b) for b in range(8)],
        0,
        mlp0,
        mlp1,
        [shape((width, hidden), F32), shape((hidden, width), F32)],
    )
    token[0], grad_up, grad_down = lax.optimization_barrier((token[0], grad_up, grad_down))
    attn0 = end(attn0)
    grad_qkv, grad_out, *small = placed(
        [attn_kind(b) for b in range(8)],
        extra,
        attn0,
        attn1,
        [shape((3, width, heads), F32), shape((heads, width), F32)]
        + [shape(dims, F32) for dims in ((1, width), (2, heads), (1, width), (1, width), (1, hidden), (1, width))],
    )

    return (
        result[None, :, : width - 1],
        grad_in[None, :, : width - 1],
        small[0],
        jnp.transpose(grad_qkv, (1, 0, 2))[None],
        small[1][None],
        grad_out[None],
        small[2],
        small[3],
        grad_up[None],
        small[4],
        grad_down[None],
        small[5],
    )


def solution(mesh):
    in_specs = (
        P(None, (GROUPS, TENSOR), None),
        P(None, GROUPS, None),
        P(SECTION, None),
        P(SECTION, None, None, TENSOR),
        P(SECTION, None, TENSOR),
        P(SECTION, TENSOR, None),
        P(SECTION, None),
        P(SECTION, None),
        P(SECTION, None, TENSOR),
        P(SECTION, TENSOR),
        P(SECTION, TENSOR, None),
        P(SECTION, None),
        P(None, (GROUPS, TENSOR), None),
    )
    out_specs = (
        P(SECTION, (GROUPS, TENSOR), None),
        P(SECTION, (GROUPS, TENSOR), None),
        P(SECTION, None),
        P(SECTION, None, None, TENSOR),
        P(SECTION, None, TENSOR),
        P(SECTION, TENSOR, None),
        P(SECTION, None),
        P(SECTION, None),
        P(SECTION, None, TENSOR),
        P(SECTION, TENSOR),
        P(SECTION, TENSOR, None),
        P(SECTION, None),
    )
    return jax.shard_map(local, mesh=mesh, in_specs=in_specs, out_specs=out_specs, check_vma=False)
```

```python
import functools
from typing import Any, NamedTuple

import jax
import jax.numpy as jnp
from jax import lax
from jax.experimental import pallas as pl
from jax.experimental.pallas import tpu as pltpu
from jax.sharding import PartitionSpec as P

HEAD_DIM = 64
LANES = 128
EPS = 1e-05
NEG = -1e30
VMEM_BYTES = 12 * 1024 * 1024

SECTION, GROUPS, TENSOR = "section", "dp", "tensor"

F32 = jnp.float32
BF16 = jnp.bfloat16

VMEM = pl.BlockSpec(memory_space=pltpu.VMEM)
SMEM = pl.BlockSpec(memory_space=pltpu.SMEM)
HBM = pl.BlockSpec(memory_space=pltpu.HBM)


def mm(left, right):
    return jnp.dot(left, right, preferred_element_type=F32)


def mm_t(left, right):
    return lax.dot_general(left, right, (((1,), (1,)), ((), ())), preferred_element_type=F32)


def t_mm(left, right):
    return lax.dot_general(left, right, (((0,), (0,)), ((), ())), preferred_element_type=F32)


def row_mean(array):
    return jnp.mean(array, axis=-1, keepdims=True)


def center(array):
    return array - row_mean(array)


def last_lane(shape):
    return lax.broadcasted_iota(jnp.int32, shape, 1) == shape[1] - 1


def expand(rows):
    return jnp.where(last_lane(rows.shape), -jnp.sum(rows, axis=-1, keepdims=True), rows)


def inv_rms(rows):
    return lax.rsqrt(row_mean(rows * rows) + EPS)


def norm_pull(rows, scaling, gain, grad):
    gained = gain * grad
    inner = row_mean(gained * rows)
    grad_rows = scaling * gained - rows * (scaling * scaling * scaling * inner)
    return center(grad_rows), grad * rows * scaling


def col_sum(array):
    return jnp.sum(array.astype(F32), axis=0, keepdims=True)


def pick(meta, layer, own, other, dst, sem):
    @pl.when(meta[0] == layer)
    def _():
        pltpu.make_async_copy(own, dst, sem).start()

    @pl.when(meta[0] != layer)
    def _():
        pltpu.make_async_copy(other, dst, sem).start()


def done(src, dst, sem):
    pltpu.make_async_copy(src, dst, sem).wait()


def halves(pair):
    first = lax.broadcasted_iota(jnp.int32, pair.shape, 1) < HEAD_DIM
    zero = jnp.zeros_like(pair)
    return jnp.concatenate([jnp.where(first, pair, zero), jnp.where(first, zero, pair)], axis=0)


def merge(stacked):
    rows = stacked.shape[0] // 2
    first = lax.broadcasted_iota(jnp.int32, (rows, stacked.shape[1]), 1) < HEAD_DIM
    return jnp.where(first, stacked[:rows], stacked[rows:])


def owner(meta, places):
    total = jnp.zeros(places.shape, jnp.int32)
    bound = 0
    for doc in range(3):
        bound = bound + meta[2 + doc]
        total = total + (places >= bound).astype(jnp.int32)
    return total


def mask_bias(meta, half, rows, keys):
    row_at = lax.broadcasted_iota(jnp.int32, (rows, 1), 0) + half * rows
    key_at = lax.broadcasted_iota(jnp.int32, (1, keys), 1)
    allowed = (owner(meta, row_at) == owner(meta, key_at)) & (key_at <= row_at)
    return jnp.where(allowed, 0.0, NEG).astype(F32)


def take(refs, count):
    out = refs[:count]
    del refs[:count]
    return out


class State(NamedTuple):
    vec: Any
    attn: Any
    up: Any
    down: Any
    rows: Any
    normed: Any
    low_normed: Any
    query: Any
    kv: Any
    att: Any
    probs: Any
    mid: Any
    act: Any
    hid: Any
    part: Any
    cot: Any
    low: Any
    grad: Any
    sums: Any


class Bench:
    def __init__(self, meta, shapes):
        self.meta = meta
        shapes, self.tree = jax.tree.flatten(shapes)
        self.arrays = shapes
        self.shapes = [pltpu.VMEM(a.shape, a.dtype) for a in shapes]

    def follow(self, arrays):
        self.meta, arrays[0] = lax.optimization_barrier((self.meta, arrays[0]))

    def run(self, body, ins=(), outs=(), hbm_ins=(), scratch=(), first=False):
        ins = [pltpu.with_memory_space_constraint(a, pltpu.VMEM) for a in ins]
        hbm_ins = [pltpu.with_memory_space_constraint(a, pltpu.HBM) for a in hbm_ins]
        held = [] if first else [pltpu.with_memory_space_constraint(a, pltpu.VMEM) for a in self.arrays]
        shapes = [(pltpu.VMEM if near else pltpu.HBM)(dims, dtype) for near, dims, dtype in outs]
        n_ins, n_hbm, n_outs, n_held = len(ins), len(hbm_ins), len(outs), len(self.shapes)

        def kernel(meta, *refs):
            refs = list(refs)
            near, far, _, made = take(refs, n_ins), take(refs, n_hbm), take(refs, len(held)), take(refs, n_outs)
            state = jax.tree.unflatten(self.tree, take(refs, n_held))
            body(meta, near, far, made, state, *refs)

        before = 1 + n_ins + n_hbm
        got = pl.pallas_call(
            kernel,
            out_shape=tuple(shapes + self.shapes),
            in_specs=[SMEM] + [VMEM] * n_ins + [HBM] * n_hbm + [VMEM] * len(held),
            out_specs=tuple([VMEM if near else HBM for near, _, _ in outs] + [VMEM] * n_held),
            input_output_aliases={before + i: n_outs + i for i in range(len(held))},
            scratch_shapes=list(scratch),
            compiler_params=pltpu.CompilerParams(vmem_limit_bytes=VMEM_BYTES),
            cost_estimate=pl.CostEstimate(flops=1, bytes_accessed=1, transcendentals=0),
        )(self.meta, *ins, *hbm_ins, *held)
        self.arrays = list(got[n_outs:])
        return list(got[:n_outs])


ATTN_GAIN, QV_BIAS, OUT_BIAS, MLP_GAIN, UP_BIAS, DOWN_BIAS = range(6)
MLP1, ATTN1, MLP0, ATTN0 = range(4)


def pack_kernel(*refs):
    count = (len(refs) - 3) // 2
    refs = list(refs)
    sources, (target, out), held, (sems,) = take(refs, count), take(refs, 2), take(refs, count), refs
    copies = [pltpu.make_async_copy(src, dst, sems.at[at]) for at, (src, dst) in enumerate(zip(sources, held))]
    for copy in copies:
        copy.start()
    out[...] = jnp.zeros(out.shape, F32)
    for row, (copy, ref) in enumerate(zip(copies, held)):
        copy.wait()
        if ref.shape[0] == 2:
            half = ref.shape[1]
            out[row : row + 1, :half] = ref[0:1]
            out[row : row + 1, half : 2 * half] = ref[1:2]
        else:
            out[row : row + 1, : ref.shape[1]] = ref[...]
    pltpu.sync_copy(out, target.at[pl.ds(0, out.shape[0])])


def load_attn(meta, layer, far, st, sems):
    qkv_own, qkv_other, out_own, out_other = far
    weights = st.attn[layer]
    local = weights.shape[2]
    work = [(qkv_own, qkv_other, weights.at[pl.ds(0, 3)])]
    for at in range(2):
        cols = pl.ds(at * local, local)
        work.append((out_own.at[:, cols], out_other.at[:, cols], weights.at[3, cols]))
    for at, (own, other, dst) in enumerate(work):
        pick(meta, layer, own, other, dst, sems.at[at])
    return lambda: [done(own, dst, sems.at[at]) for at, (own, _, dst) in enumerate(work)]


def open_kernel(meta, near, far, made, st, sems):
    vec_own, vec_other, *far = far
    for layer in range(2):
        rows = pl.ds(0, 8)
        pick(meta, layer, vec_own.at[rows], vec_other.at[rows], st.vec[layer], sems.at[layer])
    arrived = load_attn(meta, 0, far, st, sems.at[pl.ds(2, 3)])
    for layer in range(2):
        done(vec_own.at[pl.ds(0, 8)], st.vec[layer], sems.at[layer])
    arrived()


def load_kernel(meta, near, far, made, st, sems):
    *attn, up_own, up_other, down_own, down_other = far
    work = []
    for layer in range(2):
        work.append((layer, up_own, up_other, st.up[layer]))
        work.append((layer, down_own, down_other, st.down[layer]))
    for at, (layer, own, other, dst) in enumerate(work):
        pick(meta, layer, own, other, dst, sems.at[at])
    arrived = load_attn(meta, 1, attn, st, sems.at[pl.ds(4, 3)])
    for at, (layer, own, other, dst) in enumerate(work):
        done(own, dst, sems.at[at])
    arrived()


def vector(st, layer, row, first, last):
    return st.vec[layer][row : row + 1, first:last]


def attn_forward_kernel(layer, half, meta, near, far, made, st):
    weights = st.attn[layer]
    width, local = weights.shape[1:]
    count = st.part.shape[0] // 2
    here = slice(half * count, (half + 1) * count)
    if layer == 0:
        mine, other = near
        rows = jnp.where(meta[1] == half, mine[...], other[...]).astype(F32).T
    else:
        branch = st.part[here].astype(F32) + near[0][...].astype(F32) + vector(st, 0, DOWN_BIAS, 0, width)
        rows = (st.mid[0][here] + center(branch)).astype(BF16).astype(F32)
        rows = jnp.where(last_lane(rows.shape), 0.0, rows)
    st.rows[layer][here] = rows.astype(BF16)
    rows = expand(rows)
    normed = (rows * inv_rms(rows) * vector(st, layer, ATTN_GAIN, 0, width)).astype(BF16)
    st.normed[layer][here] = normed
    query = ((mm(normed, weights[0]) + vector(st, layer, QV_BIAS, 0, local)) * HEAD_DIM**-0.5).astype(BF16)
    st.query[layer][here] = query
    kv = st.kv[layer]
    kv[here, :local] = mm(normed, weights[1]).astype(BF16)
    kv[here, local:] = (mm(normed, weights[2]) + vector(st, layer, QV_BIAS, local, 2 * local)).astype(BF16)
    keys = (half + 1) * count
    masked = mask_bias(meta, half, count, keys)
    for pair in range(local // LANES):
        cols = slice(pair * LANES, (pair + 1) * LANES)
        vcols = slice(local + pair * LANES, local + (pair + 1) * LANES)
        scores = mm_t(halves(query[:, cols]), kv[:keys, cols])
        scores = (scores.reshape(2, count, keys) + masked[None]).reshape(2 * count, keys)
        expo = jnp.exp(scores - jnp.max(scores, axis=-1, keepdims=True))
        probs = (expo * (1.0 / jnp.sum(expo, axis=-1, keepdims=True))).astype(BF16)
        st.probs[layer][half][pair] = probs
        st.att[layer][here, cols] = merge(mm(probs, kv[:keys, vcols])).astype(BF16)
    attended = st.att[layer][here]
    for at in range(2):
        cols = slice(at * local, (at + 1) * local)
        part = mm(attended, weights[3, cols]).astype(BF16)
        st.part[here, cols] = part
        made[0][:, cols] = part


def mlp_middle(layer, here, received, st):
    width = st.part.shape[1]
    branch = st.part[here].astype(F32) + received[...].astype(F32) + vector(st, layer, OUT_BIAS, 0, width)
    middle = expand(st.rows[layer][here].astype(F32)) + center(branch)
    st.mid[layer][here] = middle
    normed = (middle * inv_rms(middle) * vector(st, layer, MLP_GAIN, 0, width)).astype(BF16)
    st.low_normed[layer][here] = normed
    return normed


def gelu_slope(hidden):
    root = (2.0 / jnp.pi) ** 0.5
    square = hidden * hidden
    half_up = 0.5 + 0.5 * jnp.tanh(hidden * (root + (root * 0.044715) * square))
    product = hidden * half_up
    return product, half_up + product * (1.0 - half_up) * (2 * root + (6 * root * 0.044715) * square)


def mlp_forward_kernel(chunk, half, meta, near, far, made, st, kept, sems):
    count = st.part.shape[0] // 2
    here = slice(half * count, (half + 1) * count)
    normed = mlp_middle(0, here, near[0], st)
    part = None
    for at in range(0, st.up[0].shape[1], chunk):
        cols = slice(at, at + chunk)
        hidden = mm(normed, st.up[0][:, cols]) + vector(st, 0, UP_BIAS, at, at + chunk)
        active, slope = gelu_slope(hidden)
        active = active.astype(BF16)
        kept[0, :, cols] = active
        kept[1, :, cols] = slope.astype(BF16)
        term = mm(active, st.down[0][cols, :])
        part = term if part is None else part + term
    copies = [pltpu.make_async_copy(kept.at[at], made[1 + at], sems.at[at]) for at in range(2)]
    for copy in copies:
        copy.start()
    part = part.astype(BF16)
    st.part[here] = part
    made[0][...] = part
    for copy in copies:
        copy.wait()


def add_sums(st, row, first, terms, fresh):
    places = slice(first, first + terms.shape[1])
    total = col_sum(terms)
    st.sums[row : row + 1, places] = total if fresh else total + st.sums[row : row + 1, places]


def mlp_both_kernel(chunk, half, meta, near, far, made, st, kept, sem):
    count, width = st.part.shape[0] // 2, st.part.shape[1]
    here = slice(half * count, (half + 1) * count)
    fresh = half == 0
    normed = mlp_middle(1, here, near[0], st)
    cot = jnp.where(meta[1] == half, near[1][...], near[2][...]).astype(F32).T
    st.cot[here] = cot.astype(BF16)
    low = center(cot).astype(BF16)
    st.low[here] = low
    add_sums(st, MLP1, 0, low, fresh)
    part, grad = None, None
    for at in range(0, st.up[1].shape[1], chunk):
        cols = slice(at, at + chunk)
        up, down = st.up[1][:, cols], st.down[1][cols, :]
        active, slope = gelu_slope(mm(normed, up) + vector(st, 1, UP_BIAS, at, at + chunk))
        active = active.astype(BF16)
        st.act[here, cols] = active
        hid = (mm_t(low, down) * slope).astype(BF16)
        st.hid[here, cols] = hid
        add_sums(st, MLP1, width + at, hid, fresh)
        terms = mm(active, down), mm_t(hid, up)
        part, grad = terms if part is None else (part + terms[0], grad + terms[1])
    grad = grad.astype(BF16)
    st.part[here] = grad
    made[0][...] = grad
    kept[...] = part.astype(BF16)
    pltpu.sync_copy(kept, made[1])


def mlp_backward_kernel(chunk, half, meta, near, far, made, st, slope, sem):
    load = pltpu.make_async_copy(far[0], slope, sem)
    load.start()
    count, width = st.part.shape[0] // 2, st.part.shape[1]
    here = slice(half * count, (half + 1) * count)
    fresh = half == 1
    hidden = st.up[0].shape[1]
    rows = expand(st.rows[1][here].astype(F32))
    grad = st.part[here].astype(F32) + near[0][...].astype(F32)
    pulled, gain_terms = norm_pull(rows, inv_rms(rows), vector(st, 1, ATTN_GAIN, 0, width), grad)
    grad_in = st.grad[here] + pulled
    grad_in = center((grad_in - grad_in[:, width - 1 :]).astype(BF16).astype(F32))
    st.grad[here] = grad_in
    low = grad_in.astype(BF16)
    st.low[here] = low
    add_sums(st, MLP0, 0, low, fresh)
    add_sums(st, MLP0, width + hidden, gain_terms, fresh)
    grad = None
    load.wait()
    for at in range(0, hidden, chunk):
        cols = slice(at, at + chunk)
        hid = (mm_t(low, st.down[0][cols, :]) * slope[:, cols].astype(F32)).astype(BF16)
        st.hid[here, cols] = hid
        add_sums(st, MLP0, width + at, hid, fresh)
        term = mm_t(hid, st.up[0][:, cols])
        grad = term if grad is None else grad + term
    grad = grad.astype(BF16)
    st.part[here] = grad
    made[0][...] = grad


def attn_backward_kernel(layer, half, meta, near, far, made, st, *refs):
    weights = st.attn[layer]
    width, local = weights.shape[1:]
    count = st.part.shape[0] // 2
    here = slice(half * count, (half + 1) * count)
    fresh = half == 1
    name = ATTN1 if layer else ATTN0
    middle = st.mid[layer][here]
    grad = st.part[here].astype(F32) + near[0][...].astype(F32)
    pulled, gain_terms = norm_pull(middle, inv_rms(middle), vector(st, layer, MLP_GAIN, 0, width), grad)
    upstream = center(st.cot[here].astype(F32)) if layer else st.grad[here]
    grad_mid = upstream + pulled
    st.grad[here] = grad_mid
    low = grad_mid.astype(BF16)
    st.low[here] = low
    add_sums(st, name, 0, gain_terms, fresh)
    add_sums(st, name, width, low, fresh)
    grad_att = (mm_t(low[:, :local], weights[3, :local]) + mm_t(low[:, local:], weights[3, local:])).astype(BF16)
    at = 2 * width
    query, kv, dqkv = st.query[layer], st.kv[layer], st.hid
    early = made[-1] if half else near[1]
    keys = (half + 1) * count
    for pair in range(local // LANES):
        cols = slice(pair * LANES, (pair + 1) * LANES)
        vcols = slice(local + pair * LANES, local + (pair + 1) * LANES)
        v2cols = slice(2 * local + pair * LANES, 2 * local + (pair + 1) * LANES)
        grads = halves(grad_att[:, cols])
        queries = halves(query[here, cols])
        low_probs = st.probs[layer][half][pair]
        probs = low_probs.astype(F32)
        grad_probs = mm_t(grads, kv[:keys, vcols])
        inner = jnp.sum(grad_probs * probs, axis=-1, keepdims=True)
        grad_scores = (probs * (grad_probs - inner)).astype(BF16)
        grad_query = (merge(mm(grad_scores, kv[:keys, cols])) * HEAD_DIM**-0.5).astype(BF16)
        grad_key = t_mm(grad_scores, queries)
        grad_value = t_mm(low_probs, grads)
        if half:
            early[:, cols] = grad_key[:count]
            early[:, vcols] = grad_value[:count]
            grad_key, grad_value = grad_key[count:], grad_value[count:]
        else:
            grad_key, grad_value = grad_key + early[:, cols], grad_value + early[:, vcols]
        grad_value = grad_value.astype(BF16)
        dqkv[here, cols] = grad_query
        dqkv[here, vcols] = grad_key.astype(BF16)
        dqkv[here, v2cols] = grad_value
        add_sums(st, name, at + pair * LANES, grad_query, fresh)
        add_sums(st, name, at + local + pair * LANES, grad_value, fresh)
    gpart = mm_t(dqkv[here, :local], weights[0])
    gpart = gpart + mm_t(dqkv[here, local : 2 * local], weights[1])
    gpart = gpart + mm_t(dqkv[here, 2 * local : 3 * local], weights[2])
    if layer == 0:
        rows = expand(st.rows[0][here].astype(F32))
        add_sums(st, name, at + 2 * local, gpart * rows * inv_rms(rows), fresh)
    st.part[here] = gpart.astype(BF16)
    if layer:
        made[0][...] = gpart.astype(BF16)
    elif half == 0:
        away = pl.ds(pl.multiple_of((1 - meta[1]) * count, 16), count)
        made[0][...] = st.part[away]
        row = name
        made[1][...] = st.sums[row : row + 1, at + 2 * local : at + 2 * local + width]
        own = pl.ds(pl.multiple_of(meta[1] * count, 16), count)
        sems = refs[0]
        copies = []
        for n, ref in enumerate((st.part, st.rows[0], st.grad, st.mid[1])):
            copies.append(pltpu.make_async_copy(ref.at[own], made[3 + n], sems.at[n]))
            copies[-1].start()
        for side in range(2):

            @pl.when(meta[1] == side)
            def _():
                pltpu.make_async_copy(far[1 - side], made[2], sems.at[4]).start()
                pltpu.make_async_copy(far[side], made[7], sems.at[5]).start()

        copies.append(pltpu.make_async_copy(far[0], made[2], sems.at[4]))
        copies.append(pltpu.make_async_copy(far[0], made[7], sems.at[5]))
        for copy in copies:
            copy.wait()


def mlp_weights_kernel(layer, meta, near, far, made, st, *refs):
    width, hidden = st.up[0].shape
    if far:
        active, load_sems = refs
        count = far[0].shape[0]
        loads = [
            pltpu.make_async_copy(ref, active.at[pl.ds(at * count, count)], load_sems.at[at]) for at, ref in enumerate(far)
        ]
        for load in loads:
            load.start()
    else:
        active, loads = st.act, []
    block = made[0].shape[1]
    for out, part in ((made[1], 1 - meta[0]), (made[0], meta[0])):
        rows = width // 2
        left = st.low_normed[layer][:, pl.ds(pl.multiple_of(part * rows, LANES), rows)]
        for n in range(hidden // block):
            out[n * rows : (n + 1) * rows] = t_mm(left, st.hid[:, n * block : (n + 1) * block]).astype(BF16)
        base = hidden // block * rows
        rows = hidden // 2
        while loads:
            loads.pop().wait()
        left = active[:, pl.ds(pl.multiple_of(part * rows, LANES), rows)]
        for n in range(width // block):
            total = t_mm(left, st.low[:, n * block : (n + 1) * block])
            out[base + n * rows : base + (n + 1) * rows] = total.astype(BF16)


def attn_weights_kernel(layer, extra, meta, near, far, made, st):
    width, local = st.attn[0].shape[1:]
    hidden = st.up[0].shape[1]
    piece = made[0].shape[0] // 8 - extra

    def put(out, first, total):
        for at in range(0, total.shape[0], piece):
            where = (first + at) // piece * (piece + extra)
            out[where : where + piece] = total[at : at + piece].astype(BF16)

    if extra:
        sums = st.sums
        rows = [sums[row : row + 1] for row in range(4)]
        smalls = []
        tail = 2 * width + 2 * local
        for gain, attn, mlp in (
            (rows[ATTN0][:, tail : tail + width] + near[0][...], rows[ATTN0], rows[MLP0]),
            (rows[MLP0][:, width + hidden : 2 * width + hidden], rows[ATTN1], rows[MLP1]),
        ):
            row = [gain, attn[:, 2 * width : tail], attn[:, width : 2 * width], attn[:, :width]]
            row += [mlp[:, width : width + hidden], mlp[:, :width]]
            lines = [part[:, at : at + local] for part in row for at in range(0, part.shape[1], local)]
            lines += [jnp.zeros((1, local), F32)] * (extra - len(lines))
            smalls.append(jnp.concatenate(lines, axis=0))

    for out, part in ((made[1], 1 - meta[0]), (made[0], meta[0])):
        rows = width // 2
        cols = pl.ds(pl.multiple_of(part * rows, LANES), rows)
        left = st.normed[layer][:, cols]
        for at in range(3):
            put(out, at * rows, t_mm(left, st.hid[:, at * local : (at + 1) * local]))
        put(out, 3 * rows, t_mm(st.att[layer][...], st.low[:, cols]))
        if extra:
            out[piece : piece + extra] = jnp.where(part == 0, smalls[0], smalls[1]).astype(BF16)
            for at in range(1, 8):
                where = at * (piece + extra) + piece
                out[where : where + extra] = jnp.zeros((extra, local), BF16)


def close_kernel(meta, vec_own, vec_other, grad_far, out_far, out_own, part, rows, grad, middle, result, grad_in, *refs):
    width = part.shape[1]

    *vecs, sems = refs
    for layer in range(2):
        pick(meta, layer, vec_own.at[pl.ds(0, 8)], vec_other.at[pl.ds(0, 8)], vecs[layer], sems.at[layer])
    for layer in range(2):
        done(vec_own.at[pl.ds(0, 8)], vecs[layer], sems.at[layer])

    def vec(layer, row):
        return vecs[layer][row : row + 1, :width]

    branch = out_own[...].astype(F32) + out_far[...].astype(F32) + vec(1, DOWN_BIAS)
    result[...] = (middle[...] + center(branch)).astype(BF16)
    rows = expand(rows[...].astype(F32))
    given = part[...].astype(F32) + grad_far[...].astype(F32)
    pulled, _ = norm_pull(rows, inv_rms(rows), vec(0, ATTN_GAIN), given)
    total = grad[...] + pulled
    grad_in[...] = (total - total[:, width - 1 :]).astype(BF16)


def place_kernel(kinds, extra, meta, *refs):
    refs = list(refs)
    sources = take(refs, 4)
    outs = refs[:-2]
    wide, sems = refs[-2:]
    piece = wide.shape[1]

    def copy(n):
        part = meta[0] if n < 8 else 1 - meta[0]
        which, where = kinds[n % 8]
        return pltpu.make_async_copy(wide.at[n], outs[which].at[where(part)], sems.at[n])

    for layer in range(2):

        @pl.when(meta[0] == layer)
        def _():
            step = piece + (0 if layer else extra)
            for n in range(16):
                place = meta[6 + n // 8] & 6 if extra and layer == 0 else meta[6 + n // 8]
                at = pl.multiple_of(((n % 8) ^ place) * step, 16)
                wide[n] = sources[2 * (n // 8) + layer][pl.ds(at, piece)].astype(F32)
                copy(n).start()

    if extra:
        at = pl.multiple_of((meta[6] & 6) * (piece + extra) + piece, 16)
        small = sources[0][pl.ds(at, extra)].astype(F32)
        at = 0
        for out in outs[2:]:
            for row in range(out.shape[0]):
                for col in range(0, out.shape[1], small.shape[1]):
                    out[row : row + 1, col : col + small.shape[1]] = small[at : at + 1]
                    at += 1
    for n in range(16):
        copy(n).wait()


def shape(dims, dtype=BF16):
    return jax.ShapeDtypeStruct(dims, dtype)


def call(kernel, in_specs, outs, scratch, args, out_specs, limit=VMEM_BYTES):
    return pl.pallas_call(
        kernel,
        out_shape=tuple(outs),
        in_specs=in_specs,
        out_specs=tuple(out_specs),
        scratch_shapes=scratch,
        compiler_params=pltpu.CompilerParams(vmem_limit_bytes=limit),
        cost_estimate=pl.CostEstimate(flops=1, bytes_accessed=1, transcendentals=0),
    )(*args)


def swap(array, axis):
    return lax.ppermute(array, axis, [(0, 1), (1, 0)])


def halve_kernel(step, sides, mine, other, *outs):
    rows = mine.shape[0] // len(outs)
    for at, out in enumerate(outs):
        here = slice(None)
        if len(outs) == 2:
            side = sides[step] if at == 0 else 1 - sides[step]
            here = pl.ds(pl.multiple_of(side * rows, 16), rows)
        out[...] = (mine[here].astype(F32) + other[here].astype(F32)).astype(BF16)


def join_kernel(first, second, out):
    rows = first.shape[0]
    out[:rows] = first[...]
    out[rows:] = second[...]


def in_vmem(*arrays):
    return [pltpu.with_memory_space_constraint(a, pltpu.VMEM) for a in arrays]


def add_halves(step, sides, mine, other):
    rows, width = mine.shape
    halves = 1 if step is None else 2
    outs = [pltpu.VMEM((rows // halves, width), BF16)] * halves
    kernel = functools.partial(halve_kernel, step)
    return call(kernel, [SMEM, VMEM, VMEM], outs, [], [sides, *in_vmem(mine, other)], [VMEM] * halves)


def join(first, second):
    rows, width = first.shape
    outs = [pltpu.VMEM((2 * rows, width), BF16)]
    return call(join_kernel, [VMEM, VMEM], outs, [], in_vmem(first, second), [VMEM])[0]


SWAP, HALVE, ADD, JOIN = range(4)


class GroupSum:
    def __init__(self, sides, whole, mine, theirs):
        self.sides = sides
        self.held, self.received = mine, theirs
        self.steps = list(zip(*self.orders(lax.axis_size(GROUPS).bit_length() - 1)))
        self.whole = whole
        count = len(self.steps)
        self.todo = [(SWAP, None)] + [(HALVE, k) for k in range(count - 1)]
        if whole:
            self.todo += [(ADD, count - 1), (ADD, count - 2)] + [(JOIN, k) for k in range(count - 3, -1, -1)]
        else:
            self.todo += [(HALVE, count - 1), (ADD, count - 1)] + [(JOIN, k) for k in range(count - 2, -1, -1)]

    def make(self):
        kind, at = self.todo[0]
        if kind == SWAP:
            return [self.held, self.received]
        if kind == JOIN:
            return [join(self.held, self.received)]
        return list(add_halves(at if kind == HALVE else None, self.sides, self.held, self.received))

    def send(self, arrays):
        kind, at = self.todo.pop(0)
        self.held = arrays[0]
        self.received = swap(arrays[-1], SECTION) if kind == SWAP else self.exchange(arrays[-1], self.steps[at])

    @staticmethod
    def orders(bits):
        first = list(range(bits))
        second = [1, 0] + first[2:] if bits > 1 else first
        return first, second

    @staticmethod
    def exchange(array, bits):
        count = lax.axis_size(GROUPS)
        pairs = [(core * count + i, core * count + (i ^ (1 << bit))) for core, bit in enumerate(bits) for i in range(count)]
        return lax.ppermute(array, (SECTION, GROUPS), pairs)

    @staticmethod
    def which_side(bits):
        core, index = lax.axis_index(SECTION), lax.axis_index(GROUPS)
        return jnp.stack([(index >> jnp.where(core == 0, *pair)) & 1 for pair in zip(*GroupSum.orders(bits))])

    @staticmethod
    def place(bits, core):
        index = lax.axis_index(GROUPS)
        out = jnp.int32(0)
        for first, second in zip(*GroupSum.orders(bits)):
            out = out * 2 + ((index >> jnp.where(core == 0, first, second)) & 1)
        return out


def boundary(values, flows, after=()):
    flows = [flow for flow in flows if flow.todo]
    arrived = [flow for flow in flows if flow.todo[0][0] != SWAP]
    values = list(values)
    got = lax.optimization_barrier((*values, *[flow.received for flow in arrived], *after))
    values = list(got[: len(values)])
    for flow, received in zip(arrived, got[len(values) :]):
        flow.received = received
    arrays = [flow.make() for flow in flows]
    got = list(lax.optimization_barrier((*values, *[a for group in arrays for a in group])))
    values = take(got, len(values))
    for flow, group in zip(flows, arrays):
        flow.send(take(got, len(group)))
    return values


def in_order(array, place, count):
    blocks = array.reshape((count, array.shape[0] // count) + array.shape[1:])
    return jnp.take(blocks, jnp.arange(count, dtype=jnp.int32) ^ place, axis=0).reshape(array.shape)


def local(
    inputs,
    doc_lengths,
    attn_gain,
    qkv_weight,
    qv_bias,
    out_weight,
    out_bias,
    mlp_gain,
    up_weight,
    up_bias,
    down_weight,
    down_bias,
    cotangent,
):
    core = lax.axis_index(SECTION)
    side = lax.axis_index(TENSOR)
    groups = lax.axis_size(GROUPS)
    bits = groups.bit_length() - 1
    place = GroupSum.place(bits, core)
    rows = inputs.shape[1]
    width = attn_gain.shape[1]
    heads = qkv_weight.shape[3]
    hidden = up_weight.shape[2]
    pairs = heads // LANES
    chunk = hidden // 2
    extra = 16

    def own_rows(array):
        mine = lax.dynamic_index_in_dim(jnp.transpose(array, (2, 0, 1)), core, 1, keepdims=False)
        return jnp.pad(mine, ((0, width - mine.shape[0]), (0, 0)))

    lengths = lax.dynamic_index_in_dim(doc_lengths[:, 0, :], core, 0, keepdims=False)
    if groups == 8:
        places = [place, GroupSum.place(bits, 1 - core)]
    else:
        places = [jnp.int32(0)] * 2
    meta = jnp.concatenate([jnp.stack([core, side]).astype(jnp.int32), lengths, jnp.stack(places)])
    def each(*dims, dtype=BF16):
        return (shape(dims, dtype),) * 2

    unit = 2 * rows
    layer_probs = (shape((pairs, unit, rows)), shape((pairs, unit, unit)))
    bench = Bench(
        meta,
        State(
            vec=each(8, hidden, dtype=F32),
            attn=each(4, width, heads),
            up=each(width, hidden),
            down=each(hidden, width),
            rows=each(unit, width),
            normed=each(unit, width),
            low_normed=each(unit, width),
            query=each(unit, heads),
            kv=each(unit, 2 * heads),
            att=each(unit, heads),
            probs=(layer_probs, layer_probs),
            mid=each(unit, width, dtype=F32),
            act=shape((unit, hidden)),
            hid=shape((unit, hidden)),
            part=shape((unit, width)),
            cot=shape((unit, width)),
            low=shape((unit, width)),
            grad=shape((unit, width), F32),
            sums=shape((8, 3 * width + 2 * heads), F32),
        ),
    )
    sides = GroupSum.which_side(bits)

    entry = own_rows(inputs)
    small_in = (attn_gain, qv_bias[0], out_bias, mlp_gain, up_bias, down_bias)
    qkv, out = jnp.transpose(qkv_weight[0], (1, 0, 2)), out_weight[0]
    (vectors,) = call(
        pack_kernel,
        [HBM] * len(small_in),
        [pltpu.HBM((512, hidden), F32)],
        [
            pltpu.VMEM((8, hidden), F32),
            *[pltpu.VMEM(a.shape, F32) for a in small_in],
            pltpu.SemaphoreType.DMA((len(small_in),)),
        ],
        [pltpu.with_memory_space_constraint(a, pltpu.HBM) for a in small_in],
        [HBM],
    )
    far = swap(entry, TENSOR)
    vec_pair = (vectors, swap(vectors, SECTION))
    attn_pair = (qkv, swap(qkv, SECTION), out, swap(out, SECTION))
    cots, _ = lax.optimization_barrier((cotangent, vectors))
    cots = own_rows(cots)
    *attn_pair, cots = lax.optimization_barrier((*attn_pair, cots))
    far, cots, down = lax.optimization_barrier((far, cots, down_weight[0]))
    entry = (entry, far)
    up = up_weight[0]
    up_pair = (up, swap(up, SECTION))
    down_pair = (down, swap(down, SECTION))
    cots = (cots, swap(cots, TENSOR))

    bench.run(open_kernel, hbm_ins=[*vec_pair, *attn_pair], scratch=[pltpu.SemaphoreType.DMA((5,))], first=True)
    sent = (True, (rows, width), BF16)
    partial = functools.partial

    given = [None, None]
    for half in range(2):
        (part,) = bench.run(partial(attn_forward_kernel, 0, half), entry, [sent])
        given[half] = swap(part, TENSOR)
    *down_pair, cot_far = lax.optimization_barrier((*down_pair, cots[1]))
    cots = (cots[0], cot_far)
    bench.run(load_kernel, hbm_ins=[*attn_pair, *up_pair, *down_pair], scratch=[pltpu.SemaphoreType.DMA((7,))])
    acts, slopes = [], []
    for half in range(2):
        outs = [sent] + [(False, (rows, hidden), BF16)] * 2
        scratch = [pltpu.VMEM((2, rows, hidden), BF16), pltpu.SemaphoreType.DMA((2,))]
        part, *kept = bench.run(partial(mlp_forward_kernel, chunk, half), [given[half]], outs, scratch=scratch)
        given[half] = swap(part, TENSOR)
        acts.append(kept[0])
        slopes.append(kept[1])
    for half in range(2):
        (part,) = bench.run(partial(attn_forward_kernel, 1, half), [given[half]], [sent])
        given[half] = swap(part, TENSOR)
    mlp_parts = []
    kept = (False, (rows, width), BF16)
    for half in range(2):
        scratch = [pltpu.VMEM((rows, width), BF16), pltpu.SemaphoreType.DMA]
        body = partial(mlp_both_kernel, chunk, half)
        part, mlp_part = bench.run(body, [given[half], *cots], [sent, kept], scratch=scratch)
        given[half] = swap(part, TENSOR)
        mlp_parts.append(mlp_part)

    def weights(kernel, dims):
        ins = [gain_far] if kernel is attn_weights_kernel and dims[0] % (8 * 192) else []
        layer = 0 if ins or kernel is mlp_weights_kernel and mlp1 is not None else 1
        body = partial(kernel, layer) if kernel is mlp_weights_kernel else partial(kernel, layer, extra if ins else 0)
        far = acts if kernel is mlp_weights_kernel and layer == 0 else []
        scratch = [pltpu.VMEM((2 * rows, hidden), BF16), pltpu.SemaphoreType.DMA((2,))] if far else []
        return GroupSum(sides, bool(ins), *bench.run(body, ins, [(True, dims, BF16)] * 2, far, scratch))

    mlp_dims = (hidden * width // 384, 384)
    attn_dims = (2 * width * heads // 384, 384)
    mlp1 = None
    bench.follow(given)
    mlp1 = weights(mlp_weights_kernel, mlp_dims)
    early = (True, (rows, 2 * heads), F32)
    for half in (1, 0):
        (given[half],) = boundary([given[half]], [mlp1], () if half else [part])
        ins, outs = ([given[1]], [sent, early]) if half else ([given[0], link], [sent])
        part, *rest = bench.run(partial(attn_backward_kernel, 1, half), ins, outs)
        link = rest[0] if half else None
        given[half] = swap(part, TENSOR)
    attn1 = weights(attn_weights_kernel, attn_dims)
    for half in (1, 0):
        if half:
            given[1], attn1.held, attn1.received = lax.optimization_barrier((given[1], attn1.held, attn1.received))
        else:
            (given[0],) = boundary([given[0]], [mlp1, attn1], [part])
        scratch = [pltpu.VMEM((rows, hidden), BF16), pltpu.SemaphoreType.DMA]
        body = partial(mlp_backward_kernel, chunk, half)
        (part,) = bench.run(body, [given[half]], [sent], [slopes[half]], scratch)
        given[half] = swap(part, TENSOR)
    mlp0 = weights(mlp_weights_kernel, mlp_dims)
    (given[1],) = boundary([given[1]], [mlp1, attn1, mlp0], [part])
    (link,) = bench.run(partial(attn_backward_kernel, 0, 1), [given[1]], [early])
    given[0], link = boundary([given[0], link], [mlp1, attn1, mlp0])
    own = [(False, (rows, width), dtype) for dtype in (BF16, BF16, F32, F32)]
    outs = [sent, (True, (1, width), F32), sent, *own, sent]
    body = partial(attn_backward_kernel, 0, 0)
    scratch = [pltpu.SemaphoreType.DMA((6,))]
    away_grad, gain, away_out, *own = bench.run(body, [given[0], link], outs, mlp_parts, scratch)
    (gain_far,) = boundary([swap(gain, TENSOR)], [attn1], [gain])
    gain_far, away_grad, away_out = lax.optimization_barrier((gain_far, away_grad, away_out))
    backs = [swap(away_grad, TENSOR), swap(away_out, TENSOR)]
    attn0 = weights(attn_weights_kernel, (attn_dims[0] + 8 * extra, 384))

    token = [meta]

    def end(flow):
        while flow.todo:
            token[:] = boundary(token, [flow])
        token[0], *pieces = lax.optimization_barrier((token[0], flow.held, flow.received))
        whole = join(*pieces)
        if groups != 8:
            split = groups // 2 if flow.whole else groups
            whole = in_order(whole, place // (groups // split), split)
        token[0], whole = lax.optimization_barrier((token[0], whole))
        return whole, swap(whole, SECTION)

    def close(back_grad, back_out):
        args = [*in_vmem(back_grad, back_out, own[-1]), *own[:-1]]
        specs = [SMEM, HBM, HBM] + [VMEM] * len(args)
        scratch = [pltpu.VMEM((8, hidden), F32)] * 2 + [pltpu.SemaphoreType.DMA((2,))]
        outs = [shape((rows, width))] * 2
        return call(close_kernel, specs, outs, scratch, [token[0], *vec_pair, *args], [VMEM] * 2, 2 * VMEM_BYTES)

    token[:] = boundary(token, [mlp0, mlp1, attn0])
    token[:] = boundary(token, [attn0, mlp0, attn1], [mlp1.received])
    token[0], *backs = lax.optimization_barrier((token[0], *backs))
    token[:] = boundary(token, [attn0, mlp0, mlp1, attn1])
    result, grad_in = close(*backs)
    result, grad_in = result[:, : width - 1], grad_in[:, : width - 1]
    token[0], result, grad_in = lax.optimization_barrier((token[0], result, grad_in))
    token[:] = boundary(token, [attn0, mlp0, attn1])
    mlp1 = end(mlp1)
    token[:] = boundary(token, [attn0, mlp0], [attn1.received])
    attn1 = end(attn1)
    token[:] = boundary(token, [attn0])
    mlp0 = end(mlp0)
    while attn0.todo:
        token[:] = boundary(token, [attn0])

    up_rows, down_rows = width // 2, hidden // 2

    def mlp_kind(block):
        if block < 4:
            return 0, lambda part: (pl.ds(pl.multiple_of(part * up_rows, 8), up_rows), pl.ds(block * 384, 384))
        col, row = (block - 4) // 2, (block - 4) % 2
        return 1, lambda part: (
            pl.ds(pl.multiple_of(part * down_rows + row * 384, 8), 384),
            pl.ds(col * 384, 384),
        )

    def attn_kind(block):
        which, row = block // 2, block % 2
        if which < 3:
            return 0, lambda part: (which, pl.ds(pl.multiple_of(part * up_rows + row * 192, 8), 192), slice(None))
        return 1, lambda part: (pl.ds(row * 192, 192), pl.ds(pl.multiple_of(part * 384, 128), 384))

    def placed(kinds, extra_rows, first, second, outs):
        piece = first[0].shape[0] // 8 - extra_rows
        args = [token[0], first[0], second[0], first[1], second[1]]
        scratch = [pltpu.VMEM((16, piece, 384), F32), pltpu.SemaphoreType.DMA((16,))]
        out_specs = [HBM, HBM] + [VMEM] * (len(outs) - 2)
        kernel = functools.partial(place_kernel, kinds, extra_rows)
        args[1:] = in_vmem(*args[1:])
        return call(kernel, [SMEM] + [VMEM] * 4, outs, scratch, args, out_specs, 2 * VMEM_BYTES)

    grad_up, grad_down = placed(
        [mlp_kind(b) for b in range(8)],
        0,
        mlp0,
        mlp1,
        [shape((width, hidden), F32), shape((hidden, width), F32)],
    )
    token[0], grad_up, grad_down = lax.optimization_barrier((token[0], grad_up, grad_down))
    attn0 = end(attn0)
    grad_qkv, grad_out, *small = placed(
        [attn_kind(b) for b in range(8)],
        extra,
        attn0,
        attn1,
        [shape((3, width, heads), F32), shape((heads, width), F32)]
        + [shape(dims, F32) for dims in ((1, width), (2, heads), (1, width), (1, width), (1, hidden), (1, width))],
    )

    return (
        result[None],
        grad_in[None],
        small[0],
        jnp.transpose(grad_qkv, (1, 0, 2))[None],
        small[1][None],
        grad_out[None],
        small[2],
        small[3],
        grad_up[None],
        small[4],
        grad_down[None],
        small[5],
    )


def solution(mesh):
    in_specs = (
        P(None, (GROUPS, TENSOR), None),
        P(None, GROUPS, None),
        P(SECTION, None),
        P(SECTION, None, None, TENSOR),
        P(SECTION, None, TENSOR),
        P(SECTION, TENSOR, None),
        P(SECTION, None),
        P(SECTION, None),
        P(SECTION, None, TENSOR),
        P(SECTION, TENSOR),
        P(SECTION, TENSOR, None),
        P(SECTION, None),
        P(None, (GROUPS, TENSOR), None),
    )
    out_specs = (
        P(SECTION, (GROUPS, TENSOR), None),
        P(SECTION, (GROUPS, TENSOR), None),
        P(SECTION, None),
        P(SECTION, None, None, TENSOR),
        P(SECTION, None, TENSOR),
        P(SECTION, TENSOR, None),
        P(SECTION, None),
        P(SECTION, None),
        P(SECTION, None, TENSOR),
        P(SECTION, TENSOR),
        P(SECTION, TENSOR, None),
        P(SECTION, None),
    )
    return jax.shard_map(local, mesh=mesh, in_specs=in_specs, out_specs=out_specs, check_vma=False)
```

```python
import functools
from typing import Any, NamedTuple

import jax
import jax.numpy as jnp
from jax import lax
from jax.experimental import pallas as pl
from jax.experimental.pallas import tpu as pltpu
from jax.sharding import PartitionSpec as P

HEAD_DIM = 64
LANES = 128
EPS = 1e-05
NEG = -1e30
VMEM_BYTES = 12 * 1024 * 1024

SECTION, GROUPS, TENSOR = "section", "dp", "tensor"

F32 = jnp.float32
BF16 = jnp.bfloat16

VMEM = pl.BlockSpec(memory_space=pltpu.VMEM)
SMEM = pl.BlockSpec(memory_space=pltpu.SMEM)
HBM = pl.BlockSpec(memory_space=pltpu.HBM)


def mm(left, right):
    return jnp.dot(left, right, preferred_element_type=F32)


def mm_t(left, right):
    return lax.dot_general(left, right, (((1,), (1,)), ((), ())), preferred_element_type=F32)


def t_mm(left, right):
    return lax.dot_general(left, right, (((0,), (0,)), ((), ())), preferred_element_type=F32)


def row_mean(array):
    return jnp.mean(array, axis=-1, keepdims=True)


def center(array):
    return array - row_mean(array)


def last_lane(shape):
    return lax.broadcasted_iota(jnp.int32, shape, 1) == shape[1] - 1


def expand(rows):
    return jnp.where(last_lane(rows.shape), -jnp.sum(rows, axis=-1, keepdims=True), rows)


def inv_rms(rows):
    return lax.rsqrt(row_mean(rows * rows) + EPS)


def norm_pull(rows, scaling, gain, grad):
    gained = gain * grad
    inner = row_mean(gained * rows)
    grad_rows = scaling * gained - rows * (scaling * scaling * scaling * inner)
    return center(grad_rows), grad * rows * scaling


def col_sum(array):
    return jnp.sum(array.astype(F32), axis=0, keepdims=True)


def pick(meta, layer, own, other, dst, sem):
    @pl.when(meta[0] == layer)
    def _():
        pltpu.make_async_copy(own, dst, sem).start()

    @pl.when(meta[0] != layer)
    def _():
        pltpu.make_async_copy(other, dst, sem).start()


def done(src, dst, sem):
    pltpu.make_async_copy(src, dst, sem).wait()


def halves(pair):
    first = lax.broadcasted_iota(jnp.int32, pair.shape, 1) < HEAD_DIM
    zero = jnp.zeros_like(pair)
    return jnp.concatenate([jnp.where(first, pair, zero), jnp.where(first, zero, pair)], axis=0)


def merge(stacked):
    rows = stacked.shape[0] // 2
    first = lax.broadcasted_iota(jnp.int32, (rows, stacked.shape[1]), 1) < HEAD_DIM
    return jnp.where(first, stacked[:rows], stacked[rows:])


def owner(meta, places):
    total = jnp.zeros(places.shape, jnp.int32)
    bound = 0
    for doc in range(3):
        bound = bound + meta[2 + doc]
        total = total + (places >= bound).astype(jnp.int32)
    return total


def mask_bias(meta, half, rows, keys):
    row_at = lax.broadcasted_iota(jnp.int32, (rows, 1), 0) + half * rows
    key_at = lax.broadcasted_iota(jnp.int32, (1, keys), 1)
    allowed = (owner(meta, row_at) == owner(meta, key_at)) & (key_at <= row_at)
    return jnp.where(allowed, 0.0, NEG).astype(F32)


def take(refs, count):
    out = refs[:count]
    del refs[:count]
    return out


class State(NamedTuple):
    vec: Any
    attn: Any
    up: Any
    down: Any
    rows: Any
    normed: Any
    low_normed: Any
    query: Any
    kv: Any
    att: Any
    probs: Any
    mid: Any
    act: Any
    hid: Any
    part: Any
    cot: Any
    low: Any
    grad: Any
    sums: Any


class Bench:
    def __init__(self, meta, shapes):
        self.meta = meta
        shapes, self.tree = jax.tree.flatten(shapes)
        self.arrays = shapes
        self.shapes = [pltpu.VMEM(a.shape, a.dtype) for a in shapes]

    def follow(self, arrays):
        self.meta, arrays[0] = lax.optimization_barrier((self.meta, arrays[0]))

    def run(self, body, ins=(), outs=(), hbm_ins=(), scratch=(), first=False):
        ins = [pltpu.with_memory_space_constraint(a, pltpu.VMEM) for a in ins]
        hbm_ins = [pltpu.with_memory_space_constraint(a, pltpu.HBM) for a in hbm_ins]
        held = [] if first else [pltpu.with_memory_space_constraint(a, pltpu.VMEM) for a in self.arrays]
        shapes = [(pltpu.VMEM if near else pltpu.HBM)(dims, dtype) for near, dims, dtype in outs]
        n_ins, n_hbm, n_outs, n_held = len(ins), len(hbm_ins), len(outs), len(self.shapes)

        def kernel(meta, *refs):
            refs = list(refs)
            near, far, _, made = take(refs, n_ins), take(refs, n_hbm), take(refs, len(held)), take(refs, n_outs)
            state = jax.tree.unflatten(self.tree, take(refs, n_held))
            body(meta, near, far, made, state, *refs)

        before = 1 + n_ins + n_hbm
        got = pl.pallas_call(
            kernel,
            out_shape=tuple(shapes + self.shapes),
            in_specs=[SMEM] + [VMEM] * n_ins + [HBM] * n_hbm + [VMEM] * len(held),
            out_specs=tuple([VMEM if near else HBM for near, _, _ in outs] + [VMEM] * n_held),
            input_output_aliases={before + i: n_outs + i for i in range(len(held))},
            scratch_shapes=list(scratch),
            compiler_params=pltpu.CompilerParams(vmem_limit_bytes=VMEM_BYTES),
            cost_estimate=pl.CostEstimate(flops=1, bytes_accessed=1, transcendentals=0),
        )(self.meta, *ins, *hbm_ins, *held)
        self.arrays = list(got[n_outs:])
        return list(got[:n_outs])


ATTN_GAIN, QV_BIAS, OUT_BIAS, MLP_GAIN, UP_BIAS, DOWN_BIAS = range(6)
MLP1, ATTN1, MLP0, ATTN0 = range(4)


def pack_kernel(*refs):
    count = (len(refs) - 3) // 2
    refs = list(refs)
    sources, (target, out), held, (sems,) = take(refs, count), take(refs, 2), take(refs, count), refs
    copies = [pltpu.make_async_copy(src, dst, sems.at[at]) for at, (src, dst) in enumerate(zip(sources, held))]
    for copy in copies:
        copy.start()
    out[...] = jnp.zeros(out.shape, F32)
    for row, (copy, ref) in enumerate(zip(copies, held)):
        copy.wait()
        if ref.shape[0] == 2:
            half = ref.shape[1]
            out[row : row + 1, :half] = ref[0:1]
            out[row : row + 1, half : 2 * half] = ref[1:2]
        else:
            out[row : row + 1, : ref.shape[1]] = ref[...]
    pltpu.sync_copy(out, target.at[pl.ds(0, out.shape[0])])


def load_attn(meta, layer, far, st, sems):
    qkv_own, qkv_other, out_own, out_other = far
    weights = st.attn[layer]
    local = weights.shape[2]
    work = [(qkv_own, qkv_other, weights.at[pl.ds(0, 3)])]
    for at in range(2):
        cols = pl.ds(at * local, local)
        work.append((out_own.at[:, cols], out_other.at[:, cols], weights.at[3, cols]))
    for at, (own, other, dst) in enumerate(work):
        pick(meta, layer, own, other, dst, sems.at[at])
    return lambda: [done(own, dst, sems.at[at]) for at, (own, _, dst) in enumerate(work)]


def open_kernel(meta, near, far, made, st, sems):
    vec_own, vec_other, *far = far
    for layer in range(2):
        rows = pl.ds(0, 8)
        pick(meta, layer, vec_own.at[rows], vec_other.at[rows], st.vec[layer], sems.at[layer])
    arrived = load_attn(meta, 0, far, st, sems.at[pl.ds(2, 3)])
    for layer in range(2):
        done(vec_own.at[pl.ds(0, 8)], st.vec[layer], sems.at[layer])
    arrived()


def load_kernel(meta, near, far, made, st, sems):
    *attn, up_own, up_other, down_own, down_other = far
    work = []
    for layer in range(2):
        work.append((layer, up_own, up_other, st.up[layer]))
        work.append((layer, down_own, down_other, st.down[layer]))
    for at, (layer, own, other, dst) in enumerate(work):
        pick(meta, layer, own, other, dst, sems.at[at])
    arrived = load_attn(meta, 1, attn, st, sems.at[pl.ds(4, 3)])
    for at, (layer, own, other, dst) in enumerate(work):
        done(own, dst, sems.at[at])
    arrived()


def vector(st, layer, row, first, last):
    return st.vec[layer][row : row + 1, first:last]


def attn_forward_kernel(layer, half, meta, near, far, made, st):
    weights = st.attn[layer]
    width, local = weights.shape[1:]
    count = st.part.shape[0] // 2
    here = slice(half * count, (half + 1) * count)
    if layer == 0:
        mine, other = near
        rows = jnp.where(meta[1] == half, mine[...], other[...]).astype(F32).T
    else:
        branch = st.part[here].astype(F32) + near[0][...].astype(F32) + vector(st, 0, DOWN_BIAS, 0, width)
        rows = (st.mid[0][here] + center(branch)).astype(BF16).astype(F32)
        rows = jnp.where(last_lane(rows.shape), 0.0, rows)
    st.rows[layer][here] = rows.astype(BF16)
    rows = expand(rows)
    normed = (rows * inv_rms(rows) * vector(st, layer, ATTN_GAIN, 0, width)).astype(BF16)
    st.normed[layer][here] = normed
    query = ((mm(normed, weights[0]) + vector(st, layer, QV_BIAS, 0, local)) * HEAD_DIM**-0.5).astype(BF16)
    st.query[layer][here] = query
    kv = st.kv[layer]
    kv[here, :local] = mm(normed, weights[1]).astype(BF16)
    kv[here, local:] = (mm(normed, weights[2]) + vector(st, layer, QV_BIAS, local, 2 * local)).astype(BF16)
    keys = (half + 1) * count
    masked = mask_bias(meta, half, count, keys)
    for pair in range(local // LANES):
        cols = slice(pair * LANES, (pair + 1) * LANES)
        vcols = slice(local + pair * LANES, local + (pair + 1) * LANES)
        scores = mm_t(halves(query[:, cols]), kv[:keys, cols])
        scores = (scores.reshape(2, count, keys) + masked[None]).reshape(2 * count, keys)
        expo = jnp.exp(scores - jnp.max(scores, axis=-1, keepdims=True))
        probs = (expo * (1.0 / jnp.sum(expo, axis=-1, keepdims=True))).astype(BF16)
        st.probs[layer][half][pair] = probs
        st.att[layer][here, cols] = merge(mm(probs, kv[:keys, vcols])).astype(BF16)
    attended = st.att[layer][here]
    for at in range(2):
        cols = slice(at * local, (at + 1) * local)
        part = mm(attended, weights[3, cols]).astype(BF16)
        st.part[here, cols] = part
        made[0][:, cols] = part


def mlp_middle(layer, here, received, st):
    width = st.part.shape[1]
    branch = st.part[here].astype(F32) + received[...].astype(F32) + vector(st, layer, OUT_BIAS, 0, width)
    middle = expand(st.rows[layer][here].astype(F32)) + center(branch)
    st.mid[layer][here] = middle
    normed = (middle * inv_rms(middle) * vector(st, layer, MLP_GAIN, 0, width)).astype(BF16)
    st.low_normed[layer][here] = normed
    return normed


def gelu_slope(hidden):
    root = (2.0 / jnp.pi) ** 0.5
    square = hidden * hidden
    half_up = 0.5 + 0.5 * jnp.tanh(hidden * (root + (root * 0.044715) * square))
    product = hidden * half_up
    return product, half_up + product * (1.0 - half_up) * (2 * root + (6 * root * 0.044715) * square)


def mlp_forward_kernel(chunk, half, meta, near, far, made, st, kept, sems):
    count = st.part.shape[0] // 2
    here = slice(half * count, (half + 1) * count)
    normed = mlp_middle(0, here, near[0], st)
    part = None
    for at in range(0, st.up[0].shape[1], chunk):
        cols = slice(at, at + chunk)
        hidden = mm(normed, st.up[0][:, cols]) + vector(st, 0, UP_BIAS, at, at + chunk)
        active, slope = gelu_slope(hidden)
        active = active.astype(BF16)
        kept[0, :, cols] = active
        kept[1, :, cols] = slope.astype(BF16)
        term = mm(active, st.down[0][cols, :])
        part = term if part is None else part + term
    copies = [pltpu.make_async_copy(kept.at[at], made[1 + at], sems.at[at]) for at in range(2)]
    for copy in copies:
        copy.start()
    part = part.astype(BF16)
    st.part[here] = part
    made[0][...] = part
    for copy in copies:
        copy.wait()


def add_sums(st, row, first, terms, fresh):
    places = slice(first, first + terms.shape[1])
    total = col_sum(terms)
    st.sums[row : row + 1, places] = total if fresh else total + st.sums[row : row + 1, places]


def mlp_both_kernel(chunk, half, meta, near, far, made, st, kept, sem):
    count, width = st.part.shape[0] // 2, st.part.shape[1]
    here = slice(half * count, (half + 1) * count)
    fresh = half == 0
    normed = mlp_middle(1, here, near[0], st)
    cot = jnp.where(meta[1] == half, near[1][...], near[2][...]).astype(F32).T
    st.cot[here] = cot.astype(BF16)
    low = center(cot).astype(BF16)
    st.low[here] = low
    add_sums(st, MLP1, 0, low, fresh)
    part, grad = None, None
    for at in range(0, st.up[1].shape[1], chunk):
        cols = slice(at, at + chunk)
        up, down = st.up[1][:, cols], st.down[1][cols, :]
        active, slope = gelu_slope(mm(normed, up) + vector(st, 1, UP_BIAS, at, at + chunk))
        active = active.astype(BF16)
        st.act[here, cols] = active
        hid = (mm_t(low, down) * slope).astype(BF16)
        st.hid[here, cols] = hid
        add_sums(st, MLP1, width + at, hid, fresh)
        terms = mm(active, down), mm_t(hid, up)
        part, grad = terms if part is None else (part + terms[0], grad + terms[1])
    grad = grad.astype(BF16)
    st.part[here] = grad
    made[0][...] = grad
    kept[...] = part.astype(BF16)
    pltpu.sync_copy(kept, made[1])


def mlp_backward_kernel(chunk, half, meta, near, far, made, st, slope, sem):
    load = pltpu.make_async_copy(far[0], slope, sem)
    load.start()
    count, width = st.part.shape[0] // 2, st.part.shape[1]
    here = slice(half * count, (half + 1) * count)
    fresh = half == 1
    hidden = st.up[0].shape[1]
    rows = expand(st.rows[1][here].astype(F32))
    grad = st.part[here].astype(F32) + near[0][...].astype(F32)
    pulled, gain_terms = norm_pull(rows, inv_rms(rows), vector(st, 1, ATTN_GAIN, 0, width), grad)
    grad_in = st.grad[here] + pulled
    grad_in = center((grad_in - grad_in[:, width - 1 :]).astype(BF16).astype(F32))
    st.grad[here] = grad_in
    low = grad_in.astype(BF16)
    st.low[here] = low
    add_sums(st, MLP0, 0, low, fresh)
    add_sums(st, MLP0, width + hidden, gain_terms, fresh)
    grad = None
    load.wait()
    for at in range(0, hidden, chunk):
        cols = slice(at, at + chunk)
        hid = (mm_t(low, st.down[0][cols, :]) * slope[:, cols].astype(F32)).astype(BF16)
        st.hid[here, cols] = hid
        add_sums(st, MLP0, width + at, hid, fresh)
        term = mm_t(hid, st.up[0][:, cols])
        grad = term if grad is None else grad + term
    grad = grad.astype(BF16)
    st.part[here] = grad
    made[0][...] = grad


def attn_backward_kernel(layer, half, meta, near, far, made, st, *refs):
    weights = st.attn[layer]
    width, local = weights.shape[1:]
    count = st.part.shape[0] // 2
    here = slice(half * count, (half + 1) * count)
    fresh = half == 1
    name = ATTN1 if layer else ATTN0
    middle = st.mid[layer][here]
    grad = st.part[here].astype(F32) + near[0][...].astype(F32)
    pulled, gain_terms = norm_pull(middle, inv_rms(middle), vector(st, layer, MLP_GAIN, 0, width), grad)
    upstream = center(st.cot[here].astype(F32)) if layer else st.grad[here]
    grad_mid = upstream + pulled
    st.grad[here] = grad_mid
    low = grad_mid.astype(BF16)
    st.low[here] = low
    add_sums(st, name, 0, gain_terms, fresh)
    add_sums(st, name, width, low, fresh)
    grad_att = (mm_t(low[:, :local], weights[3, :local]) + mm_t(low[:, local:], weights[3, local:])).astype(BF16)
    at = 2 * width
    query, kv, dqkv = st.query[layer], st.kv[layer], st.hid
    early = made[-1] if half else near[1]
    keys = (half + 1) * count
    for pair in range(local // LANES):
        cols = slice(pair * LANES, (pair + 1) * LANES)
        vcols = slice(local + pair * LANES, local + (pair + 1) * LANES)
        v2cols = slice(2 * local + pair * LANES, 2 * local + (pair + 1) * LANES)
        grads = halves(grad_att[:, cols])
        queries = halves(query[here, cols])
        low_probs = st.probs[layer][half][pair]
        probs = low_probs.astype(F32)
        grad_probs = mm_t(grads, kv[:keys, vcols])
        inner = jnp.sum(grad_probs * probs, axis=-1, keepdims=True)
        grad_scores = (probs * (grad_probs - inner)).astype(BF16)
        grad_query = (merge(mm(grad_scores, kv[:keys, cols])) * HEAD_DIM**-0.5).astype(BF16)
        grad_key = t_mm(grad_scores, queries)
        grad_value = t_mm(low_probs, grads)
        if half:
            early[:, cols] = grad_key[:count]
            early[:, vcols] = grad_value[:count]
            grad_key, grad_value = grad_key[count:], grad_value[count:]
        else:
            grad_key, grad_value = grad_key + early[:, cols], grad_value + early[:, vcols]
        grad_value = grad_value.astype(BF16)
        dqkv[here, cols] = grad_query
        dqkv[here, vcols] = grad_key.astype(BF16)
        dqkv[here, v2cols] = grad_value
        add_sums(st, name, at + pair * LANES, grad_query, fresh)
        add_sums(st, name, at + local + pair * LANES, grad_value, fresh)
    gpart = mm_t(dqkv[here, :local], weights[0])
    gpart = gpart + mm_t(dqkv[here, local : 2 * local], weights[1])
    gpart = gpart + mm_t(dqkv[here, 2 * local : 3 * local], weights[2])
    if layer == 0:
        rows = expand(st.rows[0][here].astype(F32))
        add_sums(st, name, at + 2 * local, gpart * rows * inv_rms(rows), fresh)
    st.part[here] = gpart.astype(BF16)
    if layer:
        made[0][...] = gpart.astype(BF16)
    elif half == 0:
        away = pl.ds(pl.multiple_of((1 - meta[1]) * count, 16), count)
        made[0][...] = st.part[away]
        row = name
        made[1][...] = st.sums[row : row + 1, at + 2 * local : at + 2 * local + width]
        own = pl.ds(pl.multiple_of(meta[1] * count, 16), count)
        sems = refs[0]
        copies = []
        for n, ref in enumerate((st.part, st.rows[0], st.grad, st.mid[1])):
            copies.append(pltpu.make_async_copy(ref.at[own], made[3 + n], sems.at[n]))
            copies[-1].start()
        for side in range(2):

            @pl.when(meta[1] == side)
            def _():
                pltpu.make_async_copy(far[1 - side], made[2], sems.at[4]).start()
                pltpu.make_async_copy(far[side], made[7], sems.at[5]).start()

        copies.append(pltpu.make_async_copy(far[0], made[2], sems.at[4]))
        copies.append(pltpu.make_async_copy(far[0], made[7], sems.at[5]))
        for copy in copies:
            copy.wait()


def mlp_weights_kernel(layer, meta, near, far, made, st, *refs):
    width, hidden = st.up[0].shape
    if far:
        active, load_sems = refs
        count = far[0].shape[0]
        loads = [
            pltpu.make_async_copy(ref, active.at[pl.ds(at * count, count)], load_sems.at[at]) for at, ref in enumerate(far)
        ]
        for load in loads:
            load.start()
    else:
        active, loads = st.act, []
    block = made[0].shape[1]
    for out, part in ((made[1], 1 - meta[0]), (made[0], meta[0])):
        rows = width // 2
        left = st.low_normed[layer][:, pl.ds(pl.multiple_of(part * rows, LANES), rows)]
        for n in range(hidden // block):
            out[n * rows : (n + 1) * rows] = t_mm(left, st.hid[:, n * block : (n + 1) * block]).astype(BF16)
        base = hidden // block * rows
        rows = hidden // 2
        while loads:
            loads.pop().wait()
        left = active[:, pl.ds(pl.multiple_of(part * rows, LANES), rows)]
        for n in range(width // block):
            total = t_mm(left, st.low[:, n * block : (n + 1) * block])
            out[base + n * rows : base + (n + 1) * rows] = total.astype(BF16)


def attn_weights_kernel(layer, extra, meta, near, far, made, st):
    width, local = st.attn[0].shape[1:]
    hidden = st.up[0].shape[1]
    piece = made[0].shape[0] // 8 - extra

    def put(out, first, total):
        for at in range(0, total.shape[0], piece):
            where = (first + at) // piece * (piece + extra)
            out[where : where + piece] = total[at : at + piece].astype(BF16)

    if extra:
        sums = st.sums
        rows = [sums[row : row + 1] for row in range(4)]
        smalls = []
        tail = 2 * width + 2 * local
        for gain, attn, mlp in (
            (rows[ATTN0][:, tail : tail + width] + near[0][...], rows[ATTN0], rows[MLP0]),
            (rows[MLP0][:, width + hidden : 2 * width + hidden], rows[ATTN1], rows[MLP1]),
        ):
            row = [gain, attn[:, 2 * width : tail], attn[:, width : 2 * width], attn[:, :width]]
            row += [mlp[:, width : width + hidden], mlp[:, :width]]
            lines = [part[:, at : at + local] for part in row for at in range(0, part.shape[1], local)]
            lines += [jnp.zeros((1, local), F32)] * (extra - len(lines))
            smalls.append(jnp.concatenate(lines, axis=0))

    for out, part in ((made[1], 1 - meta[0]), (made[0], meta[0])):
        rows = width // 2
        cols = pl.ds(pl.multiple_of(part * rows, LANES), rows)
        left = st.normed[layer][:, cols]
        for at in range(3):
            put(out, at * rows, t_mm(left, st.hid[:, at * local : (at + 1) * local]))
        put(out, 3 * rows, t_mm(st.att[layer][...], st.low[:, cols]))
        if extra:
            out[piece : piece + extra] = jnp.where(part == 0, smalls[0], smalls[1]).astype(BF16)
            for at in range(1, 8):
                where = at * (piece + extra) + piece
                out[where : where + extra] = jnp.zeros((extra, local), BF16)


def close_kernel(meta, vec_own, vec_other, grad_far, out_far, out_own, part, rows, grad, middle, result, grad_in, *refs):
    width = part.shape[1]

    *vecs, sems = refs
    for layer in range(2):
        pick(meta, layer, vec_own.at[pl.ds(0, 8)], vec_other.at[pl.ds(0, 8)], vecs[layer], sems.at[layer])
    for layer in range(2):
        done(vec_own.at[pl.ds(0, 8)], vecs[layer], sems.at[layer])

    def vec(layer, row):
        return vecs[layer][row : row + 1, :width]

    branch = out_own[...].astype(F32) + out_far[...].astype(F32) + vec(1, DOWN_BIAS)
    result[...] = (middle[...] + center(branch)).astype(BF16)
    rows = expand(rows[...].astype(F32))
    given = part[...].astype(F32) + grad_far[...].astype(F32)
    pulled, _ = norm_pull(rows, inv_rms(rows), vec(0, ATTN_GAIN), given)
    total = grad[...] + pulled
    grad_in[...] = (total - total[:, width - 1 :]).astype(BF16)


def place_kernel(kinds, extra, meta, *refs):
    refs = list(refs)
    sources = take(refs, 4)
    outs = refs[:-2]
    wide, sems = refs[-2:]
    piece = wide.shape[1]

    def copy(n):
        part = meta[0] if n < 8 else 1 - meta[0]
        which, where = kinds[n % 8]
        return pltpu.make_async_copy(wide.at[n], outs[which].at[where(part)], sems.at[n])

    for layer in range(2):

        @pl.when(meta[0] == layer)
        def _():
            step = piece + (0 if layer else extra)
            for n in range(16):
                place = meta[6 + n // 8] & 6 if extra and layer == 0 else meta[6 + n // 8]
                at = pl.multiple_of(((n % 8) ^ place) * step, 16)
                wide[n] = sources[2 * (n // 8) + layer][pl.ds(at, piece)].astype(F32)
                copy(n).start()

    if extra:
        at = pl.multiple_of((meta[6] & 6) * (piece + extra) + piece, 16)
        small = sources[0][pl.ds(at, extra)].astype(F32)
        at = 0
        for out in outs[2:]:
            for row in range(out.shape[0]):
                for col in range(0, out.shape[1], small.shape[1]):
                    out[row : row + 1, col : col + small.shape[1]] = small[at : at + 1]
                    at += 1
    for n in range(16):
        copy(n).wait()


def shape(dims, dtype=BF16):
    return jax.ShapeDtypeStruct(dims, dtype)


def call(kernel, in_specs, outs, scratch, args, out_specs, limit=VMEM_BYTES):
    return pl.pallas_call(
        kernel,
        out_shape=tuple(outs),
        in_specs=in_specs,
        out_specs=tuple(out_specs),
        scratch_shapes=scratch,
        compiler_params=pltpu.CompilerParams(vmem_limit_bytes=limit),
        cost_estimate=pl.CostEstimate(flops=1, bytes_accessed=1, transcendentals=0),
    )(*args)


def swap(array, axis):
    return lax.ppermute(array, axis, [(0, 1), (1, 0)])


def halve_kernel(step, sides, mine, other, *outs):
    rows = mine.shape[0] // len(outs)
    for at, out in enumerate(outs):
        here = slice(None)
        if len(outs) == 2:
            side = sides[step] if at == 0 else 1 - sides[step]
            here = pl.ds(pl.multiple_of(side * rows, 16), rows)
        out[...] = (mine[here].astype(F32) + other[here].astype(F32)).astype(BF16)


def join_kernel(first, second, out):
    rows = first.shape[0]
    out[:rows] = first[...]
    out[rows:] = second[...]


def in_vmem(*arrays):
    return [pltpu.with_memory_space_constraint(a, pltpu.VMEM) for a in arrays]


def add_halves(step, sides, mine, other):
    rows, width = mine.shape
    halves = 1 if step is None else 2
    outs = [pltpu.VMEM((rows // halves, width), BF16)] * halves
    kernel = functools.partial(halve_kernel, step)
    return call(kernel, [SMEM, VMEM, VMEM], outs, [], [sides, *in_vmem(mine, other)], [VMEM] * halves)


def join(first, second):
    rows, width = first.shape
    outs = [pltpu.VMEM((2 * rows, width), BF16)]
    return call(join_kernel, [VMEM, VMEM], outs, [], in_vmem(first, second), [VMEM])[0]


SWAP, HALVE, ADD, JOIN = range(4)


class GroupSum:
    def __init__(self, sides, whole, mine, theirs):
        self.sides = sides
        self.held, self.received = mine, theirs
        self.steps = list(zip(*self.orders(lax.axis_size(GROUPS).bit_length() - 1)))
        self.whole = whole
        count = len(self.steps)
        self.todo = [(SWAP, None)] + [(HALVE, k) for k in range(count - 1)]
        if whole:
            self.todo += [(ADD, count - 1), (ADD, count - 2)] + [(JOIN, k) for k in range(count - 3, -1, -1)]
        else:
            self.todo += [(HALVE, count - 1), (ADD, count - 1)] + [(JOIN, k) for k in range(count - 2, -1, -1)]

    def make(self):
        kind, at = self.todo[0]
        if kind == SWAP:
            return [self.held, self.received]
        if kind == JOIN:
            return [join(self.held, self.received)]
        return list(add_halves(at if kind == HALVE else None, self.sides, self.held, self.received))

    def send(self, arrays):
        kind, at = self.todo.pop(0)
        self.held = arrays[0]
        self.received = swap(arrays[-1], SECTION) if kind == SWAP else self.exchange(arrays[-1], self.steps[at])

    @staticmethod
    def orders(bits):
        first = list(range(bits))
        second = [1, 0] + first[2:] if bits > 1 else first
        return first, second

    @staticmethod
    def exchange(array, bits):
        count = lax.axis_size(GROUPS)
        pairs = [(core * count + i, core * count + (i ^ (1 << bit))) for core, bit in enumerate(bits) for i in range(count)]
        return lax.ppermute(array, (SECTION, GROUPS), pairs)

    @staticmethod
    def which_side(bits):
        core, index = lax.axis_index(SECTION), lax.axis_index(GROUPS)
        return jnp.stack([(index >> jnp.where(core == 0, *pair)) & 1 for pair in zip(*GroupSum.orders(bits))])

    @staticmethod
    def place(bits, core):
        index = lax.axis_index(GROUPS)
        out = jnp.int32(0)
        for first, second in zip(*GroupSum.orders(bits)):
            out = out * 2 + ((index >> jnp.where(core == 0, first, second)) & 1)
        return out


def boundary(values, flows, after=()):
    flows = [flow for flow in flows if flow.todo]
    arrived = [flow for flow in flows if flow.todo[0][0] != SWAP]
    values = list(values)
    got = lax.optimization_barrier((*values, *[flow.received for flow in arrived], *after))
    values = list(got[: len(values)])
    for flow, received in zip(arrived, got[len(values) :]):
        flow.received = received
    arrays = [flow.make() for flow in flows]
    got = list(lax.optimization_barrier((*values, *[a for group in arrays for a in group])))
    values = take(got, len(values))
    for flow, group in zip(flows, arrays):
        flow.send(take(got, len(group)))
    return values


def in_order(array, place, count):
    blocks = array.reshape((count, array.shape[0] // count) + array.shape[1:])
    return jnp.take(blocks, jnp.arange(count, dtype=jnp.int32) ^ place, axis=0).reshape(array.shape)


def local(
    inputs,
    doc_lengths,
    attn_gain,
    qkv_weight,
    qv_bias,
    out_weight,
    out_bias,
    mlp_gain,
    up_weight,
    up_bias,
    down_weight,
    down_bias,
    cotangent,
):
    core = lax.axis_index(SECTION)
    side = lax.axis_index(TENSOR)
    groups = lax.axis_size(GROUPS)
    bits = groups.bit_length() - 1
    place = GroupSum.place(bits, core)
    rows = inputs.shape[1]
    width = attn_gain.shape[1]
    heads = qkv_weight.shape[3]
    hidden = up_weight.shape[2]
    pairs = heads // LANES
    chunk = hidden // 2
    extra = 16

    def own_rows(array):
        mine = lax.dynamic_index_in_dim(jnp.transpose(array, (2, 0, 1)), core, 1, keepdims=False)
        return jnp.pad(mine, ((0, width - mine.shape[0]), (0, 0)))

    lengths = lax.dynamic_index_in_dim(doc_lengths[:, 0, :], core, 0, keepdims=False)
    if groups == 8:
        places = [place, GroupSum.place(bits, 1 - core)]
    else:
        places = [jnp.int32(0)] * 2
    meta = jnp.concatenate([jnp.stack([core, side]).astype(jnp.int32), lengths, jnp.stack(places)])
    def each(*dims, dtype=BF16):
        return (shape(dims, dtype),) * 2

    unit = 2 * rows
    layer_probs = (shape((pairs, unit, rows)), shape((pairs, unit, unit)))
    bench = Bench(
        meta,
        State(
            vec=each(8, hidden, dtype=F32),
            attn=each(4, width, heads),
            up=each(width, hidden),
            down=each(hidden, width),
            rows=each(unit, width),
            normed=each(unit, width),
            low_normed=each(unit, width),
            query=each(unit, heads),
            kv=each(unit, 2 * heads),
            att=each(unit, heads),
            probs=(layer_probs, layer_probs),
            mid=each(unit, width, dtype=F32),
            act=shape((unit, hidden)),
            hid=shape((unit, hidden)),
            part=shape((unit, width)),
            cot=shape((unit, width)),
            low=shape((unit, width)),
            grad=shape((unit, width), F32),
            sums=shape((8, 3 * width + 2 * heads), F32),
        ),
    )
    sides = GroupSum.which_side(bits)

    entry = own_rows(inputs)
    small_in = (attn_gain, qv_bias[0], out_bias, mlp_gain, up_bias, down_bias)
    qkv, out = jnp.transpose(qkv_weight[0], (1, 0, 2)), out_weight[0]
    (vectors,) = call(
        pack_kernel,
        [HBM] * len(small_in),
        [pltpu.HBM((512, hidden), F32)],
        [
            pltpu.VMEM((8, hidden), F32),
            *[pltpu.VMEM(a.shape, F32) for a in small_in],
            pltpu.SemaphoreType.DMA((len(small_in),)),
        ],
        [pltpu.with_memory_space_constraint(a, pltpu.HBM) for a in small_in],
        [HBM],
    )
    far = swap(entry, TENSOR)
    vec_pair = (vectors, swap(vectors, SECTION))
    attn_pair = (qkv, swap(qkv, SECTION), out, swap(out, SECTION))
    cots, _ = lax.optimization_barrier((cotangent, vectors))
    cots = own_rows(cots)
    *attn_pair, cots = lax.optimization_barrier((*attn_pair, cots))
    far, cots, down = lax.optimization_barrier((far, cots, down_weight[0]))
    entry = (entry, far)
    up = up_weight[0]
    up_pair = (up, swap(up, SECTION))
    down_pair = (down, swap(down, SECTION))
    cots = (cots, swap(cots, TENSOR))

    bench.run(open_kernel, hbm_ins=[*vec_pair, *attn_pair], scratch=[pltpu.SemaphoreType.DMA((5,))], first=True)
    sent = (True, (rows, width), BF16)
    partial = functools.partial

    given = [None, None]
    for half in range(2):
        (part,) = bench.run(partial(attn_forward_kernel, 0, half), entry, [sent])
        given[half] = swap(part, TENSOR)
    *down_pair, cot_far = lax.optimization_barrier((*down_pair, cots[1]))
    cots = (cots[0], cot_far)
    bench.run(load_kernel, hbm_ins=[*attn_pair, *up_pair, *down_pair], scratch=[pltpu.SemaphoreType.DMA((7,))])
    acts, slopes = [], []
    for half in range(2):
        outs = [sent] + [(False, (rows, hidden), BF16)] * 2
        scratch = [pltpu.VMEM((2, rows, hidden), BF16), pltpu.SemaphoreType.DMA((2,))]
        part, *kept = bench.run(partial(mlp_forward_kernel, chunk, half), [given[half]], outs, scratch=scratch)
        given[half] = swap(part, TENSOR)
        acts.append(kept[0])
        slopes.append(kept[1])
    for half in range(2):
        (part,) = bench.run(partial(attn_forward_kernel, 1, half), [given[half]], [sent])
        given[half] = swap(part, TENSOR)
    mlp_parts = []
    kept = (False, (rows, width), BF16)
    for half in range(2):
        scratch = [pltpu.VMEM((rows, width), BF16), pltpu.SemaphoreType.DMA]
        body = partial(mlp_both_kernel, chunk, half)
        part, mlp_part = bench.run(body, [given[half], *cots], [sent, kept], scratch=scratch)
        given[half] = swap(part, TENSOR)
        mlp_parts.append(mlp_part)

    def weights(kernel, dims):
        ins = [gain_far] if kernel is attn_weights_kernel and dims[0] % (8 * 192) else []
        layer = 0 if ins or kernel is mlp_weights_kernel and mlp1 is not None else 1
        body = partial(kernel, layer) if kernel is mlp_weights_kernel else partial(kernel, layer, extra if ins else 0)
        far = acts if kernel is mlp_weights_kernel and layer == 0 else []
        scratch = [pltpu.VMEM((2 * rows, hidden), BF16), pltpu.SemaphoreType.DMA((2,))] if far else []
        return GroupSum(sides, bool(ins), *bench.run(body, ins, [(True, dims, BF16)] * 2, far, scratch))

    mlp_dims = (hidden * width // 384, 384)
    attn_dims = (2 * width * heads // 384, 384)
    mlp1 = None
    bench.follow(given)
    mlp1 = weights(mlp_weights_kernel, mlp_dims)
    early = (True, (rows, 2 * heads), F32)
    for half in (1, 0):
        (given[half],) = boundary([given[half]], [mlp1], () if half else [part])
        ins, outs = ([given[1]], [sent, early]) if half else ([given[0], link], [sent])
        part, *rest = bench.run(partial(attn_backward_kernel, 1, half), ins, outs)
        link = rest[0] if half else None
        given[half] = swap(part, TENSOR)
    attn1 = weights(attn_weights_kernel, attn_dims)
    for half in (1, 0):
        if half:
            given[1], attn1.held, attn1.received = lax.optimization_barrier((given[1], attn1.held, attn1.received))
        else:
            (given[0],) = boundary([given[0]], [mlp1, attn1], [part])
        scratch = [pltpu.VMEM((rows, hidden), BF16), pltpu.SemaphoreType.DMA]
        body = partial(mlp_backward_kernel, chunk, half)
        (part,) = bench.run(body, [given[half]], [sent], [slopes[half]], scratch)
        given[half] = swap(part, TENSOR)
    mlp0 = weights(mlp_weights_kernel, mlp_dims)
    (given[1],) = boundary([given[1]], [mlp1, attn1, mlp0], [part])
    (link,) = bench.run(partial(attn_backward_kernel, 0, 1), [given[1]], [early])
    given[0], link = boundary([given[0], link], [mlp1, attn1, mlp0])
    own = [(False, (rows, width), dtype) for dtype in (BF16, BF16, F32, F32)]
    outs = [sent, (True, (1, width), F32), sent, *own, sent]
    body = partial(attn_backward_kernel, 0, 0)
    scratch = [pltpu.SemaphoreType.DMA((6,))]
    away_grad, gain, away_out, *own = bench.run(body, [given[0], link], outs, mlp_parts, scratch)
    (gain_far,) = boundary([swap(gain, TENSOR)], [attn1], [gain])
    gain_far, away_grad, away_out = lax.optimization_barrier((gain_far, away_grad, away_out))
    backs = [swap(away_grad, TENSOR), swap(away_out, TENSOR)]
    attn0 = weights(attn_weights_kernel, (attn_dims[0] + 8 * extra, 384))

    token = [meta]

    def end(flow):
        while flow.todo:
            token[:] = boundary(token, [flow])
        token[0], *pieces = lax.optimization_barrier((token[0], flow.held, flow.received))
        whole = join(*pieces)
        if groups != 8:
            split = groups // 2 if flow.whole else groups
            whole = in_order(whole, place // (groups // split), split)
        token[0], whole = lax.optimization_barrier((token[0], whole))
        return whole, swap(whole, SECTION)

    def close(back_grad, back_out):
        args = [*in_vmem(back_grad, back_out, own[-1]), *own[:-1]]
        specs = [SMEM, HBM, HBM] + [VMEM] * len(args)
        scratch = [pltpu.VMEM((8, hidden), F32)] * 2 + [pltpu.SemaphoreType.DMA((2,))]
        outs = [shape((rows, width))] * 2
        return call(close_kernel, specs, outs, scratch, [token[0], *vec_pair, *args], [VMEM] * 2, 2 * VMEM_BYTES)

    token[:] = boundary(token, [mlp0, attn0], [mlp1.received])
    token[:] = boundary(token, [attn0, mlp0, mlp1], [attn1.received])
    token[0], *backs = lax.optimization_barrier((token[0], *backs))
    token[:] = boundary(token, [attn0, mlp0, attn1, mlp1])
    result, grad_in = close(*backs)
    result, grad_in = result[:, : width - 1], grad_in[:, : width - 1]
    token[0], result, grad_in = lax.optimization_barrier((token[0], result, grad_in))
    token[:] = boundary(token, [attn0, mlp0, attn1])
    token[:] = boundary(token, [attn0, mlp0, attn1], [mlp1.received])
    mlp1 = end(mlp1)
    token[:] = boundary(token, [attn0])
    mlp0, attn1 = end(mlp0), end(attn1)
    while attn0.todo:
        token[:] = boundary(token, [attn0])

    up_rows, down_rows = width // 2, hidden // 2

    def mlp_kind(block):
        if block < 4:
            return 0, lambda part: (pl.ds(pl.multiple_of(part * up_rows, 8), up_rows), pl.ds(block * 384, 384))
        col, row = (block - 4) // 2, (block - 4) % 2
        return 1, lambda part: (
            pl.ds(pl.multiple_of(part * down_rows + row * 384, 8), 384),
            pl.ds(col * 384, 384),
        )

    def attn_kind(block):
        which, row = block // 2, block % 2
        if which < 3:
            return 0, lambda part: (which, pl.ds(pl.multiple_of(part * up_rows + row * 192, 8), 192), slice(None))
        return 1, lambda part: (pl.ds(row * 192, 192), pl.ds(pl.multiple_of(part * 384, 128), 384))

    def placed(kinds, extra_rows, first, second, outs):
        piece = first[0].shape[0] // 8 - extra_rows
        args = [token[0], first[0], second[0], first[1], second[1]]
        scratch = [pltpu.VMEM((16, piece, 384), F32), pltpu.SemaphoreType.DMA((16,))]
        out_specs = [HBM, HBM] + [VMEM] * (len(outs) - 2)
        kernel = functools.partial(place_kernel, kinds, extra_rows)
        args[1:] = in_vmem(*args[1:])
        return call(kernel, [SMEM] + [VMEM] * 4, outs, scratch, args, out_specs, 2 * VMEM_BYTES)

    grad_up, grad_down = placed(
        [mlp_kind(b) for b in range(8)],
        0,
        mlp0,
        mlp1,
        [shape((width, hidden), F32), shape((hidden, width), F32)],
    )
    token[0], grad_up, grad_down = lax.optimization_barrier((token[0], grad_up, grad_down))
    attn0 = end(attn0)
    grad_qkv, grad_out, *small = placed(
        [attn_kind(b) for b in range(8)],
        extra,
        attn0,
        attn1,
        [shape((3, width, heads), F32), shape((heads, width), F32)]
        + [shape(dims, F32) for dims in ((1, width), (2, heads), (1, width), (1, width), (1, hidden), (1, width))],
    )

    return (
        result[None],
        grad_in[None],
        small[0],
        jnp.transpose(grad_qkv, (1, 0, 2))[None],
        small[1][None],
        grad_out[None],
        small[2],
        small[3],
        grad_up[None],
        small[4],
        grad_down[None],
        small[5],
    )


def solution(mesh):
    in_specs = (
        P(None, (GROUPS, TENSOR), None),
        P(None, GROUPS, None),
        P(SECTION, None),
        P(SECTION, None, None, TENSOR),
        P(SECTION, None, TENSOR),
        P(SECTION, TENSOR, None),
        P(SECTION, None),
        P(SECTION, None),
        P(SECTION, None, TENSOR),
        P(SECTION, TENSOR),
        P(SECTION, TENSOR, None),
        P(SECTION, None),
        P(None, (GROUPS, TENSOR), None),
    )
    out_specs = (
        P(SECTION, (GROUPS, TENSOR), None),
        P(SECTION, (GROUPS, TENSOR), None),
        P(SECTION, None),
        P(SECTION, None, None, TENSOR),
        P(SECTION, None, TENSOR),
        P(SECTION, TENSOR, None),
        P(SECTION, None),
        P(SECTION, None),
        P(SECTION, None, TENSOR),
        P(SECTION, TENSOR),
        P(SECTION, TENSOR, None),
        P(SECTION, None),
    )
    return jax.shard_map(local, mesh=mesh, in_specs=in_specs, out_specs=out_specs, check_vma=False)
```

```python
import functools
from typing import Any, NamedTuple

import jax
import jax.numpy as jnp
from jax import lax
from jax.experimental import pallas as pl
from jax.experimental.pallas import tpu as pltpu
from jax.sharding import PartitionSpec as P

HEAD_DIM = 64
LANES = 128
EPS = 1e-05
NEG = -1e30
VMEM_BYTES = 12 * 1024 * 1024

SECTION, GROUPS, TENSOR = "section", "dp", "tensor"

F32 = jnp.float32
BF16 = jnp.bfloat16

VMEM = pl.BlockSpec(memory_space=pltpu.VMEM)
SMEM = pl.BlockSpec(memory_space=pltpu.SMEM)
HBM = pl.BlockSpec(memory_space=pltpu.HBM)


def mm(left, right):
    return jnp.dot(left, right, preferred_element_type=F32)


def mm_t(left, right):
    return lax.dot_general(left, right, (((1,), (1,)), ((), ())), preferred_element_type=F32)


def t_mm(left, right):
    return lax.dot_general(left, right, (((0,), (0,)), ((), ())), preferred_element_type=F32)


def row_mean(array):
    return jnp.mean(array, axis=-1, keepdims=True)


def center(array):
    return array - row_mean(array)


def last_lane(shape):
    return lax.broadcasted_iota(jnp.int32, shape, 1) == shape[1] - 1


def expand(rows):
    return jnp.where(last_lane(rows.shape), -jnp.sum(rows, axis=-1, keepdims=True), rows)


def inv_rms(rows):
    return lax.rsqrt(row_mean(rows * rows) + EPS)


def norm_pull(rows, scaling, gain, grad):
    gained = gain * grad
    inner = row_mean(gained * rows)
    grad_rows = scaling * gained - rows * (scaling * scaling * scaling * inner)
    return center(grad_rows), grad * rows * scaling


def col_sum(array):
    return jnp.sum(array.astype(F32), axis=0, keepdims=True)


def pick(meta, layer, own, other, dst, sem):
    @pl.when(meta[0] == layer)
    def _():
        pltpu.make_async_copy(own, dst, sem).start()

    @pl.when(meta[0] != layer)
    def _():
        pltpu.make_async_copy(other, dst, sem).start()


def done(src, dst, sem):
    pltpu.make_async_copy(src, dst, sem).wait()


def halves(pair):
    first = lax.broadcasted_iota(jnp.int32, pair.shape, 1) < HEAD_DIM
    zero = jnp.zeros_like(pair)
    return jnp.concatenate([jnp.where(first, pair, zero), jnp.where(first, zero, pair)], axis=0)


def merge(stacked):
    rows = stacked.shape[0] // 2
    first = lax.broadcasted_iota(jnp.int32, (rows, stacked.shape[1]), 1) < HEAD_DIM
    return jnp.where(first, stacked[:rows], stacked[rows:])


def owner(meta, places):
    total = jnp.zeros(places.shape, jnp.int32)
    bound = 0
    for doc in range(3):
        bound = bound + meta[2 + doc]
        total = total + (places >= bound).astype(jnp.int32)
    return total


def mask_bias(meta, half, rows, keys):
    row_at = lax.broadcasted_iota(jnp.int32, (rows, 1), 0) + half * rows
    key_at = lax.broadcasted_iota(jnp.int32, (1, keys), 1)
    allowed = (owner(meta, row_at) == owner(meta, key_at)) & (key_at <= row_at)
    return jnp.where(allowed, 0.0, NEG).astype(F32)


def take(refs, count):
    out = refs[:count]
    del refs[:count]
    return out


class State(NamedTuple):
    vec: Any
    attn: Any
    up: Any
    down: Any
    rows: Any
    normed: Any
    low_normed: Any
    query: Any
    kv: Any
    att: Any
    probs: Any
    mid: Any
    act: Any
    hid: Any
    part: Any
    cot: Any
    low: Any
    grad: Any
    sums: Any


class Bench:
    def __init__(self, meta, shapes):
        self.meta = meta
        shapes, self.tree = jax.tree.flatten(shapes)
        self.arrays = shapes
        self.shapes = [pltpu.VMEM(a.shape, a.dtype) for a in shapes]

    def follow(self, arrays):
        self.meta, arrays[0] = lax.optimization_barrier((self.meta, arrays[0]))

    def run(self, body, ins=(), outs=(), hbm_ins=(), scratch=(), first=False):
        ins = [pltpu.with_memory_space_constraint(a, pltpu.VMEM) for a in ins]
        hbm_ins = [pltpu.with_memory_space_constraint(a, pltpu.HBM) for a in hbm_ins]
        held = [] if first else [pltpu.with_memory_space_constraint(a, pltpu.VMEM) for a in self.arrays]
        shapes = [(pltpu.VMEM if near else pltpu.HBM)(dims, dtype) for near, dims, dtype in outs]
        n_ins, n_hbm, n_outs, n_held = len(ins), len(hbm_ins), len(outs), len(self.shapes)

        def kernel(meta, *refs):
            refs = list(refs)
            near, far, _, made = take(refs, n_ins), take(refs, n_hbm), take(refs, len(held)), take(refs, n_outs)
            state = jax.tree.unflatten(self.tree, take(refs, n_held))
            body(meta, near, far, made, state, *refs)

        before = 1 + n_ins + n_hbm
        got = pl.pallas_call(
            kernel,
            out_shape=tuple(shapes + self.shapes),
            in_specs=[SMEM] + [VMEM] * n_ins + [HBM] * n_hbm + [VMEM] * len(held),
            out_specs=tuple([VMEM if near else HBM for near, _, _ in outs] + [VMEM] * n_held),
            input_output_aliases={before + i: n_outs + i for i in range(len(held))},
            scratch_shapes=list(scratch),
            compiler_params=pltpu.CompilerParams(vmem_limit_bytes=VMEM_BYTES),
            cost_estimate=pl.CostEstimate(flops=1, bytes_accessed=1, transcendentals=0),
        )(self.meta, *ins, *hbm_ins, *held)
        self.arrays = list(got[n_outs:])
        return list(got[:n_outs])


ATTN_GAIN, QV_BIAS, OUT_BIAS, MLP_GAIN, UP_BIAS, DOWN_BIAS = range(6)
MLP1, ATTN1, MLP0, ATTN0 = range(4)


def pack_kernel(*refs):
    count = (len(refs) - 3) // 2
    refs = list(refs)
    sources, (target, out), held, (sems,) = take(refs, count), take(refs, 2), take(refs, count), refs
    copies = [pltpu.make_async_copy(src, dst, sems.at[at]) for at, (src, dst) in enumerate(zip(sources, held))]
    for copy in copies:
        copy.start()
    out[...] = jnp.zeros(out.shape, F32)
    for row, (copy, ref) in enumerate(zip(copies, held)):
        copy.wait()
        if ref.shape[0] == 2:
            half = ref.shape[1]
            out[row : row + 1, :half] = ref[0:1]
            out[row : row + 1, half : 2 * half] = ref[1:2]
        else:
            out[row : row + 1, : ref.shape[1]] = ref[...]
    pltpu.sync_copy(out, target.at[pl.ds(0, out.shape[0])])


def load_attn(meta, layer, far, st, sems):
    qkv_own, qkv_other, out_own, out_other = far
    weights = st.attn[layer]
    local = weights.shape[2]
    work = [(qkv_own, qkv_other, weights.at[pl.ds(0, 3)])]
    for at in range(2):
        cols = pl.ds(at * local, local)
        work.append((out_own.at[:, cols], out_other.at[:, cols], weights.at[3, cols]))
    for at, (own, other, dst) in enumerate(work):
        pick(meta, layer, own, other, dst, sems.at[at])
    return lambda: [done(own, dst, sems.at[at]) for at, (own, _, dst) in enumerate(work)]


def open_kernel(meta, near, far, made, st, sems):
    vec_own, vec_other, *far = far
    for layer in range(2):
        rows = pl.ds(0, 8)
        pick(meta, layer, vec_own.at[rows], vec_other.at[rows], st.vec[layer], sems.at[layer])
    arrived = load_attn(meta, 0, far, st, sems.at[pl.ds(2, 3)])
    for layer in range(2):
        done(vec_own.at[pl.ds(0, 8)], st.vec[layer], sems.at[layer])
    arrived()


def load_kernel(meta, near, far, made, st, sems):
    *attn, up_own, up_other, down_own, down_other = far
    work = []
    for layer in range(2):
        work.append((layer, up_own, up_other, st.up[layer]))
        work.append((layer, down_own, down_other, st.down[layer]))
    for at, (layer, own, other, dst) in enumerate(work):
        pick(meta, layer, own, other, dst, sems.at[at])
    arrived = load_attn(meta, 1, attn, st, sems.at[pl.ds(4, 3)])
    for at, (layer, own, other, dst) in enumerate(work):
        done(own, dst, sems.at[at])
    arrived()


def vector(st, layer, row, first, last):
    return st.vec[layer][row : row + 1, first:last]


def attn_forward_kernel(layer, half, meta, near, far, made, st):
    weights = st.attn[layer]
    width, local = weights.shape[1:]
    count = st.part.shape[0] // 2
    here = slice(half * count, (half + 1) * count)
    if layer == 0:
        mine, other = near
        rows = jnp.where(meta[1] == half, mine[...], other[...]).astype(F32).T
    else:
        branch = st.part[here].astype(F32) + near[0][...].astype(F32) + vector(st, 0, DOWN_BIAS, 0, width)
        rows = (st.mid[0][here] + center(branch)).astype(BF16).astype(F32)
        rows = jnp.where(last_lane(rows.shape), 0.0, rows)
    st.rows[layer][here] = rows.astype(BF16)
    rows = expand(rows)
    normed = (rows * inv_rms(rows) * vector(st, layer, ATTN_GAIN, 0, width)).astype(BF16)
    st.normed[layer][here] = normed
    query = ((mm(normed, weights[0]) + vector(st, layer, QV_BIAS, 0, local)) * HEAD_DIM**-0.5).astype(BF16)
    st.query[layer][here] = query
    kv = st.kv[layer]
    kv[here, :local] = mm(normed, weights[1]).astype(BF16)
    kv[here, local:] = (mm(normed, weights[2]) + vector(st, layer, QV_BIAS, local, 2 * local)).astype(BF16)
    keys = (half + 1) * count
    masked = mask_bias(meta, half, count, keys)
    for pair in range(local // LANES):
        cols = slice(pair * LANES, (pair + 1) * LANES)
        vcols = slice(local + pair * LANES, local + (pair + 1) * LANES)
        scores = mm_t(halves(query[:, cols]), kv[:keys, cols])
        scores = (scores.reshape(2, count, keys) + masked[None]).reshape(2 * count, keys)
        expo = jnp.exp(scores - jnp.max(scores, axis=-1, keepdims=True))
        probs = (expo * (1.0 / jnp.sum(expo, axis=-1, keepdims=True))).astype(BF16)
        st.probs[layer][half][pair] = probs
        st.att[layer][here, cols] = merge(mm(probs, kv[:keys, vcols])).astype(BF16)
    attended = st.att[layer][here]
    for at in range(2):
        cols = slice(at * local, (at + 1) * local)
        part = mm(attended, weights[3, cols]).astype(BF16)
        st.part[here, cols] = part
        made[0][:, cols] = part


def mlp_middle(layer, here, received, st):
    width = st.part.shape[1]
    branch = st.part[here].astype(F32) + received[...].astype(F32) + vector(st, layer, OUT_BIAS, 0, width)
    middle = expand(st.rows[layer][here].astype(F32)) + center(branch)
    st.mid[layer][here] = middle
    normed = (middle * inv_rms(middle) * vector(st, layer, MLP_GAIN, 0, width)).astype(BF16)
    st.low_normed[layer][here] = normed
    return normed


def gelu_slope(hidden):
    root = (2.0 / jnp.pi) ** 0.5
    square = hidden * hidden
    half_up = 0.5 + 0.5 * jnp.tanh(hidden * (root + (root * 0.044715) * square))
    product = hidden * half_up
    return product, half_up + product * (1.0 - half_up) * (2 * root + (6 * root * 0.044715) * square)


def mlp_forward_kernel(chunk, half, meta, near, far, made, st, kept, sems):
    count = st.part.shape[0] // 2
    here = slice(half * count, (half + 1) * count)
    normed = mlp_middle(0, here, near[0], st)
    part = None
    for at in range(0, st.up[0].shape[1], chunk):
        cols = slice(at, at + chunk)
        hidden = mm(normed, st.up[0][:, cols]) + vector(st, 0, UP_BIAS, at, at + chunk)
        active, slope = gelu_slope(hidden)
        active = active.astype(BF16)
        kept[0, :, cols] = active
        kept[1, :, cols] = slope.astype(BF16)
        term = mm(active, st.down[0][cols, :])
        part = term if part is None else part + term
    copies = [pltpu.make_async_copy(kept.at[at], made[1 + at], sems.at[at]) for at in range(2)]
    for copy in copies:
        copy.start()
    part = part.astype(BF16)
    st.part[here] = part
    made[0][...] = part
    for copy in copies:
        copy.wait()


def add_sums(st, row, first, terms, fresh):
    places = slice(first, first + terms.shape[1])
    total = col_sum(terms)
    st.sums[row : row + 1, places] = total if fresh else total + st.sums[row : row + 1, places]


def mlp_both_kernel(chunk, half, meta, near, far, made, st, kept, sem):
    count, width = st.part.shape[0] // 2, st.part.shape[1]
    here = slice(half * count, (half + 1) * count)
    fresh = half == 0
    normed = mlp_middle(1, here, near[0], st)
    cot = jnp.where(meta[1] == half, near[1][...], near[2][...]).astype(F32).T
    st.cot[here] = cot.astype(BF16)
    low = center(cot).astype(BF16)
    st.low[here] = low
    add_sums(st, MLP1, 0, low, fresh)
    part, grad = None, None
    for at in range(0, st.up[1].shape[1], chunk):
        cols = slice(at, at + chunk)
        up, down = st.up[1][:, cols], st.down[1][cols, :]
        active, slope = gelu_slope(mm(normed, up) + vector(st, 1, UP_BIAS, at, at + chunk))
        active = active.astype(BF16)
        st.act[here, cols] = active
        hid = (mm_t(low, down) * slope).astype(BF16)
        st.hid[here, cols] = hid
        add_sums(st, MLP1, width + at, hid, fresh)
        terms = mm(active, down), mm_t(hid, up)
        part, grad = terms if part is None else (part + terms[0], grad + terms[1])
    grad = grad.astype(BF16)
    st.part[here] = grad
    made[0][...] = grad
    kept[...] = part.astype(BF16)
    pltpu.sync_copy(kept, made[1])


def mlp_backward_kernel(chunk, half, meta, near, far, made, st, slope, sem):
    load = pltpu.make_async_copy(far[0], slope, sem)
    load.start()
    count, width = st.part.shape[0] // 2, st.part.shape[1]
    here = slice(half * count, (half + 1) * count)
    fresh = half == 1
    hidden = st.up[0].shape[1]
    rows = expand(st.rows[1][here].astype(F32))
    grad = st.part[here].astype(F32) + near[0][...].astype(F32)
    pulled, gain_terms = norm_pull(rows, inv_rms(rows), vector(st, 1, ATTN_GAIN, 0, width), grad)
    grad_in = st.grad[here] + pulled
    grad_in = center((grad_in - grad_in[:, width - 1 :]).astype(BF16).astype(F32))
    st.grad[here] = grad_in
    low = grad_in.astype(BF16)
    st.low[here] = low
    add_sums(st, MLP0, 0, low, fresh)
    add_sums(st, MLP0, width + hidden, gain_terms, fresh)
    grad = None
    load.wait()
    for at in range(0, hidden, chunk):
        cols = slice(at, at + chunk)
        hid = (mm_t(low, st.down[0][cols, :]) * slope[:, cols].astype(F32)).astype(BF16)
        st.hid[here, cols] = hid
        add_sums(st, MLP0, width + at, hid, fresh)
        term = mm_t(hid, st.up[0][:, cols])
        grad = term if grad is None else grad + term
    grad = grad.astype(BF16)
    st.part[here] = grad
    made[0][...] = grad


def attn_backward_kernel(layer, half, meta, near, far, made, st, *refs):
    weights = st.attn[layer]
    width, local = weights.shape[1:]
    count = st.part.shape[0] // 2
    here = slice(half * count, (half + 1) * count)
    fresh = half == 1
    name = ATTN1 if layer else ATTN0
    middle = st.mid[layer][here]
    grad = st.part[here].astype(F32) + near[0][...].astype(F32)
    pulled, gain_terms = norm_pull(middle, inv_rms(middle), vector(st, layer, MLP_GAIN, 0, width), grad)
    upstream = center(st.cot[here].astype(F32)) if layer else st.grad[here]
    grad_mid = upstream + pulled
    st.grad[here] = grad_mid
    low = grad_mid.astype(BF16)
    st.low[here] = low
    add_sums(st, name, 0, gain_terms, fresh)
    add_sums(st, name, width, low, fresh)
    grad_att = (mm_t(low[:, :local], weights[3, :local]) + mm_t(low[:, local:], weights[3, local:])).astype(BF16)
    at = 2 * width
    query, kv, dqkv = st.query[layer], st.kv[layer], st.hid
    early = made[-1] if half else near[1]
    keys = (half + 1) * count
    for pair in range(local // LANES):
        cols = slice(pair * LANES, (pair + 1) * LANES)
        vcols = slice(local + pair * LANES, local + (pair + 1) * LANES)
        v2cols = slice(2 * local + pair * LANES, 2 * local + (pair + 1) * LANES)
        grads = halves(grad_att[:, cols])
        queries = halves(query[here, cols])
        low_probs = st.probs[layer][half][pair]
        probs = low_probs.astype(F32)
        grad_probs = mm_t(grads, kv[:keys, vcols])
        inner = jnp.sum(grad_probs * probs, axis=-1, keepdims=True)
        grad_scores = (probs * (grad_probs - inner)).astype(BF16)
        grad_query = (merge(mm(grad_scores, kv[:keys, cols])) * HEAD_DIM**-0.5).astype(BF16)
        grad_key = t_mm(grad_scores, queries)
        grad_value = t_mm(low_probs, grads)
        if half:
            early[:, cols] = grad_key[:count]
            early[:, vcols] = grad_value[:count]
            grad_key, grad_value = grad_key[count:], grad_value[count:]
        else:
            grad_key, grad_value = grad_key + early[:, cols], grad_value + early[:, vcols]
        grad_value = grad_value.astype(BF16)
        dqkv[here, cols] = grad_query
        dqkv[here, vcols] = grad_key.astype(BF16)
        dqkv[here, v2cols] = grad_value
        add_sums(st, name, at + pair * LANES, grad_query, fresh)
        add_sums(st, name, at + local + pair * LANES, grad_value, fresh)
    gpart = mm_t(dqkv[here, :local], weights[0])
    gpart = gpart + mm_t(dqkv[here, local : 2 * local], weights[1])
    gpart = gpart + mm_t(dqkv[here, 2 * local : 3 * local], weights[2])
    if layer == 0:
        rows = expand(st.rows[0][here].astype(F32))
        add_sums(st, name, at + 2 * local, gpart * rows * inv_rms(rows), fresh)
    st.part[here] = gpart.astype(BF16)
    if layer:
        made[0][...] = gpart.astype(BF16)
    elif half == 0:
        away = pl.ds(pl.multiple_of((1 - meta[1]) * count, 16), count)
        made[0][...] = st.part[away]
        row = name
        made[1][...] = st.sums[row : row + 1, at + 2 * local : at + 2 * local + width]
        own = pl.ds(pl.multiple_of(meta[1] * count, 16), count)
        sems = refs[0]
        copies = []
        for n, ref in enumerate((st.part, st.rows[0], st.grad, st.mid[1])):
            copies.append(pltpu.make_async_copy(ref.at[own], made[3 + n], sems.at[n]))
            copies[-1].start()
        for side in range(2):

            @pl.when(meta[1] == side)
            def _():
                pltpu.make_async_copy(far[1 - side], made[2], sems.at[4]).start()
                pltpu.make_async_copy(far[side], made[7], sems.at[5]).start()

        copies.append(pltpu.make_async_copy(far[0], made[2], sems.at[4]))
        copies.append(pltpu.make_async_copy(far[0], made[7], sems.at[5]))
        for copy in copies:
            copy.wait()


def mlp_weights_kernel(layer, meta, near, far, made, st, *refs):
    width, hidden = st.up[0].shape
    if far:
        active, load_sems = refs
        count = far[0].shape[0]
        loads = [
            pltpu.make_async_copy(ref, active.at[pl.ds(at * count, count)], load_sems.at[at]) for at, ref in enumerate(far)
        ]
        for load in loads:
            load.start()
    else:
        active, loads = st.act, []
    block = made[0].shape[1]
    for out, part in ((made[1], 1 - meta[0]), (made[0], meta[0])):
        rows = width // 2
        left = st.low_normed[layer][:, pl.ds(pl.multiple_of(part * rows, LANES), rows)]
        for n in range(hidden // block):
            out[n * rows : (n + 1) * rows] = t_mm(left, st.hid[:, n * block : (n + 1) * block]).astype(BF16)
        base = hidden // block * rows
        rows = hidden // 2
        while loads:
            loads.pop().wait()
        left = active[:, pl.ds(pl.multiple_of(part * rows, LANES), rows)]
        for n in range(width // block):
            total = t_mm(left, st.low[:, n * block : (n + 1) * block])
            out[base + n * rows : base + (n + 1) * rows] = total.astype(BF16)


def attn_weights_kernel(layer, extra, meta, near, far, made, st):
    width, local = st.attn[0].shape[1:]
    hidden = st.up[0].shape[1]
    piece = made[0].shape[0] // 8 - extra

    def put(out, first, total):
        for at in range(0, total.shape[0], piece):
            where = (first + at) // piece * (piece + extra)
            out[where : where + piece] = total[at : at + piece].astype(BF16)

    if extra:
        sums = st.sums
        rows = [sums[row : row + 1] for row in range(4)]
        smalls = []
        tail = 2 * width + 2 * local
        for gain, attn, mlp in (
            (rows[ATTN0][:, tail : tail + width] + near[0][...], rows[ATTN0], rows[MLP0]),
            (rows[MLP0][:, width + hidden : 2 * width + hidden], rows[ATTN1], rows[MLP1]),
        ):
            row = [gain, attn[:, 2 * width : tail], attn[:, width : 2 * width], attn[:, :width]]
            row += [mlp[:, width : width + hidden], mlp[:, :width]]
            lines = [part[:, at : at + local] for part in row for at in range(0, part.shape[1], local)]
            lines += [jnp.zeros((1, local), F32)] * (extra - len(lines))
            smalls.append(jnp.concatenate(lines, axis=0))

    for out, part in ((made[1], 1 - meta[0]), (made[0], meta[0])):
        rows = width // 2
        cols = pl.ds(pl.multiple_of(part * rows, LANES), rows)
        left = st.normed[layer][:, cols]
        for at in range(3):
            put(out, at * rows, t_mm(left, st.hid[:, at * local : (at + 1) * local]))
        put(out, 3 * rows, t_mm(st.att[layer][...], st.low[:, cols]))
        if extra:
            out[piece : piece + extra] = jnp.where(part == 0, smalls[0], smalls[1]).astype(BF16)
            for at in range(1, 8):
                where = at * (piece + extra) + piece
                out[where : where + extra] = jnp.zeros((extra, local), BF16)


def close_kernel(meta, vec_own, vec_other, grad_far, out_far, out_own, part, rows, grad, middle, result, grad_in, *refs):
    width = part.shape[1]

    *vecs, sems = refs
    for layer in range(2):
        pick(meta, layer, vec_own.at[pl.ds(0, 8)], vec_other.at[pl.ds(0, 8)], vecs[layer], sems.at[layer])
    for layer in range(2):
        done(vec_own.at[pl.ds(0, 8)], vecs[layer], sems.at[layer])

    def vec(layer, row):
        return vecs[layer][row : row + 1, :width]

    branch = out_own[...].astype(F32) + out_far[...].astype(F32) + vec(1, DOWN_BIAS)
    result[...] = (middle[...] + center(branch)).astype(BF16)
    rows = expand(rows[...].astype(F32))
    given = part[...].astype(F32) + grad_far[...].astype(F32)
    pulled, _ = norm_pull(rows, inv_rms(rows), vec(0, ATTN_GAIN), given)
    total = grad[...] + pulled
    grad_in[...] = (total - total[:, width - 1 :]).astype(BF16)


def place_kernel(kinds, extra, meta, *refs):
    refs = list(refs)
    sources = take(refs, 4)
    outs = refs[:-2]
    wide, sems = refs[-2:]
    piece = wide.shape[1]

    def copy(n):
        part = meta[0] if n < 8 else 1 - meta[0]
        which, where = kinds[n % 8]
        return pltpu.make_async_copy(wide.at[n], outs[which].at[where(part)], sems.at[n])

    for layer in range(2):

        @pl.when(meta[0] == layer)
        def _():
            step = piece + (0 if layer else extra)
            for n in range(16):
                place = meta[6 + n // 8] & 6 if extra and layer == 0 else meta[6 + n // 8]
                at = pl.multiple_of(((n % 8) ^ place) * step, 16)
                wide[n] = sources[2 * (n // 8) + layer][pl.ds(at, piece)].astype(F32)
                copy(n).start()

    if extra:
        at = pl.multiple_of((meta[6] & 6) * (piece + extra) + piece, 16)
        small = sources[0][pl.ds(at, extra)].astype(F32)
        at = 0
        for out in outs[2:]:
            for row in range(out.shape[0]):
                for col in range(0, out.shape[1], small.shape[1]):
                    out[row : row + 1, col : col + small.shape[1]] = small[at : at + 1]
                    at += 1
    for n in range(16):
        copy(n).wait()


def shape(dims, dtype=BF16):
    return jax.ShapeDtypeStruct(dims, dtype)


def call(kernel, in_specs, outs, scratch, args, out_specs, limit=VMEM_BYTES):
    return pl.pallas_call(
        kernel,
        out_shape=tuple(outs),
        in_specs=in_specs,
        out_specs=tuple(out_specs),
        scratch_shapes=scratch,
        compiler_params=pltpu.CompilerParams(vmem_limit_bytes=limit),
        cost_estimate=pl.CostEstimate(flops=1, bytes_accessed=1, transcendentals=0),
    )(*args)


def swap(array, axis):
    return lax.ppermute(array, axis, [(0, 1), (1, 0)])


def halve_kernel(step, sides, mine, other, *outs):
    rows = mine.shape[0] // len(outs)
    for at, out in enumerate(outs):
        here = slice(None)
        if len(outs) == 2:
            side = sides[step] if at == 0 else 1 - sides[step]
            here = pl.ds(pl.multiple_of(side * rows, 16), rows)
        out[...] = (mine[here].astype(F32) + other[here].astype(F32)).astype(BF16)


def join_kernel(first, second, out):
    rows = first.shape[0]
    out[:rows] = first[...]
    out[rows:] = second[...]


def in_vmem(*arrays):
    return [pltpu.with_memory_space_constraint(a, pltpu.VMEM) for a in arrays]


def add_halves(step, sides, mine, other):
    rows, width = mine.shape
    halves = 1 if step is None else 2
    outs = [pltpu.VMEM((rows // halves, width), BF16)] * halves
    kernel = functools.partial(halve_kernel, step)
    return call(kernel, [SMEM, VMEM, VMEM], outs, [], [sides, *in_vmem(mine, other)], [VMEM] * halves)


def join(first, second):
    rows, width = first.shape
    outs = [pltpu.VMEM((2 * rows, width), BF16)]
    return call(join_kernel, [VMEM, VMEM], outs, [], in_vmem(first, second), [VMEM])[0]


SWAP, HALVE, ADD, JOIN = range(4)


class GroupSum:
    def __init__(self, sides, whole, mine, theirs):
        self.sides = sides
        self.held, self.received = mine, theirs
        self.steps = list(zip(*self.orders(lax.axis_size(GROUPS).bit_length() - 1)))
        self.whole = whole
        count = len(self.steps)
        self.todo = [(SWAP, None)] + [(HALVE, k) for k in range(count - 1)]
        if whole:
            self.todo += [(ADD, count - 1), (ADD, count - 2)] + [(JOIN, k) for k in range(count - 3, -1, -1)]
        else:
            self.todo += [(HALVE, count - 1), (ADD, count - 1)] + [(JOIN, k) for k in range(count - 2, -1, -1)]

    def make(self):
        kind, at = self.todo[0]
        if kind == SWAP:
            return [self.held, self.received]
        if kind == JOIN:
            return [join(self.held, self.received)]
        return list(add_halves(at if kind == HALVE else None, self.sides, self.held, self.received))

    def send(self, arrays):
        kind, at = self.todo.pop(0)
        self.held = arrays[0]
        self.received = swap(arrays[-1], SECTION) if kind == SWAP else self.exchange(arrays[-1], self.steps[at])

    @staticmethod
    def orders(bits):
        first = list(range(bits))
        second = [1, 0] + first[2:] if bits > 1 else first
        return first, second

    @staticmethod
    def exchange(array, bits):
        count = lax.axis_size(GROUPS)
        pairs = [(core * count + i, core * count + (i ^ (1 << bit))) for core, bit in enumerate(bits) for i in range(count)]
        return lax.ppermute(array, (SECTION, GROUPS), pairs)

    @staticmethod
    def which_side(bits):
        core, index = lax.axis_index(SECTION), lax.axis_index(GROUPS)
        return jnp.stack([(index >> jnp.where(core == 0, *pair)) & 1 for pair in zip(*GroupSum.orders(bits))])

    @staticmethod
    def place(bits, core):
        index = lax.axis_index(GROUPS)
        out = jnp.int32(0)
        for first, second in zip(*GroupSum.orders(bits)):
            out = out * 2 + ((index >> jnp.where(core == 0, first, second)) & 1)
        return out


def boundary(values, flows, after=()):
    flows = [flow for flow in flows if flow.todo]
    arrived = [flow for flow in flows if flow.todo[0][0] != SWAP]
    values = list(values)
    got = lax.optimization_barrier((*values, *[flow.received for flow in arrived], *after))
    values = list(got[: len(values)])
    for flow, received in zip(arrived, got[len(values) :]):
        flow.received = received
    arrays = [flow.make() for flow in flows]
    got = list(lax.optimization_barrier((*values, *[a for group in arrays for a in group])))
    values = take(got, len(values))
    for flow, group in zip(flows, arrays):
        flow.send(take(got, len(group)))
    return values


def in_order(array, place, count):
    blocks = array.reshape((count, array.shape[0] // count) + array.shape[1:])
    return jnp.take(blocks, jnp.arange(count, dtype=jnp.int32) ^ place, axis=0).reshape(array.shape)


def local(
    inputs,
    doc_lengths,
    attn_gain,
    qkv_weight,
    qv_bias,
    out_weight,
    out_bias,
    mlp_gain,
    up_weight,
    up_bias,
    down_weight,
    down_bias,
    cotangent,
):
    core = lax.axis_index(SECTION)
    side = lax.axis_index(TENSOR)
    groups = lax.axis_size(GROUPS)
    bits = groups.bit_length() - 1
    place = GroupSum.place(bits, core)
    rows = inputs.shape[1]
    width = attn_gain.shape[1]
    heads = qkv_weight.shape[3]
    hidden = up_weight.shape[2]
    pairs = heads // LANES
    chunk = hidden // 2
    extra = 16

    def own_rows(array):
        mine = lax.dynamic_index_in_dim(jnp.transpose(array, (2, 0, 1)), core, 1, keepdims=False)
        return jnp.pad(mine, ((0, width - mine.shape[0]), (0, 0)))

    lengths = lax.dynamic_index_in_dim(doc_lengths[:, 0, :], core, 0, keepdims=False)
    if groups == 8:
        places = [place, GroupSum.place(bits, 1 - core)]
    else:
        places = [jnp.int32(0)] * 2
    meta = jnp.concatenate([jnp.stack([core, side]).astype(jnp.int32), lengths, jnp.stack(places)])
    def each(*dims, dtype=BF16):
        return (shape(dims, dtype),) * 2

    unit = 2 * rows
    layer_probs = (shape((pairs, unit, rows)), shape((pairs, unit, unit)))
    bench = Bench(
        meta,
        State(
            vec=each(8, hidden, dtype=F32),
            attn=each(4, width, heads),
            up=each(width, hidden),
            down=each(hidden, width),
            rows=each(unit, width),
            normed=each(unit, width),
            low_normed=each(unit, width),
            query=each(unit, heads),
            kv=each(unit, 2 * heads),
            att=each(unit, heads),
            probs=(layer_probs, layer_probs),
            mid=each(unit, width, dtype=F32),
            act=shape((unit, hidden)),
            hid=shape((unit, hidden)),
            part=shape((unit, width)),
            cot=shape((unit, width)),
            low=shape((unit, width)),
            grad=shape((unit, width), F32),
            sums=shape((8, 3 * width + 2 * heads), F32),
        ),
    )
    sides = GroupSum.which_side(bits)

    entry = own_rows(inputs)
    small_in = (attn_gain, qv_bias[0], out_bias, mlp_gain, up_bias, down_bias)
    qkv, out = jnp.transpose(qkv_weight[0], (1, 0, 2)), out_weight[0]
    (vectors,) = call(
        pack_kernel,
        [HBM] * len(small_in),
        [pltpu.HBM((512, hidden), F32)],
        [
            pltpu.VMEM((8, hidden), F32),
            *[pltpu.VMEM(a.shape, F32) for a in small_in],
            pltpu.SemaphoreType.DMA((len(small_in),)),
        ],
        [pltpu.with_memory_space_constraint(a, pltpu.HBM) for a in small_in],
        [HBM],
    )
    far = swap(entry, TENSOR)
    vec_pair = (vectors, swap(vectors, SECTION))
    attn_pair = (qkv, swap(qkv, SECTION), out, swap(out, SECTION))
    cots, _ = lax.optimization_barrier((cotangent, vectors))
    cots = own_rows(cots)
    *attn_pair, cots = lax.optimization_barrier((*attn_pair, cots))
    far, cots, down = lax.optimization_barrier((far, cots, down_weight[0]))
    entry = (entry, far)
    up = up_weight[0]
    up_pair = (up, swap(up, SECTION))
    down_pair = (down, swap(down, SECTION))
    cots = (cots, swap(cots, TENSOR))

    bench.run(open_kernel, hbm_ins=[*vec_pair, *attn_pair], scratch=[pltpu.SemaphoreType.DMA((5,))], first=True)
    sent = (True, (rows, width), BF16)
    partial = functools.partial

    given = [None, None]
    for half in range(2):
        (part,) = bench.run(partial(attn_forward_kernel, 0, half), entry, [sent])
        given[half] = swap(part, TENSOR)
    *down_pair, cot_far = lax.optimization_barrier((*down_pair, cots[1]))
    cots = (cots[0], cot_far)
    bench.run(load_kernel, hbm_ins=[*attn_pair, *up_pair, *down_pair], scratch=[pltpu.SemaphoreType.DMA((7,))])
    acts, slopes = [], []
    for half in range(2):
        outs = [sent] + [(False, (rows, hidden), BF16)] * 2
        scratch = [pltpu.VMEM((2, rows, hidden), BF16), pltpu.SemaphoreType.DMA((2,))]
        part, *kept = bench.run(partial(mlp_forward_kernel, chunk, half), [given[half]], outs, scratch=scratch)
        given[half] = swap(part, TENSOR)
        acts.append(kept[0])
        slopes.append(kept[1])
    for half in range(2):
        (part,) = bench.run(partial(attn_forward_kernel, 1, half), [given[half]], [sent])
        given[half] = swap(part, TENSOR)
    mlp_parts = []
    kept = (False, (rows, width), BF16)
    for half in range(2):
        scratch = [pltpu.VMEM((rows, width), BF16), pltpu.SemaphoreType.DMA]
        body = partial(mlp_both_kernel, chunk, half)
        part, mlp_part = bench.run(body, [given[half], *cots], [sent, kept], scratch=scratch)
        given[half] = swap(part, TENSOR)
        mlp_parts.append(mlp_part)

    def weights(kernel, dims):
        ins = [gain_far] if kernel is attn_weights_kernel and dims[0] % (8 * 192) else []
        layer = 0 if ins or kernel is mlp_weights_kernel and mlp1 is not None else 1
        body = partial(kernel, layer) if kernel is mlp_weights_kernel else partial(kernel, layer, extra if ins else 0)
        far = acts if kernel is mlp_weights_kernel and layer == 0 else []
        scratch = [pltpu.VMEM((2 * rows, hidden), BF16), pltpu.SemaphoreType.DMA((2,))] if far else []
        return GroupSum(sides, bool(ins), *bench.run(body, ins, [(True, dims, BF16)] * 2, far, scratch))

    mlp_dims = (hidden * width // 384, 384)
    attn_dims = (2 * width * heads // 384, 384)
    mlp1 = None
    bench.follow(given)
    mlp1 = weights(mlp_weights_kernel, mlp_dims)
    early = (True, (rows, 2 * heads), F32)
    for half in (1, 0):
        (given[half],) = boundary([given[half]], [mlp1], () if half else [part])
        ins, outs = ([given[1]], [sent, early]) if half else ([given[0], link], [sent])
        part, *rest = bench.run(partial(attn_backward_kernel, 1, half), ins, outs)
        link = rest[0] if half else None
        given[half] = swap(part, TENSOR)
    attn1 = weights(attn_weights_kernel, attn_dims)
    for half in (1, 0):
        if half:
            given[1], attn1.held, attn1.received = lax.optimization_barrier((given[1], attn1.held, attn1.received))
        else:
            (given[0],) = boundary([given[0]], [mlp1, attn1], [part])
        scratch = [pltpu.VMEM((rows, hidden), BF16), pltpu.SemaphoreType.DMA]
        body = partial(mlp_backward_kernel, chunk, half)
        (part,) = bench.run(body, [given[half]], [sent], [slopes[half]], scratch)
        given[half] = swap(part, TENSOR)
    mlp0 = weights(mlp_weights_kernel, mlp_dims)
    (given[1],) = boundary([given[1]], [mlp1, attn1, mlp0], [part])
    (link,) = bench.run(partial(attn_backward_kernel, 0, 1), [given[1]], [early])
    given[0], link = boundary([given[0], link], [mlp1, attn1, mlp0])
    own = [(False, (rows, width), dtype) for dtype in (BF16, BF16, F32, F32)]
    outs = [sent, (True, (1, width), F32), sent, *own, sent]
    body = partial(attn_backward_kernel, 0, 0)
    scratch = [pltpu.SemaphoreType.DMA((6,))]
    away_grad, gain, away_out, *own = bench.run(body, [given[0], link], outs, mlp_parts, scratch)
    (gain_far,) = boundary([swap(gain, TENSOR)], [attn1], [gain])
    gain_far, away_grad, away_out = lax.optimization_barrier((gain_far, away_grad, away_out))
    backs = [swap(away_grad, TENSOR), swap(away_out, TENSOR)]
    attn0 = weights(attn_weights_kernel, (attn_dims[0] + 8 * extra, 384))

    token = [meta]

    def end(flow):
        while flow.todo:
            token[:] = boundary(token, [flow])
        token[0], *pieces = lax.optimization_barrier((token[0], flow.held, flow.received))
        whole = join(*pieces)
        if groups != 8:
            split = groups // 2 if flow.whole else groups
            whole = in_order(whole, place // (groups // split), split)
        token[0], whole = lax.optimization_barrier((token[0], whole))
        return whole, swap(whole, SECTION)

    def close(back_grad, back_out):
        args = [*in_vmem(back_grad, back_out, own[-1]), *own[:-1]]
        specs = [SMEM, HBM, HBM] + [VMEM] * len(args)
        scratch = [pltpu.VMEM((8, hidden), F32)] * 2 + [pltpu.SemaphoreType.DMA((2,))]
        outs = [shape((rows, width))] * 2
        return call(close_kernel, specs, outs, scratch, [token[0], *vec_pair, *args], [VMEM] * 2, 2 * VMEM_BYTES)

    token[:] = boundary(token, [mlp0, attn0], [mlp1.received])
    token[:] = boundary(token, [attn0, mlp0, mlp1], [attn1.received])
    token[0], *backs = lax.optimization_barrier((token[0], *backs))
    token[:] = boundary(token, [attn0, mlp0, attn1, mlp1])
    result, grad_in = close(*backs)
    result, grad_in = result[:, : width - 1], grad_in[:, : width - 1]
    token[0], result, grad_in = lax.optimization_barrier((token[0], result, grad_in))
    token[:] = boundary(token, [attn0, mlp0, attn1])
    token[:] = boundary(token, [attn0, mlp0, attn1], [mlp1.received])
    mlp1 = end(mlp1)
    token[:] = boundary(token, [attn0])
    token[0], attn1.received = lax.optimization_barrier((token[0], attn1.received))
    mlp0 = end(mlp0)
    attn1 = end(attn1)
    while attn0.todo:
        token[:] = boundary(token, [attn0])

    up_rows, down_rows = width // 2, hidden // 2

    def mlp_kind(block):
        if block < 4:
            return 0, lambda part: (pl.ds(pl.multiple_of(part * up_rows, 8), up_rows), pl.ds(block * 384, 384))
        col, row = (block - 4) // 2, (block - 4) % 2
        return 1, lambda part: (
            pl.ds(pl.multiple_of(part * down_rows + row * 384, 8), 384),
            pl.ds(col * 384, 384),
        )

    def attn_kind(block):
        which, row = block // 2, block % 2
        if which < 3:
            return 0, lambda part: (which, pl.ds(pl.multiple_of(part * up_rows + row * 192, 8), 192), slice(None))
        return 1, lambda part: (pl.ds(row * 192, 192), pl.ds(pl.multiple_of(part * 384, 128), 384))

    def placed(kinds, extra_rows, first, second, outs):
        piece = first[0].shape[0] // 8 - extra_rows
        args = [token[0], first[0], second[0], first[1], second[1]]
        scratch = [pltpu.VMEM((16, piece, 384), F32), pltpu.SemaphoreType.DMA((16,))]
        out_specs = [HBM, HBM] + [VMEM] * (len(outs) - 2)
        kernel = functools.partial(place_kernel, kinds, extra_rows)
        args[1:] = in_vmem(*args[1:])
        return call(kernel, [SMEM] + [VMEM] * 4, outs, scratch, args, out_specs, 2 * VMEM_BYTES)

    grad_up, grad_down = placed(
        [mlp_kind(b) for b in range(8)],
        0,
        mlp0,
        mlp1,
        [shape((width, hidden), F32), shape((hidden, width), F32)],
    )
    token[0], grad_up, grad_down = lax.optimization_barrier((token[0], grad_up, grad_down))
    attn0 = end(attn0)
    grad_qkv, grad_out, *small = placed(
        [attn_kind(b) for b in range(8)],
        extra,
        attn0,
        attn1,
        [shape((3, width, heads), F32), shape((heads, width), F32)]
        + [shape(dims, F32) for dims in ((1, width), (2, heads), (1, width), (1, width), (1, hidden), (1, width))],
    )

    return (
        result[None],
        grad_in[None],
        small[0],
        jnp.transpose(grad_qkv, (1, 0, 2))[None],
        small[1][None],
        grad_out[None],
        small[2],
        small[3],
        grad_up[None],
        small[4],
        grad_down[None],
        small[5],
    )


def solution(mesh):
    in_specs = (
        P(None, (GROUPS, TENSOR), None),
        P(None, GROUPS, None),
        P(SECTION, None),
        P(SECTION, None, None, TENSOR),
        P(SECTION, None, TENSOR),
        P(SECTION, TENSOR, None),
        P(SECTION, None),
        P(SECTION, None),
        P(SECTION, None, TENSOR),
        P(SECTION, TENSOR),
        P(SECTION, TENSOR, None),
        P(SECTION, None),
        P(None, (GROUPS, TENSOR), None),
    )
    out_specs = (
        P(SECTION, (GROUPS, TENSOR), None),
        P(SECTION, (GROUPS, TENSOR), None),
        P(SECTION, None),
        P(SECTION, None, None, TENSOR),
        P(SECTION, None, TENSOR),
        P(SECTION, TENSOR, None),
        P(SECTION, None),
        P(SECTION, None),
        P(SECTION, None, TENSOR),
        P(SECTION, TENSOR),
        P(SECTION, TENSOR, None),
        P(SECTION, None),
    )
    return jax.shard_map(local, mesh=mesh, in_specs=in_specs, out_specs=out_specs, check_vma=False)
```

```python
import functools
from typing import Any, NamedTuple

import jax
import jax.numpy as jnp
from jax import lax
from jax.experimental import pallas as pl
from jax.experimental.pallas import tpu as pltpu
from jax.sharding import PartitionSpec as P

HEAD_DIM = 64
LANES = 128
EPS = 1e-05
NEG = -1e30
VMEM_BYTES = 12 * 1024 * 1024

SECTION, GROUPS, TENSOR = "section", "dp", "tensor"

F32 = jnp.float32
BF16 = jnp.bfloat16

VMEM = pl.BlockSpec(memory_space=pltpu.VMEM)
SMEM = pl.BlockSpec(memory_space=pltpu.SMEM)
HBM = pl.BlockSpec(memory_space=pltpu.HBM)


def mm(left, right):
    return jnp.dot(left, right, preferred_element_type=F32)


def mm_t(left, right):
    return lax.dot_general(left, right, (((1,), (1,)), ((), ())), preferred_element_type=F32)


def t_mm(left, right):
    return lax.dot_general(left, right, (((0,), (0,)), ((), ())), preferred_element_type=F32)


def row_mean(array):
    return jnp.mean(array, axis=-1, keepdims=True)


def center(array):
    return array - row_mean(array)


def last_lane(shape):
    return lax.broadcasted_iota(jnp.int32, shape, 1) == shape[1] - 1


def expand(rows):
    return jnp.where(last_lane(rows.shape), -jnp.sum(rows, axis=-1, keepdims=True), rows)


def inv_rms(rows):
    return lax.rsqrt(row_mean(rows * rows) + EPS)


def norm_pull(rows, scaling, gain, grad):
    gained = gain * grad
    inner = row_mean(gained * rows)
    grad_rows = scaling * gained - rows * (scaling * scaling * scaling * inner)
    return center(grad_rows), grad * rows * scaling


def col_sum(array):
    return jnp.sum(array.astype(F32), axis=0, keepdims=True)


def pick(meta, layer, own, other, dst, sem):
    @pl.when(meta[0] == layer)
    def _():
        pltpu.make_async_copy(own, dst, sem).start()

    @pl.when(meta[0] != layer)
    def _():
        pltpu.make_async_copy(other, dst, sem).start()


def done(src, dst, sem):
    pltpu.make_async_copy(src, dst, sem).wait()


def halves(pair):
    first = lax.broadcasted_iota(jnp.int32, pair.shape, 1) < HEAD_DIM
    zero = jnp.zeros_like(pair)
    return jnp.concatenate([jnp.where(first, pair, zero), jnp.where(first, zero, pair)], axis=0)


def merge(stacked):
    rows = stacked.shape[0] // 2
    first = lax.broadcasted_iota(jnp.int32, (rows, stacked.shape[1]), 1) < HEAD_DIM
    return jnp.where(first, stacked[:rows], stacked[rows:])


def owner(meta, places):
    total = jnp.zeros(places.shape, jnp.int32)
    bound = 0
    for doc in range(3):
        bound = bound + meta[2 + doc]
        total = total + (places >= bound).astype(jnp.int32)
    return total


def mask_bias(meta, half, rows, keys):
    row_at = lax.broadcasted_iota(jnp.int32, (rows, 1), 0) + half * rows
    key_at = lax.broadcasted_iota(jnp.int32, (1, keys), 1)
    allowed = (owner(meta, row_at) == owner(meta, key_at)) & (key_at <= row_at)
    return jnp.where(allowed, 0.0, NEG).astype(F32)


def take(refs, count):
    out = refs[:count]
    del refs[:count]
    return out


class State(NamedTuple):
    vec: Any
    attn: Any
    up: Any
    down: Any
    rows: Any
    normed: Any
    low_normed: Any
    query: Any
    kv: Any
    att: Any
    probs: Any
    mid: Any
    act: Any
    hid: Any
    part: Any
    cot: Any
    low: Any
    grad: Any
    sums: Any


class Bench:
    def __init__(self, meta, shapes):
        self.meta = meta
        shapes, self.tree = jax.tree.flatten(shapes)
        self.arrays = shapes
        self.shapes = [pltpu.VMEM(a.shape, a.dtype) for a in shapes]

    def follow(self, arrays):
        self.meta, arrays[0] = lax.optimization_barrier((self.meta, arrays[0]))

    def run(self, body, ins=(), outs=(), hbm_ins=(), scratch=(), first=False):
        ins = [pltpu.with_memory_space_constraint(a, pltpu.VMEM) for a in ins]
        hbm_ins = [pltpu.with_memory_space_constraint(a, pltpu.HBM) for a in hbm_ins]
        held = [] if first else [pltpu.with_memory_space_constraint(a, pltpu.VMEM) for a in self.arrays]
        shapes = [(pltpu.VMEM if near else pltpu.HBM)(dims, dtype) for near, dims, dtype in outs]
        n_ins, n_hbm, n_outs, n_held = len(ins), len(hbm_ins), len(outs), len(self.shapes)

        def kernel(meta, *refs):
            refs = list(refs)
            near, far, _, made = take(refs, n_ins), take(refs, n_hbm), take(refs, len(held)), take(refs, n_outs)
            state = jax.tree.unflatten(self.tree, take(refs, n_held))
            body(meta, near, far, made, state, *refs)

        before = 1 + n_ins + n_hbm
        got = pl.pallas_call(
            kernel,
            out_shape=tuple(shapes + self.shapes),
            in_specs=[SMEM] + [VMEM] * n_ins + [HBM] * n_hbm + [VMEM] * len(held),
            out_specs=tuple([VMEM if near else HBM for near, _, _ in outs] + [VMEM] * n_held),
            input_output_aliases={before + i: n_outs + i for i in range(len(held))},
            scratch_shapes=list(scratch),
            compiler_params=pltpu.CompilerParams(vmem_limit_bytes=VMEM_BYTES),
            cost_estimate=pl.CostEstimate(flops=1, bytes_accessed=1, transcendentals=0),
        )(self.meta, *ins, *hbm_ins, *held)
        self.arrays = list(got[n_outs:])
        return list(got[:n_outs])


ATTN_GAIN, QV_BIAS, OUT_BIAS, MLP_GAIN, UP_BIAS, DOWN_BIAS = range(6)
MLP1, ATTN1, MLP0, ATTN0 = range(4)


def pack_kernel(*refs):
    count = (len(refs) - 3) // 2
    refs = list(refs)
    sources, (target, out), held, (sems,) = take(refs, count), take(refs, 2), take(refs, count), refs
    copies = [pltpu.make_async_copy(src, dst, sems.at[at]) for at, (src, dst) in enumerate(zip(sources, held))]
    for copy in copies:
        copy.start()
    out[...] = jnp.zeros(out.shape, F32)
    for row, (copy, ref) in enumerate(zip(copies, held)):
        copy.wait()
        if ref.shape[0] == 2:
            half = ref.shape[1]
            out[row : row + 1, :half] = ref[0:1]
            out[row : row + 1, half : 2 * half] = ref[1:2]
        else:
            out[row : row + 1, : ref.shape[1]] = ref[...]
    pltpu.sync_copy(out, target.at[pl.ds(0, out.shape[0])])


def load_attn(meta, layer, far, st, sems):
    qkv_own, qkv_other, out_own, out_other = far
    weights = st.attn[layer]
    local = weights.shape[2]
    work = [(qkv_own, qkv_other, weights.at[pl.ds(0, 3)])]
    for at in range(2):
        cols = pl.ds(at * local, local)
        work.append((out_own.at[:, cols], out_other.at[:, cols], weights.at[3, cols]))
    for at, (own, other, dst) in enumerate(work):
        pick(meta, layer, own, other, dst, sems.at[at])
    return lambda: [done(own, dst, sems.at[at]) for at, (own, _, dst) in enumerate(work)]


def open_kernel(meta, near, far, made, st, sems):
    vec_own, vec_other, *far = far
    for layer in range(2):
        rows = pl.ds(0, 8)
        pick(meta, layer, vec_own.at[rows], vec_other.at[rows], st.vec[layer], sems.at[layer])
    arrived = load_attn(meta, 0, far, st, sems.at[pl.ds(2, 3)])
    for layer in range(2):
        done(vec_own.at[pl.ds(0, 8)], st.vec[layer], sems.at[layer])
    arrived()


def load_kernel(meta, near, far, made, st, sems):
    *attn, up_own, up_other, down_own, down_other = far
    work = []
    for layer in range(2):
        work.append((layer, up_own, up_other, st.up[layer]))
        work.append((layer, down_own, down_other, st.down[layer]))
    for at, (layer, own, other, dst) in enumerate(work):
        pick(meta, layer, own, other, dst, sems.at[at])
    arrived = load_attn(meta, 1, attn, st, sems.at[pl.ds(4, 3)])
    for at, (layer, own, other, dst) in enumerate(work):
        done(own, dst, sems.at[at])
    arrived()


def vector(st, layer, row, first, last):
    return st.vec[layer][row : row + 1, first:last]


def attn_forward_kernel(layer, half, meta, near, far, made, st):
    weights = st.attn[layer]
    width, local = weights.shape[1:]
    count = st.part.shape[0] // 2
    here = slice(half * count, (half + 1) * count)
    if layer == 0:
        mine, other = near
        rows = jnp.where(meta[1] == half, mine[...], other[...]).astype(F32).T
    else:
        branch = st.part[here].astype(F32) + near[0][...].astype(F32) + vector(st, 0, DOWN_BIAS, 0, width)
        rows = (st.mid[0][here] + center(branch)).astype(BF16).astype(F32)
        rows = jnp.where(last_lane(rows.shape), 0.0, rows)
    st.rows[layer][here] = rows.astype(BF16)
    rows = expand(rows)
    normed = (rows * inv_rms(rows) * vector(st, layer, ATTN_GAIN, 0, width)).astype(BF16)
    st.normed[layer][here] = normed
    query = ((mm(normed, weights[0]) + vector(st, layer, QV_BIAS, 0, local)) * HEAD_DIM**-0.5).astype(BF16)
    st.query[layer][here] = query
    kv = st.kv[layer]
    kv[here, :local] = mm(normed, weights[1]).astype(BF16)
    kv[here, local:] = (mm(normed, weights[2]) + vector(st, layer, QV_BIAS, local, 2 * local)).astype(BF16)
    keys = (half + 1) * count
    masked = mask_bias(meta, half, count, keys)
    for pair in range(local // LANES):
        cols = slice(pair * LANES, (pair + 1) * LANES)
        vcols = slice(local + pair * LANES, local + (pair + 1) * LANES)
        scores = mm_t(halves(query[:, cols]), kv[:keys, cols])
        scores = (scores.reshape(2, count, keys) + masked[None]).reshape(2 * count, keys)
        expo = jnp.exp(scores - jnp.max(scores, axis=-1, keepdims=True))
        probs = (expo * (1.0 / jnp.sum(expo, axis=-1, keepdims=True))).astype(BF16)
        st.probs[layer][half][pair] = probs
        st.att[layer][here, cols] = merge(mm(probs, kv[:keys, vcols])).astype(BF16)
    attended = st.att[layer][here]
    for at in range(2):
        cols = slice(at * local, (at + 1) * local)
        part = mm(attended, weights[3, cols]).astype(BF16)
        st.part[here, cols] = part
        made[0][:, cols] = part


def mlp_middle(layer, here, received, st):
    width = st.part.shape[1]
    branch = st.part[here].astype(F32) + received[...].astype(F32) + vector(st, layer, OUT_BIAS, 0, width)
    middle = expand(st.rows[layer][here].astype(F32)) + center(branch)
    st.mid[layer][here] = middle
    normed = (middle * inv_rms(middle) * vector(st, layer, MLP_GAIN, 0, width)).astype(BF16)
    st.low_normed[layer][here] = normed
    return normed


def gelu_slope(hidden):
    root = (2.0 / jnp.pi) ** 0.5
    square = hidden * hidden
    half_up = 0.5 + 0.5 * jnp.tanh(hidden * (root + (root * 0.044715) * square))
    product = hidden * half_up
    return product, half_up + product * (1.0 - half_up) * (2 * root + (6 * root * 0.044715) * square)


def mlp_forward_kernel(chunk, half, meta, near, far, made, st, kept, sems):
    count = st.part.shape[0] // 2
    here = slice(half * count, (half + 1) * count)
    normed = mlp_middle(0, here, near[0], st)
    part = None
    for at in range(0, st.up[0].shape[1], chunk):
        cols = slice(at, at + chunk)
        hidden = mm(normed, st.up[0][:, cols]) + vector(st, 0, UP_BIAS, at, at + chunk)
        active, slope = gelu_slope(hidden)
        active = active.astype(BF16)
        kept[0, :, cols] = active
        kept[1, :, cols] = slope.astype(BF16)
        term = mm(active, st.down[0][cols, :])
        part = term if part is None else part + term
    copies = [pltpu.make_async_copy(kept.at[at], made[1 + at], sems.at[at]) for at in range(2)]
    for copy in copies:
        copy.start()
    part = part.astype(BF16)
    st.part[here] = part
    made[0][...] = part
    for copy in copies:
        copy.wait()


def add_sums(st, row, first, terms, fresh):
    places = slice(first, first + terms.shape[1])
    total = col_sum(terms)
    st.sums[row : row + 1, places] = total if fresh else total + st.sums[row : row + 1, places]


def mlp_both_kernel(chunk, half, meta, near, far, made, st, kept, sem):
    count, width = st.part.shape[0] // 2, st.part.shape[1]
    here = slice(half * count, (half + 1) * count)
    fresh = half == 0
    normed = mlp_middle(1, here, near[0], st)
    cot = jnp.where(meta[1] == half, near[1][...], near[2][...]).astype(F32).T
    st.cot[here] = cot.astype(BF16)
    low = center(cot).astype(BF16)
    st.low[here] = low
    add_sums(st, MLP1, 0, low, fresh)
    part, grad = None, None
    for at in range(0, st.up[1].shape[1], chunk):
        cols = slice(at, at + chunk)
        up, down = st.up[1][:, cols], st.down[1][cols, :]
        active, slope = gelu_slope(mm(normed, up) + vector(st, 1, UP_BIAS, at, at + chunk))
        active = active.astype(BF16)
        st.act[here, cols] = active
        hid = (mm_t(low, down) * slope).astype(BF16)
        st.hid[here, cols] = hid
        add_sums(st, MLP1, width + at, hid, fresh)
        terms = mm(active, down), mm_t(hid, up)
        part, grad = terms if part is None else (part + terms[0], grad + terms[1])
    grad = grad.astype(BF16)
    st.part[here] = grad
    made[0][...] = grad
    kept[...] = part.astype(BF16)
    pltpu.sync_copy(kept, made[1])


def mlp_backward_kernel(chunk, half, meta, near, far, made, st, slope, sem):
    load = pltpu.make_async_copy(far[0], slope, sem)
    load.start()
    count, width = st.part.shape[0] // 2, st.part.shape[1]
    here = slice(half * count, (half + 1) * count)
    fresh = half == 1
    hidden = st.up[0].shape[1]
    rows = expand(st.rows[1][here].astype(F32))
    grad = st.part[here].astype(F32) + near[0][...].astype(F32)
    pulled, gain_terms = norm_pull(rows, inv_rms(rows), vector(st, 1, ATTN_GAIN, 0, width), grad)
    grad_in = st.grad[here] + pulled
    grad_in = center((grad_in - grad_in[:, width - 1 :]).astype(BF16).astype(F32))
    st.grad[here] = grad_in
    low = grad_in.astype(BF16)
    st.low[here] = low
    add_sums(st, MLP0, 0, low, fresh)
    add_sums(st, MLP0, width + hidden, gain_terms, fresh)
    grad = None
    load.wait()
    for at in range(0, hidden, chunk):
        cols = slice(at, at + chunk)
        hid = (mm_t(low, st.down[0][cols, :]) * slope[:, cols].astype(F32)).astype(BF16)
        st.hid[here, cols] = hid
        add_sums(st, MLP0, width + at, hid, fresh)
        term = mm_t(hid, st.up[0][:, cols])
        grad = term if grad is None else grad + term
    grad = grad.astype(BF16)
    st.part[here] = grad
    made[0][...] = grad


def attn_backward_kernel(layer, half, meta, near, far, made, st, *refs):
    weights = st.attn[layer]
    width, local = weights.shape[1:]
    count = st.part.shape[0] // 2
    here = slice(half * count, (half + 1) * count)
    fresh = half == 1
    name = ATTN1 if layer else ATTN0
    middle = st.mid[layer][here]
    grad = st.part[here].astype(F32) + near[0][...].astype(F32)
    pulled, gain_terms = norm_pull(middle, inv_rms(middle), vector(st, layer, MLP_GAIN, 0, width), grad)
    upstream = center(st.cot[here].astype(F32)) if layer else st.grad[here]
    grad_mid = upstream + pulled
    st.grad[here] = grad_mid
    low = grad_mid.astype(BF16)
    st.low[here] = low
    add_sums(st, name, 0, gain_terms, fresh)
    add_sums(st, name, width, low, fresh)
    grad_att = (mm_t(low[:, :local], weights[3, :local]) + mm_t(low[:, local:], weights[3, local:])).astype(BF16)
    at = 2 * width
    query, kv, dqkv = st.query[layer], st.kv[layer], st.hid
    early = made[-1] if half else near[1]
    keys = (half + 1) * count
    for pair in range(local // LANES):
        cols = slice(pair * LANES, (pair + 1) * LANES)
        vcols = slice(local + pair * LANES, local + (pair + 1) * LANES)
        v2cols = slice(2 * local + pair * LANES, 2 * local + (pair + 1) * LANES)
        grads = halves(grad_att[:, cols])
        queries = halves(query[here, cols])
        low_probs = st.probs[layer][half][pair]
        probs = low_probs.astype(F32)
        grad_probs = mm_t(grads, kv[:keys, vcols])
        inner = jnp.sum(grad_probs * probs, axis=-1, keepdims=True)
        grad_scores = (probs * (grad_probs - inner)).astype(BF16)
        grad_query = (merge(mm(grad_scores, kv[:keys, cols])) * HEAD_DIM**-0.5).astype(BF16)
        grad_key = t_mm(grad_scores, queries)
        grad_value = t_mm(low_probs, grads)
        if half:
            early[:, cols] = grad_key[:count]
            early[:, vcols] = grad_value[:count]
            grad_key, grad_value = grad_key[count:], grad_value[count:]
        else:
            grad_key, grad_value = grad_key + early[:, cols], grad_value + early[:, vcols]
        grad_value = grad_value.astype(BF16)
        dqkv[here, cols] = grad_query
        dqkv[here, vcols] = grad_key.astype(BF16)
        dqkv[here, v2cols] = grad_value
        add_sums(st, name, at + pair * LANES, grad_query, fresh)
        add_sums(st, name, at + local + pair * LANES, grad_value, fresh)
    gpart = mm_t(dqkv[here, :local], weights[0])
    gpart = gpart + mm_t(dqkv[here, local : 2 * local], weights[1])
    gpart = gpart + mm_t(dqkv[here, 2 * local : 3 * local], weights[2])
    if layer == 0:
        rows = expand(st.rows[0][here].astype(F32))
        add_sums(st, name, at + 2 * local, gpart * rows * inv_rms(rows), fresh)
    st.part[here] = gpart.astype(BF16)
    if layer:
        made[0][...] = gpart.astype(BF16)
    elif half == 0:
        away = pl.ds(pl.multiple_of((1 - meta[1]) * count, 16), count)
        made[0][...] = st.part[away]
        row = name
        made[1][...] = st.sums[row : row + 1, at + 2 * local : at + 2 * local + width]
        own = pl.ds(pl.multiple_of(meta[1] * count, 16), count)
        sems = refs[0]
        copies = []
        for n, ref in enumerate((st.part, st.rows[0], st.grad, st.mid[1])):
            copies.append(pltpu.make_async_copy(ref.at[own], made[3 + n], sems.at[n]))
            copies[-1].start()
        for side in range(2):

            @pl.when(meta[1] == side)
            def _():
                pltpu.make_async_copy(far[1 - side], made[2], sems.at[4]).start()
                pltpu.make_async_copy(far[side], made[7], sems.at[5]).start()

        copies.append(pltpu.make_async_copy(far[0], made[2], sems.at[4]))
        copies.append(pltpu.make_async_copy(far[0], made[7], sems.at[5]))
        for copy in copies:
            copy.wait()


def mlp_weights_kernel(layer, meta, near, far, made, st, *refs):
    width, hidden = st.up[0].shape
    if far:
        active, load_sems = refs
        count = far[0].shape[0]
        loads = [
            pltpu.make_async_copy(ref, active.at[pl.ds(at * count, count)], load_sems.at[at]) for at, ref in enumerate(far)
        ]
        for load in loads:
            load.start()
    else:
        active, loads = st.act, []
    block = made[0].shape[1]
    for out, part in ((made[1], 1 - meta[0]), (made[0], meta[0])):
        rows = width // 2
        left = st.low_normed[layer][:, pl.ds(pl.multiple_of(part * rows, LANES), rows)]
        for n in range(hidden // block):
            out[n * rows : (n + 1) * rows] = t_mm(left, st.hid[:, n * block : (n + 1) * block]).astype(BF16)
        base = hidden // block * rows
        rows = hidden // 2
        while loads:
            loads.pop().wait()
        left = active[:, pl.ds(pl.multiple_of(part * rows, LANES), rows)]
        for n in range(width // block):
            total = t_mm(left, st.low[:, n * block : (n + 1) * block])
            out[base + n * rows : base + (n + 1) * rows] = total.astype(BF16)


def attn_weights_kernel(layer, extra, meta, near, far, made, st):
    width, local = st.attn[0].shape[1:]
    hidden = st.up[0].shape[1]
    piece = made[0].shape[0] // 8 - extra

    def put(out, first, total):
        for at in range(0, total.shape[0], piece):
            where = (first + at) // piece * (piece + extra)
            out[where : where + piece] = total[at : at + piece].astype(BF16)

    if extra:
        sums = st.sums
        rows = [sums[row : row + 1] for row in range(4)]
        smalls = []
        tail = 2 * width + 2 * local
        for gain, attn, mlp in (
            (rows[ATTN0][:, tail : tail + width] + near[0][...], rows[ATTN0], rows[MLP0]),
            (rows[MLP0][:, width + hidden : 2 * width + hidden], rows[ATTN1], rows[MLP1]),
        ):
            row = [gain, attn[:, 2 * width : tail], attn[:, width : 2 * width], attn[:, :width]]
            row += [mlp[:, width : width + hidden], mlp[:, :width]]
            lines = [part[:, at : at + local] for part in row for at in range(0, part.shape[1], local)]
            lines += [jnp.zeros((1, local), F32)] * (extra - len(lines))
            smalls.append(jnp.concatenate(lines, axis=0))

    for out, part in ((made[1], 1 - meta[0]), (made[0], meta[0])):
        rows = width // 2
        cols = pl.ds(pl.multiple_of(part * rows, LANES), rows)
        left = st.normed[layer][:, cols]
        for at in range(3):
            put(out, at * rows, t_mm(left, st.hid[:, at * local : (at + 1) * local]))
        put(out, 3 * rows, t_mm(st.att[layer][...], st.low[:, cols]))
        if extra:
            out[piece : piece + extra] = jnp.where(part == 0, smalls[0], smalls[1]).astype(BF16)
            for at in range(1, 8):
                where = at * (piece + extra) + piece
                out[where : where + extra] = jnp.zeros((extra, local), BF16)


def close_kernel(meta, vec_own, vec_other, grad_far, out_far, out_own, part, rows, grad, middle, result, grad_in, *refs):
    width = part.shape[1]

    *vecs, sems = refs
    for layer in range(2):
        pick(meta, layer, vec_own.at[pl.ds(0, 8)], vec_other.at[pl.ds(0, 8)], vecs[layer], sems.at[layer])
    for layer in range(2):
        done(vec_own.at[pl.ds(0, 8)], vecs[layer], sems.at[layer])

    def vec(layer, row):
        return vecs[layer][row : row + 1, :width]

    branch = out_own[...].astype(F32) + out_far[...].astype(F32) + vec(1, DOWN_BIAS)
    result[...] = (middle[...] + center(branch)).astype(BF16)
    rows = expand(rows[...].astype(F32))
    given = part[...].astype(F32) + grad_far[...].astype(F32)
    pulled, _ = norm_pull(rows, inv_rms(rows), vec(0, ATTN_GAIN), given)
    total = grad[...] + pulled
    grad_in[...] = (total - total[:, width - 1 :]).astype(BF16)


def place_kernel(kinds, extra, meta, *refs):
    refs = list(refs)
    sources = take(refs, 4)
    outs = refs[:-2]
    wide, sems = refs[-2:]
    piece = wide.shape[1]

    def copy(n):
        part = meta[0] if n < 8 else 1 - meta[0]
        which, where = kinds[n % 8]
        return pltpu.make_async_copy(wide.at[n], outs[which].at[where(part)], sems.at[n])

    for layer in range(2):

        @pl.when(meta[0] == layer)
        def _():
            step = piece + (0 if layer else extra)
            for n in range(16):
                place = meta[6 + n // 8] & 6 if extra and layer == 0 else meta[6 + n // 8]
                at = pl.multiple_of(((n % 8) ^ place) * step, 16)
                wide[n] = sources[2 * (n // 8) + layer][pl.ds(at, piece)].astype(F32)
                copy(n).start()

    if extra:
        at = pl.multiple_of((meta[6] & 6) * (piece + extra) + piece, 16)
        small = sources[0][pl.ds(at, extra)].astype(F32)
        at = 0
        for out in outs[2:]:
            for row in range(out.shape[0]):
                for col in range(0, out.shape[1], small.shape[1]):
                    out[row : row + 1, col : col + small.shape[1]] = small[at : at + 1]
                    at += 1
    for n in range(16):
        copy(n).wait()


def shape(dims, dtype=BF16):
    return jax.ShapeDtypeStruct(dims, dtype)


def call(kernel, in_specs, outs, scratch, args, out_specs, limit=VMEM_BYTES):
    return pl.pallas_call(
        kernel,
        out_shape=tuple(outs),
        in_specs=in_specs,
        out_specs=tuple(out_specs),
        scratch_shapes=scratch,
        compiler_params=pltpu.CompilerParams(vmem_limit_bytes=limit),
        cost_estimate=pl.CostEstimate(flops=1, bytes_accessed=1, transcendentals=0),
    )(*args)


def swap(array, axis):
    return lax.ppermute(array, axis, [(0, 1), (1, 0)])


def halve_kernel(step, sides, mine, other, *outs):
    rows = mine.shape[0] // len(outs)
    for at, out in enumerate(outs):
        here = slice(None)
        if len(outs) == 2:
            side = sides[step] if at == 0 else 1 - sides[step]
            here = pl.ds(pl.multiple_of(side * rows, 16), rows)
        out[...] = (mine[here].astype(F32) + other[here].astype(F32)).astype(BF16)


def join_kernel(first, second, out):
    rows = first.shape[0]
    out[:rows] = first[...]
    out[rows:] = second[...]


def in_vmem(*arrays):
    return [pltpu.with_memory_space_constraint(a, pltpu.VMEM) for a in arrays]


def add_halves(step, sides, mine, other):
    rows, width = mine.shape
    halves = 1 if step is None else 2
    if rows // halves % 16:
        both = (mine.astype(F32) + other.astype(F32)).astype(BF16)
        if halves == 1:
            return [both]
        return [lax.dynamic_slice_in_dim(both, at * (rows // 2), rows // 2, 0) for at in (sides[step], 1 - sides[step])]
    outs = [pltpu.VMEM((rows // halves, width), BF16)] * halves
    kernel = functools.partial(halve_kernel, step)
    return call(kernel, [SMEM, VMEM, VMEM], outs, [], [sides, *in_vmem(mine, other)], [VMEM] * halves)


def join(first, second):
    rows, width = first.shape
    if rows % 16:
        return jnp.concatenate([first, second], axis=0)
    outs = [pltpu.VMEM((2 * rows, width), BF16)]
    return call(join_kernel, [VMEM, VMEM], outs, [], in_vmem(first, second), [VMEM])[0]


SWAP, HALVE, ADD, JOIN = range(4)


class GroupSum:
    def __init__(self, sides, whole, mine, theirs):
        self.sides = sides
        self.held, self.received = mine, theirs
        self.steps = list(zip(*self.orders(lax.axis_size(GROUPS).bit_length() - 1)))
        self.whole = whole
        count = len(self.steps)
        self.todo = [(SWAP, None)] + [(HALVE, k) for k in range(count - 1)]
        if whole:
            self.todo += [(ADD, count - 1), (ADD, count - 2)] + [(JOIN, k) for k in range(count - 3, -1, -1)]
        else:
            self.todo += [(HALVE, count - 1), (ADD, count - 1)] + [(JOIN, k) for k in range(count - 2, -1, -1)]

    def make(self):
        kind, at = self.todo[0]
        if kind == SWAP:
            return [self.held, self.received]
        if kind == JOIN:
            return [join(self.held, self.received)]
        return list(add_halves(at if kind == HALVE else None, self.sides, self.held, self.received))

    def send(self, arrays):
        kind, at = self.todo.pop(0)
        self.held = arrays[0]
        self.received = swap(arrays[-1], SECTION) if kind == SWAP else self.exchange(arrays[-1], self.steps[at])

    @staticmethod
    def orders(bits):
        first = list(range(bits))
        second = [1, 0] + first[2:] if bits > 1 else first
        return first, second

    @staticmethod
    def exchange(array, bits):
        count = lax.axis_size(GROUPS)
        pairs = [(core * count + i, core * count + (i ^ (1 << bit))) for core, bit in enumerate(bits) for i in range(count)]
        return lax.ppermute(array, (SECTION, GROUPS), pairs)

    @staticmethod
    def which_side(bits):
        core, index = lax.axis_index(SECTION), lax.axis_index(GROUPS)
        return jnp.stack([(index >> jnp.where(core == 0, *pair)) & 1 for pair in zip(*GroupSum.orders(bits))])

    @staticmethod
    def place(bits, core):
        index = lax.axis_index(GROUPS)
        out = jnp.int32(0)
        for first, second in zip(*GroupSum.orders(bits)):
            out = out * 2 + ((index >> jnp.where(core == 0, first, second)) & 1)
        return out


def boundary(values, flows, after=()):
    flows = [flow for flow in flows if flow.todo]
    arrived = [flow for flow in flows if flow.todo[0][0] != SWAP]
    values = list(values)
    got = lax.optimization_barrier((*values, *[flow.received for flow in arrived], *after))
    values = list(got[: len(values)])
    for flow, received in zip(arrived, got[len(values) :]):
        flow.received = received
    arrays = [flow.make() for flow in flows]
    got = list(lax.optimization_barrier((*values, *[a for group in arrays for a in group])))
    values = take(got, len(values))
    for flow, group in zip(flows, arrays):
        flow.send(take(got, len(group)))
    return values


def in_order(array, place, count):
    blocks = array.reshape((count, array.shape[0] // count) + array.shape[1:])
    return jnp.take(blocks, jnp.arange(count, dtype=jnp.int32) ^ place, axis=0).reshape(array.shape)


def local(
    inputs,
    doc_lengths,
    attn_gain,
    qkv_weight,
    qv_bias,
    out_weight,
    out_bias,
    mlp_gain,
    up_weight,
    up_bias,
    down_weight,
    down_bias,
    cotangent,
):
    core = lax.axis_index(SECTION)
    side = lax.axis_index(TENSOR)
    groups = lax.axis_size(GROUPS)
    bits = groups.bit_length() - 1
    place = GroupSum.place(bits, core)
    rows = inputs.shape[1]
    width = attn_gain.shape[1]
    heads = qkv_weight.shape[3]
    hidden = up_weight.shape[2]
    pairs = heads // LANES
    chunk = hidden // 2
    extra = 16

    def own_rows(array):
        mine = lax.dynamic_index_in_dim(jnp.transpose(array, (2, 0, 1)), core, 1, keepdims=False)
        return jnp.pad(mine, ((0, width - mine.shape[0]), (0, 0)))

    lengths = lax.dynamic_index_in_dim(doc_lengths[:, 0, :], core, 0, keepdims=False)
    if groups == 8:
        places = [place, GroupSum.place(bits, 1 - core)]
    else:
        places = [jnp.int32(0)] * 2
    meta = jnp.concatenate([jnp.stack([core, side]).astype(jnp.int32), lengths, jnp.stack(places)])
    def each(*dims, dtype=BF16):
        return (shape(dims, dtype),) * 2

    unit = 2 * rows
    layer_probs = (shape((pairs, unit, rows)), shape((pairs, unit, unit)))
    bench = Bench(
        meta,
        State(
            vec=each(8, hidden, dtype=F32),
            attn=each(4, width, heads),
            up=each(width, hidden),
            down=each(hidden, width),
            rows=each(unit, width),
            normed=each(unit, width),
            low_normed=each(unit, width),
            query=each(unit, heads),
            kv=each(unit, 2 * heads),
            att=each(unit, heads),
            probs=(layer_probs, layer_probs),
            mid=each(unit, width, dtype=F32),
            act=shape((unit, hidden)),
            hid=shape((unit, hidden)),
            part=shape((unit, width)),
            cot=shape((unit, width)),
            low=shape((unit, width)),
            grad=shape((unit, width), F32),
            sums=shape((8, 3 * width + 2 * heads), F32),
        ),
    )
    sides = GroupSum.which_side(bits)

    entry = own_rows(inputs)
    small_in = (attn_gain, qv_bias[0], out_bias, mlp_gain, up_bias, down_bias)
    qkv, out = jnp.transpose(qkv_weight[0], (1, 0, 2)), out_weight[0]
    (vectors,) = call(
        pack_kernel,
        [HBM] * len(small_in),
        [pltpu.HBM((512, hidden), F32)],
        [
            pltpu.VMEM((8, hidden), F32),
            *[pltpu.VMEM(a.shape, F32) for a in small_in],
            pltpu.SemaphoreType.DMA((len(small_in),)),
        ],
        [pltpu.with_memory_space_constraint(a, pltpu.HBM) for a in small_in],
        [HBM],
    )
    far = swap(entry, TENSOR)
    vec_pair = (vectors, swap(vectors, SECTION))
    attn_pair = (qkv, swap(qkv, SECTION), out, swap(out, SECTION))
    cots, _ = lax.optimization_barrier((cotangent, vectors))
    cots = own_rows(cots)
    *attn_pair, cots = lax.optimization_barrier((*attn_pair, cots))
    far, cots, down = lax.optimization_barrier((far, cots, down_weight[0]))
    entry = (entry, far)
    up = up_weight[0]
    up_pair = (up, swap(up, SECTION))
    down_pair = (down, swap(down, SECTION))
    cots = (cots, swap(cots, TENSOR))

    bench.run(open_kernel, hbm_ins=[*vec_pair, *attn_pair], scratch=[pltpu.SemaphoreType.DMA((5,))], first=True)
    sent = (True, (rows, width), BF16)
    partial = functools.partial

    given = [None, None]
    for half in range(2):
        (part,) = bench.run(partial(attn_forward_kernel, 0, half), entry, [sent])
        given[half] = swap(part, TENSOR)
    *down_pair, cot_far = lax.optimization_barrier((*down_pair, cots[1]))
    cots = (cots[0], cot_far)
    bench.run(load_kernel, hbm_ins=[*attn_pair, *up_pair, *down_pair], scratch=[pltpu.SemaphoreType.DMA((7,))])
    acts, slopes = [], []
    for half in range(2):
        outs = [sent] + [(False, (rows, hidden), BF16)] * 2
        scratch = [pltpu.VMEM((2, rows, hidden), BF16), pltpu.SemaphoreType.DMA((2,))]
        part, *kept = bench.run(partial(mlp_forward_kernel, chunk, half), [given[half]], outs, scratch=scratch)
        given[half] = swap(part, TENSOR)
        acts.append(kept[0])
        slopes.append(kept[1])
    for half in range(2):
        (part,) = bench.run(partial(attn_forward_kernel, 1, half), [given[half]], [sent])
        given[half] = swap(part, TENSOR)
    mlp_parts = []
    kept = (False, (rows, width), BF16)
    for half in range(2):
        scratch = [pltpu.VMEM((rows, width), BF16), pltpu.SemaphoreType.DMA]
        body = partial(mlp_both_kernel, chunk, half)
        part, mlp_part = bench.run(body, [given[half], *cots], [sent, kept], scratch=scratch)
        given[half] = swap(part, TENSOR)
        mlp_parts.append(mlp_part)

    def weights(kernel, dims):
        ins = [gain_far] if kernel is attn_weights_kernel and dims[0] % (8 * 192) else []
        layer = 0 if ins or kernel is mlp_weights_kernel and mlp1 is not None else 1
        body = partial(kernel, layer) if kernel is mlp_weights_kernel else partial(kernel, layer, extra if ins else 0)
        far = acts if kernel is mlp_weights_kernel and layer == 0 else []
        scratch = [pltpu.VMEM((2 * rows, hidden), BF16), pltpu.SemaphoreType.DMA((2,))] if far else []
        return GroupSum(sides, bool(ins), *bench.run(body, ins, [(True, dims, BF16)] * 2, far, scratch))

    mlp_dims = (hidden * width // 384, 384)
    attn_dims = (2 * width * heads // 384, 384)
    mlp1 = None
    bench.follow(given)
    mlp1 = weights(mlp_weights_kernel, mlp_dims)
    early = (True, (rows, 2 * heads), F32)
    for half in (1, 0):
        (given[half],) = boundary([given[half]], [mlp1], () if half else [part])
        ins, outs = ([given[1]], [sent, early]) if half else ([given[0], link], [sent])
        part, *rest = bench.run(partial(attn_backward_kernel, 1, half), ins, outs)
        link = rest[0] if half else None
        given[half] = swap(part, TENSOR)
    attn1 = weights(attn_weights_kernel, attn_dims)
    for half in (1, 0):
        if half:
            given[1], attn1.held, attn1.received = lax.optimization_barrier((given[1], attn1.held, attn1.received))
        else:
            (given[0],) = boundary([given[0]], [mlp1, attn1], [part])
        scratch = [pltpu.VMEM((rows, hidden), BF16), pltpu.SemaphoreType.DMA]
        body = partial(mlp_backward_kernel, chunk, half)
        (part,) = bench.run(body, [given[half]], [sent], [slopes[half]], scratch)
        given[half] = swap(part, TENSOR)
    mlp0 = weights(mlp_weights_kernel, mlp_dims)
    (given[1],) = boundary([given[1]], [mlp1, attn1, mlp0], [part])
    (link,) = bench.run(partial(attn_backward_kernel, 0, 1), [given[1]], [early])
    given[0], link = boundary([given[0], link], [mlp1, attn1, mlp0])
    own = [(False, (rows, width), dtype) for dtype in (BF16, BF16, F32, F32)]
    outs = [sent, (True, (1, width), F32), sent, *own, sent]
    body = partial(attn_backward_kernel, 0, 0)
    scratch = [pltpu.SemaphoreType.DMA((6,))]
    away_grad, gain, away_out, *own = bench.run(body, [given[0], link], outs, mlp_parts, scratch)
    (gain_far,) = boundary([swap(gain, TENSOR)], [attn1], [gain])
    gain_far, away_grad, away_out = lax.optimization_barrier((gain_far, away_grad, away_out))
    backs = [swap(away_grad, TENSOR), swap(away_out, TENSOR)]
    attn0 = weights(attn_weights_kernel, (attn_dims[0] + 8 * extra, 384))

    token = [meta]

    def end(flow):
        while flow.todo:
            token[:] = boundary(token, [flow])
        token[0], *pieces = lax.optimization_barrier((token[0], flow.held, flow.received))
        whole = join(*pieces)
        if groups != 8:
            split = groups // 2 if flow.whole else groups
            whole = in_order(whole, place // (groups // split), split)
        token[0], whole = lax.optimization_barrier((token[0], whole))
        return whole, swap(whole, SECTION)

    def close(back_grad, back_out):
        args = [*in_vmem(back_grad, back_out, own[-1]), *own[:-1]]
        specs = [SMEM, HBM, HBM] + [VMEM] * len(args)
        scratch = [pltpu.VMEM((8, hidden), F32)] * 2 + [pltpu.SemaphoreType.DMA((2,))]
        outs = [shape((rows, width))] * 2
        return call(close_kernel, specs, outs, scratch, [token[0], *vec_pair, *args], [VMEM] * 2, 2 * VMEM_BYTES)

    token[:] = boundary(token, [mlp0, attn0], [mlp1.received])
    token[:] = boundary(token, [attn0, mlp0, mlp1], [attn1.received])
    token[0], *backs = lax.optimization_barrier((token[0], *backs))
    token[:] = boundary(token, [attn0, mlp0, attn1, mlp1])
    result, grad_in = close(*backs)
    result, grad_in = result[:, : width - 1], grad_in[:, : width - 1]
    token[0], result, grad_in = lax.optimization_barrier((token[0], result, grad_in))
    token[:] = boundary(token, [attn0, mlp0, attn1])
    token[:] = boundary(token, [attn0, mlp0, attn1], [mlp1.received])
    mlp1 = end(mlp1)
    token[:] = boundary(token, [attn0])
    token[0], attn1.received = lax.optimization_barrier((token[0], attn1.received))
    mlp0 = end(mlp0)
    attn1 = end(attn1)
    while attn0.todo:
        token[:] = boundary(token, [attn0])

    up_rows, down_rows = width // 2, hidden // 2

    def mlp_kind(block):
        if block < 4:
            return 0, lambda part: (pl.ds(pl.multiple_of(part * up_rows, 8), up_rows), pl.ds(block * 384, 384))
        col, row = (block - 4) // 2, (block - 4) % 2
        return 1, lambda part: (
            pl.ds(pl.multiple_of(part * down_rows + row * 384, 8), 384),
            pl.ds(col * 384, 384),
        )

    def attn_kind(block):
        which, row = block // 2, block % 2
        if which < 3:
            return 0, lambda part: (which, pl.ds(pl.multiple_of(part * up_rows + row * 192, 8), 192), slice(None))
        return 1, lambda part: (pl.ds(row * 192, 192), pl.ds(pl.multiple_of(part * 384, 128), 384))

    def placed(kinds, extra_rows, first, second, outs):
        piece = first[0].shape[0] // 8 - extra_rows
        args = [token[0], first[0], second[0], first[1], second[1]]
        scratch = [pltpu.VMEM((16, piece, 384), F32), pltpu.SemaphoreType.DMA((16,))]
        out_specs = [HBM, HBM] + [VMEM] * (len(outs) - 2)
        kernel = functools.partial(place_kernel, kinds, extra_rows)
        args[1:] = in_vmem(*args[1:])
        return call(kernel, [SMEM] + [VMEM] * 4, outs, scratch, args, out_specs, 2 * VMEM_BYTES)

    grad_up, grad_down = placed(
        [mlp_kind(b) for b in range(8)],
        0,
        mlp0,
        mlp1,
        [shape((width, hidden), F32), shape((hidden, width), F32)],
    )
    token[0], grad_up, grad_down = lax.optimization_barrier((token[0], grad_up, grad_down))
    attn0 = end(attn0)
    grad_qkv, grad_out, *small = placed(
        [attn_kind(b) for b in range(8)],
        extra,
        attn0,
        attn1,
        [shape((3, width, heads), F32), shape((heads, width), F32)]
        + [shape(dims, F32) for dims in ((1, width), (2, heads), (1, width), (1, width), (1, hidden), (1, width))],
    )

    return (
        result[None],
        grad_in[None],
        small[0],
        jnp.transpose(grad_qkv, (1, 0, 2))[None],
        small[1][None],
        grad_out[None],
        small[2],
        small[3],
        grad_up[None],
        small[4],
        grad_down[None],
        small[5],
    )


def solution(mesh):
    in_specs = (
        P(None, (GROUPS, TENSOR), None),
        P(None, GROUPS, None),
        P(SECTION, None),
        P(SECTION, None, None, TENSOR),
        P(SECTION, None, TENSOR),
        P(SECTION, TENSOR, None),
        P(SECTION, None),
        P(SECTION, None),
        P(SECTION, None, TENSOR),
        P(SECTION, TENSOR),
        P(SECTION, TENSOR, None),
        P(SECTION, None),
        P(None, (GROUPS, TENSOR), None),
    )
    out_specs = (
        P(SECTION, (GROUPS, TENSOR), None),
        P(SECTION, (GROUPS, TENSOR), None),
        P(SECTION, None),
        P(SECTION, None, None, TENSOR),
        P(SECTION, None, TENSOR),
        P(SECTION, TENSOR, None),
        P(SECTION, None),
        P(SECTION, None),
        P(SECTION, None, TENSOR),
        P(SECTION, TENSOR),
        P(SECTION, TENSOR, None),
        P(SECTION, None),
    )
    return jax.shard_map(local, mesh=mesh, in_specs=in_specs, out_specs=out_specs, check_vma=False)
```

```python
import functools
from typing import Any, NamedTuple

import jax
import jax.numpy as jnp
from jax import lax
from jax.experimental import pallas as pl
from jax.experimental.pallas import tpu as pltpu
from jax.sharding import PartitionSpec as P

HEAD_DIM = 64
LANES = 128
EPS = 1e-05
NEG = -1e30
VMEM_BYTES = 12 * 1024 * 1024

SECTION, GROUPS, TENSOR = "section", "dp", "tensor"

F32 = jnp.float32
BF16 = jnp.bfloat16

VMEM = pl.BlockSpec(memory_space=pltpu.VMEM)
SMEM = pl.BlockSpec(memory_space=pltpu.SMEM)
HBM = pl.BlockSpec(memory_space=pltpu.HBM)


def mm(left, right):
    return jnp.dot(left, right, preferred_element_type=F32)


def mm_t(left, right):
    return lax.dot_general(left, right, (((1,), (1,)), ((), ())), preferred_element_type=F32)


def t_mm(left, right):
    return lax.dot_general(left, right, (((0,), (0,)), ((), ())), preferred_element_type=F32)


def row_mean(array):
    return jnp.mean(array, axis=-1, keepdims=True)


def center(array):
    return array - row_mean(array)


def last_lane(shape):
    return lax.broadcasted_iota(jnp.int32, shape, 1) == shape[1] - 1


def expand(rows):
    return jnp.where(last_lane(rows.shape), -jnp.sum(rows, axis=-1, keepdims=True), rows)


def inv_rms(rows):
    return lax.rsqrt(row_mean(rows * rows) + EPS)


def norm_pull(rows, scaling, gain, grad):
    gained = gain * grad
    inner = row_mean(gained * rows)
    grad_rows = scaling * gained - rows * (scaling * scaling * scaling * inner)
    return center(grad_rows), grad * rows * scaling


def col_sum(array):
    return jnp.sum(array.astype(F32), axis=0, keepdims=True)


def pick(meta, layer, own, other, dst, sem):
    @pl.when(meta[0] == layer)
    def _():
        pltpu.make_async_copy(own, dst, sem).start()

    @pl.when(meta[0] != layer)
    def _():
        pltpu.make_async_copy(other, dst, sem).start()


def done(src, dst, sem):
    pltpu.make_async_copy(src, dst, sem).wait()


def halves(pair):
    first = lax.broadcasted_iota(jnp.int32, pair.shape, 1) < HEAD_DIM
    zero = jnp.zeros_like(pair)
    return jnp.concatenate([jnp.where(first, pair, zero), jnp.where(first, zero, pair)], axis=0)


def merge(stacked):
    rows = stacked.shape[0] // 2
    first = lax.broadcasted_iota(jnp.int32, (rows, stacked.shape[1]), 1) < HEAD_DIM
    return jnp.where(first, stacked[:rows], stacked[rows:])


def owner(meta, places):
    total = jnp.zeros(places.shape, jnp.int32)
    bound = 0
    for doc in range(3):
        bound = bound + meta[2 + doc]
        total = total + (places >= bound).astype(jnp.int32)
    return total


def mask_bias(meta, half, rows, keys):
    row_at = lax.broadcasted_iota(jnp.int32, (rows, 1), 0) + half * rows
    key_at = lax.broadcasted_iota(jnp.int32, (1, keys), 1)
    allowed = (owner(meta, row_at) == owner(meta, key_at)) & (key_at <= row_at)
    return jnp.where(allowed, 0.0, NEG).astype(F32)


def take(refs, count):
    out = refs[:count]
    del refs[:count]
    return out


class State(NamedTuple):
    vec: Any
    attn: Any
    up: Any
    down: Any
    rows: Any
    normed: Any
    low_normed: Any
    query: Any
    kv: Any
    att: Any
    probs: Any
    mid: Any
    act: Any
    hid: Any
    part: Any
    cot: Any
    low: Any
    grad: Any
    sums: Any


class Bench:
    def __init__(self, meta, shapes):
        self.meta = meta
        shapes, self.tree = jax.tree.flatten(shapes)
        self.arrays = shapes
        self.shapes = [pltpu.VMEM(a.shape, a.dtype) for a in shapes]

    def follow(self, arrays):
        self.meta, arrays[0] = lax.optimization_barrier((self.meta, arrays[0]))

    def run(self, body, ins=(), outs=(), hbm_ins=(), scratch=(), first=False):
        ins = [pltpu.with_memory_space_constraint(a, pltpu.VMEM) for a in ins]
        hbm_ins = [pltpu.with_memory_space_constraint(a, pltpu.HBM) for a in hbm_ins]
        held = [] if first else [pltpu.with_memory_space_constraint(a, pltpu.VMEM) for a in self.arrays]
        shapes = [(pltpu.VMEM if near else pltpu.HBM)(dims, dtype) for near, dims, dtype in outs]
        n_ins, n_hbm, n_outs, n_held = len(ins), len(hbm_ins), len(outs), len(self.shapes)

        def kernel(meta, *refs):
            refs = list(refs)
            near, far, _, made = take(refs, n_ins), take(refs, n_hbm), take(refs, len(held)), take(refs, n_outs)
            state = jax.tree.unflatten(self.tree, take(refs, n_held))
            body(meta, near, far, made, state, *refs)

        before = 1 + n_ins + n_hbm
        got = pl.pallas_call(
            kernel,
            out_shape=tuple(shapes + self.shapes),
            in_specs=[SMEM] + [VMEM] * n_ins + [HBM] * n_hbm + [VMEM] * len(held),
            out_specs=tuple([VMEM if near else HBM for near, _, _ in outs] + [VMEM] * n_held),
            input_output_aliases={before + i: n_outs + i for i in range(len(held))},
            scratch_shapes=list(scratch),
            compiler_params=pltpu.CompilerParams(vmem_limit_bytes=VMEM_BYTES),
            cost_estimate=pl.CostEstimate(flops=1, bytes_accessed=1, transcendentals=0),
        )(self.meta, *ins, *hbm_ins, *held)
        self.arrays = list(got[n_outs:])
        return list(got[:n_outs])


ATTN_GAIN, QV_BIAS, OUT_BIAS, MLP_GAIN, UP_BIAS, DOWN_BIAS = range(6)
MLP1, ATTN1, MLP0, ATTN0 = range(4)


def pack_kernel(*refs):
    count = (len(refs) - 3) // 2
    refs = list(refs)
    sources, (target, out), held, (sems,) = take(refs, count), take(refs, 2), take(refs, count), refs
    copies = [pltpu.make_async_copy(src, dst, sems.at[at]) for at, (src, dst) in enumerate(zip(sources, held))]
    for copy in copies:
        copy.start()
    out[...] = jnp.zeros(out.shape, F32)
    for row, (copy, ref) in enumerate(zip(copies, held)):
        copy.wait()
        if ref.shape[0] == 2:
            half = ref.shape[1]
            out[row : row + 1, :half] = ref[0:1]
            out[row : row + 1, half : 2 * half] = ref[1:2]
        else:
            out[row : row + 1, : ref.shape[1]] = ref[...]
    pltpu.sync_copy(out, target.at[pl.ds(0, out.shape[0])])


def load_attn(meta, layer, far, st, sems):
    qkv_own, qkv_other, out_own, out_other = far
    weights = st.attn[layer]
    local = weights.shape[2]
    work = [(qkv_own, qkv_other, weights.at[pl.ds(0, 3)])]
    for at in range(2):
        cols = pl.ds(at * local, local)
        work.append((out_own.at[:, cols], out_other.at[:, cols], weights.at[3, cols]))
    for at, (own, other, dst) in enumerate(work):
        pick(meta, layer, own, other, dst, sems.at[at])
    return lambda: [done(own, dst, sems.at[at]) for at, (own, _, dst) in enumerate(work)]


def open_kernel(meta, near, far, made, st, sems):
    vec_own, vec_other, *far = far
    for layer in range(2):
        rows = pl.ds(0, 8)
        pick(meta, layer, vec_own.at[rows], vec_other.at[rows], st.vec[layer], sems.at[layer])
    arrived = load_attn(meta, 0, far, st, sems.at[pl.ds(2, 3)])
    for layer in range(2):
        done(vec_own.at[pl.ds(0, 8)], st.vec[layer], sems.at[layer])
    arrived()


def load_kernel(meta, near, far, made, st, sems):
    *attn, up_own, up_other, down_own, down_other = far
    work = []
    for layer in range(2):
        work.append((layer, up_own, up_other, st.up[layer]))
        work.append((layer, down_own, down_other, st.down[layer]))
    for at, (layer, own, other, dst) in enumerate(work):
        pick(meta, layer, own, other, dst, sems.at[at])
    arrived = load_attn(meta, 1, attn, st, sems.at[pl.ds(4, 3)])
    for at, (layer, own, other, dst) in enumerate(work):
        done(own, dst, sems.at[at])
    arrived()


def vector(st, layer, row, first, last):
    return st.vec[layer][row : row + 1, first:last]


def attn_forward_kernel(layer, half, meta, near, far, made, st):
    weights = st.attn[layer]
    width, local = weights.shape[1:]
    count = st.part.shape[0] // 2
    here = slice(half * count, (half + 1) * count)
    if layer == 0:
        mine, other = near
        rows = jnp.where(meta[1] == half, mine[...], other[...]).astype(F32).T
    else:
        branch = st.part[here].astype(F32) + near[0][...].astype(F32) + vector(st, 0, DOWN_BIAS, 0, width)
        rows = (st.mid[0][here] + center(branch)).astype(BF16).astype(F32)
        rows = jnp.where(last_lane(rows.shape), 0.0, rows)
    st.rows[layer][here] = rows.astype(BF16)
    rows = expand(rows)
    normed = (rows * inv_rms(rows) * vector(st, layer, ATTN_GAIN, 0, width)).astype(BF16)
    st.normed[layer][here] = normed
    query = ((mm(normed, weights[0]) + vector(st, layer, QV_BIAS, 0, local)) * HEAD_DIM**-0.5).astype(BF16)
    st.query[layer][here] = query
    kv = st.kv[layer]
    kv[here, :local] = mm(normed, weights[1]).astype(BF16)
    kv[here, local:] = (mm(normed, weights[2]) + vector(st, layer, QV_BIAS, local, 2 * local)).astype(BF16)
    keys = (half + 1) * count
    masked = mask_bias(meta, half, count, keys)
    for pair in range(local // LANES):
        cols = slice(pair * LANES, (pair + 1) * LANES)
        vcols = slice(local + pair * LANES, local + (pair + 1) * LANES)
        scores = mm_t(halves(query[:, cols]), kv[:keys, cols])
        scores = (scores.reshape(2, count, keys) + masked[None]).reshape(2 * count, keys)
        expo = jnp.exp(scores - jnp.max(scores, axis=-1, keepdims=True))
        probs = (expo * (1.0 / jnp.sum(expo, axis=-1, keepdims=True))).astype(BF16)
        st.probs[layer][half][pair] = probs
        st.att[layer][here, cols] = merge(mm(probs, kv[:keys, vcols])).astype(BF16)
    attended = st.att[layer][here]
    for at in range(2):
        cols = slice(at * local, (at + 1) * local)
        part = mm(attended, weights[3, cols]).astype(BF16)
        st.part[here, cols] = part
        made[0][:, cols] = part


def mlp_middle(layer, here, received, st):
    width = st.part.shape[1]
    branch = st.part[here].astype(F32) + received[...].astype(F32) + vector(st, layer, OUT_BIAS, 0, width)
    middle = expand(st.rows[layer][here].astype(F32)) + center(branch)
    st.mid[layer][here] = middle
    normed = (middle * inv_rms(middle) * vector(st, layer, MLP_GAIN, 0, width)).astype(BF16)
    st.low_normed[layer][here] = normed
    return normed


def gelu_slope(hidden):
    root = (2.0 / jnp.pi) ** 0.5
    square = hidden * hidden
    half_up = 0.5 + 0.5 * jnp.tanh(hidden * (root + (root * 0.044715) * square))
    product = hidden * half_up
    return product, half_up + product * (1.0 - half_up) * (2 * root + (6 * root * 0.044715) * square)


def mlp_forward_kernel(chunk, half, meta, near, far, made, st, kept, sems):
    count = st.part.shape[0] // 2
    here = slice(half * count, (half + 1) * count)
    normed = mlp_middle(0, here, near[0], st)
    part = None
    for at in range(0, st.up[0].shape[1], chunk):
        cols = slice(at, at + chunk)
        hidden = mm(normed, st.up[0][:, cols]) + vector(st, 0, UP_BIAS, at, at + chunk)
        active, slope = gelu_slope(hidden)
        active = active.astype(BF16)
        kept[0, :, cols] = active
        kept[1, :, cols] = slope.astype(BF16)
        term = mm(active, st.down[0][cols, :])
        part = term if part is None else part + term
    copies = [pltpu.make_async_copy(kept.at[at], made[1 + at], sems.at[at]) for at in range(2)]
    for copy in copies:
        copy.start()
    part = part.astype(BF16)
    st.part[here] = part
    made[0][...] = part
    for copy in copies:
        copy.wait()


def add_sums(st, row, first, terms, fresh):
    places = slice(first, first + terms.shape[1])
    total = col_sum(terms)
    st.sums[row : row + 1, places] = total if fresh else total + st.sums[row : row + 1, places]


def mlp_both_kernel(chunk, half, meta, near, far, made, st, kept, sem):
    count, width = st.part.shape[0] // 2, st.part.shape[1]
    here = slice(half * count, (half + 1) * count)
    fresh = half == 0
    normed = mlp_middle(1, here, near[0], st)
    cot = jnp.where(meta[1] == half, near[1][...], near[2][...]).astype(F32).T
    st.cot[here] = cot.astype(BF16)
    low = center(cot).astype(BF16)
    st.low[here] = low
    add_sums(st, MLP1, 0, low, fresh)
    part, grad = None, None
    for at in range(0, st.up[1].shape[1], chunk):
        cols = slice(at, at + chunk)
        up, down = st.up[1][:, cols], st.down[1][cols, :]
        active, slope = gelu_slope(mm(normed, up) + vector(st, 1, UP_BIAS, at, at + chunk))
        active = active.astype(BF16)
        st.act[here, cols] = active
        hid = (mm_t(low, down) * slope).astype(BF16)
        st.hid[here, cols] = hid
        add_sums(st, MLP1, width + at, hid, fresh)
        terms = mm(active, down), mm_t(hid, up)
        part, grad = terms if part is None else (part + terms[0], grad + terms[1])
    grad = grad.astype(BF16)
    st.part[here] = grad
    made[0][...] = grad
    kept[...] = part.astype(BF16)
    pltpu.sync_copy(kept, made[1])


def mlp_backward_kernel(chunk, half, meta, near, far, made, st, slope, sem):
    load = pltpu.make_async_copy(far[0], slope, sem)
    load.start()
    count, width = st.part.shape[0] // 2, st.part.shape[1]
    here = slice(half * count, (half + 1) * count)
    fresh = half == 1
    hidden = st.up[0].shape[1]
    rows = expand(st.rows[1][here].astype(F32))
    grad = st.part[here].astype(F32) + near[0][...].astype(F32)
    pulled, gain_terms = norm_pull(rows, inv_rms(rows), vector(st, 1, ATTN_GAIN, 0, width), grad)
    grad_in = st.grad[here] + pulled
    grad_in = center((grad_in - grad_in[:, width - 1 :]).astype(BF16).astype(F32))
    st.grad[here] = grad_in
    low = grad_in.astype(BF16)
    st.low[here] = low
    add_sums(st, MLP0, 0, low, fresh)
    add_sums(st, MLP0, width + hidden, gain_terms, fresh)
    grad = None
    load.wait()
    for at in range(0, hidden, chunk):
        cols = slice(at, at + chunk)
        hid = (mm_t(low, st.down[0][cols, :]) * slope[:, cols].astype(F32)).astype(BF16)
        st.hid[here, cols] = hid
        add_sums(st, MLP0, width + at, hid, fresh)
        term = mm_t(hid, st.up[0][:, cols])
        grad = term if grad is None else grad + term
    grad = grad.astype(BF16)
    st.part[here] = grad
    made[0][...] = grad


def attn_backward_kernel(layer, half, meta, near, far, made, st, *refs):
    weights = st.attn[layer]
    width, local = weights.shape[1:]
    count = st.part.shape[0] // 2
    here = slice(half * count, (half + 1) * count)
    fresh = half == 1
    name = ATTN1 if layer else ATTN0
    middle = st.mid[layer][here]
    grad = st.part[here].astype(F32) + near[0][...].astype(F32)
    pulled, gain_terms = norm_pull(middle, inv_rms(middle), vector(st, layer, MLP_GAIN, 0, width), grad)
    upstream = center(st.cot[here].astype(F32)) if layer else st.grad[here]
    grad_mid = upstream + pulled
    st.grad[here] = grad_mid
    low = grad_mid.astype(BF16)
    st.low[here] = low
    add_sums(st, name, 0, gain_terms, fresh)
    add_sums(st, name, width, low, fresh)
    grad_att = (mm_t(low[:, :local], weights[3, :local]) + mm_t(low[:, local:], weights[3, local:])).astype(BF16)
    at = 2 * width
    query, kv, dqkv = st.query[layer], st.kv[layer], st.hid
    early = made[-1] if half else near[1]
    keys = (half + 1) * count
    for pair in range(local // LANES):
        cols = slice(pair * LANES, (pair + 1) * LANES)
        vcols = slice(local + pair * LANES, local + (pair + 1) * LANES)
        v2cols = slice(2 * local + pair * LANES, 2 * local + (pair + 1) * LANES)
        grads = halves(grad_att[:, cols])
        queries = halves(query[here, cols])
        low_probs = st.probs[layer][half][pair]
        probs = low_probs.astype(F32)
        grad_probs = mm_t(grads, kv[:keys, vcols])
        inner = jnp.sum(grad_probs * probs, axis=-1, keepdims=True)
        grad_scores = (probs * (grad_probs - inner)).astype(BF16)
        grad_query = (merge(mm(grad_scores, kv[:keys, cols])) * HEAD_DIM**-0.5).astype(BF16)
        grad_key = t_mm(grad_scores, queries)
        grad_value = t_mm(low_probs, grads)
        if half:
            early[:, cols] = grad_key[:count]
            early[:, vcols] = grad_value[:count]
            grad_key, grad_value = grad_key[count:], grad_value[count:]
        else:
            grad_key, grad_value = grad_key + early[:, cols], grad_value + early[:, vcols]
        grad_value = grad_value.astype(BF16)
        dqkv[here, cols] = grad_query
        dqkv[here, vcols] = grad_key.astype(BF16)
        dqkv[here, v2cols] = grad_value
        add_sums(st, name, at + pair * LANES, grad_query, fresh)
        add_sums(st, name, at + local + pair * LANES, grad_value, fresh)
    gpart = mm_t(dqkv[here, :local], weights[0])
    gpart = gpart + mm_t(dqkv[here, local : 2 * local], weights[1])
    gpart = gpart + mm_t(dqkv[here, 2 * local : 3 * local], weights[2])
    if layer == 0:
        rows = expand(st.rows[0][here].astype(F32))
        add_sums(st, name, at + 2 * local, gpart * rows * inv_rms(rows), fresh)
    st.part[here] = gpart.astype(BF16)
    if layer:
        made[0][...] = gpart.astype(BF16)
    elif half == 0:
        away = pl.ds(pl.multiple_of((1 - meta[1]) * count, 16), count)
        made[0][...] = st.part[away]
        row = name
        made[1][...] = st.sums[row : row + 1, at + 2 * local : at + 2 * local + width]
        own = pl.ds(pl.multiple_of(meta[1] * count, 16), count)
        sems = refs[0]
        copies = []
        for n, ref in enumerate((st.part, st.rows[0], st.grad, st.mid[1])):
            copies.append(pltpu.make_async_copy(ref.at[own], made[3 + n], sems.at[n]))
            copies[-1].start()
        for side in range(2):

            @pl.when(meta[1] == side)
            def _():
                pltpu.make_async_copy(far[1 - side], made[2], sems.at[4]).start()
                pltpu.make_async_copy(far[side], made[7], sems.at[5]).start()

        copies.append(pltpu.make_async_copy(far[0], made[2], sems.at[4]))
        copies.append(pltpu.make_async_copy(far[0], made[7], sems.at[5]))
        for copy in copies:
            copy.wait()


def mlp_weights_kernel(layer, meta, near, far, made, st, *refs):
    width, hidden = st.up[0].shape
    if far:
        active, load_sems = refs
        count = far[0].shape[0]
        loads = [
            pltpu.make_async_copy(ref, active.at[pl.ds(at * count, count)], load_sems.at[at]) for at, ref in enumerate(far)
        ]
        for load in loads:
            load.start()
    else:
        active, loads = st.act, []
    block = made[0].shape[1]
    for out, part in ((made[1], 1 - meta[0]), (made[0], meta[0])):
        rows = width // 2
        left = st.low_normed[layer][:, pl.ds(pl.multiple_of(part * rows, LANES), rows)]
        for n in range(hidden // block):
            out[n * rows : (n + 1) * rows] = t_mm(left, st.hid[:, n * block : (n + 1) * block]).astype(BF16)
        base = hidden // block * rows
        rows = hidden // 2
        while loads:
            loads.pop().wait()
        left = active[:, pl.ds(pl.multiple_of(part * rows, LANES), rows)]
        for n in range(width // block):
            total = t_mm(left, st.low[:, n * block : (n + 1) * block])
            out[base + n * rows : base + (n + 1) * rows] = total.astype(BF16)


def attn_weights_kernel(layer, extra, meta, near, far, made, st):
    width, local = st.attn[0].shape[1:]
    hidden = st.up[0].shape[1]
    piece = made[0].shape[0] // 8 - extra

    def put(out, first, total):
        for at in range(0, total.shape[0], piece):
            where = (first + at) // piece * (piece + extra)
            out[where : where + piece] = total[at : at + piece].astype(BF16)

    if extra:
        sums = st.sums
        rows = [sums[row : row + 1] for row in range(4)]
        smalls = []
        tail = 2 * width + 2 * local
        for gain, attn, mlp in (
            (rows[ATTN0][:, tail : tail + width] + near[0][...], rows[ATTN0], rows[MLP0]),
            (rows[MLP0][:, width + hidden : 2 * width + hidden], rows[ATTN1], rows[MLP1]),
        ):
            row = [gain, attn[:, 2 * width : tail], attn[:, width : 2 * width], attn[:, :width]]
            row += [mlp[:, width : width + hidden], mlp[:, :width]]
            lines = [part[:, at : at + local] for part in row for at in range(0, part.shape[1], local)]
            lines += [jnp.zeros((1, local), F32)] * (extra - len(lines))
            smalls.append(jnp.concatenate(lines, axis=0))

    for out, part in ((made[1], 1 - meta[0]), (made[0], meta[0])):
        rows = width // 2
        cols = pl.ds(pl.multiple_of(part * rows, LANES), rows)
        left = st.normed[layer][:, cols]
        for at in range(3):
            put(out, at * rows, t_mm(left, st.hid[:, at * local : (at + 1) * local]))
        put(out, 3 * rows, t_mm(st.att[layer][...], st.low[:, cols]))
        if extra:
            out[piece : piece + extra] = jnp.where(part == 0, smalls[0], smalls[1]).astype(BF16)
            for at in range(1, 8):
                where = at * (piece + extra) + piece
                out[where : where + extra] = jnp.zeros((extra, local), BF16)


def close_kernel(meta, vec_own, vec_other, grad_far, out_far, out_own, part, rows, grad, middle, result, grad_in, *refs):
    width = part.shape[1]

    *vecs, sems = refs
    for layer in range(2):
        pick(meta, layer, vec_own.at[pl.ds(0, 8)], vec_other.at[pl.ds(0, 8)], vecs[layer], sems.at[layer])
    for layer in range(2):
        done(vec_own.at[pl.ds(0, 8)], vecs[layer], sems.at[layer])

    def vec(layer, row):
        return vecs[layer][row : row + 1, :width]

    branch = out_own[...].astype(F32) + out_far[...].astype(F32) + vec(1, DOWN_BIAS)
    result[...] = (middle[...] + center(branch)).astype(BF16)
    rows = expand(rows[...].astype(F32))
    given = part[...].astype(F32) + grad_far[...].astype(F32)
    pulled, _ = norm_pull(rows, inv_rms(rows), vec(0, ATTN_GAIN), given)
    total = grad[...] + pulled
    grad_in[...] = (total - total[:, width - 1 :]).astype(BF16)


def place_kernel(kinds, extra, meta, *refs):
    refs = list(refs)
    sources = take(refs, 4)
    outs = refs[:-2]
    wide, sems = refs[-2:]
    piece = wide.shape[1]

    def copy(n):
        part = meta[0] if n < 8 else 1 - meta[0]
        which, where = kinds[n % 8]
        return pltpu.make_async_copy(wide.at[n], outs[which].at[where(part)], sems.at[n])

    for layer in range(2):

        @pl.when(meta[0] == layer)
        def _():
            step = piece + (0 if layer else extra)
            for n in range(16):
                place = meta[6 + n // 8] & 6 if extra and layer == 0 else meta[6 + n // 8]
                at = pl.multiple_of(((n % 8) ^ place) * step, 16)
                wide[n] = sources[2 * (n // 8) + layer][pl.ds(at, piece)].astype(F32)
                copy(n).start()

    if extra:
        at = pl.multiple_of((meta[6] & 6) * (piece + extra) + piece, 16)
        small = sources[0][pl.ds(at, extra)].astype(F32)
        at = 0
        for out in outs[2:]:
            for row in range(out.shape[0]):
                for col in range(0, out.shape[1], small.shape[1]):
                    out[row : row + 1, col : col + small.shape[1]] = small[at : at + 1]
                    at += 1
    for n in range(16):
        copy(n).wait()


def shape(dims, dtype=BF16):
    return jax.ShapeDtypeStruct(dims, dtype)


def call(kernel, in_specs, outs, scratch, args, out_specs, limit=VMEM_BYTES):
    return pl.pallas_call(
        kernel,
        out_shape=tuple(outs),
        in_specs=in_specs,
        out_specs=tuple(out_specs),
        scratch_shapes=scratch,
        compiler_params=pltpu.CompilerParams(vmem_limit_bytes=limit),
        cost_estimate=pl.CostEstimate(flops=1, bytes_accessed=1, transcendentals=0),
    )(*args)


def swap(array, axis):
    return lax.ppermute(array, axis, [(0, 1), (1, 0)])


def halve_kernel(step, sides, mine, other, *outs):
    rows = mine.shape[0] // len(outs)
    for at, out in enumerate(outs):
        here = slice(None)
        if len(outs) == 2:
            side = sides[step] if at == 0 else 1 - sides[step]
            here = pl.ds(pl.multiple_of(side * rows, 16), rows)
        out[...] = (mine[here].astype(F32) + other[here].astype(F32)).astype(BF16)


def join_kernel(first, second, out):
    rows = first.shape[0]
    out[:rows] = first[...]
    out[rows:] = second[...]


def in_vmem(*arrays):
    return [pltpu.with_memory_space_constraint(a, pltpu.VMEM) for a in arrays]


def add_halves(step, sides, mine, other):
    rows, width = mine.shape
    halves = 1 if step is None else 2
    if rows // halves % 16:
        both = (mine.astype(F32) + other.astype(F32)).astype(BF16)
        if halves == 1:
            return [both]
        return [lax.dynamic_slice_in_dim(both, at * (rows // 2), rows // 2, 0) for at in (sides[step], 1 - sides[step])]
    outs = [pltpu.VMEM((rows // halves, width), BF16)] * halves
    kernel = functools.partial(halve_kernel, step)
    return call(kernel, [SMEM, VMEM, VMEM], outs, [], [sides, *in_vmem(mine, other)], [VMEM] * halves)


def join(first, second):
    rows, width = first.shape
    if rows % 16:
        return jnp.concatenate([first, second], axis=0)
    outs = [pltpu.VMEM((2 * rows, width), BF16)]
    return call(join_kernel, [VMEM, VMEM], outs, [], in_vmem(first, second), [VMEM])[0]


SWAP, HALVE, ADD, JOIN = range(4)


class GroupSum:
    def __init__(self, sides, whole, mine, theirs):
        self.sides = sides
        self.held, self.received = mine, theirs
        self.steps = list(zip(*self.orders(lax.axis_size(GROUPS).bit_length() - 1)))
        self.whole = whole
        count = len(self.steps)
        self.todo = [(SWAP, None)] + [(HALVE, k) for k in range(count - 1)]
        if whole:
            self.todo += [(ADD, count - 1), (ADD, count - 2)] + [(JOIN, k) for k in range(count - 3, -1, -1)]
        else:
            self.todo += [(HALVE, count - 1), (ADD, count - 1)] + [(JOIN, k) for k in range(count - 2, -1, -1)]

    def make(self):
        kind, at = self.todo[0]
        if kind == SWAP:
            return [self.held, self.received]
        if kind == JOIN:
            return [join(self.held, self.received)]
        return list(add_halves(at if kind == HALVE else None, self.sides, self.held, self.received))

    def send(self, arrays):
        kind, at = self.todo.pop(0)
        self.held = arrays[0]
        self.received = swap(arrays[-1], SECTION) if kind == SWAP else self.exchange(arrays[-1], self.steps[at])

    @staticmethod
    def orders(bits):
        first = list(range(bits))
        second = [1, 0] + first[2:] if bits > 1 else first
        return first, second

    @staticmethod
    def exchange(array, bits):
        count = lax.axis_size(GROUPS)
        pairs = [(core * count + i, core * count + (i ^ (1 << bit))) for core, bit in enumerate(bits) for i in range(count)]
        return lax.ppermute(array, (SECTION, GROUPS), pairs)

    @staticmethod
    def which_side(bits):
        core, index = lax.axis_index(SECTION), lax.axis_index(GROUPS)
        return jnp.stack([(index >> jnp.where(core == 0, *pair)) & 1 for pair in zip(*GroupSum.orders(bits))])

    @staticmethod
    def place(bits, core):
        index = lax.axis_index(GROUPS)
        out = jnp.int32(0)
        for first, second in zip(*GroupSum.orders(bits)):
            out = out * 2 + ((index >> jnp.where(core == 0, first, second)) & 1)
        return out


def boundary(values, flows, after=()):
    flows = [flow for flow in flows if flow.todo]
    arrived = [flow for flow in flows if flow.todo[0][0] != SWAP]
    values = list(values)
    got = lax.optimization_barrier((*values, *[flow.received for flow in arrived], *after))
    values = list(got[: len(values)])
    for flow, received in zip(arrived, got[len(values) :]):
        flow.received = received
    arrays = [flow.make() for flow in flows]
    got = list(lax.optimization_barrier((*values, *[a for group in arrays for a in group])))
    values = take(got, len(values))
    for flow, group in zip(flows, arrays):
        flow.send(take(got, len(group)))
    return values


def in_order(array, place, count):
    blocks = array.reshape((count, array.shape[0] // count) + array.shape[1:])
    return jnp.take(blocks, jnp.arange(count, dtype=jnp.int32) ^ place, axis=0).reshape(array.shape)


def local(
    inputs,
    doc_lengths,
    attn_gain,
    qkv_weight,
    qv_bias,
    out_weight,
    out_bias,
    mlp_gain,
    up_weight,
    up_bias,
    down_weight,
    down_bias,
    cotangent,
):
    core = lax.axis_index(SECTION)
    side = lax.axis_index(TENSOR)
    groups = lax.axis_size(GROUPS)
    bits = groups.bit_length() - 1
    place = GroupSum.place(bits, core)
    rows = inputs.shape[1]
    width = attn_gain.shape[1]
    heads = qkv_weight.shape[3]
    hidden = up_weight.shape[2]
    pairs = heads // LANES
    chunk = hidden // 2
    extra = 16

    def own_rows(array):
        mine = lax.dynamic_index_in_dim(jnp.transpose(array, (2, 0, 1)), core, 1, keepdims=False)
        return jnp.pad(mine, ((0, width - mine.shape[0]), (0, 0)))

    lengths = lax.dynamic_index_in_dim(doc_lengths[:, 0, :], core, 0, keepdims=False)
    if groups == 8:
        places = [place, GroupSum.place(bits, 1 - core)]
    else:
        places = [jnp.int32(0)] * 2
    meta = jnp.concatenate([jnp.stack([core, side]).astype(jnp.int32), lengths, jnp.stack(places)])
    def each(*dims, dtype=BF16):
        return (shape(dims, dtype),) * 2

    unit = 2 * rows
    layer_probs = (shape((pairs, unit, rows)), shape((pairs, unit, unit)))
    bench = Bench(
        meta,
        State(
            vec=each(8, hidden, dtype=F32),
            attn=each(4, width, heads),
            up=each(width, hidden),
            down=each(hidden, width),
            rows=each(unit, width),
            normed=each(unit, width),
            low_normed=each(unit, width),
            query=each(unit, heads),
            kv=each(unit, 2 * heads),
            att=each(unit, heads),
            probs=(layer_probs, layer_probs),
            mid=each(unit, width, dtype=F32),
            act=shape((unit, hidden)),
            hid=shape((unit, hidden)),
            part=shape((unit, width)),
            cot=shape((unit, width)),
            low=shape((unit, width)),
            grad=shape((unit, width), F32),
            sums=shape((8, 3 * width + 2 * heads), F32),
        ),
    )
    sides = GroupSum.which_side(bits)

    entry = own_rows(inputs)
    small_in = (attn_gain, qv_bias[0], out_bias, mlp_gain, up_bias, down_bias)
    qkv, out = jnp.transpose(qkv_weight[0], (1, 0, 2)), out_weight[0]
    (vectors,) = call(
        pack_kernel,
        [HBM] * len(small_in),
        [pltpu.HBM((512, hidden), F32)],
        [
            pltpu.VMEM((8, hidden), F32),
            *[pltpu.VMEM(a.shape, F32) for a in small_in],
            pltpu.SemaphoreType.DMA((len(small_in),)),
        ],
        [pltpu.with_memory_space_constraint(a, pltpu.HBM) for a in small_in],
        [HBM],
    )
    far = swap(entry, TENSOR)
    vec_pair = (vectors, swap(vectors, SECTION))
    attn_pair = (qkv, swap(qkv, SECTION), out, swap(out, SECTION))
    cots, _ = lax.optimization_barrier((cotangent, vectors))
    cots = own_rows(cots)
    *attn_pair, cots = lax.optimization_barrier((*attn_pair, cots))
    far, cots, down = lax.optimization_barrier((far, cots, down_weight[0]))
    entry = (entry, far)
    up = up_weight[0]
    up_pair = (up, swap(up, SECTION))
    down_pair = (down, swap(down, SECTION))
    cots = (cots, swap(cots, TENSOR))

    bench.run(open_kernel, hbm_ins=[*vec_pair, *attn_pair], scratch=[pltpu.SemaphoreType.DMA((5,))], first=True)
    sent = (True, (rows, width), BF16)
    partial = functools.partial

    given = [None, None]
    for half in range(2):
        (part,) = bench.run(partial(attn_forward_kernel, 0, half), entry, [sent])
        given[half] = swap(part, TENSOR)
    *down_pair, cot_far = lax.optimization_barrier((*down_pair, cots[1]))
    cots = (cots[0], cot_far)
    bench.run(load_kernel, hbm_ins=[*attn_pair, *up_pair, *down_pair], scratch=[pltpu.SemaphoreType.DMA((7,))])
    acts, slopes = [], []
    for half in range(2):
        outs = [sent] + [(False, (rows, hidden), BF16)] * 2
        scratch = [pltpu.VMEM((2, rows, hidden), BF16), pltpu.SemaphoreType.DMA((2,))]
        part, *kept = bench.run(partial(mlp_forward_kernel, chunk, half), [given[half]], outs, scratch=scratch)
        given[half] = swap(part, TENSOR)
        acts.append(kept[0])
        slopes.append(kept[1])
    for half in range(2):
        (part,) = bench.run(partial(attn_forward_kernel, 1, half), [given[half]], [sent])
        given[half] = swap(part, TENSOR)
    mlp_parts = []
    kept = (False, (rows, width), BF16)
    for half in range(2):
        scratch = [pltpu.VMEM((rows, width), BF16), pltpu.SemaphoreType.DMA]
        body = partial(mlp_both_kernel, chunk, half)
        part, mlp_part = bench.run(body, [given[half], *cots], [sent, kept], scratch=scratch)
        given[half] = swap(part, TENSOR)
        mlp_parts.append(mlp_part)

    def weights(kernel, dims):
        ins = [gain_far] if kernel is attn_weights_kernel and dims[0] % (8 * 192) else []
        layer = 0 if ins or kernel is mlp_weights_kernel and mlp1 is not None else 1
        body = partial(kernel, layer) if kernel is mlp_weights_kernel else partial(kernel, layer, extra if ins else 0)
        far = acts if kernel is mlp_weights_kernel and layer == 0 else []
        scratch = [pltpu.VMEM((2 * rows, hidden), BF16), pltpu.SemaphoreType.DMA((2,))] if far else []
        return GroupSum(sides, bool(ins), *bench.run(body, ins, [(True, dims, BF16)] * 2, far, scratch))

    mlp_dims = (hidden * width // 384, 384)
    attn_dims = (2 * width * heads // 384, 384)
    mlp1 = None
    bench.follow(given)
    mlp1 = weights(mlp_weights_kernel, mlp_dims)
    early = (True, (rows, 2 * heads), F32)
    for half in (1, 0):
        (given[half],) = boundary([given[half]], [mlp1], () if half else [part])
        ins, outs = ([given[1]], [sent, early]) if half else ([given[0], link], [sent])
        part, *rest = bench.run(partial(attn_backward_kernel, 1, half), ins, outs)
        link = rest[0] if half else None
        given[half] = swap(part, TENSOR)
    attn1 = weights(attn_weights_kernel, attn_dims)
    for half in (1, 0):
        if half:
            given[1], attn1.held, attn1.received = lax.optimization_barrier((given[1], attn1.held, attn1.received))
        else:
            (given[0],) = boundary([given[0]], [mlp1, attn1], [part])
        scratch = [pltpu.VMEM((rows, hidden), BF16), pltpu.SemaphoreType.DMA]
        body = partial(mlp_backward_kernel, chunk, half)
        (part,) = bench.run(body, [given[half]], [sent], [slopes[half]], scratch)
        given[half] = swap(part, TENSOR)
    mlp0 = weights(mlp_weights_kernel, mlp_dims)
    (given[1],) = boundary([given[1]], [mlp1, attn1, mlp0], [part])
    (link,) = bench.run(partial(attn_backward_kernel, 0, 1), [given[1]], [early])
    given[0], link = boundary([given[0], link], [mlp0])
    given[0], link = boundary([given[0], link], [mlp1, attn1])
    own = [(False, (rows, width), dtype) for dtype in (BF16, BF16, F32, F32)]
    outs = [sent, (True, (1, width), F32), sent, *own, sent]
    body = partial(attn_backward_kernel, 0, 0)
    scratch = [pltpu.SemaphoreType.DMA((6,))]
    away_grad, gain, away_out, *own = bench.run(body, [given[0], link], outs, mlp_parts, scratch)
    (gain_far,) = boundary([swap(gain, TENSOR)], [attn1], [gain])
    gain_far, away_grad, away_out = lax.optimization_barrier((gain_far, away_grad, away_out))
    backs = [swap(away_grad, TENSOR), swap(away_out, TENSOR)]
    attn0 = weights(attn_weights_kernel, (attn_dims[0] + 8 * extra, 384))

    token = [meta]

    def end(flow):
        while flow.todo:
            token[:] = boundary(token, [flow])
        token[0], *pieces = lax.optimization_barrier((token[0], flow.held, flow.received))
        whole = join(*pieces)
        if groups != 8:
            split = groups // 2 if flow.whole else groups
            whole = in_order(whole, place // (groups // split), split)
        token[0], whole = lax.optimization_barrier((token[0], whole))
        return whole, swap(whole, SECTION)

    def close(back_grad, back_out):
        args = [*in_vmem(back_grad, back_out, own[-1]), *own[:-1]]
        specs = [SMEM, HBM, HBM] + [VMEM] * len(args)
        scratch = [pltpu.VMEM((8, hidden), F32)] * 2 + [pltpu.SemaphoreType.DMA((2,))]
        outs = [shape((rows, width))] * 2
        return call(close_kernel, specs, outs, scratch, [token[0], *vec_pair, *args], [VMEM] * 2, 2 * VMEM_BYTES)

    token[:] = boundary(token, [mlp0, attn0], [mlp1.received])
    token[:] = boundary(token, [attn0, mlp0, mlp1], [attn1.received])
    token[0], *backs = lax.optimization_barrier((token[0], *backs))
    token[:] = boundary(token, [attn0, mlp0, attn1, mlp1])
    result, grad_in = close(*backs)
    result, grad_in = result[:, : width - 1], grad_in[:, : width - 1]
    token[0], result, grad_in = lax.optimization_barrier((token[0], result, grad_in))
    token[:] = boundary(token, [attn0, mlp0, attn1])
    token[:] = boundary(token, [attn0, mlp0, attn1], [mlp1.received])
    mlp1 = end(mlp1)
    token[:] = boundary(token, [attn0])
    token[0], attn1.received = lax.optimization_barrier((token[0], attn1.received))
    mlp0 = end(mlp0)
    attn1 = end(attn1)
    while attn0.todo:
        token[:] = boundary(token, [attn0])

    up_rows, down_rows = width // 2, hidden // 2

    def mlp_kind(block):
        if block < 4:
            return 0, lambda part: (pl.ds(pl.multiple_of(part * up_rows, 8), up_rows), pl.ds(block * 384, 384))
        col, row = (block - 4) // 2, (block - 4) % 2
        return 1, lambda part: (
            pl.ds(pl.multiple_of(part * down_rows + row * 384, 8), 384),
            pl.ds(col * 384, 384),
        )

    def attn_kind(block):
        which, row = block // 2, block % 2
        if which < 3:
            return 0, lambda part: (which, pl.ds(pl.multiple_of(part * up_rows + row * 192, 8), 192), slice(None))
        return 1, lambda part: (pl.ds(row * 192, 192), pl.ds(pl.multiple_of(part * 384, 128), 384))

    def placed(kinds, extra_rows, first, second, outs):
        piece = first[0].shape[0] // 8 - extra_rows
        args = [token[0], first[0], second[0], first[1], second[1]]
        scratch = [pltpu.VMEM((16, piece, 384), F32), pltpu.SemaphoreType.DMA((16,))]
        out_specs = [HBM, HBM] + [VMEM] * (len(outs) - 2)
        kernel = functools.partial(place_kernel, kinds, extra_rows)
        args[1:] = in_vmem(*args[1:])
        return call(kernel, [SMEM] + [VMEM] * 4, outs, scratch, args, out_specs, 2 * VMEM_BYTES)

    grad_up, grad_down = placed(
        [mlp_kind(b) for b in range(8)],
        0,
        mlp0,
        mlp1,
        [shape((width, hidden), F32), shape((hidden, width), F32)],
    )
    token[0], grad_up, grad_down = lax.optimization_barrier((token[0], grad_up, grad_down))
    attn0 = end(attn0)
    grad_qkv, grad_out, *small = placed(
        [attn_kind(b) for b in range(8)],
        extra,
        attn0,
        attn1,
        [shape((3, width, heads), F32), shape((heads, width), F32)]
        + [shape(dims, F32) for dims in ((1, width), (2, heads), (1, width), (1, width), (1, hidden), (1, width))],
    )

    return (
        result[None],
        grad_in[None],
        small[0],
        jnp.transpose(grad_qkv, (1, 0, 2))[None],
        small[1][None],
        grad_out[None],
        small[2],
        small[3],
        grad_up[None],
        small[4],
        grad_down[None],
        small[5],
    )


def solution(mesh):
    in_specs = (
        P(None, (GROUPS, TENSOR), None),
        P(None, GROUPS, None),
        P(SECTION, None),
        P(SECTION, None, None, TENSOR),
        P(SECTION, None, TENSOR),
        P(SECTION, TENSOR, None),
        P(SECTION, None),
        P(SECTION, None),
        P(SECTION, None, TENSOR),
        P(SECTION, TENSOR),
        P(SECTION, TENSOR, None),
        P(SECTION, None),
        P(None, (GROUPS, TENSOR), None),
    )
    out_specs = (
        P(SECTION, (GROUPS, TENSOR), None),
        P(SECTION, (GROUPS, TENSOR), None),
        P(SECTION, None),
        P(SECTION, None, None, TENSOR),
        P(SECTION, None, TENSOR),
        P(SECTION, TENSOR, None),
        P(SECTION, None),
        P(SECTION, None),
        P(SECTION, None, TENSOR),
        P(SECTION, TENSOR),
        P(SECTION, TENSOR, None),
        P(SECTION, None),
    )
    return jax.shard_map(local, mesh=mesh, in_specs=in_specs, out_specs=out_specs, check_vma=False)
```
